32 devices in a mesh: dp: 4 (over z), tensor: 8 (over y, x, core).
Axes of the slice: x: 2, y: 2, z: 4, core: 2. Of those that a mesh axis runs over, the one named last changes fastest.
Arguments:
- tokens: bfloat16 [8192, 1024], P(('dp', 'tensor')), may hold values from -6 to 6
- out_grad: bfloat16 [8192, 1024], P(('dp', 'tensor')), may hold values from -6 to 6
- doc_lengths: int32 [32, 4], P(('dp', 'tensor')), may hold values from 0 to 256, as said below
- w_qkv: bfloat16 [1024, 3072], P(('dp', 'tensor')), may hold values from -0.1875 to 0.1875
- w_out: bfloat16 [1024, 1024], P(('dp', 'tensor')), may hold values from -0.1875 to 0.1875
- gains: float32 [1024, 3], P(('dp', 'tensor')), may hold values from 0.25 to 1.75
- biases: float32 [1024, 7], P(('dp', 'tensor')), may hold values from -3 to 3
- head_scale: float32 [16], replicated, may hold values from 0.5 to 2
- w_fc1: bfloat16 [1024, 4096], P('dp', 'tensor'), may hold values from -0.1875 to 0.1875
- w_fc2: bfloat16 [4096, 1024], P('tensor', 'dp'), may hold values from -0.09375 to 0.09375
- mid_gain: float32 [4096], P('tensor'), may hold values from 0.25 to 1.75
- ffn_biases: float32 [2, 4096], P(None, 'tensor'), may hold values from -3 to 3
Outputs:
- mixed_out: bfloat16 [8192, 1024], P(('dp', 'tensor'))
- token_grad: float32 [8192, 1024], P(('dp', 'tensor'))
- qkv_grad: float32 [1024, 3072], P(('dp', 'tensor'))
- out_weight_grad: float32 [1024, 1024], P(('dp', 'tensor'))
- gains_grad: float32 [1024, 3], P(('dp', 'tensor'))
- biases_grad: float32 [1024, 7], P(('dp', 'tensor'))
- scale_grad: float32 [16], replicated
- fc1_grad: float32 [1024, 4096], P('dp', 'tensor')
- fc2_grad: float32 [4096, 1024], P('tensor', 'dp')
- mid_gain_grad: float32 [4096], P('tensor')
- ffn_bias_grad: float32 [2, 4096], P(None, 'tensor')
The draws below stay inside these ranges and needn't reach their ends.
Inputs may be any that keep to these rules, and one draw needn't show every extreme that they name: `doc_lengths`: each row holds, in order, the lengths of the 4 documents packed into one pack's 256 slots; they sum to 256, a zero length is an empty document, and some pack holds one document of 256 tokens.
All inputs are finite; a program needn't handle non-finite values.
Results may differ from the reference program's by a relative error of at most 0.025.
Values may be sent and summed in bfloat16 or wider, within the bound.
A program may use at most 256 MiB of HBM per device.

```python
import math
import jax
import jax.numpy as jnp
from jax import lax

D = 1024
HEADS = 16
FF = 4096
TOK_DEV = 256
DOCS = 4
PACKS = 32
TOKENS = 8192


def draw_doc_lengths(key, part):
    key = jax.random.fold_in(key, 7)
    cut_key, whole_key, pick_key = jax.random.split(key, 3)
    cut_points = jax.random.randint(cut_key, (PACKS, DOCS - 1), 0, TOK_DEV + 1)
    whole_pack = jax.random.randint(whole_key, (PACKS, 1), 0, 4) == 0
    chosen = jax.random.randint(pick_key, (), 0, PACKS)
    row_index = jnp.arange(PACKS)[:, None]
    whole_pack = jnp.logical_or(whole_pack, row_index == chosen)
    cut_points = jnp.where(whole_pack, TOK_DEV, cut_points)
    cut_points = jnp.sort(cut_points, axis=1).astype(jnp.int32)
    bounds = jnp.concatenate([jnp.zeros((PACKS, 1), jnp.int32), cut_points, jnp.full((PACKS, 1), TOK_DEV, jnp.int32)], axis=1)
    return (bounds[:, 1:] - bounds[:, :-1]).astype(jnp.int32)


def steps_of(own_key, shape, shards, smallest, largest):
    def one(position, blocks):
        heights = jax.random.uniform(jax.random.fold_in(jax.random.fold_in(own_key, 6), position), (blocks,), jnp.float32, smallest / len(shards), largest / len(shards))
        return jnp.repeat(jnp.exp(heights), shape[position] // blocks).reshape((-1,) + (1,) * (len(shape) - position - 1))

    loudness = one(*shards[0])
    for cut in shards[1:]:
        loudness = loudness * one(*cut)
    return loudness


def noise(rng, dims, deviation, most, cuts=(), kind=jnp.bfloat16):
    factor_of = steps_of(rng, dims, cuts, -0.22, 0.18) if cuts else 1.0
    array = jax.random.normal(rng, dims, jnp.float32) * deviation * factor_of
    return jnp.minimum(jnp.maximum(array, -most), most).astype(kind)


def setup_inputs(seed: int = 0) -> dict:
    arg_keys = jax.random.split(jax.random.key(seed), 13)
    tokens = noise(arg_keys[0], (TOKENS, D), 1.0, 6.0, ((0, 32),))
    out_grad = noise(arg_keys[1], (TOKENS, D), 1.0, 6.0, ((0, 32),))
    doc_lengths = draw_doc_lengths(jax.random.fold_in(arg_keys[12], 71), 0)
    w_qkv = noise(arg_keys[3], (D, 3 * D), D ** -0.5, 0.1875, ((0, 32),))
    w_out = noise(arg_keys[4], (D, D), D ** -0.5, 0.1875, ((0, 32),))
    gains = jnp.clip(1.0 + 0.15 * jax.random.normal(arg_keys[5], (D, 3), jnp.float32), 0.25, 1.75)
    biases = noise(arg_keys[6], (D, 7), 0.5, 3.0, ((0, 32),), jnp.float32)
    head_scale = jnp.clip(jnp.exp(jax.random.uniform(arg_keys[7], (HEADS,), jnp.float32, math.log(0.5), math.log(2.0))), 0.5, 2.0)
    w_fc1 = noise(arg_keys[8], (D, FF), D ** -0.5, 0.1875, ((0, 4), (1, 8)))
    w_fc2 = noise(arg_keys[9], (FF, D), FF ** -0.5, 0.09375, ((0, 8), (1, 4)))
    mid_gain = jnp.clip(1.0 + 0.15 * jax.random.normal(arg_keys[10], (FF,), jnp.float32), 0.25, 1.75)
    ffn_biases = noise(arg_keys[11], (2, FF), 0.5, 3.0, ((1, 8),), jnp.float32)
    return {"tokens": tokens, "out_grad": out_grad, "doc_lengths": doc_lengths, "w_qkv": w_qkv, "w_out": w_out, "gains": gains, "biases": biases, "head_scale": head_scale, "w_fc1": w_fc1, "w_fc2": w_fc2, "mid_gain": mid_gain, "ffn_biases": ffn_biases}


EPS = 1e-05
HIGH = lax.Precision.HIGHEST

@jax.custom_vjp
def low(v):
    return lax.optimization_barrier(v.astype(jnp.bfloat16)).astype(jnp.float32)

@jax.custom_vjp
def low_back(v):
    return v

def low_keep(v):
    return (low(v), None)

def low_pass(kept, grad):
    return (grad,)

def back_keep(v):
    return (v, None)

def back_low(kept, grad):
    return (low(grad),)
low.defvjp(low_keep, low_pass)
low_back.defvjp(back_keep, back_low)

def matmul(left, right):
    return jnp.dot(left, right, precision=HIGH)

def layer_norm(values, gain, shift):
    center = lax.optimization_barrier(jnp.mean(values, axis=-1, keepdims=True))
    spread = lax.optimization_barrier(jnp.mean(values * values, axis=-1, keepdims=True)) - center * center
    return (values - center) * lax.rsqrt(spread + EPS) * gain + shift

def document_ids(lengths):
    ends = jnp.cumsum(lengths, axis=-1).astype(jnp.int32)
    places = jnp.arange(TOK_DEV, dtype=jnp.int32)
    return lax.optimization_barrier(jnp.sum((places[None, :, None] >= ends[:, None, :-1]).astype(jnp.int32), axis=-1)).astype(jnp.int32)

def attend_pack(operands):
    query_rows, key_rows, value_rows, doc_ids = operands
    head_dim = D // HEADS
    query_rows = query_rows.reshape(TOK_DEV, HEADS, head_dim)
    key_rows = key_rows.reshape(TOK_DEV, HEADS, head_dim)
    value_rows = value_rows.reshape(TOK_DEV, HEADS, head_dim)
    raw_scores = jnp.einsum('qhd,khd->hqk', query_rows, key_rows, precision=HIGH)
    scores = low_back(raw_scores) * (1.0 / math.sqrt(head_dim))
    places = jnp.arange(TOK_DEV, dtype=jnp.int32)
    allowed = jnp.logical_and(doc_ids[:, None] == doc_ids[None, :], places[None, :] <= places[:, None])
    scores = jnp.where(allowed[None], scores, -1000000000.0)
    row_peak = lax.optimization_barrier(jnp.max(scores, axis=-1, keepdims=True))
    exponent = jnp.exp(scores - row_peak)
    prob_rows = low(exponent / lax.optimization_barrier(jnp.sum(exponent, axis=-1, keepdims=True)))
    return jnp.einsum('hqk,khd->qhd', prob_rows, value_rows, precision=HIGH).reshape(TOK_DEV, D)

def forward(inputs, w_qkv, w_out, gains, biases, head_scale, w_fc1, w_fc2, mid_gain, ffn_biases, doc_ids):
    pack_count = doc_ids.shape[0]
    normed_in = low(layer_norm(inputs, gains[:, 0], biases[:, 0]))
    zero_bias = jnp.zeros((D,), jnp.float32)
    qkv_bias = jnp.concatenate([biases[:, 1], zero_bias, biases[:, 2]])
    projected = low(low_back(matmul(normed_in, w_qkv) + qkv_bias))
    query_rows = projected[:, :D].reshape(pack_count, TOK_DEV, D)
    key_rows = projected[:, D:2 * D].reshape(pack_count, TOK_DEV, D)
    value_rows = projected[:, 2 * D:].reshape(pack_count, TOK_DEV, D)
    attended = lax.map(jax.checkpoint(attend_pack), (query_rows, key_rows, value_rows, doc_ids))
    attended = attended.reshape(pack_count * TOK_DEV, D)
    scaled = low(low_back(attended) * jnp.repeat(head_scale, D // HEADS))
    branch = low_back(matmul(scaled, w_out) + biases[:, 3])
    middle = inputs + layer_norm(branch, gains[:, 1], biases[:, 4])
    normed_mid = low(layer_norm(middle, gains[:, 2], biases[:, 5]))
    hidden_pre = low_back(matmul(normed_mid, w_fc1) + ffn_biases[0])
    hidden = low(layer_norm(jax.nn.gelu(hidden_pre), mid_gain, ffn_biases[1]))
    return middle + matmul(hidden, w_fc2) + biases[:, 6]

def reference(tokens, out_grad, doc_lengths, w_qkv, w_out, gains, biases, head_scale, w_fc1, w_fc2, mid_gain, ffn_biases):
    group_size = min(PACKS, max(1, 4096 // TOK_DEV))
    group_count = PACKS // group_size
    weights = tuple((member.astype(jnp.float32) for member in (w_qkv, w_out, gains, biases, head_scale, w_fc1, w_fc2, mid_gain, ffn_biases)))
    inputs = tokens.astype(jnp.float32).reshape(group_count, group_size * TOK_DEV, D)
    cotangent = out_grad.astype(jnp.float32).reshape(group_count, group_size * TOK_DEV, D)
    lengths = doc_lengths.reshape(group_count, group_size, DOCS)

    def one_group(totals, member):
        block_in, block_grad, block_lengths = member
        doc_ids = document_ids(block_lengths)

        def apply_layer(block, *params):
            return forward(block, *params, doc_ids)
        result, pullback = jax.vjp(apply_layer, block_in, *weights)
        gradients = pullback(block_grad)
        totals = tuple((total + gradient for total, gradient in zip(totals, gradients[1:])))
        return (totals, (result.astype(jnp.bfloat16), gradients[0]))
    initial = tuple((jnp.zeros_like(member) for member in weights))
    totals, (mixed_out, token_grad) = lax.scan(one_group, initial, (inputs, cotangent, lengths))
    return (mixed_out.reshape(TOKENS, D), token_grad.reshape(TOKENS, D), totals[0], totals[1], totals[2], totals[3], totals[4], totals[5], totals[6], totals[7], totals[8])
```

```python
import functools
import math

import jax
import jax.numpy as jnp
from jax import lax
from jax.experimental import pallas as pl
from jax.experimental.pallas import tpu as pltpu
from jax.sharding import PartitionSpec as P

HEADS = 16
FF = 4096


EPS = 1e-05
NEGATIVE = -1000000000.0


def normalize(values):
    center = jnp.mean(values, axis=-1, keepdims=True)
    spread = jnp.mean(values * values, axis=-1, keepdims=True) - center * center
    inverse = lax.rsqrt(spread + EPS)
    return ((values - center) * inverse, inverse)


def normalize_back(grad_normed, normed, inverse):
    first_mean = jnp.mean(grad_normed, axis=-1, keepdims=True)
    second = jnp.mean(grad_normed * normed, axis=-1, keepdims=True)
    return inverse * (grad_normed - first_mean - normed * second)


def block_scores(query_rows, key_rows, doc_ids, row_first, row_last, factor):
    scores = (
        jnp.einsum("qhd,khd->hqk", query_rows, key_rows, preferred_element_type=jnp.float32)
        * factor
    )
    query_pos = jnp.arange(row_first, row_last)
    key_pos = jnp.arange(row_last)
    same_doc = doc_ids[row_first:row_last, None] == doc_ids[None, :row_last]
    allowed = jnp.logical_and(same_doc, key_pos[None, :] <= query_pos[:, None])
    return (jnp.where(allowed[None], scores, NEGATIVE), allowed)


def attend_forward(query_rows, key_rows, value_rows, doc_ids, factor):
    total_rows = query_rows.shape[0]
    block_rows = min(512, total_rows)
    scores, allowed = block_scores(query_rows, key_rows, doc_ids, 0, block_rows, factor)
    row_peak = jnp.max(scores, axis=-1, keepdims=True)
    exponent = jnp.exp(scores - row_peak)
    row_total = jnp.sum(exponent, axis=-1, keepdims=True)
    prob_low = (exponent / row_total).astype(jnp.bfloat16)
    pieces = jnp.einsum("hqk,khd->qhd", prob_low, value_rows, preferred_element_type=jnp.float32)
    sums_log = [row_peak + jnp.log(row_total)]
    return (pieces, sums_log)


def attend_backward(query_rows, key_rows, value_rows, grad_out, doc_ids, sums_log, factor):
    total_rows = query_rows.shape[0]
    block_rows = min(512, total_rows)
    query_parts = []
    grad_keys = jnp.zeros(key_rows.shape, jnp.float32)
    grad_values = jnp.zeros(value_rows.shape, jnp.float32)
    for block_index, row_first in enumerate(range(0, total_rows, block_rows)):
        row_last = row_first + block_rows
        scores, allowed = block_scores(query_rows, key_rows, doc_ids, row_first, row_last, factor)
        prob_rows = jnp.where(allowed[None], jnp.exp(scores - sums_log[block_index]), 0.0)
        prob_low = prob_rows.astype(jnp.bfloat16)
        grad_probs = jnp.einsum(
            "qhd,khd->hqk", grad_out, value_rows, preferred_element_type=jnp.float32
        )
        inner_sum = jnp.sum(prob_rows * grad_probs, axis=-1, keepdims=True)
        grad_scores = (prob_rows * (grad_probs - inner_sum) * factor).astype(jnp.bfloat16)
        query_parts.append(
            jnp.einsum("hqk,khd->qhd", grad_scores, key_rows, preferred_element_type=jnp.float32)
        )
        grad_keys = grad_keys.at[:row_last].add(
            jnp.einsum("hqk,qhd->khd", grad_scores, query_rows, preferred_element_type=jnp.float32)
        )
        grad_values = grad_values.at[:row_last].add(
            jnp.einsum("hqk,qhd->khd", prob_low, grad_out, preferred_element_type=jnp.float32)
        )
    return (query_parts[0], grad_keys, grad_values)


def plain(
    tokens,
    out_grad,
    doc_lengths,
    w_qkv,
    w_out,
    gains,
    biases,
    head_scale,
    w_fc1,
    w_fc2,
    mid_gain,
    ffn_biases,
):
    qkv_full, out_full, gain_full, bias_full = (
        lax.all_gather(w_qkv, ("dp", "tensor"), axis=0, tiled=True),
        lax.all_gather(w_out, ("dp", "tensor"), axis=0, tiled=True),
        lax.all_gather(gains.astype(jnp.bfloat16), ("dp", "tensor"), axis=0, tiled=True).astype(
            gains.dtype
        ),
        lax.all_gather(biases.astype(jnp.bfloat16), ("dp", "tensor"), axis=0, tiled=True).astype(
            biases.dtype
        ),
    )
    fc1_rows, fc2_cols = (
        lax.all_gather(w_fc1, "dp", axis=0, tiled=True),
        lax.all_gather(w_fc2, "dp", axis=1, tiled=True),
    )
    model_width = tokens.shape[1]
    local_rows = tokens.shape[0]
    head_dim = model_width // HEADS
    factor = 1.0 / math.sqrt(head_dim)
    doc_ends = jnp.cumsum(doc_lengths[0])[:-1]
    places = jnp.arange(local_rows)
    doc_ids = jnp.sum((places[:, None] >= doc_ends[None, :]).astype(jnp.int32), axis=1)
    inputs = tokens.astype(jnp.float32)
    normed_one, inverse_one = normalize(inputs)
    normed_in = (normed_one * gain_full[:, 0] + bias_full[:, 0]).astype(jnp.bfloat16)
    zero_bias = jnp.zeros((model_width,), jnp.float32)
    qkv_bias = jnp.concatenate([bias_full[:, 1], zero_bias, bias_full[:, 2]])
    projected = (
        jnp.dot(normed_in, qkv_full, preferred_element_type=jnp.float32) + qkv_bias
    ).astype(jnp.bfloat16)
    query_rows = projected[:, :model_width].reshape(local_rows, HEADS, head_dim)
    key_rows = projected[:, model_width : 2 * model_width].reshape(local_rows, HEADS, head_dim)
    value_rows = projected[:, 2 * model_width :].reshape(local_rows, HEADS, head_dim)
    attended, sums_log = attend_forward(query_rows, key_rows, value_rows, doc_ids, factor)
    attended = attended.reshape(local_rows, model_width)
    scale_wide = jnp.repeat(head_scale, head_dim)
    scaled = (attended * scale_wide).astype(jnp.bfloat16)
    branch = jnp.dot(scaled, out_full, preferred_element_type=jnp.float32) + bias_full[:, 3]
    normed_post, inverse_post = normalize(branch)
    middle = inputs + normed_post * gain_full[:, 1] + bias_full[:, 4]
    normed_two, inverse_two = normalize(middle)
    normed_mid = (normed_two * gain_full[:, 2] + bias_full[:, 5]).astype(jnp.bfloat16)
    gathered = lax.all_gather(normed_mid, "tensor", axis=0, tiled=True)
    hidden_pre = jnp.dot(gathered, fc1_rows, preferred_element_type=jnp.float32) + ffn_biases[0]
    activated, gelu_pull = jax.vjp(jax.nn.gelu, hidden_pre)
    act_sum, act_square = (
        lax.psum(jnp.sum(activated, axis=1).astype(jnp.bfloat16), "tensor").astype(jnp.float32),
        lax.psum(jnp.sum(activated * activated, axis=1).astype(jnp.bfloat16), "tensor").astype(
            jnp.float32
        ),
    )
    center = act_sum / FF
    inverse_mid = lax.rsqrt(act_square / FF - center * center + EPS)[:, None]
    normed_act = (activated - center[:, None]) * inverse_mid
    hidden = (normed_act * mid_gain + ffn_biases[1]).astype(jnp.bfloat16)
    hidden_rows = hidden
    ffn_out = lax.psum_scatter(
        jnp.dot(hidden_rows, fc2_cols, preferred_element_type=jnp.float32).astype(jnp.bfloat16),
        "tensor",
        scatter_dimension=0,
        tiled=True,
    ).astype(jnp.float32)
    shard_rows = lax.all_gather(out_grad, "tensor", axis=0, tiled=True)
    grad_piece = jnp.einsum("rd,fd->rf", shard_rows, fc2_cols, preferred_element_type=jnp.float32)
    hidden_rows = hidden
    fc2_run = jnp.einsum("rf,rd->fd", hidden_rows, shard_rows, preferred_element_type=jnp.float32)
    mid_gain_part = jnp.sum(grad_piece * normed_act, axis=0)
    mid_bias_part = jnp.sum(grad_piece, axis=0)
    grad_normed_act = grad_piece * mid_gain
    first_sum, second_sum = (
        lax.psum(jnp.sum(grad_normed_act, axis=1).astype(jnp.bfloat16), "tensor").astype(
            jnp.float32
        ),
        lax.psum(
            jnp.sum(grad_normed_act * normed_act, axis=1).astype(jnp.bfloat16), "tensor"
        ).astype(jnp.float32),
    )
    grad_act = inverse_mid * (
        grad_normed_act - first_sum[:, None] / FF - normed_act * (second_sum[:, None] / FF)
    )
    grad_pre = gelu_pull(grad_act)[0].astype(jnp.bfloat16)
    fc1_part = jnp.einsum("rd,rf->df", gathered, grad_pre, preferred_element_type=jnp.float32)
    fc1_bias_part = jnp.sum(grad_pre.astype(jnp.float32), axis=0)
    grad_normed_mid = lax.psum_scatter(
        jnp.einsum("rf,df->rd", grad_pre, fc1_rows, preferred_element_type=jnp.float32).astype(
            jnp.bfloat16
        ),
        "tensor",
        scatter_dimension=0,
        tiled=True,
    ).astype(jnp.float32)
    ffn_bias_part = jnp.stack([fc1_bias_part, mid_bias_part])
    fc1_grad, fc2_grad = (
        lax.psum_scatter(
            fc1_part.astype(jnp.bfloat16), "dp", scatter_dimension=0, tiled=True
        ).astype(jnp.float32),
        lax.psum_scatter(
            fc2_run.astype(jnp.bfloat16), "dp", scatter_dimension=1, tiled=True
        ).astype(jnp.float32),
    )
    mid_gain_grad, ffn_bias_grad = lax.psum((mid_gain_part, ffn_bias_part), "dp")
    mixed_out = (middle + ffn_out + bias_full[:, 6]).astype(jnp.bfloat16)
    final_grad = out_grad.astype(jnp.float32)
    grad_middle = final_grad + normalize_back(
        grad_normed_mid * gain_full[:, 2], normed_two, inverse_two
    )
    grad_post = normalize_back(grad_middle * gain_full[:, 1], normed_post, inverse_post).astype(
        jnp.bfloat16
    )
    out_local = jnp.einsum("td,te->de", scaled, grad_post, preferred_element_type=jnp.float32)
    grad_scaled = jnp.einsum("te,de->td", grad_post, out_full, preferred_element_type=jnp.float32)
    scale_local = jnp.sum(
        (grad_scaled * attended).reshape(local_rows, HEADS, head_dim), axis=(0, 2)
    )
    grad_attended = (
        (grad_scaled * scale_wide).astype(jnp.bfloat16).reshape(local_rows, HEADS, head_dim)
    )
    grad_query, grad_keys, grad_values = attend_backward(
        query_rows, key_rows, value_rows, grad_attended, doc_ids, sums_log, factor
    )
    grad_projected = jnp.concatenate(
        [
            grad_query.reshape(local_rows, model_width),
            grad_keys.reshape(local_rows, model_width),
            grad_values.reshape(local_rows, model_width),
        ],
        axis=1,
    ).astype(jnp.bfloat16)
    qkv_local = jnp.einsum(
        "td,te->de", normed_in, grad_projected, preferred_element_type=jnp.float32
    )
    grad_normed_in = jnp.einsum(
        "te,de->td", grad_projected, qkv_full, preferred_element_type=jnp.float32
    )
    token_grad = grad_middle + normalize_back(
        grad_normed_in * gain_full[:, 0], normed_one, inverse_one
    )
    projected_sums = jnp.sum(grad_projected.astype(jnp.float32), axis=0)
    gains_local = jnp.stack(
        [
            jnp.sum(grad_normed_in * normed_one, axis=0),
            jnp.sum(grad_middle * normed_post, axis=0),
            jnp.sum(grad_normed_mid * normed_two, axis=0),
        ],
        axis=1,
    )
    biases_local = jnp.stack(
        [
            jnp.sum(grad_normed_in, axis=0),
            projected_sums[:model_width],
            projected_sums[2 * model_width :],
            jnp.sum(grad_post.astype(jnp.float32), axis=0),
            jnp.sum(grad_middle, axis=0),
            jnp.sum(grad_normed_mid, axis=0),
            jnp.sum(final_grad, axis=0),
        ],
        axis=1,
    )
    qkv_grad, out_weight_grad, gains_grad, biases_grad = (
        lax.psum_scatter(qkv_local, ("dp", "tensor"), scatter_dimension=0, tiled=True),
        lax.psum_scatter(out_local, ("dp", "tensor"), scatter_dimension=0, tiled=True),
        lax.psum_scatter(gains_local, ("dp", "tensor"), scatter_dimension=0, tiled=True),
        lax.psum_scatter(biases_local, ("dp", "tensor"), scatter_dimension=0, tiled=True),
    )
    scale_grad = lax.psum(scale_local, ("dp", "tensor"))
    return (
        mixed_out,
        token_grad,
        qkv_grad,
        out_weight_grad,
        gains_grad,
        biases_grad,
        scale_grad,
        fc1_grad,
        fc2_grad,
        mid_gain_grad,
        ffn_bias_grad,
    )


MESH = pl.DeviceIdType.MESH
ANY = pl.BlockSpec(memory_space=pl.ANY)
IN_VMEM = pl.BlockSpec(memory_space=pltpu.VMEM)


def place():
    z = lax.axis_index("dp")
    t = lax.axis_index("tensor")
    return z, lax.div(t, 4), lax.rem(lax.div(t, 2), 2), lax.rem(t, 2)


def at(z, y, x, c):
    return (z, y * 4 + x * 2 + c)


def greet(partners):
    barrier = pltpu.get_barrier_semaphore()
    for partner in partners:
        pl.semaphore_signal(barrier, inc=1, device_id=partner, device_id_type=MESH)
    pl.semaphore_wait(barrier, len(partners))


class Sends:
    def __init__(self, send_sems, recv_sems):
        self.send_sems, self.recv_sems, self.copies = send_sems, recv_sems, []

    def start(self, src, dst, target):
        index = len(self.copies)
        copy = pltpu.make_async_remote_copy(
            src_ref=src,
            dst_ref=dst,
            send_sem=self.send_sems.at[index],
            recv_sem=self.recv_sems.at[index],
            device_id=target,
            device_id_type=MESH,
        )
        copy.start()
        self.copies.append(copy)
        return copy

    def finish(self):
        for copy in self.copies:
            copy.wait_send()


def gather_kernel(
    nz,
    qkv_ref,
    out_ref,
    vec_ref,
    fc1_ref,
    fc2_ref,
    grad_ref,
    qkv_all,
    out_all,
    vec_all,
    fc1_all,
    fc2_all,
    grad_all,
    local_sems,
    send_sems,
    recv_sems,
):
    z, y, x, c = place()
    to_x, to_y, to_c = at(z, y, 1 - x, c), at(z, 1 - y, x, c), at(z, y, x, 1 - c)
    others = [lax.rem(z + k, nz) for k in range(1, nz)]
    slots = [z] + [lax.rem(z + nz - k, nz) for k in range(1, nz)]
    peers = [at(other, y, x, c) for other in others]
    greet([to_x, to_y, to_c] + peers)
    sends = Sends(send_sems, recv_sems)
    shards = ((qkv_ref, qkv_all), (out_ref, out_all))
    mine = []
    width1, width2 = fc1_ref.shape[0], fc2_ref.shape[1]
    own = [
        (qkv_ref, qkv_all.at[z, y, x, c]),
        (out_ref, out_all.at[z, y, x, c]),
        (vec_ref, vec_all.at[z, y, x, c]),
        (fc1_ref, fc1_all.at[pl.ds(pl.multiple_of(z * width1, width1), width1)]),
        (fc2_ref, fc2_all.at[:, pl.ds(pl.multiple_of(z * width2, width2), width2)]),
        (grad_ref, grad_all.at[y, x, c]),
    ]
    for index, (src, dst) in enumerate(own):
        copy = pltpu.make_async_copy(src, dst, local_sems.at[index])
        copy.start()
        mine.append(copy)

    def halves(ref):
        half = ref.shape[-1] // 2
        return pl.ds(0, half), pl.ds(half, half)

    vec_z = [sends.start(vec_ref, vec_all.at[z, y, x, c], peer) for peer in peers]
    vec_x = [sends.start(vec_ref, vec_all.at[z, y, x, c], to_x)]
    qkv_z = [sends.start(qkv_ref, qkv_all.at[z, y, x, c], peer) for peer in peers]

    def first(src, whole, slot, from_input):
        lo, hi = halves(src)
        one = src if from_input else whole.at[slot, y, x, c]
        return (
            sends.start(one.at[:, lo], whole.at[slot, y, x, c, :, lo], to_x),
            sends.start(one.at[:, hi], whole.at[slot, y, x, c, :, hi], to_y),
        )

    def second(whole, slot):
        lo, hi = halves(whole)
        return (
            sends.start(whole.at[slot, y, :, c, :, lo], whole.at[slot, y, :, c, :, lo], to_y),
            sends.start(whole.at[slot, :, x, c, :, hi], whole.at[slot, :, x, c, :, hi], to_x),
        )

    def third(whole, slot):
        return sends.start(whole.at[slot, :, :, c], whole.at[slot, :, :, c], to_c)

    def wait_all(copies):
        for copy in copies:
            copy.wait_recv()

    def spread(src, whole, arrivals, between):
        stage_a = [first(src, whole, z, True)]
        stage_b = []
        for k in range(1, nz):
            arrivals[k - 1].wait_recv()
            stage_a.append(first(src, whole, slots[k], False))
            if k == 1:
                between()
            if k >= 2:
                wait_all(stage_a[k - 2])
                stage_b.append(second(whole, slots[k - 2]))
        for k in range(len(stage_b), nz):
            wait_all(stage_a[k])
            stage_b.append(second(whole, slots[k]))
        return stage_b

    rest = {}

    def after_qkv_z():
        rest["out_z"] = [sends.start(out_ref, out_all.at[z, y, x, c], peer) for peer in peers]
        rest["fc"] = []
        for peer in peers:
            rest["fc"].append(sends.start(fc1_ref, own[3][1], peer))
            rest["fc"].append(sends.start(fc2_ref, own[4][1], peer))

    for copy in mine[:3]:
        copy.wait()
    qkv_b = spread(qkv_ref, qkv_all, qkv_z, after_qkv_z)
    wait_all(vec_z)
    for k in range(1, nz):
        vec_x.append(
            sends.start(vec_all.at[slots[k], y, x, c], vec_all.at[slots[k], y, x, c], to_x)
        )
    out_b = spread(out_ref, out_all, rest.get("out_z", []), lambda: None)
    wait_all(vec_x)
    vec_y = sends.start(vec_all.at[:, y, :, c], vec_all.at[:, y, :, c], to_y)
    lo, hi = halves(grad_ref)
    grad_a = (
        sends.start(grad_ref.at[:, lo], grad_all.at[y, x, c, :, lo], to_x),
        sends.start(grad_ref.at[:, hi], grad_all.at[y, x, c, :, hi], to_y),
    )
    qkv_c = []
    for k in range(nz):
        wait_all(qkv_b[k])
        qkv_c.append(third(qkv_all, slots[k]))
    vec_y.wait_recv()
    vec_c = sends.start(vec_all.at[:, :, :, c], vec_all.at[:, :, :, c], to_c)
    mine[5].wait()
    wait_all(grad_a)
    grad_b = (
        sends.start(grad_all.at[y, :, c, :, lo], grad_all.at[y, :, c, :, lo], to_y),
        sends.start(grad_all.at[:, x, c, :, hi], grad_all.at[:, x, c, :, hi], to_x),
    )
    out_c = []
    for k in range(nz):
        wait_all(out_b[k])
        out_c.append(third(out_all, slots[k]))
    wait_all(grad_b)
    grad_c = sends.start(grad_all.at[:, :, c], grad_all.at[:, :, c], to_c)
    wait_all(qkv_c + out_c + [vec_c, grad_c] + rest.get("fc", []))
    mine[3].wait()
    mine[4].wait()
    sends.finish()


def gather(nz, w_qkv, w_out, vectors, w_fc1, w_fc2, out_grad):
    def whole(shard, lead):
        return jax.ShapeDtypeStruct(lead + shard.shape, shard.dtype)

    every, plane = (nz, 2, 2, 2), (2, 2, 2)
    count = 4 * (nz - 1) + 5 * 2 * nz + 64
    return pl.pallas_call(
        functools.partial(gather_kernel, nz),
        name="gather",
        out_shape=(
            whole(w_qkv, every),
            whole(w_out, every),
            whole(vectors, every),
            jax.ShapeDtypeStruct((w_fc1.shape[0] * nz, w_fc1.shape[1]), w_fc1.dtype),
            jax.ShapeDtypeStruct((w_fc2.shape[0], w_fc2.shape[1] * nz), w_fc2.dtype),
            whole(out_grad, plane),
        ),
        in_specs=[ANY] * 6,
        out_specs=[ANY] * 6,
        scratch_shapes=[
            pltpu.SemaphoreType.DMA((6,)),
            pltpu.SemaphoreType.DMA((count,)),
            pltpu.SemaphoreType.DMA((count,)),
        ],
        compiler_params=pltpu.CompilerParams(collective_id=1, has_side_effects=True),
    )(w_qkv, w_out, vectors, w_fc1, w_fc2, out_grad)


def spread_kernel(rows_ref, all_ref, local_sem, send_sems, recv_sems):
    z, y, x, c = place()
    to_x, to_y, to_c = at(z, y, 1 - x, c), at(z, 1 - y, x, c), at(z, y, x, 1 - c)
    greet([to_x, to_y, to_c])
    sends = Sends(send_sems, recv_sems)
    half = rows_ref.shape[1] // 2
    lo, hi = pl.ds(0, half), pl.ds(half, half)
    pieces = 4
    rows = rows_ref.shape[0] // pieces
    mine = pltpu.make_async_copy(rows_ref, all_ref.at[y, x, c], local_sem)
    mine.start()
    stage = []
    for k in range(pieces):
        part = pl.ds(k * rows, rows)
        stage.append(
            (
                sends.start(rows_ref.at[part, lo], all_ref.at[y, x, c, part, lo], to_x),
                sends.start(rows_ref.at[part, hi], all_ref.at[y, x, c, part, hi], to_y),
            )
        )
    mine.wait()
    later = []
    for k in range(pieces):
        part = pl.ds(k * rows, rows)
        for copy in stage[k]:
            copy.wait_recv()
        one, two = all_ref.at[y, :, c, part, lo], all_ref.at[:, x, c, part, hi]
        later.append((sends.start(one, one, to_y), sends.start(two, two, to_x)))
    last = []
    for k in range(pieces):
        part = pl.ds(k * rows, rows)
        for copy in later[k]:
            copy.wait_recv()
        all_four = all_ref.at[:, :, c, part]
        last.append(sends.start(all_four, all_four, to_c))
    for copy in last:
        copy.wait_recv()
    sends.finish()


def spread_rows(rows):
    return pl.pallas_call(
        spread_kernel,
        name="spread_rows",
        out_shape=jax.ShapeDtypeStruct((2, 2, 2) + rows.shape, rows.dtype),
        in_specs=[ANY],
        out_specs=ANY,
        scratch_shapes=[
            pltpu.SemaphoreType.DMA,
            pltpu.SemaphoreType.DMA((20,)),
            pltpu.SemaphoreType.DMA((20,)),
        ],
        compiler_params=pltpu.CompilerParams(collective_id=2, has_side_effects=True),
    )(rows)


def sums_kernel(mine_ref, total_ref, pair, got, send_sems, recv_sems):
    z, y, x, c = place()
    to_c = at(z, y, x, 1 - c)
    planes = [at(z, y, 1 - x, c), at(z, 1 - y, x, c), at(z, 1 - y, 1 - x, c)]
    greet([to_c] + planes)
    sends = Sends(send_sems, recv_sems)
    sends.start(mine_ref, got.at[3], to_c).wait_recv()
    pair[...] = mine_ref[...] + got[3]
    arrivals = [sends.start(pair, got.at[k], plane) for k, plane in enumerate(planes)]
    for copy in arrivals:
        copy.wait_recv()
    total_ref[...] = (pair[...] + got[0]) + (got[1] + got[2])
    sends.finish()


def tensor_sums(mine):
    return pl.pallas_call(
        sums_kernel,
        name="tensor_sums",
        out_shape=jax.ShapeDtypeStruct(mine.shape, mine.dtype),
        in_specs=[IN_VMEM],
        out_specs=IN_VMEM,
        scratch_shapes=[
            pltpu.VMEM(mine.shape, mine.dtype),
            pltpu.VMEM((4,) + mine.shape, mine.dtype),
            pltpu.SemaphoreType.DMA((4,)),
            pltpu.SemaphoreType.DMA((4,)),
        ],
        compiler_params=pltpu.CompilerParams(collective_id=3, has_side_effects=True),
    )(mine)


def add_low(left, right):
    return (left.astype(jnp.float32) + right.astype(jnp.float32)).astype(jnp.bfloat16)


def fold_kernel(
    nz,
    pieces,
    first_ref,
    second_ref,
    fc1_ref,
    fc2_ref,
    small_ref,
    first_out,
    second_out,
    fc1_out,
    fc2_out,
    small_out,
    from_core,
    sums,
    from_one,
    from_two,
    got1,
    got2,
    got_small,
    send_sems,
    recv_sems,
):
    z, y, x, c = place()
    to_x, to_y, to_c = at(z, y, 1 - x, c), at(z, 1 - y, x, c), at(z, y, x, 1 - c)
    others = [lax.rem(z + k, nz) for k in range(1, nz)]
    peers = [at(other, y, x, c) for other in others]
    greet([to_x, to_y, to_c] + peers)
    sends = Sends(send_sems, recv_sems)
    width1, width2 = fc1_out.shape[0], fc2_out.shape[1]

    def block1(which):
        return fc1_ref.at[pl.ds(pl.multiple_of(which * width1, width1), width1)]

    def block2(which):
        return fc2_ref.at[:, pl.ds(pl.multiple_of(which * width2, width2), width2)]

    rows = first_ref.shape[3] // pieces
    half = first_ref.shape[4] // 2
    lo, hi = pl.ds(0, half), pl.ds(half, half)
    parts = [pl.ds(k * rows, rows) for k in range(pieces)]
    jobs = [(i, k) for i in range(2) for k in range(pieces)]
    refs, outs = (first_ref, second_ref), (first_out, second_out)
    stage_c = {
        (i, k): sends.start(
            refs[i].at[:, :, 1 - c, parts[k]], from_core.at[i, :, :, parts[k]], to_c
        )
        for i, k in jobs
    }
    far = []
    for k, peer in enumerate(peers):
        far.append(sends.start(small_ref, got_small.at[k], peer))
        far.append(sends.start(block1(others[k]), got1.at[k], peer))
        far.append(sends.start(block2(others[k]), got2.at[k], peer))

    stage_1, stage_2 = {}, {}

    def after_core(i, k):
        part = parts[k]
        stage_c[i, k].wait_recv()
        for yy in range(2):
            for xx in range(2):
                sums[i, yy, xx, part] = add_low(
                    refs[i][yy, xx, c, part], from_core[i, yy, xx, part]
                )
        stage_1[i, k] = (
            sends.start(sums.at[i, :, 1 - x, part, lo], from_one.at[i, :, part, lo], to_x),
            sends.start(sums.at[i, 1 - y, :, part, hi], from_one.at[i, :, part, hi], to_y),
        )

    def after_one(i, k):
        part = parts[k]
        for copy in stage_1[i, k]:
            copy.wait_recv()
        for yy in range(2):
            sums[i, yy, x, part, lo] = add_low(
                sums[i, yy, x, part, lo], from_one[i, yy, part, lo]
            )
        for xx in range(2):
            sums[i, y, xx, part, hi] = add_low(
                sums[i, y, xx, part, hi], from_one[i, xx, part, hi]
            )
        stage_2[i, k] = (
            sends.start(sums.at[i, 1 - y, x, part, lo], from_two.at[i, part, lo], to_y),
            sends.start(sums.at[i, y, 1 - x, part, hi], from_two.at[i, part, hi], to_x),
        )

    def after_two(i, k):
        part = parts[k]
        for copy in stage_2[i, k]:
            copy.wait_recv()
        outs[i][part] = sums[i, y, x, part].astype(jnp.float32) + from_two[i, part].astype(
            jnp.float32
        )

    for n in range(len(jobs) + 2):
        if n < len(jobs):
            after_core(*jobs[n])
        if 1 <= n < len(jobs) + 1:
            after_one(*jobs[n - 1])
        if n >= 2:
            after_two(*jobs[n - 2])
    for copy in far:
        copy.wait_recv()
    own1, own2, small = block1(z)[...].astype(jnp.float32), block2(z)[...].astype(jnp.float32), small_ref[...]
    for k in range(nz - 1):
        own1 = own1 + got1[k].astype(jnp.float32)
        own2 = own2 + got2[k].astype(jnp.float32)
        small = small + got_small[k]
    fc1_out[...] = own1
    fc2_out[...] = own2
    small_out[...] = small
    sends.finish()


def fold(nz, first, second, fc1, fc2, small):
    rows, columns = first.shape[3:]
    low = jnp.bfloat16
    pieces = 2
    count = 5 * 2 * pieces + 3 * (nz - 1)
    out1, out2 = (fc1.shape[0] // nz, fc1.shape[1]), (fc2.shape[0], fc2.shape[1] // nz)
    kept = (jnp.float32,)
    return pl.pallas_call(
        functools.partial(fold_kernel, nz, pieces),
        name="fold",
        out_shape=tuple(
            jax.ShapeDtypeStruct(shape, *kept)
            for shape in ((rows, columns), (rows, columns), out1, out2, small.shape)
        ),
        in_specs=[IN_VMEM] * 5,
        out_specs=[IN_VMEM] * 5,
        scratch_shapes=[
            pltpu.VMEM((2, 2, 2, rows, columns), low),
            pltpu.VMEM((2, 2, 2, rows, columns), low),
            pltpu.VMEM((2, 2, rows, columns), low),
            pltpu.VMEM((2, rows, columns), low),
            pltpu.VMEM((nz - 1,) + out1, low),
            pltpu.VMEM((nz - 1,) + out2, low),
            pltpu.VMEM((nz - 1,) + small.shape, jnp.float32),
            pltpu.SemaphoreType.DMA((count,)),
            pltpu.SemaphoreType.DMA((count,)),
        ],
        compiler_params=pltpu.CompilerParams(
            collective_id=4, has_side_effects=True, vmem_limit_bytes=60 * 2**20
        ),
    )(first, second, fc1, fc2, small)


def total_kernel(
    nz,
    grad_ref,
    small_ref,
    grad_out,
    small_out,
    from_core,
    sums,
    from_one,
    from_two,
    from_far,
    small_sum,
    small_got,
    send_sems,
    recv_sems,
):
    z, y, x, c = place()
    to_x, to_y, to_c = at(z, y, 1 - x, c), at(z, 1 - y, x, c), at(z, y, x, 1 - c)
    others = [lax.rem(z + k, nz) for k in range(1, nz)]
    order = others + [z]
    peers = [at(other, y, x, c) for other in others]
    greet([to_x, to_y, to_c] + peers)
    sends = Sends(send_sems, recv_sems)
    half = grad_ref.shape[-1] // 2
    lo, hi = pl.ds(0, half), pl.ds(half, half)
    stage_c = [
        sends.start(grad_ref.at[which, :, :, 1 - c], from_core.at[which], to_c)
        for which in order
    ]
    small_c = sends.start(small_ref, small_got.at[0], to_c)
    stage_1, stage_2, far = {}, {}, {}

    def after_core(k):
        which = order[k]
        stage_c[k].wait_recv()
        for yy in range(2):
            for xx in range(2):
                sums[which, yy, xx] = add_low(
                    grad_ref[which, yy, xx, c], from_core[which, yy, xx]
                )
        stage_1[k] = (
            sends.start(sums.at[which, :, 1 - x, :, lo], from_one.at[which, :, :, lo], to_x),
            sends.start(sums.at[which, 1 - y, :, :, hi], from_one.at[which, :, :, hi], to_y),
        )

    def after_one(k):
        which = order[k]
        for copy in stage_1[k]:
            copy.wait_recv()
        for yy in range(2):
            sums[which, yy, x, :, lo] = add_low(
                sums[which, yy, x, :, lo], from_one[which, yy, :, lo]
            )
        for xx in range(2):
            sums[which, y, xx, :, hi] = add_low(
                sums[which, y, xx, :, hi], from_one[which, xx, :, hi]
            )
        stage_2[k] = (
            sends.start(sums.at[which, 1 - y, x, :, lo], from_two.at[which, :, lo], to_y),
            sends.start(sums.at[which, y, 1 - x, :, hi], from_two.at[which, :, hi], to_x),
        )

    def after_two(k):
        which = order[k]
        for copy in stage_2[k]:
            copy.wait_recv()
        if k < nz - 1:
            sums[which, y, x] = add_low(sums[which, y, x], from_two[which])
            far[k] = sends.start(sums.at[which, y, x], from_far.at[k], peers[k])

    steps = []
    small_c.wait_recv()
    small_sum[0] = small_ref[...] + small_got[0]
    small_x = sends.start(small_sum.at[0], small_got.at[1], to_x)
    for n in range(nz + 2):
        if n < nz:
            after_core(n)
        if 1 <= n < nz + 1:
            after_one(n - 1)
        if n >= 2:
            after_two(n - 2)
        if n == 1:
            small_x.wait_recv()
            small_sum[1] = small_sum[0] + small_got[1]
            small_y = sends.start(small_sum.at[1], small_got.at[2], to_y)
        if n == 3:
            small_y.wait_recv()
            small_sum[2] = small_sum[1] + small_got[2]
            small_far = [
                sends.start(small_sum.at[2], small_got.at[3 + k], peer)
                for k, peer in enumerate(peers)
            ]
    total = sums[z, y, x].astype(jnp.float32) + from_two[z].astype(jnp.float32)
    for k in range(nz - 1):
        far[k].wait_recv()
        total = total + from_far[k].astype(jnp.float32)
    grad_out[...] = total
    small = small_sum[2]
    for k in range(nz - 1):
        small_far[k].wait_recv()
        small = small + small_got[3 + k]
    small_out[...] = small
    sends.finish()


def total_all(nz, grad, small):
    rows, columns = grad.shape[4:]
    low = jnp.bfloat16
    count = 5 * nz + (nz - 1) + 3 + (nz - 1)
    return pl.pallas_call(
        functools.partial(total_kernel, nz),
        name="total_all",
        out_shape=(
            jax.ShapeDtypeStruct((rows, columns), jnp.float32),
            jax.ShapeDtypeStruct(small.shape, jnp.float32),
        ),
        in_specs=[IN_VMEM] * 2,
        out_specs=[IN_VMEM] * 2,
        scratch_shapes=[
            pltpu.VMEM((nz, 2, 2, rows, columns), low),
            pltpu.VMEM((nz, 2, 2, rows, columns), low),
            pltpu.VMEM((nz, 2, rows, columns), low),
            pltpu.VMEM((nz, rows, columns), low),
            pltpu.VMEM((nz - 1, rows, columns), low),
            pltpu.VMEM((3,) + small.shape, jnp.float32),
            pltpu.VMEM((nz + 2,) + small.shape, jnp.float32),
            pltpu.SemaphoreType.DMA((count,)),
            pltpu.SemaphoreType.DMA((count,)),
        ],
        compiler_params=pltpu.CompilerParams(
            collective_id=5, has_side_effects=True, vmem_limit_bytes=60 * 2**20
        ),
    )(grad, small)


def fused(
    nz,
    tokens,
    out_grad,
    doc_lengths,
    w_qkv,
    w_out,
    gains,
    biases,
    head_scale,
    w_fc1,
    w_fc2,
    mid_gain,
    ffn_biases,
):
    model_width = tokens.shape[1]
    local_rows = tokens.shape[0]
    head_dim = model_width // HEADS
    factor = 1.0 / math.sqrt(head_dim)
    share = gains.shape[0]
    vectors = jnp.concatenate(
        [gains, biases, jnp.zeros((share, 128 - gains.shape[1] - biases.shape[1]), jnp.float32)],
        axis=1,
    )
    qkv_full, out_full, vec_full, fc1_rows, fc2_cols, shard_rows = gather(
        nz, w_qkv, w_out, vectors, w_fc1, w_fc2, out_grad
    )
    qkv_full = qkv_full.reshape(model_width, -1)
    out_full = out_full.reshape(model_width, -1)
    vec_full = vec_full.reshape(model_width, 128)
    shard_rows = shard_rows.reshape(-1, model_width)
    vec_rows = vec_full[:, :10].T
    gain_full = vec_rows[:3]
    bias_full = vec_rows[3:]
    doc_ends = jnp.cumsum(doc_lengths[0])[:-1]
    places = jnp.arange(local_rows)
    doc_ids = jnp.sum((places[:, None] >= doc_ends[None, :]).astype(jnp.int32), axis=1)
    inputs = tokens.astype(jnp.float32)
    normed_one, inverse_one = normalize(inputs)
    normed_in = (normed_one * gain_full[0] + bias_full[0]).astype(jnp.bfloat16)
    zero_bias = jnp.zeros((model_width,), jnp.float32)
    qkv_bias = jnp.concatenate([bias_full[1], zero_bias, bias_full[2]])
    projected = (
        jnp.dot(normed_in, qkv_full, preferred_element_type=jnp.float32) + qkv_bias
    ).astype(jnp.bfloat16)
    query_rows = projected[:, :model_width].reshape(local_rows, HEADS, head_dim)
    key_rows = projected[:, model_width : 2 * model_width].reshape(local_rows, HEADS, head_dim)
    value_rows = projected[:, 2 * model_width :].reshape(local_rows, HEADS, head_dim)
    attended, sums_log = attend_forward(query_rows, key_rows, value_rows, doc_ids, factor)
    attended = attended.reshape(local_rows, model_width)
    scale_wide = jnp.repeat(head_scale, head_dim)
    scaled = (attended * scale_wide).astype(jnp.bfloat16)
    branch = jnp.dot(scaled, out_full, preferred_element_type=jnp.float32) + bias_full[3]
    normed_post, inverse_post = normalize(branch)
    middle = inputs + normed_post * gain_full[1] + bias_full[4]
    normed_two, inverse_two = normalize(middle)
    normed_mid = (normed_two * gain_full[2] + bias_full[5]).astype(jnp.bfloat16)
    gathered = spread_rows(normed_mid).reshape(-1, model_width)
    group_rows = gathered.shape[0]
    hidden_pre = jnp.dot(gathered, fc1_rows, preferred_element_type=jnp.float32) + ffn_biases[0]
    activated, gelu_pull = jax.vjp(jax.nn.gelu, hidden_pre)
    grad_piece = jnp.einsum("rd,fd->rf", shard_rows, fc2_cols, preferred_element_type=jnp.float32)
    grad_normed_act = grad_piece * mid_gain
    row_sums = jnp.stack(
        [
            jnp.sum(activated, axis=1),
            jnp.sum(activated * activated, axis=1),
            jnp.sum(grad_normed_act, axis=1),
            jnp.sum(grad_normed_act * activated, axis=1),
        ]
        + [jnp.zeros((group_rows,), jnp.float32)] * 4
    )
    row_sums = tensor_sums(row_sums) / FF
    center = row_sums[0]
    inverse_mid = lax.rsqrt(row_sums[1] - center * center + EPS)
    first_mean = row_sums[2]
    second_mean = inverse_mid * (row_sums[3] - center * row_sums[2])
    inverse_mid = inverse_mid[:, None]
    normed_act = (activated - center[:, None]) * inverse_mid
    hidden = (normed_act * mid_gain + ffn_biases[1]).astype(jnp.bfloat16)
    ffn_part = jnp.dot(hidden, fc2_cols, preferred_element_type=jnp.float32).astype(jnp.bfloat16)
    fc2_part = jnp.einsum("rf,rd->fd", hidden, shard_rows, preferred_element_type=jnp.float32)
    grad_act = inverse_mid * (
        grad_normed_act - first_mean[:, None] - normed_act * second_mean[:, None]
    )
    grad_pre = gelu_pull(grad_act)[0].astype(jnp.bfloat16)
    fc1_part = jnp.einsum("rd,rf->df", gathered, grad_pre, preferred_element_type=jnp.float32)
    mid_part = jnp.einsum("rf,df->rd", grad_pre, fc1_rows, preferred_element_type=jnp.float32)
    units = fc1_rows.shape[1]
    unit_sums = jnp.concatenate(
        [
            jnp.sum(grad_piece * normed_act, axis=0)[None],
            jnp.sum(grad_pre.astype(jnp.float32), axis=0)[None],
            jnp.sum(grad_piece, axis=0)[None],
            jnp.zeros((5, units), jnp.float32),
        ]
    )
    plane = (2, 2, 2, local_rows, model_width)
    grad_normed_mid, ffn_out, fc1_grad, fc2_grad, unit_sums = fold(
        nz,
        mid_part.astype(jnp.bfloat16).reshape(plane),
        ffn_part.reshape(plane),
        fc1_part.astype(jnp.bfloat16),
        fc2_part.astype(jnp.bfloat16),
        unit_sums,
    )
    mid_gain_grad, ffn_bias_grad = unit_sums[0], unit_sums[1:3]
    mixed_out = (middle + ffn_out + bias_full[6]).astype(jnp.bfloat16)
    final_grad = out_grad.astype(jnp.float32)
    grad_middle = final_grad + normalize_back(
        grad_normed_mid * gain_full[2], normed_two, inverse_two
    )
    grad_post = normalize_back(grad_middle * gain_full[1], normed_post, inverse_post).astype(
        jnp.bfloat16
    )
    out_local = jnp.einsum("td,te->de", scaled, grad_post, preferred_element_type=jnp.float32)
    grad_scaled = jnp.einsum("te,de->td", grad_post, out_full, preferred_element_type=jnp.float32)
    scale_local = jnp.sum(
        (grad_scaled * attended).reshape(local_rows, HEADS, head_dim), axis=(0, 2)
    )
    grad_attended = (
        (grad_scaled * scale_wide).astype(jnp.bfloat16).reshape(local_rows, HEADS, head_dim)
    )
    grad_query, grad_keys, grad_values = attend_backward(
        query_rows, key_rows, value_rows, grad_attended, doc_ids, sums_log, factor
    )
    grad_projected = jnp.concatenate(
        [
            grad_query.reshape(local_rows, model_width),
            grad_keys.reshape(local_rows, model_width),
            grad_values.reshape(local_rows, model_width),
        ],
        axis=1,
    ).astype(jnp.bfloat16)
    qkv_local = jnp.einsum(
        "td,te->de", normed_in, grad_projected, preferred_element_type=jnp.float32
    )
    grad_normed_in = jnp.einsum(
        "te,de->td", grad_projected, qkv_full, preferred_element_type=jnp.float32
    )
    token_grad = grad_middle + normalize_back(
        grad_normed_in * gain_full[0], normed_one, inverse_one
    )
    projected_sums = jnp.sum(grad_projected.astype(jnp.float32), axis=0)
    small = jnp.stack(
        [
            jnp.sum(grad_normed_in * normed_one, axis=0),
            jnp.sum(grad_middle * normed_post, axis=0),
            jnp.sum(grad_normed_mid * normed_two, axis=0),
            jnp.sum(grad_normed_in, axis=0),
            projected_sums[:model_width],
            projected_sums[2 * model_width :],
            jnp.sum(grad_post.astype(jnp.float32), axis=0),
            jnp.sum(grad_middle, axis=0),
            jnp.sum(grad_normed_mid, axis=0),
            jnp.sum(final_grad, axis=0),
            jnp.pad(scale_local, (0, model_width - HEADS)),
        ]
        + [jnp.zeros((model_width,), jnp.float32)] * 5
    )
    weights = jnp.concatenate(
        [qkv_local.astype(jnp.bfloat16), out_local.astype(jnp.bfloat16)], axis=1
    ).reshape(nz, 2, 2, 2, share, -1)
    weight_grad, small = total_all(nz, weights, small)
    index = lax.axis_index("dp") * 8 + lax.axis_index("tensor")
    ours = lax.dynamic_slice(small, (0, index * share), (10, share)).T
    return (
        mixed_out,
        token_grad,
        weight_grad[:, : w_qkv.shape[1]],
        weight_grad[:, w_qkv.shape[1] :],
        ours[:, :3],
        ours[:, 3:],
        small[10, :HEADS],
        fc1_grad,
        fc2_grad,
        mid_gain_grad,
        ffn_bias_grad,
    )


def layer(nz, nt, tokens, out_grad, doc_lengths, w_qkv, *rest):
    if nt == 8 and nz > 1 and w_qkv.shape[0] % 16 == 0:
        return fused(nz, tokens, out_grad, doc_lengths, w_qkv, *rest)
    return plain(tokens, out_grad, doc_lengths, w_qkv, *rest)


def solution(mesh):
    return jax.shard_map(
        functools.partial(layer, mesh.shape["dp"], mesh.shape["tensor"]),
        mesh=mesh,
        in_specs=(
            P(("dp", "tensor"), None),
            P(("dp", "tensor"), None),
            P(("dp", "tensor"), None),
            P(("dp", "tensor"), None),
            P(("dp", "tensor"), None),
            P(("dp", "tensor"), None),
            P(("dp", "tensor"), None),
            P(),
            P("dp", "tensor"),
            P("tensor", "dp"),
            P("tensor"),
            P(None, "tensor"),
        ),
        out_specs=(
            P(("dp", "tensor"), None),
            P(("dp", "tensor"), None),
            P(("dp", "tensor"), None),
            P(("dp", "tensor"), None),
            P(("dp", "tensor"), None),
            P(("dp", "tensor"), None),
            P(),
            P("dp", "tensor"),
            P("tensor", "dp"),
            P("tensor"),
            P(None, "tensor"),
        ),
        check_vma=False,
    )
```

```python
import functools
import math

import jax
import jax.numpy as jnp
from jax import lax
from jax.experimental import pallas as pl
from jax.experimental.pallas import tpu as pltpu
from jax.sharding import PartitionSpec as P

HEADS = 16
FF = 4096


EPS = 1e-05
NEGATIVE = -1000000000.0


def normalize(values):
    center = jnp.mean(values, axis=-1, keepdims=True)
    spread = jnp.mean(values * values, axis=-1, keepdims=True) - center * center
    inverse = lax.rsqrt(spread + EPS)
    return ((values - center) * inverse, inverse)


def normalize_back(grad_normed, normed, inverse):
    first_mean = jnp.mean(grad_normed, axis=-1, keepdims=True)
    second = jnp.mean(grad_normed * normed, axis=-1, keepdims=True)
    return inverse * (grad_normed - first_mean - normed * second)


def block_scores(query_rows, key_rows, doc_ids, row_first, row_last, factor):
    scores = (
        jnp.einsum("qhd,khd->hqk", query_rows, key_rows, preferred_element_type=jnp.float32)
        * factor
    )
    query_pos = jnp.arange(row_first, row_last)
    key_pos = jnp.arange(row_last)
    same_doc = doc_ids[row_first:row_last, None] == doc_ids[None, :row_last]
    allowed = jnp.logical_and(same_doc, key_pos[None, :] <= query_pos[:, None])
    return (jnp.where(allowed[None], scores, NEGATIVE), allowed)


def attend_forward(query_rows, key_rows, value_rows, doc_ids, factor):
    total_rows = query_rows.shape[0]
    block_rows = min(512, total_rows)
    scores, allowed = block_scores(query_rows, key_rows, doc_ids, 0, block_rows, factor)
    row_peak = jnp.max(scores, axis=-1, keepdims=True)
    exponent = jnp.exp(scores - row_peak)
    row_total = jnp.sum(exponent, axis=-1, keepdims=True)
    prob_low = (exponent / row_total).astype(jnp.bfloat16)
    pieces = jnp.einsum("hqk,khd->qhd", prob_low, value_rows, preferred_element_type=jnp.float32)
    sums_log = [row_peak + jnp.log(row_total)]
    return (pieces, sums_log)


def attend_backward(query_rows, key_rows, value_rows, grad_out, doc_ids, sums_log, factor):
    total_rows = query_rows.shape[0]
    block_rows = min(512, total_rows)
    query_parts = []
    grad_keys = jnp.zeros(key_rows.shape, jnp.float32)
    grad_values = jnp.zeros(value_rows.shape, jnp.float32)
    for block_index, row_first in enumerate(range(0, total_rows, block_rows)):
        row_last = row_first + block_rows
        scores, allowed = block_scores(query_rows, key_rows, doc_ids, row_first, row_last, factor)
        prob_rows = jnp.where(allowed[None], jnp.exp(scores - sums_log[block_index]), 0.0)
        prob_low = prob_rows.astype(jnp.bfloat16)
        grad_probs = jnp.einsum(
            "qhd,khd->hqk", grad_out, value_rows, preferred_element_type=jnp.float32
        )
        inner_sum = jnp.sum(prob_rows * grad_probs, axis=-1, keepdims=True)
        grad_scores = (prob_rows * (grad_probs - inner_sum) * factor).astype(jnp.bfloat16)
        query_parts.append(
            jnp.einsum("hqk,khd->qhd", grad_scores, key_rows, preferred_element_type=jnp.float32)
        )
        grad_keys = grad_keys.at[:row_last].add(
            jnp.einsum("hqk,qhd->khd", grad_scores, query_rows, preferred_element_type=jnp.float32)
        )
        grad_values = grad_values.at[:row_last].add(
            jnp.einsum("hqk,qhd->khd", prob_low, grad_out, preferred_element_type=jnp.float32)
        )
    return (query_parts[0], grad_keys, grad_values)


def plain(
    tokens,
    out_grad,
    doc_lengths,
    w_qkv,
    w_out,
    gains,
    biases,
    head_scale,
    w_fc1,
    w_fc2,
    mid_gain,
    ffn_biases,
):
    qkv_full, out_full, gain_full, bias_full = (
        lax.all_gather(w_qkv, ("dp", "tensor"), axis=0, tiled=True),
        lax.all_gather(w_out, ("dp", "tensor"), axis=0, tiled=True),
        lax.all_gather(gains.astype(jnp.bfloat16), ("dp", "tensor"), axis=0, tiled=True).astype(
            gains.dtype
        ),
        lax.all_gather(biases.astype(jnp.bfloat16), ("dp", "tensor"), axis=0, tiled=True).astype(
            biases.dtype
        ),
    )
    fc1_rows, fc2_cols = (
        lax.all_gather(w_fc1, "dp", axis=0, tiled=True),
        lax.all_gather(w_fc2, "dp", axis=1, tiled=True),
    )
    model_width = tokens.shape[1]
    local_rows = tokens.shape[0]
    head_dim = model_width // HEADS
    factor = 1.0 / math.sqrt(head_dim)
    doc_ends = jnp.cumsum(doc_lengths[0])[:-1]
    places = jnp.arange(local_rows)
    doc_ids = jnp.sum((places[:, None] >= doc_ends[None, :]).astype(jnp.int32), axis=1)
    inputs = tokens.astype(jnp.float32)
    normed_one, inverse_one = normalize(inputs)
    normed_in = (normed_one * gain_full[:, 0] + bias_full[:, 0]).astype(jnp.bfloat16)
    zero_bias = jnp.zeros((model_width,), jnp.float32)
    qkv_bias = jnp.concatenate([bias_full[:, 1], zero_bias, bias_full[:, 2]])
    projected = (
        jnp.dot(normed_in, qkv_full, preferred_element_type=jnp.float32) + qkv_bias
    ).astype(jnp.bfloat16)
    query_rows = projected[:, :model_width].reshape(local_rows, HEADS, head_dim)
    key_rows = projected[:, model_width : 2 * model_width].reshape(local_rows, HEADS, head_dim)
    value_rows = projected[:, 2 * model_width :].reshape(local_rows, HEADS, head_dim)
    attended, sums_log = attend_forward(query_rows, key_rows, value_rows, doc_ids, factor)
    attended = attended.reshape(local_rows, model_width)
    scale_wide = jnp.repeat(head_scale, head_dim)
    scaled = (attended * scale_wide).astype(jnp.bfloat16)
    branch = jnp.dot(scaled, out_full, preferred_element_type=jnp.float32) + bias_full[:, 3]
    normed_post, inverse_post = normalize(branch)
    middle = inputs + normed_post * gain_full[:, 1] + bias_full[:, 4]
    normed_two, inverse_two = normalize(middle)
    normed_mid = (normed_two * gain_full[:, 2] + bias_full[:, 5]).astype(jnp.bfloat16)
    gathered = lax.all_gather(normed_mid, "tensor", axis=0, tiled=True)
    hidden_pre = jnp.dot(gathered, fc1_rows, preferred_element_type=jnp.float32) + ffn_biases[0]
    activated, gelu_pull = jax.vjp(jax.nn.gelu, hidden_pre)
    act_sum, act_square = (
        lax.psum(jnp.sum(activated, axis=1).astype(jnp.bfloat16), "tensor").astype(jnp.float32),
        lax.psum(jnp.sum(activated * activated, axis=1).astype(jnp.bfloat16), "tensor").astype(
            jnp.float32
        ),
    )
    center = act_sum / FF
    inverse_mid = lax.rsqrt(act_square / FF - center * center + EPS)[:, None]
    normed_act = (activated - center[:, None]) * inverse_mid
    hidden = (normed_act * mid_gain + ffn_biases[1]).astype(jnp.bfloat16)
    hidden_rows = hidden
    ffn_out = lax.psum_scatter(
        jnp.dot(hidden_rows, fc2_cols, preferred_element_type=jnp.float32).astype(jnp.bfloat16),
        "tensor",
        scatter_dimension=0,
        tiled=True,
    ).astype(jnp.float32)
    shard_rows = lax.all_gather(out_grad, "tensor", axis=0, tiled=True)
    grad_piece = jnp.einsum("rd,fd->rf", shard_rows, fc2_cols, preferred_element_type=jnp.float32)
    hidden_rows = hidden
    fc2_run = jnp.einsum("rf,rd->fd", hidden_rows, shard_rows, preferred_element_type=jnp.float32)
    mid_gain_part = jnp.sum(grad_piece * normed_act, axis=0)
    mid_bias_part = jnp.sum(grad_piece, axis=0)
    grad_normed_act = grad_piece * mid_gain
    first_sum, second_sum = (
        lax.psum(jnp.sum(grad_normed_act, axis=1).astype(jnp.bfloat16), "tensor").astype(
            jnp.float32
        ),
        lax.psum(
            jnp.sum(grad_normed_act * normed_act, axis=1).astype(jnp.bfloat16), "tensor"
        ).astype(jnp.float32),
    )
    grad_act = inverse_mid * (
        grad_normed_act - first_sum[:, None] / FF - normed_act * (second_sum[:, None] / FF)
    )
    grad_pre = gelu_pull(grad_act)[0].astype(jnp.bfloat16)
    fc1_part = jnp.einsum("rd,rf->df", gathered, grad_pre, preferred_element_type=jnp.float32)
    fc1_bias_part = jnp.sum(grad_pre.astype(jnp.float32), axis=0)
    grad_normed_mid = lax.psum_scatter(
        jnp.einsum("rf,df->rd", grad_pre, fc1_rows, preferred_element_type=jnp.float32).astype(
            jnp.bfloat16
        ),
        "tensor",
        scatter_dimension=0,
        tiled=True,
    ).astype(jnp.float32)
    ffn_bias_part = jnp.stack([fc1_bias_part, mid_bias_part])
    fc1_grad, fc2_grad = (
        lax.psum_scatter(
            fc1_part.astype(jnp.bfloat16), "dp", scatter_dimension=0, tiled=True
        ).astype(jnp.float32),
        lax.psum_scatter(
            fc2_run.astype(jnp.bfloat16), "dp", scatter_dimension=1, tiled=True
        ).astype(jnp.float32),
    )
    mid_gain_grad, ffn_bias_grad = lax.psum((mid_gain_part, ffn_bias_part), "dp")
    mixed_out = (middle + ffn_out + bias_full[:, 6]).astype(jnp.bfloat16)
    final_grad = out_grad.astype(jnp.float32)
    grad_middle = final_grad + normalize_back(
        grad_normed_mid * gain_full[:, 2], normed_two, inverse_two
    )
    grad_post = normalize_back(grad_middle * gain_full[:, 1], normed_post, inverse_post).astype(
        jnp.bfloat16
    )
    out_local = jnp.einsum("td,te->de", scaled, grad_post, preferred_element_type=jnp.float32)
    grad_scaled = jnp.einsum("te,de->td", grad_post, out_full, preferred_element_type=jnp.float32)
    scale_local = jnp.sum(
        (grad_scaled * attended).reshape(local_rows, HEADS, head_dim), axis=(0, 2)
    )
    grad_attended = (
        (grad_scaled * scale_wide).astype(jnp.bfloat16).reshape(local_rows, HEADS, head_dim)
    )
    grad_query, grad_keys, grad_values = attend_backward(
        query_rows, key_rows, value_rows, grad_attended, doc_ids, sums_log, factor
    )
    grad_projected = jnp.concatenate(
        [
            grad_query.reshape(local_rows, model_width),
            grad_keys.reshape(local_rows, model_width),
            grad_values.reshape(local_rows, model_width),
        ],
        axis=1,
    ).astype(jnp.bfloat16)
    qkv_local = jnp.einsum(
        "td,te->de", normed_in, grad_projected, preferred_element_type=jnp.float32
    )
    grad_normed_in = jnp.einsum(
        "te,de->td", grad_projected, qkv_full, preferred_element_type=jnp.float32
    )
    token_grad = grad_middle + normalize_back(
        grad_normed_in * gain_full[:, 0], normed_one, inverse_one
    )
    projected_sums = jnp.sum(grad_projected.astype(jnp.float32), axis=0)
    gains_local = jnp.stack(
        [
            jnp.sum(grad_normed_in * normed_one, axis=0),
            jnp.sum(grad_middle * normed_post, axis=0),
            jnp.sum(grad_normed_mid * normed_two, axis=0),
        ],
        axis=1,
    )
    biases_local = jnp.stack(
        [
            jnp.sum(grad_normed_in, axis=0),
            projected_sums[:model_width],
            projected_sums[2 * model_width :],
            jnp.sum(grad_post.astype(jnp.float32), axis=0),
            jnp.sum(grad_middle, axis=0),
            jnp.sum(grad_normed_mid, axis=0),
            jnp.sum(final_grad, axis=0),
        ],
        axis=1,
    )
    qkv_grad, out_weight_grad, gains_grad, biases_grad = (
        lax.psum_scatter(qkv_local, ("dp", "tensor"), scatter_dimension=0, tiled=True),
        lax.psum_scatter(out_local, ("dp", "tensor"), scatter_dimension=0, tiled=True),
        lax.psum_scatter(gains_local, ("dp", "tensor"), scatter_dimension=0, tiled=True),
        lax.psum_scatter(biases_local, ("dp", "tensor"), scatter_dimension=0, tiled=True),
    )
    scale_grad = lax.psum(scale_local, ("dp", "tensor"))
    return (
        mixed_out,
        token_grad,
        qkv_grad,
        out_weight_grad,
        gains_grad,
        biases_grad,
        scale_grad,
        fc1_grad,
        fc2_grad,
        mid_gain_grad,
        ffn_bias_grad,
    )


MESH = pl.DeviceIdType.MESH
ANY = pl.BlockSpec(memory_space=pl.ANY)
IN_VMEM = pl.BlockSpec(memory_space=pltpu.VMEM)


def place():
    z = lax.axis_index("dp")
    t = lax.axis_index("tensor")
    return z, lax.div(t, 4), lax.rem(lax.div(t, 2), 2), lax.rem(t, 2)


def at(z, y, x, c):
    return (z, y * 4 + x * 2 + c)


def greet(partners):
    barrier = pltpu.get_barrier_semaphore()
    for partner in partners:
        pl.semaphore_signal(barrier, inc=1, device_id=partner, device_id_type=MESH)
    pl.semaphore_wait(barrier, len(partners))


class Sends:
    def __init__(self, send_sems, recv_sems):
        self.send_sems, self.recv_sems, self.copies = send_sems, recv_sems, []

    def start(self, src, dst, target):
        index = len(self.copies)
        copy = pltpu.make_async_remote_copy(
            src_ref=src,
            dst_ref=dst,
            send_sem=self.send_sems.at[index],
            recv_sem=self.recv_sems.at[index],
            device_id=target,
            device_id_type=MESH,
        )
        copy.start()
        self.copies.append(copy)
        return copy

    def finish(self):
        for copy in self.copies:
            copy.wait_send()


def gather_kernel(
    nz,
    qkv_ref,
    out_ref,
    vec_ref,
    fc1_ref,
    fc2_ref,
    grad_ref,
    qkv_all,
    out_all,
    vec_all,
    fc1_all,
    fc2_all,
    grad_all,
    local_sems,
    send_sems,
    recv_sems,
):
    z, y, x, c = place()
    to_x, to_y, to_c = at(z, y, 1 - x, c), at(z, 1 - y, x, c), at(z, y, x, 1 - c)
    others = [lax.rem(z + k, nz) for k in range(1, nz)]
    slots = [z] + [lax.rem(z + nz - k, nz) for k in range(1, nz)]
    peers = [at(other, y, x, c) for other in others]
    greet([to_x, to_y, to_c] + peers)
    sends = Sends(send_sems, recv_sems)
    shards = ((qkv_ref, qkv_all), (out_ref, out_all))
    mine = []
    width1, width2 = fc1_ref.shape[0], fc2_ref.shape[1]
    own = [
        (qkv_ref, qkv_all.at[z, y, x, c]),
        (out_ref, out_all.at[z, y, x, c]),
        (vec_ref, vec_all.at[z, y, x, c]),
        (fc1_ref, fc1_all.at[pl.ds(pl.multiple_of(z * width1, width1), width1)]),
        (fc2_ref, fc2_all.at[:, pl.ds(pl.multiple_of(z * width2, width2), width2)]),
        (grad_ref, grad_all.at[y, x, c]),
    ]
    for index, (src, dst) in enumerate(own):
        copy = pltpu.make_async_copy(src, dst, local_sems.at[index])
        copy.start()
        mine.append(copy)

    def halves(ref):
        half = ref.shape[-1] // 2
        return pl.ds(0, half), pl.ds(half, half)

    vec_z = [sends.start(vec_ref, vec_all.at[z, y, x, c], peer) for peer in peers]
    vec_x = [sends.start(vec_ref, vec_all.at[z, y, x, c], to_x)]
    qkv_z = [sends.start(qkv_ref, qkv_all.at[z, y, x, c], peer) for peer in peers]

    def first(src, whole, slot, from_input):
        lo, hi = halves(src)
        one = src if from_input else whole.at[slot, y, x, c]
        return (
            sends.start(one.at[:, lo], whole.at[slot, y, x, c, :, lo], to_x),
            sends.start(one.at[:, hi], whole.at[slot, y, x, c, :, hi], to_y),
        )

    def second(whole, slot):
        lo, hi = halves(whole)
        return (
            sends.start(whole.at[slot, y, :, c, :, lo], whole.at[slot, y, :, c, :, lo], to_y),
            sends.start(whole.at[slot, :, x, c, :, hi], whole.at[slot, :, x, c, :, hi], to_x),
        )

    def third(whole, slot):
        return sends.start(whole.at[slot, :, :, c], whole.at[slot, :, :, c], to_c)

    def wait_all(copies):
        for copy in copies:
            copy.wait_recv()

    def spread(src, whole, arrivals, between):
        stage_a = [first(src, whole, z, True)]
        stage_b = []
        for k in range(1, nz):
            arrivals[k - 1].wait_recv()
            stage_a.append(first(src, whole, slots[k], False))
            if k == 1:
                between()
            if k >= 2:
                wait_all(stage_a[k - 2])
                stage_b.append(second(whole, slots[k - 2]))
        for k in range(len(stage_b), nz):
            wait_all(stage_a[k])
            stage_b.append(second(whole, slots[k]))
        return stage_b

    rest = {}

    def after_qkv_z():
        rest["out_z"] = [sends.start(out_ref, out_all.at[z, y, x, c], peer) for peer in peers]
        rest["fc"] = []
        for peer in peers:
            rest["fc"].append(sends.start(fc1_ref, own[3][1], peer))
            rest["fc"].append(sends.start(fc2_ref, own[4][1], peer))

    for copy in mine[:3]:
        copy.wait()
    qkv_b = spread(qkv_ref, qkv_all, qkv_z, after_qkv_z)
    wait_all(vec_z)
    for k in range(1, nz):
        vec_x.append(
            sends.start(vec_all.at[slots[k], y, x, c], vec_all.at[slots[k], y, x, c], to_x)
        )
    out_b = spread(out_ref, out_all, rest.get("out_z", []), lambda: None)
    wait_all(vec_x)
    vec_y = sends.start(vec_all.at[:, y, :, c], vec_all.at[:, y, :, c], to_y)
    lo, hi = halves(grad_ref)
    grad_a = (
        sends.start(grad_ref.at[:, lo], grad_all.at[y, x, c, :, lo], to_x),
        sends.start(grad_ref.at[:, hi], grad_all.at[y, x, c, :, hi], to_y),
    )
    qkv_c = []
    for k in range(nz):
        wait_all(qkv_b[k])
        qkv_c.append(third(qkv_all, slots[k]))
    vec_y.wait_recv()
    vec_c = sends.start(vec_all.at[:, :, :, c], vec_all.at[:, :, :, c], to_c)
    mine[5].wait()
    wait_all(grad_a)
    grad_b = (
        sends.start(grad_all.at[y, :, c, :, lo], grad_all.at[y, :, c, :, lo], to_y),
        sends.start(grad_all.at[:, x, c, :, hi], grad_all.at[:, x, c, :, hi], to_x),
    )
    out_c = []
    for k in range(nz):
        wait_all(out_b[k])
        out_c.append(third(out_all, slots[k]))
    wait_all(grad_b)
    grad_c = sends.start(grad_all.at[:, :, c], grad_all.at[:, :, c], to_c)
    wait_all(qkv_c + out_c + [vec_c, grad_c] + rest.get("fc", []))
    mine[3].wait()
    mine[4].wait()
    sends.finish()


def gather(nz, w_qkv, w_out, vectors, w_fc1, w_fc2, out_grad):
    def whole(shard, lead):
        return jax.ShapeDtypeStruct(lead + shard.shape, shard.dtype)

    every, plane = (nz, 2, 2, 2), (2, 2, 2)
    count = 4 * (nz - 1) + 5 * 2 * nz + 64
    return pl.pallas_call(
        functools.partial(gather_kernel, nz),
        name="gather",
        out_shape=(
            whole(w_qkv, every),
            whole(w_out, every),
            whole(vectors, every),
            jax.ShapeDtypeStruct((w_fc1.shape[0] * nz, w_fc1.shape[1]), w_fc1.dtype),
            jax.ShapeDtypeStruct((w_fc2.shape[0], w_fc2.shape[1] * nz), w_fc2.dtype),
            whole(out_grad, plane),
        ),
        in_specs=[ANY] * 6,
        out_specs=[ANY] * 6,
        scratch_shapes=[
            pltpu.SemaphoreType.DMA((6,)),
            pltpu.SemaphoreType.DMA((count,)),
            pltpu.SemaphoreType.DMA((count,)),
        ],
        compiler_params=pltpu.CompilerParams(collective_id=1, has_side_effects=True),
    )(w_qkv, w_out, vectors, w_fc1, w_fc2, out_grad)


def add_low(left, right):
    return (left.astype(jnp.float32) + right.astype(jnp.float32)).astype(jnp.bfloat16)


SQRT_2_PI = math.sqrt(2.0 / math.pi)
NT = (((1,), (1,)), ((), ()))
TN = (((0,), (0,)), ((), ()))


def dot(left, right, dims=None):
    if dims is None:
        return jnp.dot(left, right, preferred_element_type=jnp.float32)
    return lax.dot_general(left, right, dims, preferred_element_type=jnp.float32)


def ffn_kernel(
    mid_ref,
    og_ref,
    fc1_ref,
    fc2_ref,
    unit_ref,
    gnm_out,
    ffn_part,
    fc1_part,
    fc2_part,
    unit_out,
    mid_all,
    act,
    slope,
    grad,
    hidden,
    grad_pre,
    mid_part,
    pre,
    columns,
    stats,
    pair,
    got,
    totals,
    from_core,
    sums,
    from_one,
    from_two,
    local_sem,
    send_sems,
    recv_sems,
):
    z, y, x, c = place()
    to_x, to_y, to_c = at(z, y, 1 - x, c), at(z, 1 - y, x, c), at(z, y, x, 1 - c)
    to_xy = at(z, 1 - y, 1 - x, c)
    greet([to_x, to_y, to_c, to_xy])
    sends = Sends(send_sems, recv_sems)
    rows = mid_ref.shape[0]
    width = mid_ref.shape[1]
    units = fc1_ref.shape[1]
    half = rows // 2
    lo, hi = pl.ds(0, half), pl.ds(half, half)
    one_x = sends.start(mid_ref.at[lo], mid_all.at[y, x, c, lo], to_x)
    one_y = sends.start(mid_ref.at[hi], mid_all.at[y, x, c, hi], to_y)
    own_c = sends.start(mid_ref, mid_all.at[y, x, c], to_c)
    two_y = sends.start(mid_ref.at[lo], mid_all.at[y, x, c, lo], to_y)
    two_x = sends.start(mid_ref.at[hi], mid_all.at[y, x, c, hi], to_x)
    mine = pltpu.make_async_copy(mid_ref, mid_all.at[y, x, c], local_sem)
    mine.start()
    step = 32
    lane = lax.broadcasted_iota(jnp.int32, (step, 128), 1)

    def grads(yy, xx, cc):
        grad[yy, xx, cc] = dot(og_ref[yy, xx, cc], fc2_ref[...], NT)

    def forward(yy, xx, cc):
        pre[...] = dot(mid_all[yy, xx, cc], fc1_ref[...])

        def block(k, carry):
            part = pl.ds(pl.multiple_of(k * step, step), step)
            u = pre[part] + unit_ref[0:1]
            square = u * u
            th = jnp.tanh(SQRT_2_PI * u * (1.0 + 0.044715 * square))
            lift = 0.5 + 0.5 * th
            a = u * lift
            act[yy, xx, cc, part] = a
            slope[yy, xx, cc, part] = lift + (0.5 * SQRT_2_PI) * u * (1.0 - th * th) * (
                1.0 + (3 * 0.044715) * square
            )
            gm = grad[yy, xx, cc, part] * unit_ref[1:2]
            four = [
                jnp.sum(a, axis=1, keepdims=True),
                jnp.sum(a * a, axis=1, keepdims=True),
                jnp.sum(gm, axis=1, keepdims=True),
                jnp.sum(gm * a, axis=1, keepdims=True),
            ]
            tile = jnp.where(lane == 0, four[0], 0.0)
            for j in range(1, 4):
                tile = jnp.where(lane == j, four[j], tile)
            columns[part] = tile
            return carry

        lax.fori_loop(0, rows // step, block, 0)
        stats[yy, xx, cc] = columns[...].T[:8]

    grads(y, x, c)
    mine.wait()
    forward(y, x, c)
    grads(y, x, 1 - c)
    grads(y, 1 - x, c)
    one_x.wait_recv()
    one_y.wait_recv()
    ref_x, ref_y = mid_all.at[y, 1 - x, c, lo], mid_all.at[1 - y, x, c, hi]
    three_y = sends.start(ref_x, ref_x, to_y)
    three_x = sends.start(ref_y, ref_y, to_x)
    c_one = [sends.start(ref_x, ref_x, to_c), sends.start(ref_y, ref_y, to_c)]
    grads(1 - y, x, c)
    own_c.wait_recv()
    forward(y, x, 1 - c)
    grads(y, 1 - x, 1 - c)
    grads(1 - y, x, 1 - c)
    two_x.wait_recv()
    two_y.wait_recv()
    ref_x, ref_y = mid_all.at[y, 1 - x, c, hi], mid_all.at[1 - y, x, c, lo]
    c_two = [sends.start(ref_x, ref_x, to_c), sends.start(ref_y, ref_y, to_c)]
    forward(y, 1 - x, c)
    forward(1 - y, x, c)
    grads(1 - y, 1 - x, c)
    grads(1 - y, 1 - x, 1 - c)
    for copy in c_one + c_two:
        copy.wait_recv()
    forward(y, 1 - x, 1 - c)
    three_x.wait_recv()
    three_y.wait_recv()
    ref_xy = mid_all.at[1 - y, 1 - x, c]
    c_three = sends.start(ref_xy, ref_xy, to_c)
    forward(1 - y, x, 1 - c)
    forward(1 - y, 1 - x, c)
    c_three.wait_recv()
    forward(1 - y, 1 - x, 1 - c)

    sends.start(stats, got.at[3], to_c).wait_recv()
    pair[...] = stats[...] + got[3]
    arrivals = [
        sends.start(pair, got.at[k], plane) for k, plane in enumerate((to_x, to_y, to_xy))
    ]
    for copy in arrivals:
        copy.wait_recv()
    total = (pair[...] + got[0]) + (got[1] + got[2])
    total = total * (1.0 / (units * 8))
    center, second = total[:, :, :, 0:1], total[:, :, :, 1:2]
    first, cross = total[:, :, :, 2:3], total[:, :, :, 3:4]
    inverse = lax.rsqrt(second - center * center + EPS)
    totals[:, :, :, 0:1] = center
    totals[:, :, :, 1:2] = inverse
    totals[:, :, :, 2:3] = first
    totals[:, :, :, 3:4] = inverse * (cross - center * first)
    totals[:, :, :, 4:8] = jnp.zeros_like(total[:, :, :, 4:8])
    unit_out[...] = jnp.zeros_like(unit_out)

    def backward(yy, xx, cc):
        columns[...] = jnp.concatenate(
            [totals[yy, xx, cc], jnp.zeros((120, rows), jnp.float32)], axis=0
        ).T

        def block(k, carry):
            part = pl.ds(pl.multiple_of(k * step, step), step)
            center, inverse = columns[part, 0:1], columns[part, 1:2]
            first, second = columns[part, 2:3], columns[part, 3:4]
            gain = unit_ref[1:2]
            g = grad[yy, xx, cc, part]
            normed = (act[yy, xx, cc, part] - center) * inverse
            hidden[yy, xx, cc, part] = (normed * gain + unit_ref[2:3]).astype(jnp.bfloat16)
            back = inverse * (g * gain - first - normed * second)
            low = (back * slope[yy, xx, cc, part]).astype(jnp.bfloat16)
            grad_pre[yy, xx, cc, part] = low
            eight = (step // 8, 8, units)
            return (
                carry[0] + jnp.sum((g * normed).reshape(eight), axis=0),
                carry[1] + jnp.sum(low.astype(jnp.float32).reshape(eight), axis=0),
                carry[2] + jnp.sum(g.reshape(eight), axis=0),
            )

        zero = jnp.zeros((8, units), jnp.float32)
        parts = lax.fori_loop(0, rows // step, block, (zero, zero, zero))
        for j, part in enumerate(parts):
            unit_out[j : j + 1] += jnp.sum(part, axis=0, keepdims=True)
        mid_part[yy, xx, cc] = dot(grad_pre[yy, xx, cc], fc1_ref[...], NT).astype(jnp.bfloat16)

    left, right = pl.ds(0, width // 2), pl.ds(width // 2, width // 2)
    order = [(1 - y, 1 - x), (y, 1 - x), (1 - y, x), (y, x)]
    cores = []
    for yy, xx in order:
        backward(yy, xx, 1 - c)
        cores.append(sends.start(mid_part.at[yy, xx, 1 - c], from_core.at[yy, xx], to_c))
    stage_x, stage_y = [], []
    for k, (yy, xx) in enumerate(order):
        backward(yy, xx, c)
        cores[k].wait_recv()
        sums[yy, xx] = add_low(mid_part[yy, xx, c], from_core[yy, xx])
        if k in (0, 1):
            stage_x.append(
                sends.start(sums.at[yy, xx, :, left], from_one.at[0, yy, :, left], to_x)
            )
        if k in (0, 2):
            stage_y.append(
                sends.start(sums.at[yy, xx, :, right], from_one.at[1, xx, :, right], to_y)
            )

    def ffn_of(yy, xx, cc):
        ffn_part[yy, xx, cc] = dot(hidden[yy, xx, cc], fc2_ref[...]).astype(jnp.bfloat16)

    for yy, xx in order[:2]:
        ffn_of(yy, xx, 1 - c)
        ffn_of(yy, xx, c)
    for copy in (stage_x[0], stage_y[0]):
        copy.wait_recv()
    sums[1 - y, x, :, left] = add_low(sums[1 - y, x, :, left], from_one[0, 1 - y, :, left])
    sums[y, 1 - x, :, right] = add_low(sums[y, 1 - x, :, right], from_one[1, 1 - x, :, right])
    last_y = sends.start(sums.at[1 - y, x, :, left], from_two.at[:, left], to_y)
    last_x = sends.start(sums.at[y, 1 - x, :, right], from_two.at[:, right], to_x)
    for yy, xx in order[2:]:
        ffn_of(yy, xx, 1 - c)
        ffn_of(yy, xx, c)
    blocks = 4

    def fc1_block(k, carry):
        part = pl.ds(pl.multiple_of(k * (width // blocks), 128), width // blocks)
        block = jnp.zeros((width // blocks, units), jnp.float32)
        for j in range(8):
            yxc = (j // 4, (j // 2) % 2, j % 2)
            block = block + dot(mid_all[(*yxc, slice(None), part)], grad_pre[yxc], TN)
        fc1_part[part] = block.astype(jnp.bfloat16)
        return carry

    def fc2_block(k, carry):
        part = pl.ds(pl.multiple_of(k * (width // blocks), 128), width // blocks)
        block = jnp.zeros((units, width // blocks), jnp.float32)
        for j in range(8):
            yxc = (j // 4, (j // 2) % 2, j % 2)
            block = block + dot(hidden[yxc], og_ref[(*yxc, slice(None), part)], TN)
        fc2_part[:, part] = block.astype(jnp.bfloat16)
        return carry

    lax.fori_loop(0, blocks, fc1_block, 0)
    for copy in (stage_x[1], stage_y[1]):
        copy.wait_recv()
    lax.fori_loop(0, blocks, fc2_block, 0)
    last_x.wait_recv()
    last_y.wait_recv()
    own = sums[y, x].astype(jnp.float32)
    gnm_out[:, left] = (
        own[:, : width // 2]
        + from_one[0, y, :, left].astype(jnp.float32)
        + from_two[:, left].astype(jnp.float32)
    )
    gnm_out[:, right] = (
        own[:, width // 2 :]
        + from_one[1, x, :, right].astype(jnp.float32)
        + from_two[:, right].astype(jnp.float32)
    )
    sends.finish()


def ffn(mid, og_all, fc1, fc2, unit_rows):
    rows, width = mid.shape
    units = fc1.shape[1]
    low, plane = jnp.bfloat16, (2, 2, 2)
    sds = jax.ShapeDtypeStruct
    count = 32
    return pl.pallas_call(
        ffn_kernel,
        name="ffn",
        out_shape=(
            sds((rows, width), jnp.float32),
            sds(plane + (rows, width), low),
            sds(fc1.shape, low),
            sds(fc2.shape, low),
            sds((8, units), jnp.float32),
        ),
        in_specs=[IN_VMEM] * 5,
        out_specs=[IN_VMEM] * 5,
        scratch_shapes=[
            pltpu.VMEM(plane + (rows, width), low),
            pltpu.VMEM(plane + (rows, units), jnp.float32),
            pltpu.VMEM(plane + (rows, units), jnp.float32),
            pltpu.VMEM(plane + (rows, units), jnp.float32),
            pltpu.VMEM(plane + (rows, units), low),
            pltpu.VMEM(plane + (rows, units), low),
            pltpu.VMEM(plane + (rows, width), low),
            pltpu.VMEM((rows, units), jnp.float32),
            pltpu.VMEM((rows, 128), jnp.float32),
            pltpu.VMEM(plane + (8, rows), jnp.float32),
            pltpu.VMEM(plane + (8, rows), jnp.float32),
            pltpu.VMEM((4,) + plane + (8, rows), jnp.float32),
            pltpu.VMEM(plane + (8, rows), jnp.float32),
            pltpu.VMEM((2, 2, rows, width), low),
            pltpu.VMEM((2, 2, rows, width), low),
            pltpu.VMEM((2, 2, rows, width), low),
            pltpu.VMEM((rows, width), low),
            pltpu.SemaphoreType.DMA,
            pltpu.SemaphoreType.DMA((count,)),
            pltpu.SemaphoreType.DMA((count,)),
        ],
        compiler_params=pltpu.CompilerParams(
            collective_id=2, has_side_effects=True, vmem_limit_bytes=62 * 2**20
        ),
    )(mid, og_all, fc1, fc2, unit_rows)


def fold_kernel(
    nz,
    pieces,
    first_ref,
    fc1_ref,
    fc2_ref,
    small_ref,
    first_out,
    fc1_out,
    fc2_out,
    small_out,
    from_core,
    sums,
    from_one,
    from_two,
    got1,
    got2,
    got_small,
    send_sems,
    recv_sems,
):
    z, y, x, c = place()
    to_x, to_y, to_c = at(z, y, 1 - x, c), at(z, 1 - y, x, c), at(z, y, x, 1 - c)
    others = [lax.rem(z + k, nz) for k in range(1, nz)]
    peers = [at(other, y, x, c) for other in others]
    greet([to_x, to_y, to_c] + peers)
    sends = Sends(send_sems, recv_sems)
    width1, width2 = fc1_out.shape[0], fc2_out.shape[1]

    def block1(which):
        return fc1_ref.at[pl.ds(pl.multiple_of(which * width1, width1), width1)]

    def block2(which):
        return fc2_ref.at[:, pl.ds(pl.multiple_of(which * width2, width2), width2)]

    rows = first_ref.shape[3] // pieces
    half = first_ref.shape[4] // 2
    lo, hi = pl.ds(0, half), pl.ds(half, half)
    parts = [pl.ds(k * rows, rows) for k in range(pieces)]
    jobs = [(i, k) for i in range(1) for k in range(pieces)]
    refs, outs = (first_ref,), (first_out,)
    stage_c = {
        (i, k): sends.start(
            refs[i].at[:, :, 1 - c, parts[k]], from_core.at[i, :, :, parts[k]], to_c
        )
        for i, k in jobs
    }
    far = []
    for k, peer in enumerate(peers):
        far.append(sends.start(small_ref, got_small.at[k], peer))
        far.append(sends.start(block1(others[k]), got1.at[k], peer))
        far.append(sends.start(block2(others[k]), got2.at[k], peer))

    stage_1, stage_2 = {}, {}

    def after_core(i, k):
        part = parts[k]
        stage_c[i, k].wait_recv()
        for yy in range(2):
            for xx in range(2):
                sums[i, yy, xx, part] = add_low(
                    refs[i][yy, xx, c, part], from_core[i, yy, xx, part]
                )
        stage_1[i, k] = (
            sends.start(sums.at[i, :, 1 - x, part, lo], from_one.at[i, :, part, lo], to_x),
            sends.start(sums.at[i, 1 - y, :, part, hi], from_one.at[i, :, part, hi], to_y),
        )

    def after_one(i, k):
        part = parts[k]
        for copy in stage_1[i, k]:
            copy.wait_recv()
        for yy in range(2):
            sums[i, yy, x, part, lo] = add_low(
                sums[i, yy, x, part, lo], from_one[i, yy, part, lo]
            )
        for xx in range(2):
            sums[i, y, xx, part, hi] = add_low(
                sums[i, y, xx, part, hi], from_one[i, xx, part, hi]
            )
        stage_2[i, k] = (
            sends.start(sums.at[i, 1 - y, x, part, lo], from_two.at[i, part, lo], to_y),
            sends.start(sums.at[i, y, 1 - x, part, hi], from_two.at[i, part, hi], to_x),
        )

    def after_two(i, k):
        part = parts[k]
        for copy in stage_2[i, k]:
            copy.wait_recv()
        outs[i][part] = sums[i, y, x, part].astype(jnp.float32) + from_two[i, part].astype(
            jnp.float32
        )

    for n in range(len(jobs) + 2):
        if n < len(jobs):
            after_core(*jobs[n])
        if 1 <= n < len(jobs) + 1:
            after_one(*jobs[n - 1])
        if n >= 2:
            after_two(*jobs[n - 2])
    for copy in far:
        copy.wait_recv()
    own1, own2, small = block1(z)[...].astype(jnp.float32), block2(z)[...].astype(jnp.float32), small_ref[...]
    for k in range(nz - 1):
        own1 = own1 + got1[k].astype(jnp.float32)
        own2 = own2 + got2[k].astype(jnp.float32)
        small = small + got_small[k]
    fc1_out[...] = own1
    fc2_out[...] = own2
    small_out[...] = small
    sends.finish()


def fold(nz, first, fc1, fc2, small):
    rows, columns = first.shape[3:]
    low = jnp.bfloat16
    pieces = 2
    count = 5 * 2 * pieces + 3 * (nz - 1)
    out1, out2 = (fc1.shape[0] // nz, fc1.shape[1]), (fc2.shape[0], fc2.shape[1] // nz)
    kept = (jnp.float32,)
    return pl.pallas_call(
        functools.partial(fold_kernel, nz, pieces),
        name="fold",
        out_shape=tuple(
            jax.ShapeDtypeStruct(shape, *kept)
            for shape in ((rows, columns), out1, out2, small.shape)
        ),
        in_specs=[IN_VMEM] * 4,
        out_specs=[IN_VMEM] * 4,
        scratch_shapes=[
            pltpu.VMEM((1, 2, 2, rows, columns), low),
            pltpu.VMEM((1, 2, 2, rows, columns), low),
            pltpu.VMEM((1, 2, rows, columns), low),
            pltpu.VMEM((1, rows, columns), low),
            pltpu.VMEM((nz - 1,) + out1, low),
            pltpu.VMEM((nz - 1,) + out2, low),
            pltpu.VMEM((nz - 1,) + small.shape, jnp.float32),
            pltpu.SemaphoreType.DMA((count,)),
            pltpu.SemaphoreType.DMA((count,)),
        ],
        compiler_params=pltpu.CompilerParams(
            collective_id=4, has_side_effects=True, vmem_limit_bytes=60 * 2**20
        ),
    )(first, fc1, fc2, small)


def total_kernel(
    nz,
    grad_ref,
    small_ref,
    grad_out,
    small_out,
    from_core,
    sums,
    from_one,
    from_two,
    from_far,
    small_sum,
    small_got,
    send_sems,
    recv_sems,
):
    z, y, x, c = place()
    to_x, to_y, to_c = at(z, y, 1 - x, c), at(z, 1 - y, x, c), at(z, y, x, 1 - c)
    others = [lax.rem(z + k, nz) for k in range(1, nz)]
    order = others + [z]
    peers = [at(other, y, x, c) for other in others]
    greet([to_x, to_y, to_c] + peers)
    sends = Sends(send_sems, recv_sems)
    half = grad_ref.shape[-1] // 2
    lo, hi = pl.ds(0, half), pl.ds(half, half)
    stage_c = [
        sends.start(grad_ref.at[which, :, :, 1 - c], from_core.at[which], to_c)
        for which in order
    ]
    small_c = sends.start(small_ref, small_got.at[0], to_c)
    stage_1, stage_2, far = {}, {}, {}

    def after_core(k):
        which = order[k]
        stage_c[k].wait_recv()
        for yy in range(2):
            for xx in range(2):
                sums[which, yy, xx] = add_low(
                    grad_ref[which, yy, xx, c], from_core[which, yy, xx]
                )
        stage_1[k] = (
            sends.start(sums.at[which, :, 1 - x, :, lo], from_one.at[which, :, :, lo], to_x),
            sends.start(sums.at[which, 1 - y, :, :, hi], from_one.at[which, :, :, hi], to_y),
        )

    def after_one(k):
        which = order[k]
        for copy in stage_1[k]:
            copy.wait_recv()
        for yy in range(2):
            sums[which, yy, x, :, lo] = add_low(
                sums[which, yy, x, :, lo], from_one[which, yy, :, lo]
            )
        for xx in range(2):
            sums[which, y, xx, :, hi] = add_low(
                sums[which, y, xx, :, hi], from_one[which, xx, :, hi]
            )
        stage_2[k] = (
            sends.start(sums.at[which, 1 - y, x, :, lo], from_two.at[which, :, lo], to_y),
            sends.start(sums.at[which, y, 1 - x, :, hi], from_two.at[which, :, hi], to_x),
        )

    def after_two(k):
        which = order[k]
        for copy in stage_2[k]:
            copy.wait_recv()
        if k < nz - 1:
            sums[which, y, x] = add_low(sums[which, y, x], from_two[which])
            far[k] = sends.start(sums.at[which, y, x], from_far.at[k], peers[k])

    steps = []
    small_c.wait_recv()
    small_sum[0] = small_ref[...] + small_got[0]
    small_x = sends.start(small_sum.at[0], small_got.at[1], to_x)
    for n in range(nz + 2):
        if n < nz:
            after_core(n)
        if 1 <= n < nz + 1:
            after_one(n - 1)
        if n >= 2:
            after_two(n - 2)
        if n == 1:
            small_x.wait_recv()
            small_sum[1] = small_sum[0] + small_got[1]
            small_y = sends.start(small_sum.at[1], small_got.at[2], to_y)
        if n == 3:
            small_y.wait_recv()
            small_sum[2] = small_sum[1] + small_got[2]
            small_far = [
                sends.start(small_sum.at[2], small_got.at[3 + k], peer)
                for k, peer in enumerate(peers)
            ]
    total = sums[z, y, x].astype(jnp.float32) + from_two[z].astype(jnp.float32)
    for k in range(nz - 1):
        far[k].wait_recv()
        total = total + from_far[k].astype(jnp.float32)
    grad_out[...] = total
    small = small_sum[2]
    for k in range(nz - 1):
        small_far[k].wait_recv()
        small = small + small_got[3 + k]
    small_out[...] = small
    sends.finish()


def total_all(nz, grad, small):
    rows, columns = grad.shape[4:]
    low = jnp.bfloat16
    count = 5 * nz + (nz - 1) + 3 + (nz - 1)
    return pl.pallas_call(
        functools.partial(total_kernel, nz),
        name="total_all",
        out_shape=(
            jax.ShapeDtypeStruct((rows, columns), jnp.float32),
            jax.ShapeDtypeStruct(small.shape, jnp.float32),
        ),
        in_specs=[IN_VMEM] * 2,
        out_specs=[IN_VMEM] * 2,
        scratch_shapes=[
            pltpu.VMEM((nz, 2, 2, rows, columns), low),
            pltpu.VMEM((nz, 2, 2, rows, columns), low),
            pltpu.VMEM((nz, 2, rows, columns), low),
            pltpu.VMEM((nz, rows, columns), low),
            pltpu.VMEM((nz - 1, rows, columns), low),
            pltpu.VMEM((3,) + small.shape, jnp.float32),
            pltpu.VMEM((nz + 2,) + small.shape, jnp.float32),
            pltpu.SemaphoreType.DMA((count,)),
            pltpu.SemaphoreType.DMA((count,)),
        ],
        compiler_params=pltpu.CompilerParams(
            collective_id=5, has_side_effects=True, vmem_limit_bytes=60 * 2**20
        ),
    )(grad, small)


def fused(
    nz,
    tokens,
    out_grad,
    doc_lengths,
    w_qkv,
    w_out,
    gains,
    biases,
    head_scale,
    w_fc1,
    w_fc2,
    mid_gain,
    ffn_biases,
):
    model_width = tokens.shape[1]
    local_rows = tokens.shape[0]
    head_dim = model_width // HEADS
    factor = 1.0 / math.sqrt(head_dim)
    share = gains.shape[0]
    vectors = jnp.concatenate(
        [gains, biases, jnp.zeros((share, 128 - gains.shape[1] - biases.shape[1]), jnp.float32)],
        axis=1,
    )
    qkv_full, out_full, vec_full, fc1_rows, fc2_cols, shard_rows = gather(
        nz, w_qkv, w_out, vectors, w_fc1, w_fc2, out_grad
    )
    qkv_full = qkv_full.reshape(model_width, -1)
    out_full = out_full.reshape(model_width, -1)
    vec_full = vec_full.reshape(model_width, 128)
    vec_rows = vec_full[:, :10].T
    gain_full = vec_rows[:3]
    bias_full = vec_rows[3:]
    doc_ends = jnp.cumsum(doc_lengths[0])[:-1]
    places = jnp.arange(local_rows)
    doc_ids = jnp.sum((places[:, None] >= doc_ends[None, :]).astype(jnp.int32), axis=1)
    inputs = tokens.astype(jnp.float32)
    normed_one, inverse_one = normalize(inputs)
    normed_in = (normed_one * gain_full[0] + bias_full[0]).astype(jnp.bfloat16)
    zero_bias = jnp.zeros((model_width,), jnp.float32)
    qkv_bias = jnp.concatenate([bias_full[1], zero_bias, bias_full[2]])
    projected = (
        jnp.dot(normed_in, qkv_full, preferred_element_type=jnp.float32) + qkv_bias
    ).astype(jnp.bfloat16)
    query_rows = projected[:, :model_width].reshape(local_rows, HEADS, head_dim)
    key_rows = projected[:, model_width : 2 * model_width].reshape(local_rows, HEADS, head_dim)
    value_rows = projected[:, 2 * model_width :].reshape(local_rows, HEADS, head_dim)
    attended, sums_log = attend_forward(query_rows, key_rows, value_rows, doc_ids, factor)
    attended = attended.reshape(local_rows, model_width)
    scale_wide = jnp.repeat(head_scale, head_dim)
    scaled = (attended * scale_wide).astype(jnp.bfloat16)
    branch = jnp.dot(scaled, out_full, preferred_element_type=jnp.float32) + bias_full[3]
    normed_post, inverse_post = normalize(branch)
    middle = inputs + normed_post * gain_full[1] + bias_full[4]
    normed_two, inverse_two = normalize(middle)
    normed_mid = (normed_two * gain_full[2] + bias_full[5]).astype(jnp.bfloat16)
    units = w_fc1.shape[1]
    unit_rows = jnp.concatenate(
        [ffn_biases[:1], mid_gain[None], ffn_biases[1:], jnp.zeros((5, units), jnp.float32)]
    )
    grad_normed_mid, ffn_part, fc1_part, fc2_part, unit_sums = ffn(
        normed_mid, shard_rows, fc1_rows, fc2_cols, unit_rows
    )
    ffn_out, fc1_grad, fc2_grad, unit_sums = fold(nz, ffn_part, fc1_part, fc2_part, unit_sums)
    mid_gain_grad, ffn_bias_grad = unit_sums[0], unit_sums[1:3]
    mixed_out = (middle + ffn_out + bias_full[6]).astype(jnp.bfloat16)
    final_grad = out_grad.astype(jnp.float32)
    grad_middle = final_grad + normalize_back(
        grad_normed_mid * gain_full[2], normed_two, inverse_two
    )
    grad_post = normalize_back(grad_middle * gain_full[1], normed_post, inverse_post).astype(
        jnp.bfloat16
    )
    out_local = jnp.einsum("td,te->de", scaled, grad_post, preferred_element_type=jnp.float32)
    grad_scaled = jnp.einsum("te,de->td", grad_post, out_full, preferred_element_type=jnp.float32)
    scale_local = jnp.sum(
        (grad_scaled * attended).reshape(local_rows, HEADS, head_dim), axis=(0, 2)
    )
    grad_attended = (
        (grad_scaled * scale_wide).astype(jnp.bfloat16).reshape(local_rows, HEADS, head_dim)
    )
    grad_query, grad_keys, grad_values = attend_backward(
        query_rows, key_rows, value_rows, grad_attended, doc_ids, sums_log, factor
    )
    grad_projected = jnp.concatenate(
        [
            grad_query.reshape(local_rows, model_width),
            grad_keys.reshape(local_rows, model_width),
            grad_values.reshape(local_rows, model_width),
        ],
        axis=1,
    ).astype(jnp.bfloat16)
    qkv_local = jnp.einsum(
        "td,te->de", normed_in, grad_projected, preferred_element_type=jnp.float32
    )
    grad_normed_in = jnp.einsum(
        "te,de->td", grad_projected, qkv_full, preferred_element_type=jnp.float32
    )
    token_grad = grad_middle + normalize_back(
        grad_normed_in * gain_full[0], normed_one, inverse_one
    )
    projected_sums = jnp.sum(grad_projected.astype(jnp.float32), axis=0)
    small = jnp.stack(
        [
            jnp.sum(grad_normed_in * normed_one, axis=0),
            jnp.sum(grad_middle * normed_post, axis=0),
            jnp.sum(grad_normed_mid * normed_two, axis=0),
            jnp.sum(grad_normed_in, axis=0),
            projected_sums[:model_width],
            projected_sums[2 * model_width :],
            jnp.sum(grad_post.astype(jnp.float32), axis=0),
            jnp.sum(grad_middle, axis=0),
            jnp.sum(grad_normed_mid, axis=0),
            jnp.sum(final_grad, axis=0),
            jnp.pad(scale_local, (0, model_width - HEADS)),
        ]
        + [jnp.zeros((model_width,), jnp.float32)] * 5
    )
    weights = jnp.concatenate(
        [qkv_local.astype(jnp.bfloat16), out_local.astype(jnp.bfloat16)], axis=1
    ).reshape(nz, 2, 2, 2, share, -1)
    weight_grad, small = total_all(nz, weights, small)
    index = lax.axis_index("dp") * 8 + lax.axis_index("tensor")
    ours = lax.dynamic_slice(small, (0, index * share), (10, share)).T
    return (
        mixed_out,
        token_grad,
        weight_grad[:, : w_qkv.shape[1]],
        weight_grad[:, w_qkv.shape[1] :],
        ours[:, :3],
        ours[:, 3:],
        small[10, :HEADS],
        fc1_grad,
        fc2_grad,
        mid_gain_grad,
        ffn_bias_grad,
    )


def layer(nz, nt, tokens, out_grad, doc_lengths, w_qkv, *rest):
    if nt == 8 and nz > 1 and w_qkv.shape[0] % 16 == 0:
        return fused(nz, tokens, out_grad, doc_lengths, w_qkv, *rest)
    return plain(tokens, out_grad, doc_lengths, w_qkv, *rest)


def solution(mesh):
    return jax.shard_map(
        functools.partial(layer, mesh.shape["dp"], mesh.shape["tensor"]),
        mesh=mesh,
        in_specs=(
            P(("dp", "tensor"), None),
            P(("dp", "tensor"), None),
            P(("dp", "tensor"), None),
            P(("dp", "tensor"), None),
            P(("dp", "tensor"), None),
            P(("dp", "tensor"), None),
            P(("dp", "tensor"), None),
            P(),
            P("dp", "tensor"),
            P("tensor", "dp"),
            P("tensor"),
            P(None, "tensor"),
        ),
        out_specs=(
            P(("dp", "tensor"), None),
            P(("dp", "tensor"), None),
            P(("dp", "tensor"), None),
            P(("dp", "tensor"), None),
            P(("dp", "tensor"), None),
            P(("dp", "tensor"), None),
            P(),
            P("dp", "tensor"),
            P("tensor", "dp"),
            P("tensor"),
            P(None, "tensor"),
        ),
        check_vma=False,
    )
```

```python
import functools
import math

import jax
import jax.numpy as jnp
from jax import lax
from jax.experimental import pallas as pl
from jax.experimental.pallas import tpu as pltpu
from jax.sharding import PartitionSpec as P

HEADS = 16
FF = 4096


EPS = 1e-05
NEGATIVE = -1000000000.0


def normalize(values):
    center = jnp.mean(values, axis=-1, keepdims=True)
    spread = jnp.mean(values * values, axis=-1, keepdims=True) - center * center
    inverse = lax.rsqrt(spread + EPS)
    return ((values - center) * inverse, inverse)


def normalize_back(grad_normed, normed, inverse):
    first_mean = jnp.mean(grad_normed, axis=-1, keepdims=True)
    second = jnp.mean(grad_normed * normed, axis=-1, keepdims=True)
    return inverse * (grad_normed - first_mean - normed * second)


def block_scores(query_rows, key_rows, doc_ids, row_first, row_last, factor):
    scores = (
        jnp.einsum("qhd,khd->hqk", query_rows, key_rows, preferred_element_type=jnp.float32)
        * factor
    )
    query_pos = jnp.arange(row_first, row_last)
    key_pos = jnp.arange(row_last)
    same_doc = doc_ids[row_first:row_last, None] == doc_ids[None, :row_last]
    allowed = jnp.logical_and(same_doc, key_pos[None, :] <= query_pos[:, None])
    return (jnp.where(allowed[None], scores, NEGATIVE), allowed)


def attend_forward(query_rows, key_rows, value_rows, doc_ids, factor):
    total_rows = query_rows.shape[0]
    block_rows = min(512, total_rows)
    scores, allowed = block_scores(query_rows, key_rows, doc_ids, 0, block_rows, factor)
    row_peak = jnp.max(scores, axis=-1, keepdims=True)
    exponent = jnp.exp(scores - row_peak)
    row_total = jnp.sum(exponent, axis=-1, keepdims=True)
    prob_low = (exponent / row_total).astype(jnp.bfloat16)
    pieces = jnp.einsum("hqk,khd->qhd", prob_low, value_rows, preferred_element_type=jnp.float32)
    sums_log = [row_peak + jnp.log(row_total)]
    return (pieces, sums_log)


def attend_backward(query_rows, key_rows, value_rows, grad_out, doc_ids, sums_log, factor):
    total_rows = query_rows.shape[0]
    block_rows = min(512, total_rows)
    query_parts = []
    grad_keys = jnp.zeros(key_rows.shape, jnp.float32)
    grad_values = jnp.zeros(value_rows.shape, jnp.float32)
    for block_index, row_first in enumerate(range(0, total_rows, block_rows)):
        row_last = row_first + block_rows
        scores, allowed = block_scores(query_rows, key_rows, doc_ids, row_first, row_last, factor)
        prob_rows = jnp.where(allowed[None], jnp.exp(scores - sums_log[block_index]), 0.0)
        prob_low = prob_rows.astype(jnp.bfloat16)
        grad_probs = jnp.einsum(
            "qhd,khd->hqk", grad_out, value_rows, preferred_element_type=jnp.float32
        )
        inner_sum = jnp.sum(prob_rows * grad_probs, axis=-1, keepdims=True)
        grad_scores = (prob_rows * (grad_probs - inner_sum) * factor).astype(jnp.bfloat16)
        query_parts.append(
            jnp.einsum("hqk,khd->qhd", grad_scores, key_rows, preferred_element_type=jnp.float32)
        )
        grad_keys = grad_keys.at[:row_last].add(
            jnp.einsum("hqk,qhd->khd", grad_scores, query_rows, preferred_element_type=jnp.float32)
        )
        grad_values = grad_values.at[:row_last].add(
            jnp.einsum("hqk,qhd->khd", prob_low, grad_out, preferred_element_type=jnp.float32)
        )
    return (query_parts[0], grad_keys, grad_values)


def plain(
    tokens,
    out_grad,
    doc_lengths,
    w_qkv,
    w_out,
    gains,
    biases,
    head_scale,
    w_fc1,
    w_fc2,
    mid_gain,
    ffn_biases,
):
    qkv_full, out_full, gain_full, bias_full = (
        lax.all_gather(w_qkv, ("dp", "tensor"), axis=0, tiled=True),
        lax.all_gather(w_out, ("dp", "tensor"), axis=0, tiled=True),
        lax.all_gather(gains.astype(jnp.bfloat16), ("dp", "tensor"), axis=0, tiled=True).astype(
            gains.dtype
        ),
        lax.all_gather(biases.astype(jnp.bfloat16), ("dp", "tensor"), axis=0, tiled=True).astype(
            biases.dtype
        ),
    )
    fc1_rows, fc2_cols = (
        lax.all_gather(w_fc1, "dp", axis=0, tiled=True),
        lax.all_gather(w_fc2, "dp", axis=1, tiled=True),
    )
    model_width = tokens.shape[1]
    local_rows = tokens.shape[0]
    head_dim = model_width // HEADS
    factor = 1.0 / math.sqrt(head_dim)
    doc_ends = jnp.cumsum(doc_lengths[0])[:-1]
    places = jnp.arange(local_rows)
    doc_ids = jnp.sum((places[:, None] >= doc_ends[None, :]).astype(jnp.int32), axis=1)
    inputs = tokens.astype(jnp.float32)
    normed_one, inverse_one = normalize(inputs)
    normed_in = (normed_one * gain_full[:, 0] + bias_full[:, 0]).astype(jnp.bfloat16)
    zero_bias = jnp.zeros((model_width,), jnp.float32)
    qkv_bias = jnp.concatenate([bias_full[:, 1], zero_bias, bias_full[:, 2]])
    projected = (
        jnp.dot(normed_in, qkv_full, preferred_element_type=jnp.float32) + qkv_bias
    ).astype(jnp.bfloat16)
    query_rows = projected[:, :model_width].reshape(local_rows, HEADS, head_dim)
    key_rows = projected[:, model_width : 2 * model_width].reshape(local_rows, HEADS, head_dim)
    value_rows = projected[:, 2 * model_width :].reshape(local_rows, HEADS, head_dim)
    attended, sums_log = attend_forward(query_rows, key_rows, value_rows, doc_ids, factor)
    attended = attended.reshape(local_rows, model_width)
    scale_wide = jnp.repeat(head_scale, head_dim)
    scaled = (attended * scale_wide).astype(jnp.bfloat16)
    branch = jnp.dot(scaled, out_full, preferred_element_type=jnp.float32) + bias_full[:, 3]
    normed_post, inverse_post = normalize(branch)
    middle = inputs + normed_post * gain_full[:, 1] + bias_full[:, 4]
    normed_two, inverse_two = normalize(middle)
    normed_mid = (normed_two * gain_full[:, 2] + bias_full[:, 5]).astype(jnp.bfloat16)
    gathered = lax.all_gather(normed_mid, "tensor", axis=0, tiled=True)
    hidden_pre = jnp.dot(gathered, fc1_rows, preferred_element_type=jnp.float32) + ffn_biases[0]
    activated, gelu_pull = jax.vjp(jax.nn.gelu, hidden_pre)
    act_sum, act_square = (
        lax.psum(jnp.sum(activated, axis=1).astype(jnp.bfloat16), "tensor").astype(jnp.float32),
        lax.psum(jnp.sum(activated * activated, axis=1).astype(jnp.bfloat16), "tensor").astype(
            jnp.float32
        ),
    )
    center = act_sum / FF
    inverse_mid = lax.rsqrt(act_square / FF - center * center + EPS)[:, None]
    normed_act = (activated - center[:, None]) * inverse_mid
    hidden = (normed_act * mid_gain + ffn_biases[1]).astype(jnp.bfloat16)
    hidden_rows = hidden
    ffn_out = lax.psum_scatter(
        jnp.dot(hidden_rows, fc2_cols, preferred_element_type=jnp.float32).astype(jnp.bfloat16),
        "tensor",
        scatter_dimension=0,
        tiled=True,
    ).astype(jnp.float32)
    shard_rows = lax.all_gather(out_grad, "tensor", axis=0, tiled=True)
    grad_piece = jnp.einsum("rd,fd->rf", shard_rows, fc2_cols, preferred_element_type=jnp.float32)
    hidden_rows = hidden
    fc2_run = jnp.einsum("rf,rd->fd", hidden_rows, shard_rows, preferred_element_type=jnp.float32)
    mid_gain_part = jnp.sum(grad_piece * normed_act, axis=0)
    mid_bias_part = jnp.sum(grad_piece, axis=0)
    grad_normed_act = grad_piece * mid_gain
    first_sum, second_sum = (
        lax.psum(jnp.sum(grad_normed_act, axis=1).astype(jnp.bfloat16), "tensor").astype(
            jnp.float32
        ),
        lax.psum(
            jnp.sum(grad_normed_act * normed_act, axis=1).astype(jnp.bfloat16), "tensor"
        ).astype(jnp.float32),
    )
    grad_act = inverse_mid * (
        grad_normed_act - first_sum[:, None] / FF - normed_act * (second_sum[:, None] / FF)
    )
    grad_pre = gelu_pull(grad_act)[0].astype(jnp.bfloat16)
    fc1_part = jnp.einsum("rd,rf->df", gathered, grad_pre, preferred_element_type=jnp.float32)
    fc1_bias_part = jnp.sum(grad_pre.astype(jnp.float32), axis=0)
    grad_normed_mid = lax.psum_scatter(
        jnp.einsum("rf,df->rd", grad_pre, fc1_rows, preferred_element_type=jnp.float32).astype(
            jnp.bfloat16
        ),
        "tensor",
        scatter_dimension=0,
        tiled=True,
    ).astype(jnp.float32)
    ffn_bias_part = jnp.stack([fc1_bias_part, mid_bias_part])
    fc1_grad, fc2_grad = (
        lax.psum_scatter(
            fc1_part.astype(jnp.bfloat16), "dp", scatter_dimension=0, tiled=True
        ).astype(jnp.float32),
        lax.psum_scatter(
            fc2_run.astype(jnp.bfloat16), "dp", scatter_dimension=1, tiled=True
        ).astype(jnp.float32),
    )
    mid_gain_grad, ffn_bias_grad = lax.psum((mid_gain_part, ffn_bias_part), "dp")
    mixed_out = (middle + ffn_out + bias_full[:, 6]).astype(jnp.bfloat16)
    final_grad = out_grad.astype(jnp.float32)
    grad_middle = final_grad + normalize_back(
        grad_normed_mid * gain_full[:, 2], normed_two, inverse_two
    )
    grad_post = normalize_back(grad_middle * gain_full[:, 1], normed_post, inverse_post).astype(
        jnp.bfloat16
    )
    out_local = jnp.einsum("td,te->de", scaled, grad_post, preferred_element_type=jnp.float32)
    grad_scaled = jnp.einsum("te,de->td", grad_post, out_full, preferred_element_type=jnp.float32)
    scale_local = jnp.sum(
        (grad_scaled * attended).reshape(local_rows, HEADS, head_dim), axis=(0, 2)
    )
    grad_attended = (
        (grad_scaled * scale_wide).astype(jnp.bfloat16).reshape(local_rows, HEADS, head_dim)
    )
    grad_query, grad_keys, grad_values = attend_backward(
        query_rows, key_rows, value_rows, grad_attended, doc_ids, sums_log, factor
    )
    grad_projected = jnp.concatenate(
        [
            grad_query.reshape(local_rows, model_width),
            grad_keys.reshape(local_rows, model_width),
            grad_values.reshape(local_rows, model_width),
        ],
        axis=1,
    ).astype(jnp.bfloat16)
    qkv_local = jnp.einsum(
        "td,te->de", normed_in, grad_projected, preferred_element_type=jnp.float32
    )
    grad_normed_in = jnp.einsum(
        "te,de->td", grad_projected, qkv_full, preferred_element_type=jnp.float32
    )
    token_grad = grad_middle + normalize_back(
        grad_normed_in * gain_full[:, 0], normed_one, inverse_one
    )
    projected_sums = jnp.sum(grad_projected.astype(jnp.float32), axis=0)
    gains_local = jnp.stack(
        [
            jnp.sum(grad_normed_in * normed_one, axis=0),
            jnp.sum(grad_middle * normed_post, axis=0),
            jnp.sum(grad_normed_mid * normed_two, axis=0),
        ],
        axis=1,
    )
    biases_local = jnp.stack(
        [
            jnp.sum(grad_normed_in, axis=0),
            projected_sums[:model_width],
            projected_sums[2 * model_width :],
            jnp.sum(grad_post.astype(jnp.float32), axis=0),
            jnp.sum(grad_middle, axis=0),
            jnp.sum(grad_normed_mid, axis=0),
            jnp.sum(final_grad, axis=0),
        ],
        axis=1,
    )
    qkv_grad, out_weight_grad, gains_grad, biases_grad = (
        lax.psum_scatter(qkv_local, ("dp", "tensor"), scatter_dimension=0, tiled=True),
        lax.psum_scatter(out_local, ("dp", "tensor"), scatter_dimension=0, tiled=True),
        lax.psum_scatter(gains_local, ("dp", "tensor"), scatter_dimension=0, tiled=True),
        lax.psum_scatter(biases_local, ("dp", "tensor"), scatter_dimension=0, tiled=True),
    )
    scale_grad = lax.psum(scale_local, ("dp", "tensor"))
    return (
        mixed_out,
        token_grad,
        qkv_grad,
        out_weight_grad,
        gains_grad,
        biases_grad,
        scale_grad,
        fc1_grad,
        fc2_grad,
        mid_gain_grad,
        ffn_bias_grad,
    )


MESH = pl.DeviceIdType.MESH
ANY = pl.BlockSpec(memory_space=pl.ANY)
IN_VMEM = pl.BlockSpec(memory_space=pltpu.VMEM)


def place():
    z = lax.axis_index("dp")
    t = lax.axis_index("tensor")
    return z, lax.div(t, 4), lax.rem(lax.div(t, 2), 2), lax.rem(t, 2)


def at(z, y, x, c):
    return (z, y * 4 + x * 2 + c)


def greet(partners):
    barrier = pltpu.get_barrier_semaphore()
    for partner in partners:
        pl.semaphore_signal(barrier, inc=1, device_id=partner, device_id_type=MESH)
    pl.semaphore_wait(barrier, len(partners))


class Sends:
    def __init__(self, send_sems, recv_sems):
        self.send_sems, self.recv_sems, self.copies = send_sems, recv_sems, []

    def start(self, src, dst, target):
        index = len(self.copies)
        copy = pltpu.make_async_remote_copy(
            src_ref=src,
            dst_ref=dst,
            send_sem=self.send_sems.at[index],
            recv_sem=self.recv_sems.at[index],
            device_id=target,
            device_id_type=MESH,
        )
        copy.start()
        self.copies.append(copy)
        return copy

    def finish(self):
        for copy in self.copies:
            copy.wait_send()


def gather_kernel(
    nz,
    qkv_ref,
    out_ref,
    vec_ref,
    fc1_ref,
    fc2_ref,
    grad_ref,
    qkv_all,
    out_all,
    vec_all,
    fc1_all,
    fc2_all,
    grad_all,
    local_sems,
    send_sems,
    recv_sems,
):
    z, y, x, c = place()
    to_x, to_y, to_c = at(z, y, 1 - x, c), at(z, 1 - y, x, c), at(z, y, x, 1 - c)
    others = [lax.rem(z + k, nz) for k in range(1, nz)]
    slots = [z] + [lax.rem(z + nz - k, nz) for k in range(1, nz)]
    peers = [at(other, y, x, c) for other in others]
    greet([to_x, to_y, to_c] + peers)
    sends = Sends(send_sems, recv_sems)
    shards = ((qkv_ref, qkv_all), (out_ref, out_all))
    mine = []
    width1, width2 = fc1_ref.shape[0], fc2_ref.shape[1]
    own = [
        (qkv_ref, qkv_all.at[z, y, x, c]),
        (out_ref, out_all.at[z, y, x, c]),
        (vec_ref, vec_all.at[z, y, x, c]),
        (fc1_ref, fc1_all.at[pl.ds(pl.multiple_of(z * width1, width1), width1)]),
        (fc2_ref, fc2_all.at[:, pl.ds(pl.multiple_of(z * width2, width2), width2)]),
        (grad_ref, grad_all.at[y, x, c]),
    ]
    for index, (src, dst) in enumerate(own):
        copy = pltpu.make_async_copy(src, dst, local_sems.at[index])
        copy.start()
        mine.append(copy)

    def halves(ref):
        half = ref.shape[-1] // 2
        return pl.ds(0, half), pl.ds(half, half)

    vec_z = [sends.start(vec_ref, vec_all.at[z, y, x, c], peer) for peer in peers]
    vec_x = [sends.start(vec_ref, vec_all.at[z, y, x, c], to_x)]
    qkv_z = [sends.start(qkv_ref, qkv_all.at[z, y, x, c], peer) for peer in peers]

    def first(src, whole, slot, from_input):
        lo, hi = halves(src)
        one = src if from_input else whole.at[slot, y, x, c]
        return (
            sends.start(one.at[:, lo], whole.at[slot, y, x, c, :, lo], to_x),
            sends.start(one.at[:, hi], whole.at[slot, y, x, c, :, hi], to_y),
        )

    def second(whole, slot):
        lo, hi = halves(whole)
        return (
            sends.start(whole.at[slot, y, :, c, :, lo], whole.at[slot, y, :, c, :, lo], to_y),
            sends.start(whole.at[slot, :, x, c, :, hi], whole.at[slot, :, x, c, :, hi], to_x),
        )

    def third(whole, slot):
        return sends.start(whole.at[slot, :, :, c], whole.at[slot, :, :, c], to_c)

    def wait_all(copies):
        for copy in copies:
            copy.wait_recv()

    def spread(src, whole, arrivals, between):
        stage_a = [first(src, whole, z, True)]
        stage_b = []
        for k in range(1, nz):
            arrivals[k - 1].wait_recv()
            stage_a.append(first(src, whole, slots[k], False))
            if k == 1:
                between()
            if k >= 2:
                wait_all(stage_a[k - 2])
                stage_b.append(second(whole, slots[k - 2]))
        for k in range(len(stage_b), nz):
            wait_all(stage_a[k])
            stage_b.append(second(whole, slots[k]))
        return stage_b

    rest = {}

    def after_qkv_z():
        rest["out_z"] = [sends.start(out_ref, out_all.at[z, y, x, c], peer) for peer in peers]
        rest["fc"] = []
        for peer in peers:
            rest["fc"].append(sends.start(fc1_ref, own[3][1], peer))
            rest["fc"].append(sends.start(fc2_ref, own[4][1], peer))

    for copy in mine[:3]:
        copy.wait()
    qkv_b = spread(qkv_ref, qkv_all, qkv_z, after_qkv_z)
    wait_all(vec_z)
    for k in range(1, nz):
        vec_x.append(
            sends.start(vec_all.at[slots[k], y, x, c], vec_all.at[slots[k], y, x, c], to_x)
        )
    out_b = spread(out_ref, out_all, rest.get("out_z", []), lambda: None)
    wait_all(vec_x)
    vec_y = sends.start(vec_all.at[:, y, :, c], vec_all.at[:, y, :, c], to_y)
    lo, hi = halves(grad_ref)
    grad_a = (
        sends.start(grad_ref.at[:, lo], grad_all.at[y, x, c, :, lo], to_x),
        sends.start(grad_ref.at[:, hi], grad_all.at[y, x, c, :, hi], to_y),
    )
    qkv_c = []
    for k in range(nz):
        wait_all(qkv_b[k])
        qkv_c.append(third(qkv_all, slots[k]))
    vec_y.wait_recv()
    vec_c = sends.start(vec_all.at[:, :, :, c], vec_all.at[:, :, :, c], to_c)
    mine[5].wait()
    wait_all(grad_a)
    grad_b = (
        sends.start(grad_all.at[y, :, c, :, lo], grad_all.at[y, :, c, :, lo], to_y),
        sends.start(grad_all.at[:, x, c, :, hi], grad_all.at[:, x, c, :, hi], to_x),
    )
    out_c = []
    for k in range(nz):
        wait_all(out_b[k])
        out_c.append(third(out_all, slots[k]))
    wait_all(grad_b)
    grad_c = sends.start(grad_all.at[:, :, c], grad_all.at[:, :, c], to_c)
    wait_all(qkv_c + out_c + [vec_c, grad_c] + rest.get("fc", []))
    mine[3].wait()
    mine[4].wait()
    sends.finish()


def gather(nz, w_qkv, w_out, vectors, w_fc1, w_fc2, out_grad):
    def whole(shard, lead):
        return jax.ShapeDtypeStruct(lead + shard.shape, shard.dtype)

    every, plane = (nz, 2, 2, 2), (2, 2, 2)
    count = 4 * (nz - 1) + 5 * 2 * nz + 64
    return pl.pallas_call(
        functools.partial(gather_kernel, nz),
        name="gather",
        out_shape=(
            whole(w_qkv, every),
            whole(w_out, every),
            whole(vectors, every),
            jax.ShapeDtypeStruct((w_fc1.shape[0] * nz, w_fc1.shape[1]), w_fc1.dtype),
            jax.ShapeDtypeStruct((w_fc2.shape[0], w_fc2.shape[1] * nz), w_fc2.dtype),
            whole(out_grad, plane),
        ),
        in_specs=[ANY] * 6,
        out_specs=[ANY] * 6,
        scratch_shapes=[
            pltpu.SemaphoreType.DMA((6,)),
            pltpu.SemaphoreType.DMA((count,)),
            pltpu.SemaphoreType.DMA((count,)),
        ],
        compiler_params=pltpu.CompilerParams(collective_id=1, has_side_effects=True),
    )(w_qkv, w_out, vectors, w_fc1, w_fc2, out_grad)


def add_low(left, right):
    return (left.astype(jnp.float32) + right.astype(jnp.float32)).astype(jnp.bfloat16)


SQRT_2_PI = math.sqrt(2.0 / math.pi)
NT = (((1,), (1,)), ((), ()))
TN = (((0,), (0,)), ((), ()))


def dot(left, right, dims=None):
    if dims is None:
        return jnp.dot(left, right, preferred_element_type=jnp.float32)
    return lax.dot_general(left, right, dims, preferred_element_type=jnp.float32)


def ffn_kernel(
    mid_ref,
    og_ref,
    fc1_ref,
    fc2_ref,
    unit_ref,
    gnm_out,
    ffn_part,
    fc1_part,
    fc2_part,
    unit_out,
    mid_all,
    act,
    slope,
    grad,
    hidden,
    grad_pre,
    mid_part,
    pre,
    columns,
    stats,
    pair,
    got,
    totals,
    from_core,
    sums,
    from_one,
    from_two,
    local_sem,
    send_sems,
    recv_sems,
):
    z, y, x, c = place()
    to_x, to_y, to_c = at(z, y, 1 - x, c), at(z, 1 - y, x, c), at(z, y, x, 1 - c)
    to_xy = at(z, 1 - y, 1 - x, c)
    greet([to_x, to_y, to_c, to_xy])
    sends = Sends(send_sems, recv_sems)
    rows = mid_ref.shape[0]
    width = mid_ref.shape[1]
    units = fc1_ref.shape[1]
    half = rows // 2
    lo, hi = pl.ds(0, half), pl.ds(half, half)
    one_x = sends.start(mid_ref.at[lo], mid_all.at[y, x, c, lo], to_x)
    one_y = sends.start(mid_ref.at[hi], mid_all.at[y, x, c, hi], to_y)
    own_c = sends.start(mid_ref, mid_all.at[y, x, c], to_c)
    two_y = sends.start(mid_ref.at[lo], mid_all.at[y, x, c, lo], to_y)
    two_x = sends.start(mid_ref.at[hi], mid_all.at[y, x, c, hi], to_x)
    mine = pltpu.make_async_copy(mid_ref, mid_all.at[y, x, c], local_sem)
    mine.start()
    step = 32
    lane = lax.broadcasted_iota(jnp.int32, (step, 128), 1)

    def grads(yy, xx, cc):
        grad[yy, xx, cc] = dot(og_ref[yy, xx, cc], fc2_ref[...], NT)

    def forward(yy, xx, cc):
        pre[...] = dot(mid_all[yy, xx, cc], fc1_ref[...])

        def block(k, carry):
            part = pl.ds(pl.multiple_of(k * step, step), step)
            u = pre[part] + unit_ref[0:1]
            square = u * u
            th = jnp.tanh(SQRT_2_PI * u * (1.0 + 0.044715 * square))
            lift = 0.5 + 0.5 * th
            a = u * lift
            act[yy, xx, cc, part] = a
            slope[yy, xx, cc, part] = lift + (0.5 * SQRT_2_PI) * u * (1.0 - th * th) * (
                1.0 + (3 * 0.044715) * square
            )
            gm = grad[yy, xx, cc, part] * unit_ref[1:2]
            four = [
                jnp.sum(a, axis=1, keepdims=True),
                jnp.sum(a * a, axis=1, keepdims=True),
                jnp.sum(gm, axis=1, keepdims=True),
                jnp.sum(gm * a, axis=1, keepdims=True),
            ]
            tile = jnp.where(lane == 0, four[0], 0.0)
            for j in range(1, 4):
                tile = jnp.where(lane == j, four[j], tile)
            columns[part] = tile
            return carry

        lax.fori_loop(0, rows // step, block, 0)
        stats[yy, xx, cc] = columns[...].T[:8]

    grads(y, x, c)
    mine.wait()
    forward(y, x, c)
    grads(y, x, 1 - c)
    grads(y, 1 - x, c)
    one_x.wait_recv()
    one_y.wait_recv()
    ref_x, ref_y = mid_all.at[y, 1 - x, c, lo], mid_all.at[1 - y, x, c, hi]
    three_y = sends.start(ref_x, ref_x, to_y)
    three_x = sends.start(ref_y, ref_y, to_x)
    c_one = [sends.start(ref_x, ref_x, to_c), sends.start(ref_y, ref_y, to_c)]
    grads(1 - y, x, c)
    own_c.wait_recv()
    forward(y, x, 1 - c)
    grads(y, 1 - x, 1 - c)
    grads(1 - y, x, 1 - c)
    two_x.wait_recv()
    two_y.wait_recv()
    ref_x, ref_y = mid_all.at[y, 1 - x, c, hi], mid_all.at[1 - y, x, c, lo]
    c_two = [sends.start(ref_x, ref_x, to_c), sends.start(ref_y, ref_y, to_c)]
    forward(y, 1 - x, c)
    forward(1 - y, x, c)
    grads(1 - y, 1 - x, c)
    grads(1 - y, 1 - x, 1 - c)
    for copy in c_one + c_two:
        copy.wait_recv()
    forward(y, 1 - x, 1 - c)
    three_x.wait_recv()
    three_y.wait_recv()
    ref_xy = mid_all.at[1 - y, 1 - x, c]
    c_three = sends.start(ref_xy, ref_xy, to_c)
    forward(1 - y, x, 1 - c)
    forward(1 - y, 1 - x, c)
    c_three.wait_recv()
    forward(1 - y, 1 - x, 1 - c)

    sends.start(stats, got.at[3], to_c).wait_recv()
    pair[...] = stats[...] + got[3]
    arrivals = [
        sends.start(pair, got.at[k], plane) for k, plane in enumerate((to_x, to_y, to_xy))
    ]
    for copy in arrivals:
        copy.wait_recv()
    total = (pair[...] + got[0]) + (got[1] + got[2])
    total = total * (1.0 / (units * 8))
    center, second = total[:, :, :, 0:1], total[:, :, :, 1:2]
    first, cross = total[:, :, :, 2:3], total[:, :, :, 3:4]
    inverse = lax.rsqrt(second - center * center + EPS)
    totals[:, :, :, 0:1] = center
    totals[:, :, :, 1:2] = inverse
    totals[:, :, :, 2:3] = first
    totals[:, :, :, 3:4] = inverse * (cross - center * first)
    totals[:, :, :, 4:8] = jnp.zeros_like(total[:, :, :, 4:8])
    unit_out[...] = jnp.zeros_like(unit_out)

    def backward(yy, xx, cc):
        columns[...] = jnp.concatenate(
            [totals[yy, xx, cc], jnp.zeros((120, rows), jnp.float32)], axis=0
        ).T

        def block(k, carry):
            part = pl.ds(pl.multiple_of(k * step, step), step)
            center, inverse = columns[part, 0:1], columns[part, 1:2]
            first, second = columns[part, 2:3], columns[part, 3:4]
            gain = unit_ref[1:2]
            g = grad[yy, xx, cc, part]
            normed = (act[yy, xx, cc, part] - center) * inverse
            hidden[yy, xx, cc, part] = (normed * gain + unit_ref[2:3]).astype(jnp.bfloat16)
            back = inverse * (g * gain - first - normed * second)
            low = (back * slope[yy, xx, cc, part]).astype(jnp.bfloat16)
            grad_pre[yy, xx, cc, part] = low
            eight = (step // 8, 8, units)
            return (
                carry[0] + jnp.sum((g * normed).reshape(eight), axis=0),
                carry[1] + jnp.sum(low.astype(jnp.float32).reshape(eight), axis=0),
                carry[2] + jnp.sum(g.reshape(eight), axis=0),
            )

        zero = jnp.zeros((8, units), jnp.float32)
        parts = lax.fori_loop(0, rows // step, block, (zero, zero, zero))
        for j, part in enumerate(parts):
            unit_out[j : j + 1] += jnp.sum(part, axis=0, keepdims=True)
        mid_part[yy, xx, cc] = dot(grad_pre[yy, xx, cc], fc1_ref[...], NT).astype(jnp.bfloat16)

    left, right = pl.ds(0, width // 2), pl.ds(width // 2, width // 2)
    order = [(1 - y, 1 - x), (y, 1 - x), (1 - y, x), (y, x)]
    cores = []
    for yy, xx in order:
        backward(yy, xx, 1 - c)
        cores.append(sends.start(mid_part.at[yy, xx, 1 - c], from_core.at[yy, xx], to_c))
    stage_x, stage_y = [], []
    for k, (yy, xx) in enumerate(order):
        backward(yy, xx, c)
        cores[k].wait_recv()
        sums[yy, xx] = add_low(mid_part[yy, xx, c], from_core[yy, xx])
        if k in (0, 1):
            stage_x.append(
                sends.start(sums.at[yy, xx, :, left], from_one.at[0, yy, :, left], to_x)
            )
        if k in (0, 2):
            stage_y.append(
                sends.start(sums.at[yy, xx, :, right], from_one.at[1, xx, :, right], to_y)
            )

    def ffn_of(yy, xx, cc):
        ffn_part[yy, xx, cc] = dot(hidden[yy, xx, cc], fc2_ref[...]).astype(jnp.bfloat16)

    for yy, xx in order[:2]:
        ffn_of(yy, xx, 1 - c)
        ffn_of(yy, xx, c)
    for copy in (stage_x[0], stage_y[0]):
        copy.wait_recv()
    sums[1 - y, x, :, left] = add_low(sums[1 - y, x, :, left], from_one[0, 1 - y, :, left])
    sums[y, 1 - x, :, right] = add_low(sums[y, 1 - x, :, right], from_one[1, 1 - x, :, right])
    last_y = sends.start(sums.at[1 - y, x, :, left], from_two.at[:, left], to_y)
    last_x = sends.start(sums.at[y, 1 - x, :, right], from_two.at[:, right], to_x)
    for yy, xx in order[2:]:
        ffn_of(yy, xx, 1 - c)
        ffn_of(yy, xx, c)
    blocks = 4

    def fc1_block(k, carry):
        part = pl.ds(pl.multiple_of(k * (width // blocks), 128), width // blocks)
        block = jnp.zeros((width // blocks, units), jnp.float32)
        for j in range(8):
            yxc = (j // 4, (j // 2) % 2, j % 2)
            block = block + dot(mid_all[(*yxc, slice(None), part)], grad_pre[yxc], TN)
        fc1_part[part] = block.astype(jnp.bfloat16)
        return carry

    def fc2_block(k, carry):
        part = pl.ds(pl.multiple_of(k * (width // blocks), 128), width // blocks)
        block = jnp.zeros((units, width // blocks), jnp.float32)
        for j in range(8):
            yxc = (j // 4, (j // 2) % 2, j % 2)
            block = block + dot(hidden[yxc], og_ref[(*yxc, slice(None), part)], TN)
        fc2_part[:, part] = block.astype(jnp.bfloat16)
        return carry

    lax.fori_loop(0, blocks, fc1_block, 0)
    for copy in (stage_x[1], stage_y[1]):
        copy.wait_recv()
    lax.fori_loop(0, blocks, fc2_block, 0)
    last_x.wait_recv()
    last_y.wait_recv()
    own = sums[y, x].astype(jnp.float32)
    gnm_out[:, left] = (
        own[:, : width // 2]
        + from_one[0, y, :, left].astype(jnp.float32)
        + from_two[:, left].astype(jnp.float32)
    )
    gnm_out[:, right] = (
        own[:, width // 2 :]
        + from_one[1, x, :, right].astype(jnp.float32)
        + from_two[:, right].astype(jnp.float32)
    )
    sends.finish()


def ffn(mid, og_all, fc1, fc2, unit_rows):
    rows, width = mid.shape
    units = fc1.shape[1]
    low, plane = jnp.bfloat16, (2, 2, 2)
    sds = jax.ShapeDtypeStruct
    count = 32
    return pl.pallas_call(
        ffn_kernel,
        name="ffn",
        out_shape=(
            sds((rows, width), jnp.float32),
            sds(plane + (rows, width), low),
            sds(fc1.shape, low),
            sds(fc2.shape, low),
            sds((8, units), jnp.float32),
        ),
        in_specs=[IN_VMEM] * 5,
        out_specs=[IN_VMEM] * 5,
        scratch_shapes=[
            pltpu.VMEM(plane + (rows, width), low),
            pltpu.VMEM(plane + (rows, units), jnp.float32),
            pltpu.VMEM(plane + (rows, units), jnp.float32),
            pltpu.VMEM(plane + (rows, units), jnp.float32),
            pltpu.VMEM(plane + (rows, units), low),
            pltpu.VMEM(plane + (rows, units), low),
            pltpu.VMEM(plane + (rows, width), low),
            pltpu.VMEM((rows, units), jnp.float32),
            pltpu.VMEM((rows, 128), jnp.float32),
            pltpu.VMEM(plane + (8, rows), jnp.float32),
            pltpu.VMEM(plane + (8, rows), jnp.float32),
            pltpu.VMEM((4,) + plane + (8, rows), jnp.float32),
            pltpu.VMEM(plane + (8, rows), jnp.float32),
            pltpu.VMEM((2, 2, rows, width), low),
            pltpu.VMEM((2, 2, rows, width), low),
            pltpu.VMEM((2, 2, rows, width), low),
            pltpu.VMEM((rows, width), low),
            pltpu.SemaphoreType.DMA,
            pltpu.SemaphoreType.DMA((count,)),
            pltpu.SemaphoreType.DMA((count,)),
        ],
        compiler_params=pltpu.CompilerParams(
            collective_id=2, has_side_effects=True, vmem_limit_bytes=62 * 2**20
        ),
    )(mid, og_all, fc1, fc2, unit_rows)


def centered(values):
    center = jnp.mean(values, axis=-1, keepdims=True)
    spread = jnp.mean(values * values, axis=-1, keepdims=True) - center * center
    inverse = lax.rsqrt(spread + EPS)
    return (values - center) * inverse, inverse


def centered_back(grad, normed, inverse):
    first = jnp.mean(grad, axis=-1, keepdims=True)
    second = jnp.mean(grad * normed, axis=-1, keepdims=True)
    return inverse * (grad - first - normed * second)


def eights(values):
    return jnp.sum(values.reshape(values.shape[0] // 8, 8, values.shape[1]), axis=0)


def doc_mask(doc_ref, rows):
    query = lax.broadcasted_iota(jnp.int32, (rows, rows), 0)
    key = lax.broadcasted_iota(jnp.int32, (rows, rows), 1)
    query_doc, key_doc = jnp.zeros_like(query), jnp.zeros_like(key)
    end = 0
    for j in range(doc_ref.shape[1] - 1):
        end = end + doc_ref[0, j]
        query_doc = query_doc + (query >= end).astype(jnp.int32)
        key_doc = key_doc + (key >= end).astype(jnp.int32)
    allowed = jnp.logical_and(query_doc == key_doc, key <= query)
    return allowed.astype(jnp.float32)


def back_kernel(
    nz,
    gnm_ref,
    ffn_ref,
    fc1_ref,
    fc2_ref,
    unit_ref,
    proj_ref,
    att_ref,
    lse_ref,
    branch_ref,
    middle_ref,
    scaled_ref,
    nin_ref,
    qkv_ref,
    out_ref,
    vec_ref,
    og_ref,
    tok_ref,
    doc_ref,
    mixed_out,
    token_out,
    weight_out,
    gains_out,
    biases_out,
    scale_out,
    fc1_out,
    fc2_out,
    unit_out,
    f_core,
    f_sums,
    f_one,
    f_two,
    got1,
    got2,
    got_unit,
    w_part,
    w_core,
    w_sums,
    w_one,
    w_two,
    w_far,
    gpost,
    gmid,
    gatt,
    gni,
    dproj,
    nin_t,
    mask,
    accs,
    small,
    small_got,
    turned,
    local_sems,
    send_sems,
    recv_sems,
):
    z, y, x, c = place()
    to_x, to_y, to_c = at(z, y, 1 - x, c), at(z, 1 - y, x, c), at(z, y, x, 1 - c)
    to_xy = at(z, 1 - y, 1 - x, c)
    others = [lax.rem(z + k, nz) for k in range(1, nz)]
    peers = [at(other, y, x, c) for other in others]
    greet([to_x, to_y, to_c, to_xy] + peers)
    sends = Sends(send_sems, recv_sems)
    rows, width = middle_ref.shape
    low = jnp.bfloat16
    f32 = jnp.float32
    share = weight_out.shape[0]
    width1, width2 = fc1_out.shape[0], fc2_out.shape[1]

    pieces = 2
    parts = [pl.ds(k * (rows // pieces), rows // pieces) for k in range(pieces)]
    left, right = pl.ds(0, width // 2), pl.ds(width // 2, width // 2)
    f_c = [
        sends.start(ffn_ref.at[:, :, 1 - c, part], f_core.at[:, :, part], to_c) for part in parts
    ]
    locals_ = [
        pltpu.make_async_copy(ffn_ref.at[:, :, c], f_sums, local_sems.at[0]),
    ]

    def block1(which):
        return fc1_ref.at[pl.ds(pl.multiple_of(which * width1, width1), width1)]

    def block2(which):
        return fc2_ref.at[:, pl.ds(pl.multiple_of(which * width2, width2), width2)]

    locals_.append(pltpu.make_async_copy(block1(z), got1.at[nz - 1], local_sems.at[1]))
    locals_.append(pltpu.make_async_copy(block2(z), got2.at[nz - 1], local_sems.at[2]))
    for copy in locals_:
        copy.start()
    far = []
    for k, peer in enumerate(peers):
        far.append(sends.start(unit_ref, got_unit.at[k], peer))
        far.append(sends.start(block1(others[k]), got1.at[k], peer))
        far.append(sends.start(block2(others[k]), got2.at[k], peer))

    f_first, f_second = [], []

    def ffn_one(k):
        part = parts[k]
        f_c[k].wait_recv()
        if k == 0:
            locals_[0].wait()
        for yy in range(2):
            for xx in range(2):
                f_sums[yy, xx, part] = add_low(f_sums[yy, xx, part], f_core[yy, xx, part])
        f_first.append(
            (
                sends.start(f_sums.at[:, 1 - x, part, left], f_one.at[0, :, part, left], to_x),
                sends.start(f_sums.at[1 - y, :, part, right], f_one.at[1, :, part, right], to_y),
            )
        )

    def ffn_two(k):
        part = parts[k]
        for copy in f_first[k]:
            copy.wait_recv()
        f_sums[1 - y, x, part, left] = add_low(
            f_sums[1 - y, x, part, left], f_one[0, 1 - y, part, left]
        )
        f_sums[y, 1 - x, part, right] = add_low(
            f_sums[y, 1 - x, part, right], f_one[1, 1 - x, part, right]
        )
        f_second.append(
            (
                sends.start(f_sums.at[1 - y, x, part, left], f_two.at[part, left], to_y),
                sends.start(f_sums.at[y, 1 - x, part, right], f_two.at[part, right], to_x),
            )
        )

    def ffn_three(k):
        part = parts[k]
        for copy in f_second[k]:
            copy.wait_recv()
        for i, (cols, at_) in enumerate(((left, y), (right, x))):
            total = (
                f_sums[y, x, part, cols].astype(f32)
                + f_one[i, at_, part, cols].astype(f32)
                + f_two[part, cols].astype(f32)
            )
            mixed_out[part, cols] = (
                middle_ref[part, cols] + total + vec_ref[9:10, cols]
            ).astype(low)

    spans = [(0, width)] + [(width + g * 3 * width // 4, 3 * width // 4) for g in range(4)]
    w_first, w_second, w_third, w_c = {}, {}, {}, {}

    def sides(j):
        start, size = spans[j]
        return pl.ds(start, size), pl.ds(start, size // 2), pl.ds(start + size // 2, size // 2)

    def w_zero(j):
        every = sides(j)[0]
        w_c[j] = sends.start(w_part.at[:, :, :, 1 - c, :, every], w_core.at[..., every], to_c)

    def w_step1(j):
        every, lo, hi = sides(j)
        w_c[j].wait_recv()

        def one(which, carry):
            for yy in range(2):
                for xx in range(2):
                    w_sums[which, yy, xx, :, every] = add_low(
                        w_part[which, yy, xx, c, :, every], w_core[which, yy, xx, :, every]
                    )
            return carry

        lax.fori_loop(0, nz, one, 0)
        w_first[j] = (
            sends.start(w_sums.at[:, :, 1 - x, :, lo], w_one.at[:, :, :, lo], to_x),
            sends.start(w_sums.at[:, 1 - y, :, :, hi], w_one.at[:, :, :, hi], to_y),
        )

    def w_step2(j):
        every, lo, hi = sides(j)
        for copy in w_first[j]:
            copy.wait_recv()

        def one(which, carry):
            for k in range(2):
                w_sums[which, k, x, :, lo] = add_low(
                    w_sums[which, k, x, :, lo], w_one[which, k, :, lo]
                )
                w_sums[which, y, k, :, hi] = add_low(
                    w_sums[which, y, k, :, hi], w_one[which, k, :, hi]
                )
            return carry

        lax.fori_loop(0, nz, one, 0)
        w_second[j] = (
            sends.start(w_sums.at[:, 1 - y, x, :, lo], w_two.at[:, :, lo], to_y),
            sends.start(w_sums.at[:, y, 1 - x, :, hi], w_two.at[:, :, hi], to_x),
        )

    def w_step3(j):
        every = sides(j)[0]
        for copy in w_second[j]:
            copy.wait_recv()
        for which in range(nz):
            w_sums[which, y, x, :, every] = add_low(
                w_sums[which, y, x, :, every], w_two[which, :, every]
            )
        w_third[j] = [
            sends.start(w_sums.at[others[k], y, x, :, every], w_far.at[k, :, every], peer)
            for k, peer in enumerate(peers)
        ]

    def w_step4(j):
        start, size = spans[j]
        every = sides(j)[0]
        total = w_sums[z, y, x, :, every].astype(f32)
        for k in range(nz - 1):
            w_third[j][k].wait_recv()
            total = total + w_far[k, :, every].astype(f32)
        if j == 0:
            weight_out[:, 3 * width :] = total
        else:
            third = size // 3
            for i in range(3):
                first = i * width + (j - 1) * third
                weight_out[:, first : first + third] = total[:, i * third : (i + 1) * third]

    accs[...] = jnp.zeros_like(accs)
    step = 32

    def norms(k, carry):
        part = pl.ds(pl.multiple_of(k * step, step), step)
        normed_two, inverse_two = centered(middle_ref[part])
        grad = gnm_ref[part]
        og = og_ref[part].astype(f32)
        grad_middle = og + centered_back(grad * vec_ref[2:3], normed_two, inverse_two)
        accs[2] += eights(grad * normed_two)
        accs[8] += eights(grad)
        accs[9] += eights(og)
        normed_post, inverse_post = centered(branch_ref[part])
        post = centered_back(grad_middle * vec_ref[1:2], normed_post, inverse_post).astype(low)
        accs[1] += eights(grad_middle * normed_post)
        accs[7] += eights(grad_middle)
        accs[6] += eights(post.astype(f32))
        gpost[part] = post
        gmid[part] = grad_middle
        return carry

    lax.fori_loop(0, rows // step, norms, 0)
    mask[...] = doc_mask(doc_ref, rows)
    ffn_one(0)
    ffn_one(1)
    quarter = width // 4

    def scaled_block(k, carry):
        part = pl.ds(pl.multiple_of(k * quarter, quarter), quarter)
        block = dot(gpost[...], out_ref[part], NT)
        accs[10, :, part] = eights(block * att_ref[:, part])
        gatt[:, part] = (block * vec_ref[10:11, part]).astype(low)
        return carry

    lax.fori_loop(0, 4, scaled_block, 0)

    def out_block(k, carry):
        part = pl.ds(pl.multiple_of(k * (width // nz), width // nz), width // nz)
        block = dot(scaled_ref[:, part], gpost[...], TN).astype(low)
        w_part[k, :, :, :, :, pl.ds(0, width)] = block.reshape(2, 2, 2, share, width)
        return carry

    lax.fori_loop(0, nz, out_block, 0)
    w_zero(0)
    nin_t[...] = nin_ref[...].T
    head = 64
    lane = lax.broadcasted_iota(jnp.int32, (1, 128), 1)
    is_low = lane < head
    factor = 1.0 / math.sqrt(head)
    lane_wide = lax.broadcasted_iota(jnp.int32, (rows, 128), 1)
    keep = (is_low.astype(low), (lane >= head).astype(low))

    def pair(p, carry):
        q_at = pl.ds(pl.multiple_of(p * 128, 128), 128)
        k_at = pl.ds(pl.multiple_of(width + p * 128, 128), 128)
        v_at = pl.ds(pl.multiple_of(2 * width + p * 128, 128), 128)
        q2, k2, v2, do2 = proj_ref[:, q_at], proj_ref[:, k_at], proj_ref[:, v_at], gatt[:, q_at]
        lses = lse_ref[...]
        found = []
        for i in range(2):
            scores = dot(q2 * keep[i], k2, NT) * factor
            scores = jnp.where(mask[...] > 0, scores, NEGATIVE)
            lse = jnp.sum(jnp.where(lane_wide == 2 * p + i, lses, 0.0), axis=1, keepdims=True)
            prob = jnp.exp(scores - lse)
            grad_prob = dot(do2 * keep[i], v2, NT)
            inner = jnp.sum(prob * grad_prob, axis=1, keepdims=True)
            ds = (prob * (grad_prob - inner) * factor).astype(low)
            found.append(
                (dot(ds, k2), dot(ds, q2, TN), dot(prob.astype(low), do2, TN))
            )
        for where, a, b in zip((q_at, k_at, v_at), *found):
            dproj[:, where] = jnp.where(is_low, a, b).astype(low)
        accs[4, :, q_at] = eights(dproj[:, q_at].astype(f32))
        accs[5, :, q_at] = eights(dproj[:, v_at].astype(f32))
        return carry

    def wgrad(j):
        start, size = spans[j]
        third = size // 3

        def one(k, carry):
            part = pl.ds(pl.multiple_of(k * (width // nz), width // nz), width // nz)
            for i in range(3):
                first = i * width + (j - 1) * third
                block = dot(nin_t[part], dproj[:, first : first + third]).astype(low)
                w_part[k, :, :, :, :, pl.ds(start + i * third, third)] = block.reshape(
                    2, 2, 2, share, third
                )
            return carry

        lax.fori_loop(0, nz, one, 0)
        w_zero(j)

    lax.fori_loop(0, 2, pair, 0)
    wgrad(1)
    w_step1(0)
    ffn_two(0)
    lax.fori_loop(2, 4, pair, 0)
    wgrad(2)
    w_step1(1)
    ffn_two(1)
    lax.fori_loop(4, 6, pair, 0)
    wgrad(3)
    w_step1(2)
    lax.fori_loop(6, 8, pair, 0)
    wgrad(4)
    w_step1(3)
    w_step1(4)

    def gni_block(k, carry):
        part = pl.ds(pl.multiple_of(k * quarter, quarter), quarter)
        gni[:, part] = dot(dproj[...], qkv_ref[part], NT)
        return carry

    lax.fori_loop(0, 4, gni_block, 0)

    def tokens_back(k, carry):
        part = pl.ds(pl.multiple_of(k * step, step), step)
        normed, inverse = centered(tok_ref[part].astype(f32))
        grad = gni[part]
        token_out[part] = gmid[part] + centered_back(grad * vec_ref[0:1], normed, inverse)
        accs[0] += eights(grad * normed)
        accs[3] += eights(grad)
        return carry

    lax.fori_loop(0, rows // step, tokens_back, 0)
    for j in range(16):
        small[0, j : j + 1] = jnp.sum(accs[j], axis=0, keepdims=True)
    small_c = sends.start(small.at[0], small_got.at[0], to_c)
    w_step2(0)
    small_c.wait_recv()
    small[1] = small[0] + small_got[0]
    small_p = [
        sends.start(small.at[1], small_got.at[1 + k], to)
        for k, to in enumerate((to_x, to_y, to_xy))
    ]
    ffn_three(0)
    ffn_three(1)
    w_step2(1)
    for copy in small_p:
        copy.wait_recv()
    small[2] = (small[1] + small_got[1]) + (small_got[2] + small_got[3])
    small_z = [
        sends.start(small.at[2], small_got.at[4 + k], peer) for k, peer in enumerate(peers)
    ]
    w_step3(0)
    w_step2(2)
    w_step3(1)
    w_step2(3)
    w_step3(2)
    w_step2(4)
    w_step3(3)
    w_step4(0)
    total = small[2]
    for k in range(nz - 1):
        small_z[k].wait_recv()
        total = total + small_got[4 + k]
    scale_out[...] = total[8:16]
    index = (lax.axis_index("dp") * 8 + lax.axis_index("tensor")) * share
    mine = pl.ds(pl.multiple_of(index, share), share)
    pad = jnp.zeros((112, width), f32)
    turned[...] = jnp.concatenate([total, pad], axis=0).T
    gains_out[...] = turned[mine, 0:3]
    turned[...] = jnp.concatenate([total[3:10], pad, total[:9]], axis=0).T
    biases_out[...] = turned[mine, 0:7]
    w_step4(1)
    w_step4(2)
    w_step3(4)
    for copy in far:
        copy.wait_recv()
    for copy in locals_[1:]:
        copy.wait()
    own1, own2, unit = got1[nz - 1].astype(f32), got2[nz - 1].astype(f32), unit_ref[...]
    for k in range(nz - 1):
        own1 = own1 + got1[k].astype(f32)
        own2 = own2 + got2[k].astype(f32)
        unit = unit + got_unit[k]
    fc1_out[...] = own1
    fc2_out[...] = own2
    unit_out[...] = unit
    w_step4(3)
    w_step4(4)
    sends.finish()


def back(nz, *operands):
    (gnm, ffn_part, fc1, fc2, unit, proj, att, lse, branch, middle, scaled, nin, qkv, out, vec) = (
        operands[:15]
    )
    rows, width = middle.shape
    share = width // (nz * 8)
    columns = proj.shape[1] + width
    low, f32 = jnp.bfloat16, jnp.float32
    sds = jax.ShapeDtypeStruct
    fc1_own, fc2_own = (fc1.shape[0] // nz, fc1.shape[1]), (fc2.shape[0], fc2.shape[1] // nz)
    count = 64 + 8 * nz
    specs = [IN_VMEM] + [ANY] * 3 + [IN_VMEM] * 13 + [pl.BlockSpec(memory_space=pltpu.SMEM)]
    return pl.pallas_call(
        functools.partial(back_kernel, nz),
        name="back",
        out_shape=(
            sds((rows, width), low),
            sds((rows, width), f32),
            sds((share, columns), f32),
            sds((share, 3), f32),
            sds((share, 7), f32),
            sds((8, width), f32),
            sds(fc1_own, f32),
            sds(fc2_own, f32),
            sds(unit.shape, f32),
        ),
        in_specs=specs,
        out_specs=[IN_VMEM] * 9,
        scratch_shapes=[
            pltpu.VMEM((2, 2, rows, width), low),
            pltpu.VMEM((2, 2, rows, width), low),
            pltpu.VMEM((2, 2, rows, width), low),
            pltpu.VMEM((rows, width), low),
            pltpu.VMEM((nz,) + fc1_own, low),
            pltpu.VMEM((nz,) + fc2_own, low),
            pltpu.VMEM((nz - 1,) + unit.shape, f32),
            pltpu.VMEM((nz, 2, 2, 2, share, columns), low),
            pltpu.VMEM((nz, 2, 2, share, columns), low),
            pltpu.VMEM((nz, 2, 2, share, columns), low),
            pltpu.VMEM((nz, 2, share, columns), low),
            pltpu.VMEM((nz, share, columns), low),
            pltpu.VMEM((nz - 1, share, columns), low),
            pltpu.VMEM((rows, width), low),
            pltpu.VMEM((rows, width), f32),
            pltpu.VMEM((rows, width), low),
            pltpu.VMEM((rows, width), f32),
            pltpu.VMEM((rows, 3 * width), low),
            pltpu.VMEM((width, rows), low),
            pltpu.VMEM((rows, rows), f32),
            pltpu.VMEM((16, 8, width), f32),
            pltpu.VMEM((3, 16, width), f32),
            pltpu.VMEM((nz + 3, 16, width), f32),
            pltpu.VMEM((width, 128), f32),
            pltpu.SemaphoreType.DMA((3,)),
            pltpu.SemaphoreType.DMA((count,)),
            pltpu.SemaphoreType.DMA((count,)),
        ],
        compiler_params=pltpu.CompilerParams(
            collective_id=3, has_side_effects=True, vmem_limit_bytes=63 * 2**20
        ),
    )(*operands)


def fused(
    nz,
    tokens,
    out_grad,
    doc_lengths,
    w_qkv,
    w_out,
    gains,
    biases,
    head_scale,
    w_fc1,
    w_fc2,
    mid_gain,
    ffn_biases,
):
    model_width = tokens.shape[1]
    local_rows = tokens.shape[0]
    head_dim = model_width // HEADS
    factor = 1.0 / math.sqrt(head_dim)
    share = gains.shape[0]
    vectors = jnp.concatenate(
        [gains, biases, jnp.zeros((share, 128 - gains.shape[1] - biases.shape[1]), jnp.float32)],
        axis=1,
    )
    qkv_full, out_full, vec_full, fc1_rows, fc2_cols, shard_rows = gather(
        nz, w_qkv, w_out, vectors, w_fc1, w_fc2, out_grad
    )
    qkv_full = qkv_full.reshape(model_width, -1)
    out_full = out_full.reshape(model_width, -1)
    vec_full = vec_full.reshape(model_width, 128)
    vec_rows = vec_full[:, :10].T
    gain_full = vec_rows[:3]
    bias_full = vec_rows[3:]
    doc_ends = jnp.cumsum(doc_lengths[0])[:-1]
    places = jnp.arange(local_rows)
    doc_ids = jnp.sum((places[:, None] >= doc_ends[None, :]).astype(jnp.int32), axis=1)
    inputs = tokens.astype(jnp.float32)
    normed_one, inverse_one = normalize(inputs)
    normed_in = (normed_one * gain_full[0] + bias_full[0]).astype(jnp.bfloat16)
    zero_bias = jnp.zeros((model_width,), jnp.float32)
    qkv_bias = jnp.concatenate([bias_full[1], zero_bias, bias_full[2]])
    projected = (
        jnp.dot(normed_in, qkv_full, preferred_element_type=jnp.float32) + qkv_bias
    ).astype(jnp.bfloat16)
    query_rows = projected[:, :model_width].reshape(local_rows, HEADS, head_dim)
    key_rows = projected[:, model_width : 2 * model_width].reshape(local_rows, HEADS, head_dim)
    value_rows = projected[:, 2 * model_width :].reshape(local_rows, HEADS, head_dim)
    attended, sums_log = attend_forward(query_rows, key_rows, value_rows, doc_ids, factor)
    attended = attended.reshape(local_rows, model_width)
    scale_wide = jnp.repeat(head_scale, head_dim)
    scaled = (attended * scale_wide).astype(jnp.bfloat16)
    branch = jnp.dot(scaled, out_full, preferred_element_type=jnp.float32) + bias_full[3]
    normed_post, inverse_post = normalize(branch)
    middle = inputs + normed_post * gain_full[1] + bias_full[4]
    normed_two, inverse_two = normalize(middle)
    normed_mid = (normed_two * gain_full[2] + bias_full[5]).astype(jnp.bfloat16)
    units = w_fc1.shape[1]
    unit_rows = jnp.concatenate(
        [ffn_biases[:1], mid_gain[None], ffn_biases[1:], jnp.zeros((5, units), jnp.float32)]
    )
    grad_normed_mid, ffn_part, fc1_part, fc2_part, unit_sums = ffn(
        normed_mid, shard_rows, fc1_rows, fc2_cols, unit_rows
    )
    lse = jnp.pad(sums_log[0][:, :, 0].T, ((0, 0), (0, 128 - HEADS)))
    vec = jnp.concatenate([vec_rows, scale_wide[None], jnp.zeros((5, model_width), jnp.float32)])
    (
        mixed_out,
        token_grad,
        weight_grad,
        gains_grad,
        biases_grad,
        scale_sums,
        fc1_grad,
        fc2_grad,
        unit_sums,
    ) = back(
        nz,
        grad_normed_mid,
        ffn_part,
        fc1_part,
        fc2_part,
        unit_sums,
        projected,
        attended,
        lse,
        branch,
        middle,
        scaled,
        normed_in,
        qkv_full,
        out_full,
        vec,
        out_grad,
        tokens,
        doc_lengths,
    )
    return (
        mixed_out,
        token_grad,
        weight_grad[:, : w_qkv.shape[1]],
        weight_grad[:, w_qkv.shape[1] :],
        gains_grad,
        biases_grad,
        jnp.sum(scale_sums[2].reshape(HEADS, head_dim), axis=1),
        fc1_grad,
        fc2_grad,
        unit_sums[0],
        unit_sums[1:3],
    )


def layer(nz, nt, tokens, out_grad, doc_lengths, w_qkv, *rest):
    if nt == 8 and nz > 1 and w_qkv.shape[0] % 16 == 0:
        return fused(nz, tokens, out_grad, doc_lengths, w_qkv, *rest)
    return plain(tokens, out_grad, doc_lengths, w_qkv, *rest)


def solution(mesh):
    return jax.shard_map(
        functools.partial(layer, mesh.shape["dp"], mesh.shape["tensor"]),
        mesh=mesh,
        in_specs=(
            P(("dp", "tensor"), None),
            P(("dp", "tensor"), None),
            P(("dp", "tensor"), None),
            P(("dp", "tensor"), None),
            P(("dp", "tensor"), None),
            P(("dp", "tensor"), None),
            P(("dp", "tensor"), None),
            P(),
            P("dp", "tensor"),
            P("tensor", "dp"),
            P("tensor"),
            P(None, "tensor"),
        ),
        out_specs=(
            P(("dp", "tensor"), None),
            P(("dp", "tensor"), None),
            P(("dp", "tensor"), None),
            P(("dp", "tensor"), None),
            P(("dp", "tensor"), None),
            P(("dp", "tensor"), None),
            P(),
            P("dp", "tensor"),
            P("tensor", "dp"),
            P("tensor"),
            P(None, "tensor"),
        ),
        check_vma=False,
    )
```

```python
import functools
import math

import jax
import jax.numpy as jnp
from jax import lax
from jax.experimental import pallas as pl
from jax.experimental.pallas import tpu as pltpu
from jax.sharding import PartitionSpec as P

HEADS = 16
FF = 4096


EPS = 1e-05
NEGATIVE = -1000000000.0


def normalize(values):
    center = jnp.mean(values, axis=-1, keepdims=True)
    spread = jnp.mean(values * values, axis=-1, keepdims=True) - center * center
    inverse = lax.rsqrt(spread + EPS)
    return ((values - center) * inverse, inverse)


def normalize_back(grad_normed, normed, inverse):
    first_mean = jnp.mean(grad_normed, axis=-1, keepdims=True)
    second = jnp.mean(grad_normed * normed, axis=-1, keepdims=True)
    return inverse * (grad_normed - first_mean - normed * second)


def block_scores(query_rows, key_rows, doc_ids, row_first, row_last, factor):
    scores = (
        jnp.einsum("qhd,khd->hqk", query_rows, key_rows, preferred_element_type=jnp.float32)
        * factor
    )
    query_pos = jnp.arange(row_first, row_last)
    key_pos = jnp.arange(row_last)
    same_doc = doc_ids[row_first:row_last, None] == doc_ids[None, :row_last]
    allowed = jnp.logical_and(same_doc, key_pos[None, :] <= query_pos[:, None])
    return (jnp.where(allowed[None], scores, NEGATIVE), allowed)


def attend_forward(query_rows, key_rows, value_rows, doc_ids, factor):
    total_rows = query_rows.shape[0]
    block_rows = min(512, total_rows)
    scores, allowed = block_scores(query_rows, key_rows, doc_ids, 0, block_rows, factor)
    row_peak = jnp.max(scores, axis=-1, keepdims=True)
    exponent = jnp.exp(scores - row_peak)
    row_total = jnp.sum(exponent, axis=-1, keepdims=True)
    prob_low = (exponent / row_total).astype(jnp.bfloat16)
    pieces = jnp.einsum("hqk,khd->qhd", prob_low, value_rows, preferred_element_type=jnp.float32)
    sums_log = [row_peak + jnp.log(row_total)]
    return (pieces, sums_log)


def attend_backward(query_rows, key_rows, value_rows, grad_out, doc_ids, sums_log, factor):
    total_rows = query_rows.shape[0]
    block_rows = min(512, total_rows)
    query_parts = []
    grad_keys = jnp.zeros(key_rows.shape, jnp.float32)
    grad_values = jnp.zeros(value_rows.shape, jnp.float32)
    for block_index, row_first in enumerate(range(0, total_rows, block_rows)):
        row_last = row_first + block_rows
        scores, allowed = block_scores(query_rows, key_rows, doc_ids, row_first, row_last, factor)
        prob_rows = jnp.where(allowed[None], jnp.exp(scores - sums_log[block_index]), 0.0)
        prob_low = prob_rows.astype(jnp.bfloat16)
        grad_probs = jnp.einsum(
            "qhd,khd->hqk", grad_out, value_rows, preferred_element_type=jnp.float32
        )
        inner_sum = jnp.sum(prob_rows * grad_probs, axis=-1, keepdims=True)
        grad_scores = (prob_rows * (grad_probs - inner_sum) * factor).astype(jnp.bfloat16)
        query_parts.append(
            jnp.einsum("hqk,khd->qhd", grad_scores, key_rows, preferred_element_type=jnp.float32)
        )
        grad_keys = grad_keys.at[:row_last].add(
            jnp.einsum("hqk,qhd->khd", grad_scores, query_rows, preferred_element_type=jnp.float32)
        )
        grad_values = grad_values.at[:row_last].add(
            jnp.einsum("hqk,qhd->khd", prob_low, grad_out, preferred_element_type=jnp.float32)
        )
    return (query_parts[0], grad_keys, grad_values)


def plain(
    tokens,
    out_grad,
    doc_lengths,
    w_qkv,
    w_out,
    gains,
    biases,
    head_scale,
    w_fc1,
    w_fc2,
    mid_gain,
    ffn_biases,
):
    qkv_full, out_full, gain_full, bias_full = (
        lax.all_gather(w_qkv, ("dp", "tensor"), axis=0, tiled=True),
        lax.all_gather(w_out, ("dp", "tensor"), axis=0, tiled=True),
        lax.all_gather(gains.astype(jnp.bfloat16), ("dp", "tensor"), axis=0, tiled=True).astype(
            gains.dtype
        ),
        lax.all_gather(biases.astype(jnp.bfloat16), ("dp", "tensor"), axis=0, tiled=True).astype(
            biases.dtype
        ),
    )
    fc1_rows, fc2_cols = (
        lax.all_gather(w_fc1, "dp", axis=0, tiled=True),
        lax.all_gather(w_fc2, "dp", axis=1, tiled=True),
    )
    model_width = tokens.shape[1]
    local_rows = tokens.shape[0]
    head_dim = model_width // HEADS
    factor = 1.0 / math.sqrt(head_dim)
    doc_ends = jnp.cumsum(doc_lengths[0])[:-1]
    places = jnp.arange(local_rows)
    doc_ids = jnp.sum((places[:, None] >= doc_ends[None, :]).astype(jnp.int32), axis=1)
    inputs = tokens.astype(jnp.float32)
    normed_one, inverse_one = normalize(inputs)
    normed_in = (normed_one * gain_full[:, 0] + bias_full[:, 0]).astype(jnp.bfloat16)
    zero_bias = jnp.zeros((model_width,), jnp.float32)
    qkv_bias = jnp.concatenate([bias_full[:, 1], zero_bias, bias_full[:, 2]])
    projected = (
        jnp.dot(normed_in, qkv_full, preferred_element_type=jnp.float32) + qkv_bias
    ).astype(jnp.bfloat16)
    query_rows = projected[:, :model_width].reshape(local_rows, HEADS, head_dim)
    key_rows = projected[:, model_width : 2 * model_width].reshape(local_rows, HEADS, head_dim)
    value_rows = projected[:, 2 * model_width :].reshape(local_rows, HEADS, head_dim)
    attended, sums_log = attend_forward(query_rows, key_rows, value_rows, doc_ids, factor)
    attended = attended.reshape(local_rows, model_width)
    scale_wide = jnp.repeat(head_scale, head_dim)
    scaled = (attended * scale_wide).astype(jnp.bfloat16)
    branch = jnp.dot(scaled, out_full, preferred_element_type=jnp.float32) + bias_full[:, 3]
    normed_post, inverse_post = normalize(branch)
    middle = inputs + normed_post * gain_full[:, 1] + bias_full[:, 4]
    normed_two, inverse_two = normalize(middle)
    normed_mid = (normed_two * gain_full[:, 2] + bias_full[:, 5]).astype(jnp.bfloat16)
    gathered = lax.all_gather(normed_mid, "tensor", axis=0, tiled=True)
    hidden_pre = jnp.dot(gathered, fc1_rows, preferred_element_type=jnp.float32) + ffn_biases[0]
    activated, gelu_pull = jax.vjp(jax.nn.gelu, hidden_pre)
    act_sum, act_square = (
        lax.psum(jnp.sum(activated, axis=1).astype(jnp.bfloat16), "tensor").astype(jnp.float32),
        lax.psum(jnp.sum(activated * activated, axis=1).astype(jnp.bfloat16), "tensor").astype(
            jnp.float32
        ),
    )
    center = act_sum / FF
    inverse_mid = lax.rsqrt(act_square / FF - center * center + EPS)[:, None]
    normed_act = (activated - center[:, None]) * inverse_mid
    hidden = (normed_act * mid_gain + ffn_biases[1]).astype(jnp.bfloat16)
    hidden_rows = hidden
    ffn_out = lax.psum_scatter(
        jnp.dot(hidden_rows, fc2_cols, preferred_element_type=jnp.float32).astype(jnp.bfloat16),
        "tensor",
        scatter_dimension=0,
        tiled=True,
    ).astype(jnp.float32)
    shard_rows = lax.all_gather(out_grad, "tensor", axis=0, tiled=True)
    grad_piece = jnp.einsum("rd,fd->rf", shard_rows, fc2_cols, preferred_element_type=jnp.float32)
    hidden_rows = hidden
    fc2_run = jnp.einsum("rf,rd->fd", hidden_rows, shard_rows, preferred_element_type=jnp.float32)
    mid_gain_part = jnp.sum(grad_piece * normed_act, axis=0)
    mid_bias_part = jnp.sum(grad_piece, axis=0)
    grad_normed_act = grad_piece * mid_gain
    first_sum, second_sum = (
        lax.psum(jnp.sum(grad_normed_act, axis=1).astype(jnp.bfloat16), "tensor").astype(
            jnp.float32
        ),
        lax.psum(
            jnp.sum(grad_normed_act * normed_act, axis=1).astype(jnp.bfloat16), "tensor"
        ).astype(jnp.float32),
    )
    grad_act = inverse_mid * (
        grad_normed_act - first_sum[:, None] / FF - normed_act * (second_sum[:, None] / FF)
    )
    grad_pre = gelu_pull(grad_act)[0].astype(jnp.bfloat16)
    fc1_part = jnp.einsum("rd,rf->df", gathered, grad_pre, preferred_element_type=jnp.float32)
    fc1_bias_part = jnp.sum(grad_pre.astype(jnp.float32), axis=0)
    grad_normed_mid = lax.psum_scatter(
        jnp.einsum("rf,df->rd", grad_pre, fc1_rows, preferred_element_type=jnp.float32).astype(
            jnp.bfloat16
        ),
        "tensor",
        scatter_dimension=0,
        tiled=True,
    ).astype(jnp.float32)
    ffn_bias_part = jnp.stack([fc1_bias_part, mid_bias_part])
    fc1_grad, fc2_grad = (
        lax.psum_scatter(
            fc1_part.astype(jnp.bfloat16), "dp", scatter_dimension=0, tiled=True
        ).astype(jnp.float32),
        lax.psum_scatter(
            fc2_run.astype(jnp.bfloat16), "dp", scatter_dimension=1, tiled=True
        ).astype(jnp.float32),
    )
    mid_gain_grad, ffn_bias_grad = lax.psum((mid_gain_part, ffn_bias_part), "dp")
    mixed_out = (middle + ffn_out + bias_full[:, 6]).astype(jnp.bfloat16)
    final_grad = out_grad.astype(jnp.float32)
    grad_middle = final_grad + normalize_back(
        grad_normed_mid * gain_full[:, 2], normed_two, inverse_two
    )
    grad_post = normalize_back(grad_middle * gain_full[:, 1], normed_post, inverse_post).astype(
        jnp.bfloat16
    )
    out_local = jnp.einsum("td,te->de", scaled, grad_post, preferred_element_type=jnp.float32)
    grad_scaled = jnp.einsum("te,de->td", grad_post, out_full, preferred_element_type=jnp.float32)
    scale_local = jnp.sum(
        (grad_scaled * attended).reshape(local_rows, HEADS, head_dim), axis=(0, 2)
    )
    grad_attended = (
        (grad_scaled * scale_wide).astype(jnp.bfloat16).reshape(local_rows, HEADS, head_dim)
    )
    grad_query, grad_keys, grad_values = attend_backward(
        query_rows, key_rows, value_rows, grad_attended, doc_ids, sums_log, factor
    )
    grad_projected = jnp.concatenate(
        [
            grad_query.reshape(local_rows, model_width),
            grad_keys.reshape(local_rows, model_width),
            grad_values.reshape(local_rows, model_width),
        ],
        axis=1,
    ).astype(jnp.bfloat16)
    qkv_local = jnp.einsum(
        "td,te->de", normed_in, grad_projected, preferred_element_type=jnp.float32
    )
    grad_normed_in = jnp.einsum(
        "te,de->td", grad_projected, qkv_full, preferred_element_type=jnp.float32
    )
    token_grad = grad_middle + normalize_back(
        grad_normed_in * gain_full[:, 0], normed_one, inverse_one
    )
    projected_sums = jnp.sum(grad_projected.astype(jnp.float32), axis=0)
    gains_local = jnp.stack(
        [
            jnp.sum(grad_normed_in * normed_one, axis=0),
            jnp.sum(grad_middle * normed_post, axis=0),
            jnp.sum(grad_normed_mid * normed_two, axis=0),
        ],
        axis=1,
    )
    biases_local = jnp.stack(
        [
            jnp.sum(grad_normed_in, axis=0),
            projected_sums[:model_width],
            projected_sums[2 * model_width :],
            jnp.sum(grad_post.astype(jnp.float32), axis=0),
            jnp.sum(grad_middle, axis=0),
            jnp.sum(grad_normed_mid, axis=0),
            jnp.sum(final_grad, axis=0),
        ],
        axis=1,
    )
    qkv_grad, out_weight_grad, gains_grad, biases_grad = (
        lax.psum_scatter(qkv_local, ("dp", "tensor"), scatter_dimension=0, tiled=True),
        lax.psum_scatter(out_local, ("dp", "tensor"), scatter_dimension=0, tiled=True),
        lax.psum_scatter(gains_local, ("dp", "tensor"), scatter_dimension=0, tiled=True),
        lax.psum_scatter(biases_local, ("dp", "tensor"), scatter_dimension=0, tiled=True),
    )
    scale_grad = lax.psum(scale_local, ("dp", "tensor"))
    return (
        mixed_out,
        token_grad,
        qkv_grad,
        out_weight_grad,
        gains_grad,
        biases_grad,
        scale_grad,
        fc1_grad,
        fc2_grad,
        mid_gain_grad,
        ffn_bias_grad,
    )


MESH = pl.DeviceIdType.MESH
ANY = pl.BlockSpec(memory_space=pl.ANY)
IN_VMEM = pl.BlockSpec(memory_space=pltpu.VMEM)


def place():
    z = lax.axis_index("dp")
    t = lax.axis_index("tensor")
    return z, lax.div(t, 4), lax.rem(lax.div(t, 2), 2), lax.rem(t, 2)


def at(z, y, x, c):
    return (z, y * 4 + x * 2 + c)


def greet(partners):
    barrier = pltpu.get_barrier_semaphore()
    for partner in partners:
        pl.semaphore_signal(barrier, inc=1, device_id=partner, device_id_type=MESH)
    pl.semaphore_wait(barrier, len(partners))


class Sends:
    def __init__(self, send_sems, recv_sems):
        self.send_sems, self.recv_sems, self.copies = send_sems, recv_sems, []

    def start(self, src, dst, target):
        index = len(self.copies)
        copy = pltpu.make_async_remote_copy(
            src_ref=src,
            dst_ref=dst,
            send_sem=self.send_sems.at[index],
            recv_sem=self.recv_sems.at[index],
            device_id=target,
            device_id_type=MESH,
        )
        copy.start()
        self.copies.append(copy)
        return copy

    def finish(self):
        for copy in self.copies:
            copy.wait_send()


def add_low(left, right):
    return (left.astype(jnp.float32) + right.astype(jnp.float32)).astype(jnp.bfloat16)


SQRT_2_PI = math.sqrt(2.0 / math.pi)
NT = (((1,), (1,)), ((), ()))
TN = (((0,), (0,)), ((), ()))


def dot(left, right, dims=None):
    if dims is None:
        return jnp.dot(left, right, preferred_element_type=jnp.float32)
    return lax.dot_general(left, right, dims, preferred_element_type=jnp.float32)


def centered(values):
    center = jnp.mean(values, axis=-1, keepdims=True)
    spread = jnp.mean(values * values, axis=-1, keepdims=True) - center * center
    inverse = lax.rsqrt(spread + EPS)
    return (values - center) * inverse, inverse


def centered_back(grad, normed, inverse):
    first = jnp.mean(grad, axis=-1, keepdims=True)
    second = jnp.mean(grad * normed, axis=-1, keepdims=True)
    return inverse * (grad - first - normed * second)


def eights(values):
    return jnp.sum(values.reshape(values.shape[0] // 8, 8, values.shape[1]), axis=0)


def doc_mask(doc_ref, rows):
    query = lax.broadcasted_iota(jnp.int32, (rows, rows), 0)
    key = lax.broadcasted_iota(jnp.int32, (rows, rows), 1)
    query_doc, key_doc = jnp.zeros_like(query), jnp.zeros_like(key)
    end = 0
    for j in range(doc_ref.shape[1] - 1):
        end = end + doc_ref[0, j]
        query_doc = query_doc + (query >= end).astype(jnp.int32)
        key_doc = key_doc + (key >= end).astype(jnp.int32)
    allowed = jnp.logical_and(query_doc == key_doc, key <= query)
    return allowed.astype(jnp.float32)


class Plane:
    def __init__(self, sends, whole, here, targets):
        self.sends, self.whole, self.here, self.targets = sends, whole, here, targets
        half = whole.shape[3] // 2
        self.lo, self.hi = pl.ds(0, half), pl.ds(half, half)

    def part(self, y, x, c, rows):
        return self.whole.at[y, x, c, rows]

    def start(self, src):
        (y, x, c), (to_x, to_y, to_c), lo, hi = self.here, self.targets, self.lo, self.hi
        go = self.sends.start
        self.first = [
            go(src.at[lo], self.part(y, x, c, lo), to_x),
            go(src.at[hi], self.part(y, x, c, hi), to_y),
        ]
        self.core = [go(src, self.whole.at[y, x, c], to_c)]
        self.second = [
            go(src.at[lo], self.part(y, x, c, lo), to_y),
            go(src.at[hi], self.part(y, x, c, hi), to_x),
        ]

    def after_first(self):
        (y, x, c), (to_x, to_y, to_c), lo, hi = self.here, self.targets, self.lo, self.hi
        for copy in self.first:
            copy.wait_recv()
        by_x, by_y = self.part(y, 1 - x, c, lo), self.part(1 - y, x, c, hi)
        go = self.sends.start
        self.third = [go(by_x, by_x, to_y), go(by_y, by_y, to_x)]
        self.side = [go(by_x, by_x, to_c), go(by_y, by_y, to_c)]

    def after_second(self):
        (y, x, c), (to_x, to_y, to_c), lo, hi = self.here, self.targets, self.lo, self.hi
        for copy in self.second:
            copy.wait_recv()
        by_x, by_y = self.part(y, 1 - x, c, hi), self.part(1 - y, x, c, lo)
        go = self.sends.start
        self.side += [go(by_x, by_x, to_c), go(by_y, by_y, to_c)]

    def after_third(self):
        y, x, c = self.here
        for copy in self.third:
            copy.wait_recv()
        ref = self.whole.at[1 - y, 1 - x, c]
        self.last = self.sends.start(ref, ref, self.targets[2])


def fore_kernel(
    nz,
    tok_ref,
    og_ref,
    qkv_ref,
    out_ref,
    gains_ref,
    biases_ref,
    fc1_ref,
    fc2_ref,
    unit_ref,
    doc_ref,
    scale_ref,
    qkv_out,
    out_out,
    vec_out,
    proj_out,
    att_out,
    lse_out,
    branch_out,
    middle_out,
    nin_out,
    scaled_out,
    ffn_out,
    fc1_out,
    fc2_out,
    gnm_out,
    unit_out,
    qkv_all,
    out_all,
    vec_all,
    vec_mine,
    fc1_all,
    fc2_all,
    og_all,
    tok,
    branch,
    nin,
    proj,
    att,
    lse,
    scaled,
    middle,
    mask,
    vec,
    mid_all,
    act,
    slope,
    grad,
    hidden,
    grad_pre,
    mid_part,
    pre,
    stats,
    pair,
    got,
    totals,
    from_core,
    sums,
    from_one,
    from_two,
    ffn_part,
    fc1_part,
    fc2_part,
    local_sems,
    send_sems,
    recv_sems,
):
    z, y, x, c = place()
    to_x, to_y, to_c = at(z, y, 1 - x, c), at(z, 1 - y, x, c), at(z, y, x, 1 - c)
    to_xy = at(z, 1 - y, 1 - x, c)
    others = [lax.rem(z + k, nz) for k in range(1, nz)]
    slots = [z] + [lax.rem(z + nz - k, nz) for k in range(1, nz)]
    peers = [at(other, y, x, c) for other in others]
    greet([to_x, to_y, to_c, to_xy] + peers)
    sends = Sends(send_sems, recv_sems)
    low, f32 = jnp.bfloat16, jnp.float32
    rows, width = tok.shape
    units = fc1_all.shape[1]
    width1, width2 = fc1_ref.shape[0], fc2_ref.shape[1]
    own1 = fc1_all.at[pl.ds(pl.multiple_of(z * width1, width1), width1)]
    own2 = fc2_all.at[:, pl.ds(pl.multiple_of(z * width2, width2), width2)]
    locals_ = []

    def fetch(src, dst):
        copy = pltpu.make_async_copy(src, dst, local_sems.at[len(locals_)])
        copy.start()
        locals_.append(copy)
        return copy

    def wait_all(copies):
        for copy in copies:
            copy.wait_recv()

    vec_mine[...] = jnp.zeros_like(vec_mine)
    vec_mine[:, 0:3] = gains_ref[...]
    vec_mine[:, 3:10] = biases_ref[...]
    vec_z = [sends.start(vec_mine, vec_all.at[z, y, x, c], peer) for peer in peers]
    qkv_z = [sends.start(qkv_ref, qkv_all.at[z, y, x, c], peer) for peer in peers]

    def halves(ref):
        half = ref.shape[-1] // 2
        return pl.ds(0, half), pl.ds(half, half)

    def first(src, whole, slot):
        lo, hi = halves(whole)
        one = src if src is not None else whole.at[slot, y, x, c]
        return (
            sends.start(one.at[:, lo], whole.at[slot, y, x, c, :, lo], to_x),
            sends.start(one.at[:, hi], whole.at[slot, y, x, c, :, hi], to_y),
        )

    def second(whole, slot):
        lo, hi = halves(whole)
        by_x, by_y = whole.at[slot, y, :, c, :, lo], whole.at[slot, :, x, c, :, hi]
        return (sends.start(by_x, by_x, to_y), sends.start(by_y, by_y, to_x))

    def third(whole, slot):
        ref = whole.at[slot, :, :, c]
        return sends.start(ref, ref, to_c)

    qkv_a = [first(qkv_ref, qkv_all, z)]
    tok_in = fetch(tok_ref, tok)
    qkv_in = fetch(qkv_ref, qkv_all.at[z, y, x, c])
    out_in = fetch(out_ref, out_all.at[z, y, x, c])
    fc1_in = fetch(fc1_ref, own1)
    fc2_in = fetch(fc2_ref, own2)
    og_in = fetch(og_ref, og_all.at[y, x, c])
    vec_all[z, y, x, c] = vec_mine[...]
    mask[...] = doc_mask(doc_ref, rows)
    step = 32
    tok_in.wait()

    def normed(k, carry):
        part = pl.ds(pl.multiple_of(k * step, step), step)
        branch[part] = centered(tok[part].astype(f32))[0]
        return carry

    lax.fori_loop(0, rows // step, normed, 0)
    wait_all(vec_z)
    by_x = vec_all.at[:, y, x, c]
    vec_x = sends.start(by_x, by_x, to_x)
    qkv_z[0].wait_recv()
    qkv_a.append(first(None, qkv_all, slots[1]))
    vec_x.wait_recv()
    by_y = vec_all.at[:, y, :, c]
    vec_y = sends.start(by_y, by_y, to_y)
    qkv_in.wait()
    wait_all(qkv_a[0])
    qkv_b = [second(qkv_all, slots[0])]
    vec_y.wait_recv()
    by_c = vec_all.at[:, :, :, c]
    vec_c = sends.start(by_c, by_c, to_c)
    for k in range(2, nz):
        qkv_z[k - 1].wait_recv()
        qkv_a.append(first(None, qkv_all, slots[k]))
    out_z = [sends.start(out_ref, out_all.at[z, y, x, c], peer) for peer in peers]
    pair_peer = at(z + 1 - 2 * lax.rem(z, 2), y, x, c)
    far_peer = peers[1]
    fc2_far = sends.start(fc2_ref, own2, far_peer)
    fc2_near = sends.start(fc2_ref, own2, pair_peer)
    fc1_z = [sends.start(fc1_ref, own1, peer) for peer in peers]
    vec_c.wait_recv()
    rows16 = vec_all[...].reshape(width, 128).T[:16]
    vec[...] = rows16
    spot = lax.broadcasted_iota(jnp.int32, (1, width), 1)
    head = 64
    wide = jnp.zeros((1, width), f32)
    for h in range(HEADS):
        inside = jnp.logical_and(spot >= h * head, spot < (h + 1) * head)
        wide = jnp.where(inside, scale_ref[h], wide)
    vec[10:11] = wide

    def scaled_in(k, carry):
        part = pl.ds(pl.multiple_of(k * step, step), step)
        nin[part] = (branch[part] * vec[0:1] + vec[3:4]).astype(low)
        return carry

    lax.fori_loop(0, rows // step, scaled_in, 0)
    for k in range(1, nz):
        wait_all(qkv_a[k])
        qkv_b.append(second(qkv_all, slots[k]))
    out_a = [first(out_ref, out_all, z)]
    for k in range(1, nz):
        out_z[k - 1].wait_recv()
        out_a.append(first(None, out_all, slots[k]))
    og = Plane(sends, og_all, (y, x, c), (to_x, to_y, to_c))
    og.start(og_ref)
    qkv_c = []
    for k in range(nz):
        wait_all(qkv_b[k])
        qkv_c.append(third(qkv_all, slots[k]))
    wait_all(qkv_c)
    saves = [fetch(qkv_all, qkv_out), fetch(vec, vec_out), fetch(nin, nin_out)]

    tile = width // 2
    for k in range(6):
        cols = pl.ds(k * tile, tile)
        block = dot(nin[...], qkv_all[:, :, :, :, :, cols].reshape(width, tile))
        if k < 2:
            block = block + vec[4:5, cols]
        if k >= 4:
            block = block + vec[5:6, pl.ds((k - 4) * tile, tile)]
        proj[:, cols] = block.astype(low)
    saves.append(fetch(proj, proj_out))
    out_in.wait()
    out_b = []
    for k in range(nz):
        wait_all(out_a[k])
        out_b.append(second(out_all, slots[k]))
    lane = lax.broadcasted_iota(jnp.int32, (1, 128), 1)
    is_low = lane < head
    keep = (is_low.astype(low), (lane >= head).astype(low))
    factor = 1.0 / math.sqrt(head)
    lane_wide = lax.broadcasted_iota(jnp.int32, (rows, 128), 1)
    lse[...] = jnp.zeros_like(lse)

    def attend(p, carry):
        q_at = pl.ds(pl.multiple_of(p * 128, 128), 128)
        k_at = pl.ds(pl.multiple_of(width + p * 128, 128), 128)
        v_at = pl.ds(pl.multiple_of(2 * width + p * 128, 128), 128)
        q2, k2, v2 = proj[:, q_at], proj[:, k_at], proj[:, v_at]
        found = []
        for i in range(2):
            scores = dot(q2 * keep[i], k2, NT) * factor
            scores = jnp.where(mask[...] > 0, scores, NEGATIVE)
            peak = jnp.max(scores, axis=1, keepdims=True)
            exponent = jnp.exp(scores - peak)
            total = jnp.sum(exponent, axis=1, keepdims=True)
            prob = (exponent * (1.0 / total)).astype(low)
            found.append(dot(prob, v2))
            lse[...] = jnp.where(lane_wide == 2 * p + i, peak + jnp.log(total), lse[...])
        both = jnp.where(is_low, *found)
        att[:, q_at] = both
        scaled[:, q_at] = (both * vec[10:11, q_at]).astype(low)
        return carry

    lax.fori_loop(0, 4, attend, 0)
    og.after_first()
    out_c = []
    for k in range(nz):
        wait_all(out_b[k])
        out_c.append(third(out_all, slots[k]))
    lax.fori_loop(4, 8, attend, 0)
    saves += [fetch(att, att_out), fetch(lse, lse_out), fetch(scaled, scaled_out)]
    wait_all(out_c)
    saves.append(fetch(out_all, out_out))
    quarter = width // 4
    for k in range(4):
        cols = pl.ds(k * quarter, quarter)
        block = dot(scaled[...], out_all[:, :, :, :, :, cols].reshape(width, quarter))
        branch[:, cols] = block + vec[6:7, cols]

    def middles(k, carry):
        part = pl.ds(pl.multiple_of(k * step, step), step)
        post = centered(branch[part])[0]
        value = tok[part].astype(f32) + post * vec[1:2] + vec[7:8]
        middle[part] = value
        mid_all[y, x, c, part] = (centered(value)[0] * vec[2:3] + vec[8:9]).astype(low)
        return carry

    lax.fori_loop(0, rows // step, middles, 0)
    mid = Plane(sends, mid_all, (y, x, c), (to_x, to_y, to_c))
    mid.start(mid_all.at[y, x, c])
    saves += [fetch(branch, branch_out), fetch(middle, middle_out)]

    def grads(yy, xx, cc):
        grad[yy, xx, cc] = dot(og_all[yy, xx, cc], fc2_all[...], NT)

    def fold(v):
        quarters = [v[:, k * (units // 4) : (k + 1) * (units // 4)] for k in range(4)]
        return (quarters[0] + quarters[1]) + (quarters[2] + quarters[3])

    def forward(yy, xx, cc):
        pre[...] = dot(mid_all[yy, xx, cc], fc1_all[...])

        def block(k, carry):
            part = pl.ds(pl.multiple_of(k * step, step), step)
            u = pre[part] + unit_ref[0:1]
            square = u * u
            th = jnp.tanh(u * (SQRT_2_PI + (SQRT_2_PI * 0.044715) * square))
            lift = 0.5 + 0.5 * th
            a = u * lift
            act[yy, xx, cc, part] = a
            bend = u * (2.0 * SQRT_2_PI + (6.0 * 0.044715 * SQRT_2_PI) * square)
            slope[yy, xx, cc, part] = lift + bend * (lift - lift * lift)
            gm = grad[yy, xx, cc, part] * unit_ref[1:2]
            for j, value in enumerate((a, a * a, gm, gm * a)):
                pre[part, j * (units // 4) : (j + 1) * (units // 4)] = fold(value)
            return carry

        lax.fori_loop(0, rows // step, block, 0)
        for j in range(4):
            folded = pre[:, j * (units // 4) : (j + 1) * (units // 4)]
            stats[yy, xx, cc, j : j + 1] = jnp.sum(folded.T, axis=0, keepdims=True)

    stats[...] = jnp.zeros_like(stats)
    og.after_second()
    fc2_in.wait()
    fc2_far.wait_recv()
    near = fc2_all.at[:, pl.ds(pl.multiple_of(others[1] * width2, width2), width2)]
    fc2_last = sends.start(near, near, pair_peer)
    fc2_near.wait_recv()
    og.after_third()
    fc1_in.wait()
    mid.after_first()
    fc2_last.wait_recv()
    og_in.wait()
    grads(y, x, c)
    wait_all(og.core)
    grads(y, x, 1 - c)
    grads(y, 1 - x, c)
    grads(1 - y, x, c)
    mid.after_second()
    wait_all(og.side)
    grads(y, 1 - x, 1 - c)
    grads(1 - y, x, 1 - c)
    grads(1 - y, 1 - x, c)
    og.last.wait_recv()
    grads(1 - y, 1 - x, 1 - c)
    wait_all(fc1_z)
    forward(y, x, c)
    wait_all(mid.core)
    forward(y, x, 1 - c)
    mid.after_third()
    forward(y, 1 - x, c)
    forward(1 - y, x, c)
    wait_all(mid.side)
    forward(y, 1 - x, 1 - c)
    forward(1 - y, x, 1 - c)
    forward(1 - y, 1 - x, c)
    mid.last.wait_recv()
    forward(1 - y, 1 - x, 1 - c)

    sends.start(stats, got.at[3], to_c).wait_recv()
    pair[...] = stats[...] + got[3]
    wait_all([sends.start(pair, got.at[k], to) for k, to in enumerate((to_x, to_y, to_xy))])
    total = (pair[...] + got[0]) + (got[1] + got[2])
    total = total * (1.0 / (units * 8))
    center, square = total[:, :, :, 0:1], total[:, :, :, 1:2]
    mean, cross = total[:, :, :, 2:3], total[:, :, :, 3:4]
    inverse = lax.rsqrt(square - center * center + EPS)
    totals[:, :, :, 0:1] = inverse
    totals[:, :, :, 1:2] = -center * inverse
    totals[:, :, :, 2:3] = inverse * mean
    totals[:, :, :, 3:4] = inverse * (inverse * (cross - center * mean))
    unit_out[...] = jnp.zeros_like(unit_out)

    def backward(yy, xx, cc):
        for j in range(4):
            spread = jnp.broadcast_to(totals[yy, xx, cc, j : j + 1], (128, rows))
            pre[:, j * 128 : (j + 1) * 128] = spread.T

        def block(k, carry):
            part = pl.ds(pl.multiple_of(k * step, step), step)

            def across(j):
                return jnp.concatenate([pre[part, j * 128 : (j + 1) * 128]] * (units // 128), axis=1)

            g = grad[yy, xx, cc, part]
            inverse = across(0)
            normed = act[yy, xx, cc, part] * inverse + across(1)
            gain = unit_ref[1:2]
            hidden[yy, xx, cc, part] = (normed * gain + unit_ref[2:3]).astype(low)
            back = g * gain * inverse - across(2) - normed * across(3)
            value = (back * slope[yy, xx, cc, part]).astype(low)
            grad_pre[yy, xx, cc, part] = value
            return (
                carry[0] + eights(g * normed),
                carry[1] + eights(value.astype(f32)),
                carry[2] + eights(g),
            )

        zero = jnp.zeros((8, units), f32)
        parts = lax.fori_loop(0, rows // step, block, (zero, zero, zero))
        for j, part in enumerate(parts):
            unit_out[j : j + 1] += jnp.sum(part, axis=0, keepdims=True)
        return dot(grad_pre[yy, xx, cc], fc1_all[...], NT)

    left, right = pl.ds(0, width // 2), pl.ds(width // 2, width // 2)
    order = [(1 - y, 1 - x), (y, 1 - x), (1 - y, x), (y, x)]
    stage_x, stage_y = [], []
    for k, (yy, xx) in enumerate(order):
        mid_part[yy, xx] = backward(yy, xx, 1 - c).astype(low)
        core = sends.start(mid_part.at[yy, xx], from_core.at[yy, xx], to_c)
        block = backward(yy, xx, c)
        core.wait_recv()
        sums[yy, xx] = (block + from_core[yy, xx].astype(f32)).astype(low)
        if k in (0, 1):
            stage_x.append(sends.start(sums.at[yy, xx, :, left], from_one.at[yy, :, left], to_x))
        if k in (0, 2):
            stage_y.append(sends.start(sums.at[yy, xx, :, right], from_one.at[xx, :, right], to_y))

    def ffn_of(yy, xx, cc):
        ffn_part[yy, xx, cc] = dot(hidden[yy, xx, cc], fc2_all[...]).astype(low)

    for yy, xx in order[:2]:
        ffn_of(yy, xx, 1 - c)
        ffn_of(yy, xx, c)
    wait_all((stage_x[0], stage_y[0]))
    sums[1 - y, x, :, left] = add_low(sums[1 - y, x, :, left], from_one[1 - y, :, left])
    sums[y, 1 - x, :, right] = add_low(sums[y, 1 - x, :, right], from_one[1 - x, :, right])
    last_y = sends.start(sums.at[1 - y, x, :, left], from_two.at[:, left], to_y)
    last_x = sends.start(sums.at[y, 1 - x, :, right], from_two.at[:, right], to_x)
    for yy, xx in order[2:]:
        ffn_of(yy, xx, 1 - c)
        ffn_of(yy, xx, c)
    saves.append(fetch(ffn_part, ffn_out))
    blocks = 4

    def fc1_block(k, carry):
        part = pl.ds(pl.multiple_of(k * (width // blocks), 128), width // blocks)
        block = jnp.zeros((width // blocks, units), f32)
        for j in range(8):
            yxc = (j // 4, (j // 2) % 2, j % 2)
            block = block + dot(mid_all[(*yxc, slice(None), part)], grad_pre[yxc], TN)
        fc1_part[part] = block.astype(low)
        return carry

    def fc2_block(k, carry):
        part = pl.ds(pl.multiple_of(k * (width // blocks), 128), width // blocks)
        block = jnp.zeros((units, width // blocks), f32)
        for j in range(8):
            yxc = (j // 4, (j // 2) % 2, j % 2)
            block = block + dot(hidden[yxc], og_all[(*yxc, slice(None), part)], TN)
        fc2_part[:, part] = block.astype(low)
        return carry

    lax.fori_loop(0, blocks, fc1_block, 0)
    saves.append(fetch(fc1_part, fc1_out))
    lax.fori_loop(0, blocks, fc2_block, 0)
    saves.append(fetch(fc2_part, fc2_out))
    wait_all((stage_x[1], stage_y[1], last_x, last_y))
    for cols, k in ((left, y), (right, x)):
        gnm_out[:, cols] = (
            sums[y, x, :, cols].astype(f32)
            + from_one[k, :, cols].astype(f32)
            + from_two[:, cols].astype(f32)
        )
    for copy in saves:
        copy.wait()
    sends.finish()


def fore(nz, tokens, og, doc_lengths, w_qkv, w_out, gains, biases, scale, fc1, fc2, unit_rows):
    rows, width = tokens.shape
    share, units = w_qkv.shape[0], fc1.shape[1]
    low, f32, plane, every = jnp.bfloat16, jnp.float32, (2, 2, 2), (nz, 2, 2, 2)
    sds, vm = jax.ShapeDtypeStruct, pltpu.VMEM
    count = 160
    smem = pl.BlockSpec(memory_space=pltpu.SMEM)
    shapes = (
        (every + w_qkv.shape, low),
        (every + w_out.shape, low),
        ((16, width), f32),
        ((rows, w_qkv.shape[1]), low),
        ((rows, width), f32),
        ((rows, 128), f32),
        ((rows, width), f32),
        ((rows, width), f32),
        ((rows, width), low),
        ((rows, width), low),
        (plane + (rows, width), low),
        ((width, units), low),
        ((units, width), low),
        ((rows, width), f32),
        ((8, units), f32),
    )
    return pl.pallas_call(
        functools.partial(fore_kernel, nz),
        name="fore",
        out_shape=tuple(sds(shape, kind) for shape, kind in shapes),
        in_specs=[ANY] * 4 + [IN_VMEM] * 2 + [ANY] * 2 + [IN_VMEM, smem, smem],
        out_specs=[ANY] * 13 + [IN_VMEM] * 2,
        scratch_shapes=[
            vm(every + w_qkv.shape, low),
            vm(every + w_out.shape, low),
            vm(every + (share, 128), f32),
            vm((share, 128), f32),
            vm((width, units), low),
            vm((units, width), low),
            vm(plane + (rows, width), low),
            vm((rows, width), low),
            vm((rows, width), f32),
            vm((rows, width), low),
            vm((rows, w_qkv.shape[1]), low),
            vm((rows, width), f32),
            vm((rows, 128), f32),
            vm((rows, width), low),
            vm((rows, width), f32),
            vm((rows, rows), f32),
            vm((16, width), f32),
            vm(plane + (rows, width), low),
            vm(plane + (rows, units), f32),
            vm(plane + (rows, units), f32),
            vm(plane + (rows, units), f32),
            vm(plane + (rows, units), low),
            vm(plane + (rows, units), low),
            vm((2, 2, rows, width), low),
            vm((rows, units), f32),
            vm(plane + (8, rows), f32),
            vm(plane + (8, rows), f32),
            vm((4,) + plane + (8, rows), f32),
            vm(plane + (8, rows), f32),
            vm((2, 2, rows, width), low),
            vm((2, 2, rows, width), low),
            vm((2, rows, width), low),
            vm((rows, width), low),
            vm(plane + (rows, width), low),
            vm((width, units), low),
            vm((units, width), low),
            pltpu.SemaphoreType.DMA((24,)),
            pltpu.SemaphoreType.DMA((count,)),
            pltpu.SemaphoreType.DMA((count,)),
        ],
        compiler_params=pltpu.CompilerParams(
            collective_id=1, has_side_effects=True, vmem_limit_bytes=63 * 2**20
        ),
    )(tokens, og, w_qkv, w_out, gains, biases, fc1, fc2, unit_rows, doc_lengths, scale)


def back_kernel(
    nz,
    gnm_ref,
    ffn_ref,
    fc1_ref,
    fc2_ref,
    unit_ref,
    proj_ref,
    att_ref,
    lse_ref,
    branch_ref,
    middle_ref,
    scaled_ref,
    nin_ref,
    qkv_ref,
    out_ref,
    vec_ref,
    og_ref,
    tok_ref,
    doc_ref,
    mixed_out,
    token_out,
    weight_out,
    gains_out,
    biases_out,
    scale_out,
    fc1_out,
    fc2_out,
    unit_out,
    f_core,
    f_sums,
    f_one,
    f_two,
    got1,
    got2,
    got_unit,
    w_part,
    w_core,
    w_sums,
    w_one,
    w_two,
    w_far,
    gpost,
    gmid,
    gatt,
    gni,
    dproj,
    nin_t,
    mask,
    accs,
    small,
    small_got,
    turned,
    local_sems,
    send_sems,
    recv_sems,
):
    z, y, x, c = place()
    to_x, to_y, to_c = at(z, y, 1 - x, c), at(z, 1 - y, x, c), at(z, y, x, 1 - c)
    to_xy = at(z, 1 - y, 1 - x, c)
    others = [lax.rem(z + k, nz) for k in range(1, nz)]
    peers = [at(other, y, x, c) for other in others]
    greet([to_x, to_y, to_c, to_xy] + peers)
    sends = Sends(send_sems, recv_sems)
    rows, width = middle_ref.shape
    low = jnp.bfloat16
    f32 = jnp.float32
    share = weight_out.shape[0]
    width1, width2 = fc1_out.shape[0], fc2_out.shape[1]

    pieces = 2
    parts = [pl.ds(k * (rows // pieces), rows // pieces) for k in range(pieces)]
    left, right = pl.ds(0, width // 2), pl.ds(width // 2, width // 2)
    f_c = [
        sends.start(ffn_ref.at[:, :, 1 - c, part], f_core.at[:, :, part], to_c) for part in parts
    ]
    locals_ = [
        pltpu.make_async_copy(ffn_ref.at[:, :, c], f_sums, local_sems.at[0]),
    ]

    def block1(which):
        return fc1_ref.at[pl.ds(pl.multiple_of(which * width1, width1), width1)]

    def block2(which):
        return fc2_ref.at[:, pl.ds(pl.multiple_of(which * width2, width2), width2)]

    locals_.append(pltpu.make_async_copy(block1(z), got1.at[nz - 1], local_sems.at[1]))
    locals_.append(pltpu.make_async_copy(block2(z), got2.at[nz - 1], local_sems.at[2]))
    for copy in locals_:
        copy.start()
    far = []
    for k, peer in enumerate(peers):
        far.append(sends.start(unit_ref, got_unit.at[k], peer))
        far.append(sends.start(block1(others[k]), got1.at[k], peer))
        far.append(sends.start(block2(others[k]), got2.at[k], peer))

    f_first, f_second = [], []

    def ffn_one(k):
        part = parts[k]
        f_c[k].wait_recv()
        if k == 0:
            locals_[0].wait()
        for yy in range(2):
            for xx in range(2):
                f_sums[yy, xx, part] = add_low(f_sums[yy, xx, part], f_core[yy, xx, part])
        f_first.append(
            (
                sends.start(f_sums.at[:, 1 - x, part, left], f_one.at[0, :, part, left], to_x),
                sends.start(f_sums.at[1 - y, :, part, right], f_one.at[1, :, part, right], to_y),
            )
        )

    def ffn_two(k):
        part = parts[k]
        for copy in f_first[k]:
            copy.wait_recv()
        f_sums[1 - y, x, part, left] = add_low(
            f_sums[1 - y, x, part, left], f_one[0, 1 - y, part, left]
        )
        f_sums[y, 1 - x, part, right] = add_low(
            f_sums[y, 1 - x, part, right], f_one[1, 1 - x, part, right]
        )
        f_second.append(
            (
                sends.start(f_sums.at[1 - y, x, part, left], f_two.at[part, left], to_y),
                sends.start(f_sums.at[y, 1 - x, part, right], f_two.at[part, right], to_x),
            )
        )

    def ffn_three(k):
        part = parts[k]
        for copy in f_second[k]:
            copy.wait_recv()
        for i, (cols, at_) in enumerate(((left, y), (right, x))):
            total = (
                f_sums[y, x, part, cols].astype(f32)
                + f_one[i, at_, part, cols].astype(f32)
                + f_two[part, cols].astype(f32)
            )
            mixed_out[part, cols] = (
                middle_ref[part, cols] + total + vec_ref[9:10, cols]
            ).astype(low)

    spans = [(0, width)] + [(width + g * 3 * width // 4, 3 * width // 4) for g in range(4)]
    w_first, w_second, w_third, w_c = {}, {}, {}, {}

    def sides(j):
        start, size = spans[j]
        return pl.ds(start, size), pl.ds(start, size // 2), pl.ds(start + size // 2, size // 2)

    def w_zero(j):
        every = sides(j)[0]
        w_c[j] = sends.start(w_part.at[:, :, :, 1 - c, :, every], w_core.at[..., every], to_c)

    def w_step1(j):
        every, lo, hi = sides(j)
        w_c[j].wait_recv()

        def one(which, carry):
            for yy in range(2):
                for xx in range(2):
                    w_sums[which, yy, xx, :, every] = add_low(
                        w_part[which, yy, xx, c, :, every], w_core[which, yy, xx, :, every]
                    )
            return carry

        lax.fori_loop(0, nz, one, 0)
        w_first[j] = (
            sends.start(w_sums.at[:, :, 1 - x, :, lo], w_one.at[:, :, :, lo], to_x),
            sends.start(w_sums.at[:, 1 - y, :, :, hi], w_one.at[:, :, :, hi], to_y),
        )

    def w_step2(j):
        every, lo, hi = sides(j)
        for copy in w_first[j]:
            copy.wait_recv()

        def one(which, carry):
            for k in range(2):
                w_sums[which, k, x, :, lo] = add_low(
                    w_sums[which, k, x, :, lo], w_one[which, k, :, lo]
                )
                w_sums[which, y, k, :, hi] = add_low(
                    w_sums[which, y, k, :, hi], w_one[which, k, :, hi]
                )
            return carry

        lax.fori_loop(0, nz, one, 0)
        w_second[j] = (
            sends.start(w_sums.at[:, 1 - y, x, :, lo], w_two.at[:, :, lo], to_y),
            sends.start(w_sums.at[:, y, 1 - x, :, hi], w_two.at[:, :, hi], to_x),
        )

    def w_step3(j):
        every = sides(j)[0]
        for copy in w_second[j]:
            copy.wait_recv()
        for which in range(nz):
            w_sums[which, y, x, :, every] = add_low(
                w_sums[which, y, x, :, every], w_two[which, :, every]
            )
        w_third[j] = [
            sends.start(w_sums.at[others[k], y, x, :, every], w_far.at[k, :, every], peer)
            for k, peer in enumerate(peers)
        ]

    def w_step4(j):
        start, size = spans[j]
        every = sides(j)[0]
        total = w_sums[z, y, x, :, every].astype(f32)
        for k in range(nz - 1):
            w_third[j][k].wait_recv()
            total = total + w_far[k, :, every].astype(f32)
        if j == 0:
            weight_out[:, 3 * width :] = total
        else:
            third = size // 3
            for i in range(3):
                first = i * width + (j - 1) * third
                weight_out[:, first : first + third] = total[:, i * third : (i + 1) * third]

    accs[...] = jnp.zeros_like(accs)
    step = 32

    def norms(k, carry):
        part = pl.ds(pl.multiple_of(k * step, step), step)
        normed_two, inverse_two = centered(middle_ref[part])
        grad = gnm_ref[part]
        og = og_ref[part].astype(f32)
        grad_middle = og + centered_back(grad * vec_ref[2:3], normed_two, inverse_two)
        accs[2] += eights(grad * normed_two)
        accs[8] += eights(grad)
        accs[9] += eights(og)
        normed_post, inverse_post = centered(branch_ref[part])
        post = centered_back(grad_middle * vec_ref[1:2], normed_post, inverse_post).astype(low)
        accs[1] += eights(grad_middle * normed_post)
        accs[7] += eights(grad_middle)
        accs[6] += eights(post.astype(f32))
        gpost[part] = post
        gmid[part] = grad_middle
        return carry

    lax.fori_loop(0, rows // step, norms, 0)
    mask[...] = doc_mask(doc_ref, rows)
    ffn_one(0)
    ffn_one(1)
    quarter = width // 4

    def scaled_block(k, carry):
        part = pl.ds(pl.multiple_of(k * quarter, quarter), quarter)
        block = dot(gpost[...], out_ref[part], NT)
        accs[10, :, part] = eights(block * att_ref[:, part])
        gatt[:, part] = (block * vec_ref[10:11, part]).astype(low)
        return carry

    lax.fori_loop(0, 4, scaled_block, 0)

    def out_block(k, carry):
        part = pl.ds(pl.multiple_of(k * (width // nz), width // nz), width // nz)
        block = dot(scaled_ref[:, part], gpost[...], TN).astype(low)
        w_part[k, :, :, :, :, pl.ds(0, width)] = block.reshape(2, 2, 2, share, width)
        return carry

    lax.fori_loop(0, nz, out_block, 0)
    w_zero(0)
    nin_t[...] = nin_ref[...].T
    head = 64
    lane = lax.broadcasted_iota(jnp.int32, (1, 128), 1)
    is_low = lane < head
    factor = 1.0 / math.sqrt(head)
    lane_wide = lax.broadcasted_iota(jnp.int32, (rows, 128), 1)
    keep = (is_low.astype(low), (lane >= head).astype(low))

    def pair(p, carry):
        q_at = pl.ds(pl.multiple_of(p * 128, 128), 128)
        k_at = pl.ds(pl.multiple_of(width + p * 128, 128), 128)
        v_at = pl.ds(pl.multiple_of(2 * width + p * 128, 128), 128)
        q2, k2, v2, do2 = proj_ref[:, q_at], proj_ref[:, k_at], proj_ref[:, v_at], gatt[:, q_at]
        lses = lse_ref[...]
        found = []
        for i in range(2):
            scores = dot(q2 * keep[i], k2, NT) * factor
            scores = jnp.where(mask[...] > 0, scores, NEGATIVE)
            lse = jnp.sum(jnp.where(lane_wide == 2 * p + i, lses, 0.0), axis=1, keepdims=True)
            prob = jnp.exp(scores - lse)
            grad_prob = dot(do2 * keep[i], v2, NT)
            inner = jnp.sum(prob * grad_prob, axis=1, keepdims=True)
            ds = (prob * (grad_prob - inner) * factor).astype(low)
            found.append(
                (dot(ds, k2), dot(ds, q2, TN), dot(prob.astype(low), do2, TN))
            )
        for where, a, b in zip((q_at, k_at, v_at), *found):
            dproj[:, where] = jnp.where(is_low, a, b).astype(low)
        accs[4, :, q_at] = eights(dproj[:, q_at].astype(f32))
        accs[5, :, q_at] = eights(dproj[:, v_at].astype(f32))
        return carry

    def wgrad(j):
        start, size = spans[j]
        third = size // 3

        def one(k, carry):
            part = pl.ds(pl.multiple_of(k * (width // nz), width // nz), width // nz)
            for i in range(3):
                first = i * width + (j - 1) * third
                block = dot(nin_t[part], dproj[:, first : first + third]).astype(low)
                w_part[k, :, :, :, :, pl.ds(start + i * third, third)] = block.reshape(
                    2, 2, 2, share, third
                )
            return carry

        lax.fori_loop(0, nz, one, 0)
        w_zero(j)

    lax.fori_loop(0, 2, pair, 0)
    wgrad(1)
    w_step1(0)
    ffn_two(0)
    lax.fori_loop(2, 4, pair, 0)
    wgrad(2)
    w_step1(1)
    ffn_two(1)
    lax.fori_loop(4, 6, pair, 0)
    wgrad(3)
    w_step1(2)
    lax.fori_loop(6, 8, pair, 0)
    wgrad(4)
    w_step1(3)
    w_step1(4)

    def gni_block(k, carry):
        part = pl.ds(pl.multiple_of(k * quarter, quarter), quarter)
        gni[:, part] = dot(dproj[...], qkv_ref[part], NT)
        return carry

    lax.fori_loop(0, 4, gni_block, 0)

    def tokens_back(k, carry):
        part = pl.ds(pl.multiple_of(k * step, step), step)
        normed, inverse = centered(tok_ref[part].astype(f32))
        grad = gni[part]
        token_out[part] = gmid[part] + centered_back(grad * vec_ref[0:1], normed, inverse)
        accs[0] += eights(grad * normed)
        accs[3] += eights(grad)
        return carry

    lax.fori_loop(0, rows // step, tokens_back, 0)
    for j in range(16):
        small[0, j : j + 1] = jnp.sum(accs[j], axis=0, keepdims=True)
    small_c = sends.start(small.at[0], small_got.at[0], to_c)
    w_step2(0)
    small_c.wait_recv()
    small[1] = small[0] + small_got[0]
    small_p = [
        sends.start(small.at[1], small_got.at[1 + k], to)
        for k, to in enumerate((to_x, to_y, to_xy))
    ]
    ffn_three(0)
    ffn_three(1)
    w_step2(1)
    for copy in small_p:
        copy.wait_recv()
    small[2] = (small[1] + small_got[1]) + (small_got[2] + small_got[3])
    small_z = [
        sends.start(small.at[2], small_got.at[4 + k], peer) for k, peer in enumerate(peers)
    ]
    w_step3(0)
    w_step2(2)
    w_step3(1)
    w_step2(3)
    w_step3(2)
    w_step2(4)
    w_step3(3)
    w_step4(0)
    total = small[2]
    for k in range(nz - 1):
        small_z[k].wait_recv()
        total = total + small_got[4 + k]
    scale_out[...] = total[8:16]
    index = (lax.axis_index("dp") * 8 + lax.axis_index("tensor")) * share
    mine = pl.ds(pl.multiple_of(index, share), share)
    pad = jnp.zeros((112, width), f32)
    turned[...] = jnp.concatenate([total, pad], axis=0).T
    gains_out[...] = turned[mine, 0:3]
    turned[...] = jnp.concatenate([total[3:10], pad, total[:9]], axis=0).T
    biases_out[...] = turned[mine, 0:7]
    w_step4(1)
    w_step4(2)
    w_step3(4)
    for copy in far:
        copy.wait_recv()
    for copy in locals_[1:]:
        copy.wait()
    own1, own2, unit = got1[nz - 1].astype(f32), got2[nz - 1].astype(f32), unit_ref[...]
    for k in range(nz - 1):
        own1 = own1 + got1[k].astype(f32)
        own2 = own2 + got2[k].astype(f32)
        unit = unit + got_unit[k]
    fc1_out[...] = own1
    fc2_out[...] = own2
    unit_out[...] = unit
    w_step4(3)
    w_step4(4)
    sends.finish()


def back(nz, *operands):
    (gnm, ffn_part, fc1, fc2, unit, proj, att, lse, branch, middle, scaled, nin, qkv, out, vec) = (
        operands[:15]
    )
    rows, width = middle.shape
    share = width // (nz * 8)
    columns = proj.shape[1] + width
    low, f32 = jnp.bfloat16, jnp.float32
    sds = jax.ShapeDtypeStruct
    fc1_own, fc2_own = (fc1.shape[0] // nz, fc1.shape[1]), (fc2.shape[0], fc2.shape[1] // nz)
    count = 64 + 8 * nz
    specs = [IN_VMEM] + [ANY] * 3 + [IN_VMEM] * 13 + [pl.BlockSpec(memory_space=pltpu.SMEM)]
    return pl.pallas_call(
        functools.partial(back_kernel, nz),
        name="back",
        out_shape=(
            sds((rows, width), low),
            sds((rows, width), f32),
            sds((share, columns), f32),
            sds((share, 3), f32),
            sds((share, 7), f32),
            sds((8, width), f32),
            sds(fc1_own, f32),
            sds(fc2_own, f32),
            sds(unit.shape, f32),
        ),
        in_specs=specs,
        out_specs=[IN_VMEM] * 9,
        scratch_shapes=[
            pltpu.VMEM((2, 2, rows, width), low),
            pltpu.VMEM((2, 2, rows, width), low),
            pltpu.VMEM((2, 2, rows, width), low),
            pltpu.VMEM((rows, width), low),
            pltpu.VMEM((nz,) + fc1_own, low),
            pltpu.VMEM((nz,) + fc2_own, low),
            pltpu.VMEM((nz - 1,) + unit.shape, f32),
            pltpu.VMEM((nz, 2, 2, 2, share, columns), low),
            pltpu.VMEM((nz, 2, 2, share, columns), low),
            pltpu.VMEM((nz, 2, 2, share, columns), low),
            pltpu.VMEM((nz, 2, share, columns), low),
            pltpu.VMEM((nz, share, columns), low),
            pltpu.VMEM((nz - 1, share, columns), low),
            pltpu.VMEM((rows, width), low),
            pltpu.VMEM((rows, width), f32),
            pltpu.VMEM((rows, width), low),
            pltpu.VMEM((rows, width), f32),
            pltpu.VMEM((rows, 3 * width), low),
            pltpu.VMEM((width, rows), low),
            pltpu.VMEM((rows, rows), f32),
            pltpu.VMEM((16, 8, width), f32),
            pltpu.VMEM((3, 16, width), f32),
            pltpu.VMEM((nz + 3, 16, width), f32),
            pltpu.VMEM((width, 128), f32),
            pltpu.SemaphoreType.DMA((3,)),
            pltpu.SemaphoreType.DMA((count,)),
            pltpu.SemaphoreType.DMA((count,)),
        ],
        compiler_params=pltpu.CompilerParams(
            collective_id=3, has_side_effects=True, vmem_limit_bytes=63 * 2**20
        ),
    )(*operands)


def fused(
    nz,
    tokens,
    out_grad,
    doc_lengths,
    w_qkv,
    w_out,
    gains,
    biases,
    head_scale,
    w_fc1,
    w_fc2,
    mid_gain,
    ffn_biases,
):
    units = w_fc1.shape[1]
    unit_rows = jnp.concatenate(
        [ffn_biases[:1], mid_gain[None], ffn_biases[1:], jnp.zeros((5, units), jnp.float32)]
    )
    (
        qkv_full,
        out_full,
        vec,
        proj,
        att,
        lse,
        branch,
        middle,
        nin,
        scaled,
        ffn_part,
        fc1_part,
        fc2_part,
        gnm,
        unit_sums,
    ) = fore(
        nz,
        tokens,
        out_grad,
        doc_lengths,
        w_qkv,
        w_out,
        gains,
        biases,
        head_scale,
        w_fc1,
        w_fc2,
        unit_rows,
    )
    model_width = tokens.shape[1]
    (
        mixed_out,
        token_grad,
        weight_grad,
        gains_grad,
        biases_grad,
        scale_sums,
        fc1_grad,
        fc2_grad,
        unit_sums,
    ) = back(
        nz,
        gnm,
        ffn_part,
        fc1_part,
        fc2_part,
        unit_sums,
        proj,
        att,
        lse,
        branch,
        middle,
        scaled,
        nin,
        qkv_full.reshape(model_width, -1),
        out_full.reshape(model_width, -1),
        vec,
        out_grad,
        tokens,
        doc_lengths,
    )
    return (
        mixed_out,
        token_grad,
        weight_grad[:, : w_qkv.shape[1]],
        weight_grad[:, w_qkv.shape[1] :],
        gains_grad,
        biases_grad,
        jnp.sum(scale_sums[2].reshape(HEADS, -1), axis=1),
        fc1_grad,
        fc2_grad,
        unit_sums[0],
        unit_sums[1:3],
    )


def layer(nz, nt, tokens, out_grad, doc_lengths, w_qkv, *rest):
    if nz == 4 and nt == 8 and w_qkv.shape[0] % 16 == 0:
        return fused(nz, tokens, out_grad, doc_lengths, w_qkv, *rest)
    return plain(tokens, out_grad, doc_lengths, w_qkv, *rest)


def solution(mesh):
    return jax.shard_map(
        functools.partial(layer, mesh.shape["dp"], mesh.shape["tensor"]),
        mesh=mesh,
        in_specs=(
            P(("dp", "tensor"), None),
            P(("dp", "tensor"), None),
            P(("dp", "tensor"), None),
            P(("dp", "tensor"), None),
            P(("dp", "tensor"), None),
            P(("dp", "tensor"), None),
            P(("dp", "tensor"), None),
            P(),
            P("dp", "tensor"),
            P("tensor", "dp"),
            P("tensor"),
            P(None, "tensor"),
        ),
        out_specs=(
            P(("dp", "tensor"), None),
            P(("dp", "tensor"), None),
            P(("dp", "tensor"), None),
            P(("dp", "tensor"), None),
            P(("dp", "tensor"), None),
            P(("dp", "tensor"), None),
            P(),
            P("dp", "tensor"),
            P("tensor", "dp"),
            P("tensor"),
            P(None, "tensor"),
        ),
        check_vma=False,
    )
```

```python
import functools
import math

import jax
import jax.numpy as jnp
from jax import lax
from jax.experimental import pallas as pl
from jax.experimental.pallas import tpu as pltpu
from jax.sharding import PartitionSpec as P

HEADS = 16
FF = 4096


EPS = 1e-05
NEGATIVE = -1000000000.0


def normalize(values):
    center = jnp.mean(values, axis=-1, keepdims=True)
    spread = jnp.mean(values * values, axis=-1, keepdims=True) - center * center
    inverse = lax.rsqrt(spread + EPS)
    return ((values - center) * inverse, inverse)


def normalize_back(grad_normed, normed, inverse):
    first_mean = jnp.mean(grad_normed, axis=-1, keepdims=True)
    second = jnp.mean(grad_normed * normed, axis=-1, keepdims=True)
    return inverse * (grad_normed - first_mean - normed * second)


def block_scores(query_rows, key_rows, doc_ids, row_first, row_last, factor):
    scores = (
        jnp.einsum("qhd,khd->hqk", query_rows, key_rows, preferred_element_type=jnp.float32)
        * factor
    )
    query_pos = jnp.arange(row_first, row_last)
    key_pos = jnp.arange(row_last)
    same_doc = doc_ids[row_first:row_last, None] == doc_ids[None, :row_last]
    allowed = jnp.logical_and(same_doc, key_pos[None, :] <= query_pos[:, None])
    return (jnp.where(allowed[None], scores, NEGATIVE), allowed)


def attend_forward(query_rows, key_rows, value_rows, doc_ids, factor):
    total_rows = query_rows.shape[0]
    block_rows = min(512, total_rows)
    scores, allowed = block_scores(query_rows, key_rows, doc_ids, 0, block_rows, factor)
    row_peak = jnp.max(scores, axis=-1, keepdims=True)
    exponent = jnp.exp(scores - row_peak)
    row_total = jnp.sum(exponent, axis=-1, keepdims=True)
    prob_low = (exponent / row_total).astype(jnp.bfloat16)
    pieces = jnp.einsum("hqk,khd->qhd", prob_low, value_rows, preferred_element_type=jnp.float32)
    sums_log = [row_peak + jnp.log(row_total)]
    return (pieces, sums_log)


def attend_backward(query_rows, key_rows, value_rows, grad_out, doc_ids, sums_log, factor):
    total_rows = query_rows.shape[0]
    block_rows = min(512, total_rows)
    query_parts = []
    grad_keys = jnp.zeros(key_rows.shape, jnp.float32)
    grad_values = jnp.zeros(value_rows.shape, jnp.float32)
    for block_index, row_first in enumerate(range(0, total_rows, block_rows)):
        row_last = row_first + block_rows
        scores, allowed = block_scores(query_rows, key_rows, doc_ids, row_first, row_last, factor)
        prob_rows = jnp.where(allowed[None], jnp.exp(scores - sums_log[block_index]), 0.0)
        prob_low = prob_rows.astype(jnp.bfloat16)
        grad_probs = jnp.einsum(
            "qhd,khd->hqk", grad_out, value_rows, preferred_element_type=jnp.float32
        )
        inner_sum = jnp.sum(prob_rows * grad_probs, axis=-1, keepdims=True)
        grad_scores = (prob_rows * (grad_probs - inner_sum) * factor).astype(jnp.bfloat16)
        query_parts.append(
            jnp.einsum("hqk,khd->qhd", grad_scores, key_rows, preferred_element_type=jnp.float32)
        )
        grad_keys = grad_keys.at[:row_last].add(
            jnp.einsum("hqk,qhd->khd", grad_scores, query_rows, preferred_element_type=jnp.float32)
        )
        grad_values = grad_values.at[:row_last].add(
            jnp.einsum("hqk,qhd->khd", prob_low, grad_out, preferred_element_type=jnp.float32)
        )
    return (query_parts[0], grad_keys, grad_values)


def plain(
    tokens,
    out_grad,
    doc_lengths,
    w_qkv,
    w_out,
    gains,
    biases,
    head_scale,
    w_fc1,
    w_fc2,
    mid_gain,
    ffn_biases,
):
    qkv_full, out_full, gain_full, bias_full = (
        lax.all_gather(w_qkv, ("dp", "tensor"), axis=0, tiled=True),
        lax.all_gather(w_out, ("dp", "tensor"), axis=0, tiled=True),
        lax.all_gather(gains.astype(jnp.bfloat16), ("dp", "tensor"), axis=0, tiled=True).astype(
            gains.dtype
        ),
        lax.all_gather(biases.astype(jnp.bfloat16), ("dp", "tensor"), axis=0, tiled=True).astype(
            biases.dtype
        ),
    )
    fc1_rows, fc2_cols = (
        lax.all_gather(w_fc1, "dp", axis=0, tiled=True),
        lax.all_gather(w_fc2, "dp", axis=1, tiled=True),
    )
    model_width = tokens.shape[1]
    local_rows = tokens.shape[0]
    head_dim = model_width // HEADS
    factor = 1.0 / math.sqrt(head_dim)
    doc_ends = jnp.cumsum(doc_lengths[0])[:-1]
    places = jnp.arange(local_rows)
    doc_ids = jnp.sum((places[:, None] >= doc_ends[None, :]).astype(jnp.int32), axis=1)
    inputs = tokens.astype(jnp.float32)
    normed_one, inverse_one = normalize(inputs)
    normed_in = (normed_one * gain_full[:, 0] + bias_full[:, 0]).astype(jnp.bfloat16)
    zero_bias = jnp.zeros((model_width,), jnp.float32)
    qkv_bias = jnp.concatenate([bias_full[:, 1], zero_bias, bias_full[:, 2]])
    projected = (
        jnp.dot(normed_in, qkv_full, preferred_element_type=jnp.float32) + qkv_bias
    ).astype(jnp.bfloat16)
    query_rows = projected[:, :model_width].reshape(local_rows, HEADS, head_dim)
    key_rows = projected[:, model_width : 2 * model_width].reshape(local_rows, HEADS, head_dim)
    value_rows = projected[:, 2 * model_width :].reshape(local_rows, HEADS, head_dim)
    attended, sums_log = attend_forward(query_rows, key_rows, value_rows, doc_ids, factor)
    attended = attended.reshape(local_rows, model_width)
    scale_wide = jnp.repeat(head_scale, head_dim)
    scaled = (attended * scale_wide).astype(jnp.bfloat16)
    branch = jnp.dot(scaled, out_full, preferred_element_type=jnp.float32) + bias_full[:, 3]
    normed_post, inverse_post = normalize(branch)
    middle = inputs + normed_post * gain_full[:, 1] + bias_full[:, 4]
    normed_two, inverse_two = normalize(middle)
    normed_mid = (normed_two * gain_full[:, 2] + bias_full[:, 5]).astype(jnp.bfloat16)
    gathered = lax.all_gather(normed_mid, "tensor", axis=0, tiled=True)
    hidden_pre = jnp.dot(gathered, fc1_rows, preferred_element_type=jnp.float32) + ffn_biases[0]
    activated, gelu_pull = jax.vjp(jax.nn.gelu, hidden_pre)
    act_sum, act_square = (
        lax.psum(jnp.sum(activated, axis=1).astype(jnp.bfloat16), "tensor").astype(jnp.float32),
        lax.psum(jnp.sum(activated * activated, axis=1).astype(jnp.bfloat16), "tensor").astype(
            jnp.float32
        ),
    )
    center = act_sum / FF
    inverse_mid = lax.rsqrt(act_square / FF - center * center + EPS)[:, None]
    normed_act = (activated - center[:, None]) * inverse_mid
    hidden = (normed_act * mid_gain + ffn_biases[1]).astype(jnp.bfloat16)
    hidden_rows = hidden
    ffn_out = lax.psum_scatter(
        jnp.dot(hidden_rows, fc2_cols, preferred_element_type=jnp.float32).astype(jnp.bfloat16),
        "tensor",
        scatter_dimension=0,
        tiled=True,
    ).astype(jnp.float32)
    shard_rows = lax.all_gather(out_grad, "tensor", axis=0, tiled=True)
    grad_piece = jnp.einsum("rd,fd->rf", shard_rows, fc2_cols, preferred_element_type=jnp.float32)
    hidden_rows = hidden
    fc2_run = jnp.einsum("rf,rd->fd", hidden_rows, shard_rows, preferred_element_type=jnp.float32)
    mid_gain_part = jnp.sum(grad_piece * normed_act, axis=0)
    mid_bias_part = jnp.sum(grad_piece, axis=0)
    grad_normed_act = grad_piece * mid_gain
    first_sum, second_sum = (
        lax.psum(jnp.sum(grad_normed_act, axis=1).astype(jnp.bfloat16), "tensor").astype(
            jnp.float32
        ),
        lax.psum(
            jnp.sum(grad_normed_act * normed_act, axis=1).astype(jnp.bfloat16), "tensor"
        ).astype(jnp.float32),
    )
    grad_act = inverse_mid * (
        grad_normed_act - first_sum[:, None] / FF - normed_act * (second_sum[:, None] / FF)
    )
    grad_pre = gelu_pull(grad_act)[0].astype(jnp.bfloat16)
    fc1_part = jnp.einsum("rd,rf->df", gathered, grad_pre, preferred_element_type=jnp.float32)
    fc1_bias_part = jnp.sum(grad_pre.astype(jnp.float32), axis=0)
    grad_normed_mid = lax.psum_scatter(
        jnp.einsum("rf,df->rd", grad_pre, fc1_rows, preferred_element_type=jnp.float32).astype(
            jnp.bfloat16
        ),
        "tensor",
        scatter_dimension=0,
        tiled=True,
    ).astype(jnp.float32)
    ffn_bias_part = jnp.stack([fc1_bias_part, mid_bias_part])
    fc1_grad, fc2_grad = (
        lax.psum_scatter(
            fc1_part.astype(jnp.bfloat16), "dp", scatter_dimension=0, tiled=True
        ).astype(jnp.float32),
        lax.psum_scatter(
            fc2_run.astype(jnp.bfloat16), "dp", scatter_dimension=1, tiled=True
        ).astype(jnp.float32),
    )
    mid_gain_grad, ffn_bias_grad = lax.psum((mid_gain_part, ffn_bias_part), "dp")
    mixed_out = (middle + ffn_out + bias_full[:, 6]).astype(jnp.bfloat16)
    final_grad = out_grad.astype(jnp.float32)
    grad_middle = final_grad + normalize_back(
        grad_normed_mid * gain_full[:, 2], normed_two, inverse_two
    )
    grad_post = normalize_back(grad_middle * gain_full[:, 1], normed_post, inverse_post).astype(
        jnp.bfloat16
    )
    out_local = jnp.einsum("td,te->de", scaled, grad_post, preferred_element_type=jnp.float32)
    grad_scaled = jnp.einsum("te,de->td", grad_post, out_full, preferred_element_type=jnp.float32)
    scale_local = jnp.sum(
        (grad_scaled * attended).reshape(local_rows, HEADS, head_dim), axis=(0, 2)
    )
    grad_attended = (
        (grad_scaled * scale_wide).astype(jnp.bfloat16).reshape(local_rows, HEADS, head_dim)
    )
    grad_query, grad_keys, grad_values = attend_backward(
        query_rows, key_rows, value_rows, grad_attended, doc_ids, sums_log, factor
    )
    grad_projected = jnp.concatenate(
        [
            grad_query.reshape(local_rows, model_width),
            grad_keys.reshape(local_rows, model_width),
            grad_values.reshape(local_rows, model_width),
        ],
        axis=1,
    ).astype(jnp.bfloat16)
    qkv_local = jnp.einsum(
        "td,te->de", normed_in, grad_projected, preferred_element_type=jnp.float32
    )
    grad_normed_in = jnp.einsum(
        "te,de->td", grad_projected, qkv_full, preferred_element_type=jnp.float32
    )
    token_grad = grad_middle + normalize_back(
        grad_normed_in * gain_full[:, 0], normed_one, inverse_one
    )
    projected_sums = jnp.sum(grad_projected.astype(jnp.float32), axis=0)
    gains_local = jnp.stack(
        [
            jnp.sum(grad_normed_in * normed_one, axis=0),
            jnp.sum(grad_middle * normed_post, axis=0),
            jnp.sum(grad_normed_mid * normed_two, axis=0),
        ],
        axis=1,
    )
    biases_local = jnp.stack(
        [
            jnp.sum(grad_normed_in, axis=0),
            projected_sums[:model_width],
            projected_sums[2 * model_width :],
            jnp.sum(grad_post.astype(jnp.float32), axis=0),
            jnp.sum(grad_middle, axis=0),
            jnp.sum(grad_normed_mid, axis=0),
            jnp.sum(final_grad, axis=0),
        ],
        axis=1,
    )
    qkv_grad, out_weight_grad, gains_grad, biases_grad = (
        lax.psum_scatter(qkv_local, ("dp", "tensor"), scatter_dimension=0, tiled=True),
        lax.psum_scatter(out_local, ("dp", "tensor"), scatter_dimension=0, tiled=True),
        lax.psum_scatter(gains_local, ("dp", "tensor"), scatter_dimension=0, tiled=True),
        lax.psum_scatter(biases_local, ("dp", "tensor"), scatter_dimension=0, tiled=True),
    )
    scale_grad = lax.psum(scale_local, ("dp", "tensor"))
    return (
        mixed_out,
        token_grad,
        qkv_grad,
        out_weight_grad,
        gains_grad,
        biases_grad,
        scale_grad,
        fc1_grad,
        fc2_grad,
        mid_gain_grad,
        ffn_bias_grad,
    )


MESH = pl.DeviceIdType.MESH
ANY = pl.BlockSpec(memory_space=pl.ANY)
IN_VMEM = pl.BlockSpec(memory_space=pltpu.VMEM)


def place():
    z = lax.axis_index("dp")
    t = lax.axis_index("tensor")
    return z, lax.div(t, 4), lax.rem(lax.div(t, 2), 2), lax.rem(t, 2)


def at(z, y, x, c):
    return (z, y * 4 + x * 2 + c)


def greet(partners):
    barrier = pltpu.get_barrier_semaphore()
    for partner in partners:
        pl.semaphore_signal(barrier, inc=1, device_id=partner, device_id_type=MESH)
    pl.semaphore_wait(barrier, len(partners))


class Sends:
    def __init__(self, send_sems, recv_sems):
        self.send_sems, self.recv_sems, self.copies = send_sems, recv_sems, []

    def start(self, src, dst, target):
        index = len(self.copies)
        copy = pltpu.make_async_remote_copy(
            src_ref=src,
            dst_ref=dst,
            send_sem=self.send_sems.at[index],
            recv_sem=self.recv_sems.at[index],
            device_id=target,
            device_id_type=MESH,
        )
        copy.start()
        self.copies.append(copy)
        return copy

    def finish(self):
        for copy in self.copies:
            copy.wait_send()


def add_low(left, right):
    return (left.astype(jnp.float32) + right.astype(jnp.float32)).astype(jnp.bfloat16)


SQRT_2_PI = math.sqrt(2.0 / math.pi)
NT = (((1,), (1,)), ((), ()))
TN = (((0,), (0,)), ((), ()))


def dot(left, right, dims=None):
    if dims is None:
        return jnp.dot(left, right, preferred_element_type=jnp.float32)
    return lax.dot_general(left, right, dims, preferred_element_type=jnp.float32)


def centered(values):
    center = jnp.mean(values, axis=-1, keepdims=True)
    spread = jnp.mean(values * values, axis=-1, keepdims=True) - center * center
    inverse = lax.rsqrt(spread + EPS)
    return (values - center) * inverse, inverse


def centered_back(grad, normed, inverse):
    first = jnp.mean(grad, axis=-1, keepdims=True)
    second = jnp.mean(grad * normed, axis=-1, keepdims=True)
    return inverse * (grad - first - normed * second)


def eights(values):
    return jnp.sum(values.reshape(values.shape[0] // 8, 8, values.shape[1]), axis=0)


def doc_mask(doc_ref, rows):
    query = lax.broadcasted_iota(jnp.int32, (rows, rows), 0)
    key = lax.broadcasted_iota(jnp.int32, (rows, rows), 1)
    query_doc, key_doc = jnp.zeros_like(query), jnp.zeros_like(key)
    end = 0
    for j in range(doc_ref.shape[1] - 1):
        end = end + doc_ref[0, j]
        query_doc = query_doc + (query >= end).astype(jnp.int32)
        key_doc = key_doc + (key >= end).astype(jnp.int32)
    allowed = jnp.logical_and(query_doc == key_doc, key <= query)
    return allowed.astype(jnp.float32)


class Plane:
    def __init__(self, sends, whole, here, targets):
        self.sends, self.whole, self.here, self.targets = sends, whole, here, targets
        half = whole.shape[3] // 2
        self.lo, self.hi = pl.ds(0, half), pl.ds(half, half)

    def part(self, y, x, c, rows):
        return self.whole.at[y, x, c, rows]

    def start(self, src):
        (y, x, c), (to_x, to_y, to_c), lo, hi = self.here, self.targets, self.lo, self.hi
        go = self.sends.start
        self.first = [
            go(src.at[lo], self.part(y, x, c, lo), to_x),
            go(src.at[hi], self.part(y, x, c, hi), to_y),
        ]
        self.core = [go(src, self.whole.at[y, x, c], to_c)]
        self.second = [
            go(src.at[lo], self.part(y, x, c, lo), to_y),
            go(src.at[hi], self.part(y, x, c, hi), to_x),
        ]

    def after_first(self):
        (y, x, c), (to_x, to_y, to_c), lo, hi = self.here, self.targets, self.lo, self.hi
        for copy in self.first:
            copy.wait_recv()
        by_x, by_y = self.part(y, 1 - x, c, lo), self.part(1 - y, x, c, hi)
        go = self.sends.start
        self.third = [go(by_x, by_x, to_y), go(by_y, by_y, to_x)]
        self.side = [go(by_x, by_x, to_c), go(by_y, by_y, to_c)]

    def after_second(self):
        (y, x, c), (to_x, to_y, to_c), lo, hi = self.here, self.targets, self.lo, self.hi
        for copy in self.second:
            copy.wait_recv()
        by_x, by_y = self.part(y, 1 - x, c, hi), self.part(1 - y, x, c, lo)
        go = self.sends.start
        self.side += [go(by_x, by_x, to_c), go(by_y, by_y, to_c)]

    def after_third(self):
        y, x, c = self.here
        for copy in self.third:
            copy.wait_recv()
        ref = self.whole.at[1 - y, 1 - x, c]
        self.last = self.sends.start(ref, ref, self.targets[2])


def fore_kernel(
    nz,
    tok_ref,
    og_ref,
    qkv_ref,
    out_ref,
    gains_ref,
    biases_ref,
    fc1_ref,
    fc2_ref,
    gain_ref,
    shift_ref,
    doc_ref,
    scale_ref,
    qkv_out,
    out_out,
    vec_out,
    proj_out,
    att_out,
    lse_out,
    branch_out,
    middle_out,
    nin_out,
    scaled_out,
    ffn_out,
    fc2_out,
    late_out,
    fc1_out,
    gnm_out,
    unit_out,
    qkv_all,
    out_all,
    vec_all,
    vec_mine,
    vec_turn,
    unit_ref,
    fc1_all,
    fc2_all,
    og_all,
    tok,
    branch,
    nin,
    proj,
    att,
    lse,
    scaled,
    middle,
    mask,
    vec,
    mid_all,
    act,
    slope,
    grad,
    hidden,
    grad_pre,
    mid_part,
    pre,
    stats,
    pair,
    got,
    totals,
    from_core,
    sums,
    from_one,
    from_two,
    ffn_part,
    fc1_part,
    late_part,
    fc2_part,
    fc1_got,
    local_sems,
    send_sems,
    recv_sems,
):
    z, y, x, c = place()
    to_x, to_y, to_c = at(z, y, 1 - x, c), at(z, 1 - y, x, c), at(z, y, x, 1 - c)
    to_xy = at(z, 1 - y, 1 - x, c)
    others = [lax.rem(z + k, nz) for k in range(1, nz)]
    slots = [z] + [lax.rem(z + nz - k, nz) for k in range(1, nz)]
    peers = [at(other, y, x, c) for other in others]
    locals_ = []

    def fetch(src, dst):
        copy = pltpu.make_async_copy(src, dst, local_sems.at[len(locals_)])
        copy.start()
        locals_.append(copy)
        return copy

    rows, width = tok.shape
    fourth = width // 4
    qkv_in = [
        fetch(
            qkv_ref.at[:, pl.ds(i * width + g * fourth, fourth)],
            qkv_all.at[z, y, x, c, :, pl.ds((3 * g + i) * fourth, fourth)],
        )
        for g in range(4)
        for i in range(3)
    ]
    vec_turn[...] = jnp.zeros_like(vec_turn)
    share = vec_mine.shape[0]
    vec_turn[0:3, 0:share] = gains_ref[...]
    vec_turn[3:10, 0:share] = biases_ref[...]
    vec_mine[...] = vec_turn[...].T[:share]
    greet([to_x, to_y, to_c, to_xy] + peers)
    sends = Sends(send_sems, recv_sems)
    low, f32 = jnp.bfloat16, jnp.float32
    units = fc1_all.shape[1]
    width1, width2 = fc1_ref.shape[0], fc2_ref.shape[1]
    own1 = fc1_all.at[pl.ds(pl.multiple_of(z * width1, width1), width1)]
    own2 = fc2_all.at[:, pl.ds(pl.multiple_of(z * width2, width2), width2)]
    def wait_all(copies):
        for copy in copies:
            copy.wait_recv()

    vec_z = [sends.start(vec_mine, vec_all.at[z, y, x, c], peer) for peer in peers]
    phase = 6 * fourth
    spans = (pl.ds(0, phase), pl.ds(phase, phase))
    for copy in qkv_in:
        copy.wait()
    own_qkv = qkv_all.at[z, y, x, c]
    qkv_z = [
        [sends.start(own_qkv.at[:, span], own_qkv.at[:, span], peer) for peer in peers]
        for span in spans
    ]

    def sides(whole, p):
        size = phase // 2 if whole is qkv_all else whole.shape[-1] // 2
        return pl.ds(2 * p * size, size), pl.ds((2 * p + 1) * size, size)

    def first(whole, slot, p=0):
        lo, hi = sides(whole, p)
        by_x, by_y = whole.at[slot, y, x, c, :, lo], whole.at[slot, y, x, c, :, hi]
        return (sends.start(by_x, by_x, to_x), sends.start(by_y, by_y, to_y))

    def second(whole, slot, p=0):
        lo, hi = sides(whole, p)
        by_x, by_y = whole.at[slot, y, :, c, :, lo], whole.at[slot, :, x, c, :, hi]
        return (sends.start(by_x, by_x, to_y), sends.start(by_y, by_y, to_x))

    def third(whole, slot, p=None):
        ref = whole.at[slot, :, :, c] if p is None else whole.at[slot, :, :, c, :, spans[p]]
        return sends.start(ref, ref, to_c)

    a0, a1 = [first(qkv_all, z, 0)], [first(qkv_all, z, 1)]
    tok_in = fetch(tok_ref, tok)
    out_in = fetch(out_ref, out_all.at[z, y, x, c])
    fc1_in = fetch(fc1_ref, own1)
    fc2_in = fetch(fc2_ref, own2)
    og_in = fetch(og_ref, og_all.at[y, x, c])
    vec_all[z, y, x, c] = vec_mine[...]
    unit_ref[...] = jnp.zeros_like(unit_ref)
    unit_ref[0:1] = shift_ref[0:1]
    unit_ref[1:2] = gain_ref[...]
    unit_ref[2:3] = shift_ref[1:2]
    step = 32
    wait_all(vec_z)
    by_x = vec_all.at[:, y, x, c]
    vec_x = sends.start(by_x, by_x, to_x)
    qkv_z[0][0].wait_recv()
    a0.append(first(qkv_all, slots[1], 0))
    vec_x.wait_recv()
    by_y = vec_all.at[:, y, :, c]
    vec_y = sends.start(by_y, by_y, to_y)
    for k in range(2, nz):
        qkv_z[0][k - 1].wait_recv()
        a0.append(first(qkv_all, slots[k], 0))
    b0 = []
    for k in range(nz):
        wait_all(a0[k])
        b0.append(second(qkv_all, slots[k], 0))
        if k == 0:
            vec_y.wait_recv()
            by_c = vec_all.at[:, :, :, c]
            vec_c = sends.start(by_c, by_c, to_c)
    mask[...] = doc_mask(doc_ref, rows)
    tok_in.wait()

    def normed(k, carry):
        part = pl.ds(pl.multiple_of(k * step, step), step)
        branch[part] = centered(tok[part].astype(f32))[0]
        return carry

    lax.fori_loop(0, rows // step, normed, 0)
    vec_c.wait_recv()
    vec[...] = vec_all[...].reshape(width, 128).T[:16]
    spot = lax.broadcasted_iota(jnp.int32, (1, width), 1)
    head = 64
    wide = jnp.zeros((1, width), f32)
    for h in range(HEADS):
        inside = jnp.logical_and(spot >= h * head, spot < (h + 1) * head)
        wide = jnp.where(inside, scale_ref[h], wide)
    vec[10:11] = wide

    def scaled_in(k, carry):
        part = pl.ds(pl.multiple_of(k * step, step), step)
        nin[part] = (branch[part] * vec[0:1] + vec[3:4]).astype(low)
        return carry

    lax.fori_loop(0, rows // step, scaled_in, 0)
    c0 = []
    for k in range(1, nz):
        qkv_z[1][k - 1].wait_recv()
        a1.append(first(qkv_all, slots[k], 1))
        wait_all(b0[k - 1])
        c0.append(third(qkv_all, slots[k - 1], 0))
    out_in.wait()
    own_out = out_all.at[z, y, x, c]
    out_z = [sends.start(own_out, own_out, peer) for peer in peers]
    pair_peer = at(z + 1 - 2 * lax.rem(z, 2), y, x, c)
    far_peer = peers[1]
    fc2_far = sends.start(fc2_ref, own2, far_peer)
    fc2_near = sends.start(fc2_ref, own2, pair_peer)
    fc1_z = [sends.start(fc1_ref, own1, peer) for peer in peers]
    wait_all(b0[nz - 1])
    c0.append(third(qkv_all, slots[nz - 1], 0))
    b1 = []
    for k in range(2):
        wait_all(a1[k])
        b1.append(second(qkv_all, slots[k], 1))
    wait_all(c0)

    def project(p):
        for g in (2 * p, 2 * p + 1):
            cols = pl.ds(3 * g * fourth, 3 * fourth)
            here = pl.ds(g * fourth, fourth)
            bias = jnp.concatenate(
                [vec[4:5, here], jnp.zeros((1, fourth), f32), vec[5:6, here]], axis=1
            )
            block = dot(nin[...], qkv_all[:, :, :, :, :, cols].reshape(width, 3 * fourth))
            proj[:, cols] = (block + bias).astype(low)

    project(0)
    lane = lax.broadcasted_iota(jnp.int32, (1, 128), 1)
    is_low = lane < head
    keep = (is_low.astype(low), (lane >= head).astype(low))
    factor = 1.0 / math.sqrt(head)
    lane_wide = lax.broadcasted_iota(jnp.int32, (rows, 128), 1)
    lse[...] = jnp.zeros_like(lse)

    def attend(p, carry):
        base = lax.div(p, 2) * (3 * fourth) + lax.rem(p, 2) * 128
        q_at = pl.ds(pl.multiple_of(base, 128), 128)
        k_at = pl.ds(pl.multiple_of(base + fourth, 128), 128)
        v_at = pl.ds(pl.multiple_of(base + 2 * fourth, 128), 128)
        here = pl.ds(pl.multiple_of(p * 128, 128), 128)
        q2, k2, v2 = proj[:, q_at], proj[:, k_at], proj[:, v_at]
        found = []
        for i in range(2):
            scores = dot(q2 * keep[i], k2, NT) * factor
            scores = jnp.where(mask[...] > 0, scores, NEGATIVE)
            peak = jnp.max(scores, axis=1, keepdims=True)
            exponent = jnp.exp(scores - peak)
            total = jnp.sum(exponent, axis=1, keepdims=True)
            prob = (exponent * (1.0 / total)).astype(low)
            found.append(dot(prob, v2))
            lse[...] = jnp.where(lane_wide == 2 * p + i, peak + jnp.log(total), lse[...])
        both = jnp.where(is_low, *found)
        att[:, here] = both
        scaled[:, here] = (both * vec[10:11, here]).astype(low)
        return carry

    lax.fori_loop(0, 1, attend, 0)
    for k in range(2, nz):
        wait_all(a1[k])
        b1.append(second(qkv_all, slots[k], 1))
    out_a = [first(out_all, z)]
    for k in range(1, nz):
        out_z[k - 1].wait_recv()
        out_a.append(first(out_all, slots[k]))
    og = Plane(sends, og_all, (y, x, c), (to_x, to_y, to_c))
    og.start(og_ref)
    lax.fori_loop(1, 2, attend, 0)
    c1 = []
    for k in range(2):
        wait_all(b1[k])
        c1.append(third(qkv_all, slots[k], 1))
    lax.fori_loop(2, 4, attend, 0)
    for k in range(2, nz):
        wait_all(b1[k])
        c1.append(third(qkv_all, slots[k], 1))
    wait_all(c1)
    saves = [fetch(qkv_all, qkv_out), fetch(vec, vec_out), fetch(nin, nin_out)]
    project(1)
    saves.append(fetch(proj, proj_out))
    out_b = []
    for k in range(nz):
        wait_all(out_a[k])
        out_b.append(second(out_all, slots[k]))
    lax.fori_loop(4, 6, attend, 0)
    og.after_first()
    lax.fori_loop(6, 8, attend, 0)
    out_c = []
    for k in range(nz):
        wait_all(out_b[k])
        out_c.append(third(out_all, slots[k]))
    saves += [fetch(att, att_out), fetch(lse, lse_out), fetch(scaled, scaled_out)]
    wait_all(out_c)
    saves.append(fetch(out_all, out_out))
    quarter = width // 4
    for k in range(4):
        cols = pl.ds(k * quarter, quarter)
        block = dot(scaled[...], out_all[:, :, :, :, :, cols].reshape(width, quarter))
        branch[:, cols] = block + vec[6:7, cols]

    def middles(k, carry):
        part = pl.ds(pl.multiple_of(k * step, step), step)
        post = centered(branch[part])[0]
        value = tok[part].astype(f32) + post * vec[1:2] + vec[7:8]
        middle[part] = value
        mid_all[y, x, c, part] = (centered(value)[0] * vec[2:3] + vec[8:9]).astype(low)
        return carry

    lax.fori_loop(0, rows // step, middles, 0)
    mid = Plane(sends, mid_all, (y, x, c), (to_x, to_y, to_c))
    mid.start(mid_all.at[y, x, c])
    saves += [fetch(branch, branch_out), fetch(middle, middle_out)]

    def grads(yy, xx, cc):
        grad[yy, xx, cc] = dot(og_all[yy, xx, cc], fc2_all[...], NT)

    def fold(v):
        quarters = [v[:, k * (units // 4) : (k + 1) * (units // 4)] for k in range(4)]
        return (quarters[0] + quarters[1]) + (quarters[2] + quarters[3])

    def forward(yy, xx, cc):
        pre[...] = dot(mid_all[yy, xx, cc], fc1_all[...])

        def block(k, carry):
            part = pl.ds(pl.multiple_of(k * step, step), step)
            u = pre[part] + unit_ref[0:1]
            square = u * u
            th = jnp.tanh(u * (SQRT_2_PI + (SQRT_2_PI * 0.044715) * square))
            lift = 0.5 + 0.5 * th
            a = u * lift
            act[yy, xx, cc, part] = a
            bend = u * (2.0 * SQRT_2_PI + (6.0 * 0.044715 * SQRT_2_PI) * square)
            slope[yy, xx, cc, part] = lift + bend * (lift - lift * lift)
            gm = grad[yy, xx, cc, part] * unit_ref[1:2]
            for j, value in enumerate((a, a * a, gm, gm * a)):
                pre[part, j * (units // 4) : (j + 1) * (units // 4)] = fold(value)
            return carry

        lax.fori_loop(0, rows // step, block, 0)
        for j in range(4):
            folded = pre[:, j * (units // 4) : (j + 1) * (units // 4)]
            stats[yy, xx, cc, j : j + 1] = jnp.sum(folded.T, axis=0, keepdims=True)

    stats[...] = jnp.zeros_like(stats)
    og.after_second()
    fc2_in.wait()
    fc2_far.wait_recv()
    near = fc2_all.at[:, pl.ds(pl.multiple_of(others[1] * width2, width2), width2)]
    fc2_last = sends.start(near, near, pair_peer)
    fc2_near.wait_recv()
    og.after_third()
    fc1_in.wait()
    mid.after_first()
    fc2_last.wait_recv()
    og_in.wait()
    grads(y, x, c)
    wait_all(og.core)
    grads(y, x, 1 - c)
    grads(y, 1 - x, c)
    grads(1 - y, x, c)
    mid.after_second()
    wait_all(og.side)
    grads(y, 1 - x, 1 - c)
    grads(1 - y, x, 1 - c)
    grads(1 - y, 1 - x, c)
    og.last.wait_recv()
    grads(1 - y, 1 - x, 1 - c)
    wait_all(fc1_z)
    forward(y, x, c)
    wait_all(mid.core)
    forward(y, x, 1 - c)
    mid.after_third()
    forward(y, 1 - x, c)
    forward(1 - y, x, c)
    wait_all(mid.side)
    forward(y, 1 - x, 1 - c)
    forward(1 - y, x, 1 - c)
    forward(1 - y, 1 - x, c)
    mid.last.wait_recv()
    forward(1 - y, 1 - x, 1 - c)

    sends.start(stats, got.at[3], to_c).wait_recv()
    pair[...] = stats[...] + got[3]
    wait_all([sends.start(pair, got.at[k], to) for k, to in enumerate((to_x, to_y, to_xy))])
    total = (pair[...] + got[0]) + (got[1] + got[2])
    total = total * (1.0 / (units * 8))
    center, square = total[:, :, :, 0:1], total[:, :, :, 1:2]
    mean, cross = total[:, :, :, 2:3], total[:, :, :, 3:4]
    inverse = lax.rsqrt(square - center * center + EPS)
    totals[:, :, :, 0:1] = inverse
    totals[:, :, :, 1:2] = -center * inverse
    totals[:, :, :, 2:3] = inverse * mean
    totals[:, :, :, 3:4] = inverse * (inverse * (cross - center * mean))
    unit_out[...] = jnp.zeros_like(unit_out)

    def backward(yy, xx, cc):
        for j in range(4):
            spread = jnp.broadcast_to(totals[yy, xx, cc, j : j + 1], (128, rows))
            pre[:, j * 128 : (j + 1) * 128] = spread.T

        def block(k, carry):
            part = pl.ds(pl.multiple_of(k * step, step), step)

            def across(j):
                return jnp.concatenate([pre[part, j * 128 : (j + 1) * 128]] * (units // 128), axis=1)

            g = grad[yy, xx, cc, part]
            inverse = across(0)
            normed = act[yy, xx, cc, part] * inverse + across(1)
            gain = unit_ref[1:2]
            hidden[yy, xx, cc, part] = (normed * gain + unit_ref[2:3]).astype(low)
            back = g * gain * inverse - across(2) - normed * across(3)
            value = (back * slope[yy, xx, cc, part]).astype(low)
            grad_pre[yy, xx, cc, part] = value
            return (
                carry[0] + eights(g * normed),
                carry[1] + eights(value.astype(f32)),
                carry[2] + eights(g),
            )

        zero = jnp.zeros((8, units), f32)
        parts = lax.fori_loop(0, rows // step, block, (zero, zero, zero))
        for j, part in enumerate(parts):
            unit_out[j : j + 1] += jnp.sum(part, axis=0, keepdims=True)
        return dot(grad_pre[yy, xx, cc], fc1_all[...], NT)

    left, right = pl.ds(0, width // 2), pl.ds(width // 2, width // 2)
    order = [(1 - y, 1 - x), (y, 1 - x), (1 - y, x), (y, x)]
    stage_x, stage_y = [], []
    for k, (yy, xx) in enumerate(order):
        mid_part[yy, xx] = backward(yy, xx, 1 - c).astype(low)
        core = sends.start(mid_part.at[yy, xx], from_core.at[yy, xx], to_c)
        block = backward(yy, xx, c)
        core.wait_recv()
        sums[yy, xx] = (block + from_core[yy, xx].astype(f32)).astype(low)
        if k in (0, 1):
            stage_x.append(sends.start(sums.at[yy, xx, :, left], from_one.at[yy, :, left], to_x))
        if k in (0, 2):
            stage_y.append(sends.start(sums.at[yy, xx, :, right], from_one.at[xx, :, right], to_y))

    def ffn_of(yy, xx, cc):
        ffn_part[yy, xx, cc] = dot(hidden[yy, xx, cc], fc2_all[...]).astype(low)

    blocks = nz
    size = width // blocks

    early = fc1_part.shape[-1]
    soon, late = slice(0, early), slice(early, units)

    def fc1_block(which, cols):
        part = pl.ds(pl.multiple_of(which * size, 128), size)
        block = jnp.zeros((size, cols.stop - cols.start), f32)
        for j in range(8):
            yxc = (j // 4, (j // 2) % 2, j % 2)
            block = block + dot(mid_all[(*yxc, slice(None), part)], grad_pre[(*yxc, slice(None), cols)], TN)
        return block

    fc1_far = {}
    for k in (1, 0, 2):
        fc1_part[k] = fc1_block(others[k], soon).astype(low)
        fc1_far[k] = sends.start(fc1_part.at[k], fc1_got.at[k], peers[k])
    wait_all((stage_x[0], stage_y[0]))
    sums[1 - y, x, :, left] = add_low(sums[1 - y, x, :, left], from_one[1 - y, :, left])
    sums[y, 1 - x, :, right] = add_low(sums[y, 1 - x, :, right], from_one[1 - x, :, right])
    last_y = sends.start(sums.at[1 - y, x, :, left], from_two.at[:, left], to_y)
    last_x = sends.start(sums.at[y, 1 - x, :, right], from_two.at[:, right], to_x)
    fc1_out[:, soon] = fc1_block(z, soon)
    fc1_out[:, late] = fc1_block(z, late)

    def late_block(k, carry):
        part = pl.ds(pl.multiple_of(k * size, 128), size)
        late_part[part] = fc1_block(k, late).astype(low)
        return carry

    lax.fori_loop(0, blocks, late_block, 0)
    saves.append(fetch(late_part, late_out))
    for yy, xx in order:
        ffn_of(yy, xx, 1 - c)
        ffn_of(yy, xx, c)
    saves.append(fetch(ffn_part, ffn_out))

    def fc2_block(k, carry):
        part = pl.ds(pl.multiple_of(k * size, 128), size)
        block = jnp.zeros((units, size), f32)
        for j in range(8):
            yxc = (j // 4, (j // 2) % 2, j % 2)
            block = block + dot(hidden[yxc], og_all[(*yxc, slice(None), part)], TN)
        fc2_part[:, part] = block.astype(low)
        return carry

    lax.fori_loop(0, blocks, fc2_block, 0)
    saves.append(fetch(fc2_part, fc2_out))
    wait_all((stage_x[1], stage_y[1], last_x, last_y))
    for cols, k in ((left, y), (right, x)):
        gnm_out[:, cols] = (
            sums[y, x, :, cols].astype(f32)
            + from_one[k, :, cols].astype(f32)
            + from_two[:, cols].astype(f32)
        )
    for k in range(nz - 1):
        fc1_far[k].wait_recv()
        fc1_out[:, soon] += fc1_got[k].astype(f32)
    for copy in saves:
        copy.wait()
    sends.finish()


def fore(nz, tokens, og, doc_lengths, w_qkv, w_out, gains, biases, scale, fc1, fc2, gain, shift):
    rows, width = tokens.shape
    share, units = w_qkv.shape[0], fc1.shape[1]
    low, f32, plane, every = jnp.bfloat16, jnp.float32, (2, 2, 2), (nz, 2, 2, 2)
    sds, vm = jax.ShapeDtypeStruct, pltpu.VMEM
    count = 160
    smem = pl.BlockSpec(memory_space=pltpu.SMEM)
    shapes = (
        (every + w_qkv.shape, low),
        (every + w_out.shape, low),
        ((16, width), f32),
        ((rows, w_qkv.shape[1]), low),
        ((rows, width), f32),
        ((rows, 128), f32),
        ((rows, width), f32),
        ((rows, width), f32),
        ((rows, width), low),
        ((rows, width), low),
        (plane + (rows, width), low),
        ((units, width), low),
        ((width, units // 2), low),
        (fc1.shape, f32),
        ((rows, width), f32),
        ((8, units), f32),
    )
    return pl.pallas_call(
        functools.partial(fore_kernel, nz),
        name="fore",
        out_shape=tuple(sds(shape, kind) for shape, kind in shapes),
        in_specs=[ANY] * 4 + [IN_VMEM] * 2 + [ANY] * 2 + [IN_VMEM] * 2 + [smem] * 2,
        out_specs=[ANY] * 13 + [IN_VMEM] * 3,
        scratch_shapes=[
            vm(every + w_qkv.shape, low),
            vm(every + w_out.shape, low),
            vm(every + (share, 128), f32),
            vm((share, 128), f32),
            vm((128, 128), f32),
            vm((8, units), f32),
            vm((width, units), low),
            vm((units, width), low),
            vm(plane + (rows, width), low),
            vm((rows, width), low),
            vm((rows, width), f32),
            vm((rows, width), low),
            vm((rows, w_qkv.shape[1]), low),
            vm((rows, width), f32),
            vm((rows, 128), f32),
            vm((rows, width), low),
            vm((rows, width), f32),
            vm((rows, rows), f32),
            vm((16, width), f32),
            vm(plane + (rows, width), low),
            vm(plane + (rows, units), f32),
            vm(plane + (rows, units), f32),
            vm(plane + (rows, units), f32),
            vm(plane + (rows, units), low),
            vm(plane + (rows, units), low),
            vm((2, 2, rows, width), low),
            vm((rows, units), f32),
            vm(plane + (8, rows), f32),
            vm(plane + (8, rows), f32),
            vm((4,) + plane + (8, rows), f32),
            vm(plane + (8, rows), f32),
            vm((2, 2, rows, width), low),
            vm((2, 2, rows, width), low),
            vm((2, rows, width), low),
            vm((rows, width), low),
            vm(plane + (rows, width), low),
            vm((nz - 1, fc1.shape[0], units // 2), low),
            vm((width, units // 2), low),
            vm((units, width), low),
            vm((nz - 1, fc1.shape[0], units // 2), low),
            pltpu.SemaphoreType.DMA((36,)),
            pltpu.SemaphoreType.DMA((count,)),
            pltpu.SemaphoreType.DMA((count,)),
        ],
        compiler_params=pltpu.CompilerParams(
            collective_id=1, has_side_effects=True, vmem_limit_bytes=63 * 2**20
        ),
    )(tokens, og, w_qkv, w_out, gains.T, biases.T, fc1, fc2, gain, shift, doc_lengths, scale)


def back_kernel(
    nz,
    gnm_in,
    ffn_ref,
    late_ref,
    own1_in,
    fc2_ref,
    unit_ref,
    proj_in,
    att_in,
    lse_in,
    branch_in,
    middle_in,
    scaled_in,
    nin_in,
    qkv_in,
    out_in,
    vec_ref,
    og_in,
    tok_in,
    doc_ref,
    mixed_out,
    token_out,
    weight_out,
    gains_out,
    biases_out,
    scale_out,
    fc1_out,
    fc2_out,
    unit_out,
    f_core,
    f_sums,
    f_one,
    f_two,
    got1,
    got2,
    got_unit,
    w_part,
    w_core,
    w_sums,
    w_one,
    w_two,
    w_far,
    gpost,
    gmid,
    gatt,
    gni,
    dproj,
    nin_t,
    mask,
    accs,
    small,
    small_far,
    small_y,
    small_half,
    small_got,
    turned,
    gnm_ref,
    proj_ref,
    att_ref,
    lse_ref,
    branch_ref,
    middle_ref,
    scaled_ref,
    nin_ref,
    qkv_ref,
    out_ref,
    og_ref,
    tok_ref,
    local_sems,
    send_sems,
    recv_sems,
):
    z, y, x, c = place()
    to_x, to_y, to_c = at(z, y, 1 - x, c), at(z, 1 - y, x, c), at(z, y, x, 1 - c)
    to_xy = at(z, 1 - y, 1 - x, c)
    others = [lax.rem(z + k, nz) for k in range(1, nz)]
    peers = [at(other, y, x, c) for other in others]
    greet([to_x, to_y, to_c, to_xy] + peers)
    sends = Sends(send_sems, recv_sems)
    rows, width = middle_ref.shape
    low = jnp.bfloat16
    f32 = jnp.float32
    share = weight_out.shape[0]
    width1, width2 = fc1_out.shape[0], fc2_out.shape[1]

    pieces = 2
    parts = [pl.ds(k * (rows // pieces), rows // pieces) for k in range(pieces)]
    left, right = pl.ds(0, width // 2), pl.ds(width // 2, width // 2)
    f_c = [
        sends.start(ffn_ref.at[:, :, 1 - c, part], f_core.at[:, :, part], to_c) for part in parts
    ]
    locals_ = []

    def fetch(src, dst):
        copy = pltpu.make_async_copy(src, dst, local_sems.at[len(locals_)])
        copy.start()
        locals_.append(copy)
        return copy

    middle_got = fetch(middle_in, middle_ref)
    gnm_got = fetch(gnm_in, gnm_ref)
    og_got = fetch(og_in, og_ref)
    branch_got = fetch(branch_in, branch_ref)
    ffn_got = fetch(ffn_ref.at[:, :, c], f_sums)
    out_got = fetch(out_in, out_ref)
    att_got = fetch(att_in, att_ref)
    scaled_got = fetch(scaled_in, scaled_ref)
    nin_got = fetch(nin_in, nin_ref)
    proj_got = fetch(proj_in, proj_ref)
    lse_got = fetch(lse_in, lse_ref)
    qkv_got = fetch(qkv_in, qkv_ref)
    tok_got = fetch(tok_in, tok_ref)

    def block1(which):
        return late_ref.at[pl.ds(pl.multiple_of(which * width1, width1), width1)]

    def block2(which):
        return fc2_ref.at[:, pl.ds(pl.multiple_of(which * width2, width2), width2)]

    own1_got = fetch(own1_in, fc1_out)
    own2_got = fetch(block2(z), got2.at[nz - 1])
    far = []
    for k, peer in enumerate(peers):
        far.append(sends.start(unit_ref, got_unit.at[k], peer))
        far.append(sends.start(block1(others[k]), got1.at[k], peer))
        far.append(sends.start(block2(others[k]), got2.at[k], peer))

    f_first, f_second = [], []

    def ffn_one(k):
        part = parts[k]
        f_c[k].wait_recv()
        if k == 0:
            ffn_got.wait()
        for yy in range(2):
            for xx in range(2):
                f_sums[yy, xx, part] = add_low(f_sums[yy, xx, part], f_core[yy, xx, part])
        f_first.append(
            (
                sends.start(f_sums.at[:, 1 - x, part, left], f_one.at[0, :, part, left], to_x),
                sends.start(f_sums.at[1 - y, :, part, right], f_one.at[1, :, part, right], to_y),
            )
        )

    def ffn_two(k):
        part = parts[k]
        for copy in f_first[k]:
            copy.wait_recv()
        f_sums[1 - y, x, part, left] = add_low(
            f_sums[1 - y, x, part, left], f_one[0, 1 - y, part, left]
        )
        f_sums[y, 1 - x, part, right] = add_low(
            f_sums[y, 1 - x, part, right], f_one[1, 1 - x, part, right]
        )
        f_second.append(
            (
                sends.start(f_sums.at[1 - y, x, part, left], f_two.at[part, left], to_y),
                sends.start(f_sums.at[y, 1 - x, part, right], f_two.at[part, right], to_x),
            )
        )

    def ffn_three(k):
        part = parts[k]
        for copy in f_second[k]:
            copy.wait_recv()
        for i, (cols, at_) in enumerate(((left, y), (right, x))):
            total = (
                f_sums[y, x, part, cols].astype(f32)
                + f_one[i, at_, part, cols].astype(f32)
                + f_two[part, cols].astype(f32)
            )
            mixed_out[part, cols] = (
                middle_ref[part, cols] + total + vec_ref[9:10, cols]
            ).astype(low)

    spans = [(0, width)] + [(width + g * 3 * width // 4, 3 * width // 4) for g in range(4)]
    w_first, w_second, w_third, w_c = {}, {}, {}, {}

    def sides(j):
        start, size = spans[j]
        return pl.ds(start, size), pl.ds(start, size // 2), pl.ds(start + size // 2, size // 2)

    def w_zero(j):
        every = sides(j)[0]
        w_c[j] = sends.start(w_part.at[:, :, :, 1 - c, :, every], w_core.at[..., every], to_c)

    def w_step1(j):
        every, lo, hi = sides(j)
        w_c[j].wait_recv()

        def one(which, carry):
            for yy in range(2):
                for xx in range(2):
                    w_sums[which, yy, xx, :, every] = add_low(
                        w_part[which, yy, xx, c, :, every], w_core[which, yy, xx, :, every]
                    )
            return carry

        lax.fori_loop(0, nz, one, 0)
        w_first[j] = (
            sends.start(w_sums.at[:, :, 1 - x, :, lo], w_one.at[:, :, :, lo], to_x),
            sends.start(w_sums.at[:, 1 - y, :, :, hi], w_one.at[:, :, :, hi], to_y),
        )

    def w_step2(j):
        every, lo, hi = sides(j)
        for copy in w_first[j]:
            copy.wait_recv()

        def one(which, carry):
            for k in range(2):
                w_sums[which, k, x, :, lo] = add_low(
                    w_sums[which, k, x, :, lo], w_one[which, k, :, lo]
                )
                w_sums[which, y, k, :, hi] = add_low(
                    w_sums[which, y, k, :, hi], w_one[which, k, :, hi]
                )
            return carry

        lax.fori_loop(0, nz, one, 0)
        w_second[j] = (
            sends.start(w_sums.at[:, 1 - y, x, :, lo], w_two.at[:, :, lo], to_y),
            sends.start(w_sums.at[:, y, 1 - x, :, hi], w_two.at[:, :, hi], to_x),
        )

    def w_step3(j):
        every = sides(j)[0]
        for copy in w_second[j]:
            copy.wait_recv()
        for which in range(nz):
            w_sums[which, y, x, :, every] = add_low(
                w_sums[which, y, x, :, every], w_two[which, :, every]
            )
        w_third[j] = [
            sends.start(w_sums.at[others[k], y, x, :, every], w_far.at[k, :, every], peer)
            for k, peer in enumerate(peers)
        ]

    def w_step4(j):
        start, size = spans[j]
        every = sides(j)[0]
        total = w_sums[z, y, x, :, every].astype(f32)
        for k in range(nz - 1):
            w_third[j][k].wait_recv()
            total = total + w_far[k, :, every].astype(f32)
        if j == 0:
            weight_out[:, 3 * width :] = total
        else:
            third = size // 3
            for i in range(3):
                first = i * width + (j - 1) * third
                weight_out[:, first : first + third] = total[:, i * third : (i + 1) * third]

    accs[...] = jnp.zeros_like(accs)
    step = 32

    def norms(k, carry):
        part = pl.ds(pl.multiple_of(k * step, step), step)
        normed_two, inverse_two = centered(middle_ref[part])
        grad = gnm_ref[part]
        og = og_ref[part].astype(f32)
        grad_middle = og + centered_back(grad * vec_ref[2:3], normed_two, inverse_two)
        accs[2] += eights(grad * normed_two)
        accs[8] += eights(grad)
        accs[9] += eights(og)
        normed_post, inverse_post = centered(branch_ref[part])
        post = centered_back(grad_middle * vec_ref[1:2], normed_post, inverse_post).astype(low)
        accs[1] += eights(grad_middle * normed_post)
        accs[7] += eights(grad_middle)
        accs[6] += eights(post.astype(f32))
        gpost[part] = post
        gmid[part] = grad_middle
        return carry

    for copy in (middle_got, gnm_got, og_got, branch_got):
        copy.wait()
    lax.fori_loop(0, rows // step, norms, 0)
    mask[...] = doc_mask(doc_ref, rows)
    ffn_one(0)
    quarter = width // 4

    def scaled_block(k, carry):
        part = pl.ds(pl.multiple_of(k * quarter, quarter), quarter)
        block = dot(gpost[...], out_ref[part], NT)
        accs[10, :, part] = eights(block * att_ref[:, part])
        gatt[:, part] = (block * vec_ref[10:11, part]).astype(low)
        return carry

    out_got.wait()
    att_got.wait()
    lax.fori_loop(0, 4, scaled_block, 0)

    def out_block(k, carry):
        part = pl.ds(pl.multiple_of(k * (width // nz), width // nz), width // nz)
        block = dot(scaled_ref[:, part], gpost[...], TN).astype(low)
        w_part[k, :, :, :, :, pl.ds(0, width)] = block.reshape(2, 2, 2, share, width)
        return carry

    scaled_got.wait()
    lax.fori_loop(0, nz, out_block, 0)
    w_zero(0)
    nin_got.wait()
    nin_t[...] = nin_ref[...].T
    proj_got.wait()
    lse_got.wait()
    head = 64
    lane = lax.broadcasted_iota(jnp.int32, (1, 128), 1)
    is_low = lane < head
    factor = 1.0 / math.sqrt(head)
    lane_wide = lax.broadcasted_iota(jnp.int32, (rows, 128), 1)
    keep = (is_low.astype(low), (lane >= head).astype(low))

    def pair(p, carry):
        base = lax.div(p, 2) * (3 * quarter) + lax.rem(p, 2) * 128
        q_at = pl.ds(pl.multiple_of(base, 128), 128)
        k_at = pl.ds(pl.multiple_of(base + quarter, 128), 128)
        v_at = pl.ds(pl.multiple_of(base + 2 * quarter, 128), 128)
        here = pl.ds(pl.multiple_of(p * 128, 128), 128)
        q2, k2, v2, do2 = proj_ref[:, q_at], proj_ref[:, k_at], proj_ref[:, v_at], gatt[:, here]
        lses = lse_ref[...]
        found = []
        for i in range(2):
            scores = dot(q2 * keep[i], k2, NT) * factor
            scores = jnp.where(mask[...] > 0, scores, NEGATIVE)
            lse = jnp.sum(jnp.where(lane_wide == 2 * p + i, lses, 0.0), axis=1, keepdims=True)
            prob = jnp.exp(scores - lse)
            grad_prob = dot(do2 * keep[i], v2, NT)
            inner = jnp.sum(prob * grad_prob, axis=1, keepdims=True)
            ds = (prob * (grad_prob - inner) * factor).astype(low)
            found.append(
                (dot(ds, k2), dot(ds, q2, TN), dot(prob.astype(low), do2, TN))
            )
        for where, a, b in zip((q_at, k_at, v_at), *found):
            dproj[:, where] = jnp.where(is_low, a, b).astype(low)
        accs[4, :, here] = eights(dproj[:, q_at].astype(f32))
        accs[5, :, here] = eights(dproj[:, v_at].astype(f32))
        return carry

    def wgrad(j):
        start, size = spans[j]
        cols = pl.ds((j - 1) * size, size)

        def one(k, carry):
            part = pl.ds(pl.multiple_of(k * (width // nz), width // nz), width // nz)
            block = dot(nin_t[part], dproj[:, cols]).astype(low)
            w_part[k, :, :, :, :, pl.ds(start, size)] = block.reshape(2, 2, 2, share, size)
            return carry

        lax.fori_loop(0, nz, one, 0)
        w_zero(j)

    lax.fori_loop(0, 1, pair, 0)
    w_step1(0)
    lax.fori_loop(1, 2, pair, 0)
    wgrad(1)
    ffn_two(0)
    lax.fori_loop(2, 3, pair, 0)
    w_step1(1)
    lax.fori_loop(3, 4, pair, 0)
    wgrad(2)
    w_step2(0)
    lax.fori_loop(4, 5, pair, 0)
    w_step1(2)
    lax.fori_loop(5, 6, pair, 0)
    wgrad(3)
    w_step2(1)
    w_step3(0)
    lax.fori_loop(6, 7, pair, 0)
    w_step1(3)
    lax.fori_loop(7, 8, pair, 0)
    wgrad(4)

    def gni_block(k, carry):
        part = pl.ds(pl.multiple_of(k * quarter, quarter), quarter)
        gni[:, part] = dot(dproj[...], qkv_ref[part], NT)
        return carry

    qkv_got.wait()
    lax.fori_loop(0, 4, gni_block, 0)

    def tokens_back(k, carry):
        part = pl.ds(pl.multiple_of(k * step, step), step)
        normed, inverse = centered(tok_ref[part].astype(f32))
        grad = gni[part]
        token_out[part] = gmid[part] + centered_back(grad * vec_ref[0:1], normed, inverse)
        accs[0] += eights(grad * normed)
        accs[3] += eights(grad)
        return carry

    tok_got.wait()
    lax.fori_loop(0, rows // step, tokens_back, 0)
    for j in range(16):
        small[j : j + 1] = jnp.sum(accs[j], axis=0, keepdims=True)
    spot = lax.broadcasted_iota(jnp.int32, (1, width), 1)
    tile = jnp.zeros((1, 128), f32)
    for h in range(HEADS):
        inside = jnp.logical_and(spot >= h * head, spot < (h + 1) * head)
        found = jnp.sum(jnp.where(inside, small[10:11], 0.0), axis=1, keepdims=True)
        tile = jnp.where(lane == h, found, tile)
    small[11:12] = jnp.concatenate([tile] * (width // 128), axis=1)
    part_z = width // nz

    def lanes(which):
        return pl.ds(pl.multiple_of(which * part_z, 128), part_z)

    small_z = [
        sends.start(small.at[:, lanes(others[k])], small_far.at[k], peer)
        for k, peer in enumerate(peers)
    ]
    w_step2(2)
    w_step3(1)
    w_step1(4)
    total = small[:, lanes(z)]
    for k in range(nz - 1):
        small_z[k].wait_recv()
        total = total + small_far[k]
    small_y[...] = total
    mine = small_y.at[:, pl.ds(pl.multiple_of(y * 128, 128), 128)]
    other = small_y.at[:, pl.ds(pl.multiple_of((1 - y) * 128, 128), 128)]
    by_y = sends.start(other, small_got.at[0], to_y)
    w_step2(3)
    by_y.wait_recv()
    small_half[0] = mine[...] + small_got[0]
    by_x = sends.start(small_half.at[0], small_got.at[1], to_x)
    w_step3(2)
    ffn_three(0)
    ffn_one(1)
    by_x.wait_recv()
    small_half[1] = small_half[0] + small_got[1]
    by_c = sends.start(small_half.at[1], small_got.at[2], to_c)
    w_step2(4)
    w_step3(3)
    by_c.wait_recv()
    total = small_half[1] + small_got[2]
    scale_out[...] = jnp.broadcast_to(total[11:12], (8, 128))
    ours = pl.ds(pl.multiple_of(x * 64 + c * 32, 32), 32)
    turned[...] = jnp.concatenate([total, jnp.zeros((112, 128), f32)], axis=0).T
    ours = jnp.concatenate([turned[ours], jnp.zeros((96, 128), f32)], axis=0).T
    gains_out[...] = ours[0:3, :share]
    biases_out[...] = ours[3:10, :share]
    ffn_two(1)
    w_step4(0)
    w_step4(1)
    w_step3(4)
    w_step4(2)
    for copy in far:
        copy.wait_recv()
    own1_got.wait()
    own2_got.wait()
    late = pl.ds(fc1_out.shape[1] - got1.shape[2], got1.shape[2])
    own2, unit = got2[nz - 1].astype(f32), unit_ref[...]
    for k in range(nz - 1):
        fc1_out[:, late] += got1[k].astype(f32)
        own2 = own2 + got2[k].astype(f32)
        unit = unit + got_unit[k]
    fc2_out[...] = own2
    unit_out[...] = unit
    w_step4(3)
    ffn_three(1)
    w_step4(4)
    sends.finish()


def back(nz, *operands):
    gnm, ffn_part, late, fc1, fc2, unit, proj, att, lse, branch, middle = operands[:11]
    scaled, nin, qkv, out, vec = operands[11:16]
    rows, width = middle.shape
    share = width // (nz * 8)
    columns = proj.shape[1] + width
    low, f32 = jnp.bfloat16, jnp.float32
    sds = jax.ShapeDtypeStruct
    fc2_own = (fc2.shape[0], fc2.shape[1] // nz)
    count = 64 + 8 * nz
    specs = [ANY] * 5 + [IN_VMEM] + [ANY] * 9 + [IN_VMEM] + [ANY] * 2
    specs.append(pl.BlockSpec(memory_space=pltpu.SMEM))
    return pl.pallas_call(
        functools.partial(back_kernel, nz),
        name="back",
        out_shape=(
            sds((rows, width), low),
            sds((rows, width), f32),
            sds((share, columns), f32),
            sds((3, share), f32),
            sds((7, share), f32),
            sds((8, 128), f32),
            sds(fc1.shape, f32),
            sds(fc2_own, f32),
            sds(unit.shape, f32),
        ),
        in_specs=specs,
        out_specs=[IN_VMEM] * 9,
        scratch_shapes=[
            pltpu.VMEM((2, 2, rows, width), low),
            pltpu.VMEM((2, 2, rows, width), low),
            pltpu.VMEM((2, 2, rows, width), low),
            pltpu.VMEM((rows, width), low),
            pltpu.VMEM((nz - 1, fc1.shape[0], late.shape[1]), low),
            pltpu.VMEM((nz,) + fc2_own, low),
            pltpu.VMEM((nz - 1,) + unit.shape, f32),
            pltpu.VMEM((nz, 2, 2, 2, share, columns), low),
            pltpu.VMEM((nz, 2, 2, share, columns), low),
            pltpu.VMEM((nz, 2, 2, share, columns), low),
            pltpu.VMEM((nz, 2, share, columns), low),
            pltpu.VMEM((nz, share, columns), low),
            pltpu.VMEM((nz - 1, share, columns), low),
            pltpu.VMEM((rows, width), low),
            pltpu.VMEM((rows, width), f32),
            pltpu.VMEM((rows, width), low),
            pltpu.VMEM((rows, width), f32),
            pltpu.VMEM((rows, 3 * width), low),
            pltpu.VMEM((width, rows), low),
            pltpu.VMEM((rows, rows), f32),
            pltpu.VMEM((16, 8, width), f32),
            pltpu.VMEM((16, width), f32),
            pltpu.VMEM((nz - 1, 16, width // nz), f32),
            pltpu.VMEM((16, width // nz), f32),
            pltpu.VMEM((3, 16, 128), f32),
            pltpu.VMEM((3, 16, 128), f32),
            pltpu.VMEM((128, 128), f32),
            pltpu.VMEM((rows, width), f32),
            pltpu.VMEM(proj.shape, low),
            pltpu.VMEM((rows, width), f32),
            pltpu.VMEM(lse.shape, f32),
            pltpu.VMEM((rows, width), f32),
            pltpu.VMEM((rows, width), f32),
            pltpu.VMEM((rows, width), low),
            pltpu.VMEM((rows, width), low),
            pltpu.VMEM(qkv.shape, low),
            pltpu.VMEM(out.shape, low),
            pltpu.VMEM((rows, width), low),
            pltpu.VMEM((rows, width), low),
            pltpu.SemaphoreType.DMA((20,)),
            pltpu.SemaphoreType.DMA((count,)),
            pltpu.SemaphoreType.DMA((count,)),
        ],
        compiler_params=pltpu.CompilerParams(
            collective_id=3, has_side_effects=True, vmem_limit_bytes=63 * 2**20
        ),
    )(*operands)


def finish_kernel(
    mixed,
    token,
    weight,
    fc1,
    fc2,
    gains,
    biases,
    scale,
    unit,
    mixed_out,
    token_out,
    qkv_out,
    out_out,
    fc1_out,
    fc2_out,
    gains_out,
    biases_out,
    scale_out,
    gain_out,
    shift_out,
    mixed_at,
    token_at,
    weight_at,
    fc1_at,
    fc2_at,
    in_sems,
    out_sems,
):
    columns = qkv_out.shape[1]
    moves = (
        (token, token_at, ((token_at, token_out),)),
        (
            weight,
            weight_at,
            (
                (weight_at.at[:, pl.ds(0, columns)], qkv_out),
                (weight_at.at[:, pl.ds(columns, out_out.shape[1])], out_out),
            ),
        ),
        (mixed, mixed_at, ((mixed_at, mixed_out),)),
        (fc1, fc1_at, ((fc1_at, fc1_out),)),
        (fc2, fc2_at, ((fc2_at, fc2_out),)),
    )
    reads, writes = [], []
    for k, (src, here, _) in enumerate(moves):
        reads.append(pltpu.make_async_copy(src, here, in_sems.at[k]))
        reads[-1].start()
    gains_out[...] = gains[...]
    biases_out[...] = biases[...]
    scale_out[...] = scale[0:1, : scale_out.shape[1]]
    gain_out[...] = unit[0:1]
    shift_out[0:1] = unit[1:2]
    shift_out[1:2] = unit[2:3]
    for read, (_, _, outs) in zip(reads, moves):
        read.wait()
        for src, dst in outs:
            writes.append(pltpu.make_async_copy(src, dst, out_sems.at[len(writes)]))
            writes[-1].start()
    for write in writes:
        write.wait()


def finish(mixed, token, weight, gains, biases, scale, fc1, fc2, unit):
    share, columns = weight.shape
    width, units = token.shape[1], unit.shape[1]
    f32 = jnp.float32
    shapes = (
        (mixed.shape, mixed.dtype),
        (token.shape, f32),
        ((share, columns - width), f32),
        ((share, width), f32),
        (fc1.shape, f32),
        (fc2.shape, f32),
        (gains.shape, f32),
        (biases.shape, f32),
        ((1, HEADS), f32),
        ((1, units), f32),
        ((2, units), f32),
    )
    return pl.pallas_call(
        finish_kernel,
        name="finish",
        out_shape=tuple(jax.ShapeDtypeStruct(shape, kind) for shape, kind in shapes),
        in_specs=[ANY] * 5 + [IN_VMEM] * 4,
        out_specs=[ANY] * 6 + [IN_VMEM] * 5,
        scratch_shapes=[
            pltpu.VMEM(mixed.shape, mixed.dtype),
            pltpu.VMEM(token.shape, f32),
            pltpu.VMEM(weight.shape, f32),
            pltpu.VMEM(fc1.shape, f32),
            pltpu.VMEM(fc2.shape, f32),
            pltpu.SemaphoreType.DMA((5,)),
            pltpu.SemaphoreType.DMA((6,)),
        ],
        compiler_params=pltpu.CompilerParams(vmem_limit_bytes=63 * 2**20),
    )(mixed, token, weight, fc1, fc2, gains, biases, scale, unit)


def fused(
    nz,
    tokens,
    out_grad,
    doc_lengths,
    w_qkv,
    w_out,
    gains,
    biases,
    head_scale,
    w_fc1,
    w_fc2,
    mid_gain,
    ffn_biases,
):
    (
        qkv_full,
        out_full,
        vec,
        proj,
        att,
        lse,
        branch,
        middle,
        nin,
        scaled,
        ffn_part,
        fc2_part,
        fc1_late,
        fc1_own,
        gnm,
        unit_sums,
    ) = fore(
        nz,
        tokens,
        out_grad,
        doc_lengths,
        w_qkv,
        w_out,
        gains,
        biases,
        head_scale,
        w_fc1,
        w_fc2,
        mid_gain[None],
        ffn_biases,
    )
    model_width = tokens.shape[1]
    (
        mixed,
        token_grad,
        weight_grad,
        gains_grad,
        biases_grad,
        scale,
        fc1_grad,
        fc2_grad,
        unit_sums,
    ) = back(
        nz,
        gnm,
        ffn_part,
        fc1_late,
        fc1_own,
        fc2_part,
        unit_sums,
        proj,
        att,
        lse,
        branch,
        middle,
        scaled,
        nin,
        qkv_full.reshape(model_width, -1),
        out_full.reshape(model_width, -1),
        vec,
        out_grad,
        tokens,
        doc_lengths,
    )
    mixed, token_grad, qkv, out, fc1, fc2, gains_grad, biases_grad, scale, gain, shift = finish(
        mixed,
        token_grad,
        weight_grad,
        gains_grad,
        biases_grad,
        scale,
        fc1_grad,
        fc2_grad,
        unit_sums,
    )
    return (
        mixed,
        token_grad,
        qkv,
        out,
        gains_grad.T,
        biases_grad.T,
        scale[0],
        fc1,
        fc2,
        gain[0],
        shift,
    )


def layer(nz, nt, tokens, out_grad, doc_lengths, w_qkv, *rest):
    if nz == 4 and nt == 8 and w_qkv.shape[0] % 16 == 0:
        return fused(nz, tokens, out_grad, doc_lengths, w_qkv, *rest)
    return plain(tokens, out_grad, doc_lengths, w_qkv, *rest)


def solution(mesh):
    return jax.shard_map(
        functools.partial(layer, mesh.shape["dp"], mesh.shape["tensor"]),
        mesh=mesh,
        in_specs=(
            P(("dp", "tensor"), None),
            P(("dp", "tensor"), None),
            P(("dp", "tensor"), None),
            P(("dp", "tensor"), None),
            P(("dp", "tensor"), None),
            P(("dp", "tensor"), None),
            P(("dp", "tensor"), None),
            P(),
            P("dp", "tensor"),
            P("tensor", "dp"),
            P("tensor"),
            P(None, "tensor"),
        ),
        out_specs=(
            P(("dp", "tensor"), None),
            P(("dp", "tensor"), None),
            P(("dp", "tensor"), None),
            P(("dp", "tensor"), None),
            P(("dp", "tensor"), None),
            P(("dp", "tensor"), None),
            P(),
            P("dp", "tensor"),
            P("tensor", "dp"),
            P("tensor"),
            P(None, "tensor"),
        ),
        check_vma=False,
    )
```

```python
import functools
import math

import jax
import jax.numpy as jnp
from jax import lax
from jax.experimental import pallas as pl
from jax.experimental.pallas import tpu as pltpu
from jax.sharding import PartitionSpec as P

HEADS = 16
FF = 4096


EPS = 1e-05
NEGATIVE = -1000000000.0


def normalize(values):
    center = jnp.mean(values, axis=-1, keepdims=True)
    spread = jnp.mean(values * values, axis=-1, keepdims=True) - center * center
    inverse = lax.rsqrt(spread + EPS)
    return ((values - center) * inverse, inverse)


def normalize_back(grad_normed, normed, inverse):
    first_mean = jnp.mean(grad_normed, axis=-1, keepdims=True)
    second = jnp.mean(grad_normed * normed, axis=-1, keepdims=True)
    return inverse * (grad_normed - first_mean - normed * second)


def block_scores(query_rows, key_rows, doc_ids, row_first, row_last, factor):
    scores = (
        jnp.einsum("qhd,khd->hqk", query_rows, key_rows, preferred_element_type=jnp.float32)
        * factor
    )
    query_pos = jnp.arange(row_first, row_last)
    key_pos = jnp.arange(row_last)
    same_doc = doc_ids[row_first:row_last, None] == doc_ids[None, :row_last]
    allowed = jnp.logical_and(same_doc, key_pos[None, :] <= query_pos[:, None])
    return (jnp.where(allowed[None], scores, NEGATIVE), allowed)


def attend_forward(query_rows, key_rows, value_rows, doc_ids, factor):
    total_rows = query_rows.shape[0]
    block_rows = min(512, total_rows)
    scores, allowed = block_scores(query_rows, key_rows, doc_ids, 0, block_rows, factor)
    row_peak = jnp.max(scores, axis=-1, keepdims=True)
    exponent = jnp.exp(scores - row_peak)
    row_total = jnp.sum(exponent, axis=-1, keepdims=True)
    prob_low = (exponent / row_total).astype(jnp.bfloat16)
    pieces = jnp.einsum("hqk,khd->qhd", prob_low, value_rows, preferred_element_type=jnp.float32)
    sums_log = [row_peak + jnp.log(row_total)]
    return (pieces, sums_log)


def attend_backward(query_rows, key_rows, value_rows, grad_out, doc_ids, sums_log, factor):
    total_rows = query_rows.shape[0]
    block_rows = min(512, total_rows)
    query_parts = []
    grad_keys = jnp.zeros(key_rows.shape, jnp.float32)
    grad_values = jnp.zeros(value_rows.shape, jnp.float32)
    for block_index, row_first in enumerate(range(0, total_rows, block_rows)):
        row_last = row_first + block_rows
        scores, allowed = block_scores(query_rows, key_rows, doc_ids, row_first, row_last, factor)
        prob_rows = jnp.where(allowed[None], jnp.exp(scores - sums_log[block_index]), 0.0)
        prob_low = prob_rows.astype(jnp.bfloat16)
        grad_probs = jnp.einsum(
            "qhd,khd->hqk", grad_out, value_rows, preferred_element_type=jnp.float32
        )
        inner_sum = jnp.sum(prob_rows * grad_probs, axis=-1, keepdims=True)
        grad_scores = (prob_rows * (grad_probs - inner_sum) * factor).astype(jnp.bfloat16)
        query_parts.append(
            jnp.einsum("hqk,khd->qhd", grad_scores, key_rows, preferred_element_type=jnp.float32)
        )
        grad_keys = grad_keys.at[:row_last].add(
            jnp.einsum("hqk,qhd->khd", grad_scores, query_rows, preferred_element_type=jnp.float32)
        )
        grad_values = grad_values.at[:row_last].add(
            jnp.einsum("hqk,qhd->khd", prob_low, grad_out, preferred_element_type=jnp.float32)
        )
    return (query_parts[0], grad_keys, grad_values)


def plain(
    tokens,
    out_grad,
    doc_lengths,
    w_qkv,
    w_out,
    gains,
    biases,
    head_scale,
    w_fc1,
    w_fc2,
    mid_gain,
    ffn_biases,
):
    qkv_full, out_full, gain_full, bias_full = (
        lax.all_gather(w_qkv, ("dp", "tensor"), axis=0, tiled=True),
        lax.all_gather(w_out, ("dp", "tensor"), axis=0, tiled=True),
        lax.all_gather(gains.astype(jnp.bfloat16), ("dp", "tensor"), axis=0, tiled=True).astype(
            gains.dtype
        ),
        lax.all_gather(biases.astype(jnp.bfloat16), ("dp", "tensor"), axis=0, tiled=True).astype(
            biases.dtype
        ),
    )
    fc1_rows, fc2_cols = (
        lax.all_gather(w_fc1, "dp", axis=0, tiled=True),
        lax.all_gather(w_fc2, "dp", axis=1, tiled=True),
    )
    model_width = tokens.shape[1]
    local_rows = tokens.shape[0]
    head_dim = model_width // HEADS
    factor = 1.0 / math.sqrt(head_dim)
    doc_ends = jnp.cumsum(doc_lengths[0])[:-1]
    places = jnp.arange(local_rows)
    doc_ids = jnp.sum((places[:, None] >= doc_ends[None, :]).astype(jnp.int32), axis=1)
    inputs = tokens.astype(jnp.float32)
    normed_one, inverse_one = normalize(inputs)
    normed_in = (normed_one * gain_full[:, 0] + bias_full[:, 0]).astype(jnp.bfloat16)
    zero_bias = jnp.zeros((model_width,), jnp.float32)
    qkv_bias = jnp.concatenate([bias_full[:, 1], zero_bias, bias_full[:, 2]])
    projected = (
        jnp.dot(normed_in, qkv_full, preferred_element_type=jnp.float32) + qkv_bias
    ).astype(jnp.bfloat16)
    query_rows = projected[:, :model_width].reshape(local_rows, HEADS, head_dim)
    key_rows = projected[:, model_width : 2 * model_width].reshape(local_rows, HEADS, head_dim)
    value_rows = projected[:, 2 * model_width :].reshape(local_rows, HEADS, head_dim)
    attended, sums_log = attend_forward(query_rows, key_rows, value_rows, doc_ids, factor)
    attended = attended.reshape(local_rows, model_width)
    scale_wide = jnp.repeat(head_scale, head_dim)
    scaled = (attended * scale_wide).astype(jnp.bfloat16)
    branch = jnp.dot(scaled, out_full, preferred_element_type=jnp.float32) + bias_full[:, 3]
    normed_post, inverse_post = normalize(branch)
    middle = inputs + normed_post * gain_full[:, 1] + bias_full[:, 4]
    normed_two, inverse_two = normalize(middle)
    normed_mid = (normed_two * gain_full[:, 2] + bias_full[:, 5]).astype(jnp.bfloat16)
    gathered = lax.all_gather(normed_mid, "tensor", axis=0, tiled=True)
    hidden_pre = jnp.dot(gathered, fc1_rows, preferred_element_type=jnp.float32) + ffn_biases[0]
    activated, gelu_pull = jax.vjp(jax.nn.gelu, hidden_pre)
    act_sum, act_square = (
        lax.psum(jnp.sum(activated, axis=1).astype(jnp.bfloat16), "tensor").astype(jnp.float32),
        lax.psum(jnp.sum(activated * activated, axis=1).astype(jnp.bfloat16), "tensor").astype(
            jnp.float32
        ),
    )
    center = act_sum / FF
    inverse_mid = lax.rsqrt(act_square / FF - center * center + EPS)[:, None]
    normed_act = (activated - center[:, None]) * inverse_mid
    hidden = (normed_act * mid_gain + ffn_biases[1]).astype(jnp.bfloat16)
    hidden_rows = hidden
    ffn_out = lax.psum_scatter(
        jnp.dot(hidden_rows, fc2_cols, preferred_element_type=jnp.float32).astype(jnp.bfloat16),
        "tensor",
        scatter_dimension=0,
        tiled=True,
    ).astype(jnp.float32)
    shard_rows = lax.all_gather(out_grad, "tensor", axis=0, tiled=True)
    grad_piece = jnp.einsum("rd,fd->rf", shard_rows, fc2_cols, preferred_element_type=jnp.float32)
    hidden_rows = hidden
    fc2_run = jnp.einsum("rf,rd->fd", hidden_rows, shard_rows, preferred_element_type=jnp.float32)
    mid_gain_part = jnp.sum(grad_piece * normed_act, axis=0)
    mid_bias_part = jnp.sum(grad_piece, axis=0)
    grad_normed_act = grad_piece * mid_gain
    first_sum, second_sum = (
        lax.psum(jnp.sum(grad_normed_act, axis=1).astype(jnp.bfloat16), "tensor").astype(
            jnp.float32
        ),
        lax.psum(
            jnp.sum(grad_normed_act * normed_act, axis=1).astype(jnp.bfloat16), "tensor"
        ).astype(jnp.float32),
    )
    grad_act = inverse_mid * (
        grad_normed_act - first_sum[:, None] / FF - normed_act * (second_sum[:, None] / FF)
    )
    grad_pre = gelu_pull(grad_act)[0].astype(jnp.bfloat16)
    fc1_part = jnp.einsum("rd,rf->df", gathered, grad_pre, preferred_element_type=jnp.float32)
    fc1_bias_part = jnp.sum(grad_pre.astype(jnp.float32), axis=0)
    grad_normed_mid = lax.psum_scatter(
        jnp.einsum("rf,df->rd", grad_pre, fc1_rows, preferred_element_type=jnp.float32).astype(
            jnp.bfloat16
        ),
        "tensor",
        scatter_dimension=0,
        tiled=True,
    ).astype(jnp.float32)
    ffn_bias_part = jnp.stack([fc1_bias_part, mid_bias_part])
    fc1_grad, fc2_grad = (
        lax.psum_scatter(
            fc1_part.astype(jnp.bfloat16), "dp", scatter_dimension=0, tiled=True
        ).astype(jnp.float32),
        lax.psum_scatter(
            fc2_run.astype(jnp.bfloat16), "dp", scatter_dimension=1, tiled=True
        ).astype(jnp.float32),
    )
    mid_gain_grad, ffn_bias_grad = lax.psum((mid_gain_part, ffn_bias_part), "dp")
    mixed_out = (middle + ffn_out + bias_full[:, 6]).astype(jnp.bfloat16)
    final_grad = out_grad.astype(jnp.float32)
    grad_middle = final_grad + normalize_back(
        grad_normed_mid * gain_full[:, 2], normed_two, inverse_two
    )
    grad_post = normalize_back(grad_middle * gain_full[:, 1], normed_post, inverse_post).astype(
        jnp.bfloat16
    )
    out_local = jnp.einsum("td,te->de", scaled, grad_post, preferred_element_type=jnp.float32)
    grad_scaled = jnp.einsum("te,de->td", grad_post, out_full, preferred_element_type=jnp.float32)
    scale_local = jnp.sum(
        (grad_scaled * attended).reshape(local_rows, HEADS, head_dim), axis=(0, 2)
    )
    grad_attended = (
        (grad_scaled * scale_wide).astype(jnp.bfloat16).reshape(local_rows, HEADS, head_dim)
    )
    grad_query, grad_keys, grad_values = attend_backward(
        query_rows, key_rows, value_rows, grad_attended, doc_ids, sums_log, factor
    )
    grad_projected = jnp.concatenate(
        [
            grad_query.reshape(local_rows, model_width),
            grad_keys.reshape(local_rows, model_width),
            grad_values.reshape(local_rows, model_width),
        ],
        axis=1,
    ).astype(jnp.bfloat16)
    qkv_local = jnp.einsum(
        "td,te->de", normed_in, grad_projected, preferred_element_type=jnp.float32
    )
    grad_normed_in = jnp.einsum(
        "te,de->td", grad_projected, qkv_full, preferred_element_type=jnp.float32
    )
    token_grad = grad_middle + normalize_back(
        grad_normed_in * gain_full[:, 0], normed_one, inverse_one
    )
    projected_sums = jnp.sum(grad_projected.astype(jnp.float32), axis=0)
    gains_local = jnp.stack(
        [
            jnp.sum(grad_normed_in * normed_one, axis=0),
            jnp.sum(grad_middle * normed_post, axis=0),
            jnp.sum(grad_normed_mid * normed_two, axis=0),
        ],
        axis=1,
    )
    biases_local = jnp.stack(
        [
            jnp.sum(grad_normed_in, axis=0),
            projected_sums[:model_width],
            projected_sums[2 * model_width :],
            jnp.sum(grad_post.astype(jnp.float32), axis=0),
            jnp.sum(grad_middle, axis=0),
            jnp.sum(grad_normed_mid, axis=0),
            jnp.sum(final_grad, axis=0),
        ],
        axis=1,
    )
    qkv_grad, out_weight_grad, gains_grad, biases_grad = (
        lax.psum_scatter(qkv_local, ("dp", "tensor"), scatter_dimension=0, tiled=True),
        lax.psum_scatter(out_local, ("dp", "tensor"), scatter_dimension=0, tiled=True),
        lax.psum_scatter(gains_local, ("dp", "tensor"), scatter_dimension=0, tiled=True),
        lax.psum_scatter(biases_local, ("dp", "tensor"), scatter_dimension=0, tiled=True),
    )
    scale_grad = lax.psum(scale_local, ("dp", "tensor"))
    return (
        mixed_out,
        token_grad,
        qkv_grad,
        out_weight_grad,
        gains_grad,
        biases_grad,
        scale_grad,
        fc1_grad,
        fc2_grad,
        mid_gain_grad,
        ffn_bias_grad,
    )


MESH = pl.DeviceIdType.MESH
ANY = pl.BlockSpec(memory_space=pl.ANY)
IN_VMEM = pl.BlockSpec(memory_space=pltpu.VMEM)


def place():
    z = lax.axis_index("dp")
    t = lax.axis_index("tensor")
    return z, lax.div(t, 4), lax.rem(lax.div(t, 2), 2), lax.rem(t, 2)


def at(z, y, x, c):
    return (z, y * 4 + x * 2 + c)


def greet(partners):
    barrier = pltpu.get_barrier_semaphore()
    for partner in partners:
        pl.semaphore_signal(barrier, inc=1, device_id=partner, device_id_type=MESH)
    pl.semaphore_wait(barrier, len(partners))


class Sends:
    def __init__(self, send_sems, recv_sems):
        self.send_sems, self.recv_sems, self.copies = send_sems, recv_sems, []

    def start(self, src, dst, target):
        index = len(self.copies)
        copy = pltpu.make_async_remote_copy(
            src_ref=src,
            dst_ref=dst,
            send_sem=self.send_sems.at[index],
            recv_sem=self.recv_sems.at[index],
            device_id=target,
            device_id_type=MESH,
        )
        copy.start()
        self.copies.append(copy)
        return copy

    def finish(self):
        for copy in self.copies:
            copy.wait_send()


def add_low(left, right):
    return (left.astype(jnp.float32) + right.astype(jnp.float32)).astype(jnp.bfloat16)


SQRT_2_PI = math.sqrt(2.0 / math.pi)
NT = (((1,), (1,)), ((), ()))
TN = (((0,), (0,)), ((), ()))


def dot(left, right, dims=None):
    if dims is None:
        return jnp.dot(left, right, preferred_element_type=jnp.float32)
    return lax.dot_general(left, right, dims, preferred_element_type=jnp.float32)


def centered(values):
    center = jnp.mean(values, axis=-1, keepdims=True)
    spread = jnp.mean(values * values, axis=-1, keepdims=True) - center * center
    inverse = lax.rsqrt(spread + EPS)
    return (values - center) * inverse, inverse


def centered_back(grad, normed, inverse):
    first = jnp.mean(grad, axis=-1, keepdims=True)
    second = jnp.mean(grad * normed, axis=-1, keepdims=True)
    return inverse * (grad - first - normed * second)


def eights(values):
    return jnp.sum(values.reshape(values.shape[0] // 8, 8, values.shape[1]), axis=0)


def doc_mask(doc_ref, rows):
    query = lax.broadcasted_iota(jnp.int32, (rows, rows), 0)
    key = lax.broadcasted_iota(jnp.int32, (rows, rows), 1)
    query_doc, key_doc = jnp.zeros_like(query), jnp.zeros_like(key)
    end = 0
    for j in range(doc_ref.shape[1] - 1):
        end = end + doc_ref[0, j]
        query_doc = query_doc + (query >= end).astype(jnp.int32)
        key_doc = key_doc + (key >= end).astype(jnp.int32)
    allowed = jnp.logical_and(query_doc == key_doc, key <= query)
    return allowed.astype(jnp.float32)


class Plane:
    def __init__(self, sends, whole, here, targets):
        self.sends, self.whole, self.here, self.targets = sends, whole, here, targets
        half = whole.shape[3] // 2
        self.lo, self.hi = pl.ds(0, half), pl.ds(half, half)

    def part(self, y, x, c, rows):
        return self.whole.at[y, x, c, rows]

    def start_first(self, src):
        (y, x, c), (to_x, to_y, to_c), lo, hi = self.here, self.targets, self.lo, self.hi
        go = self.sends.start
        self.first = [
            go(src.at[lo], self.part(y, x, c, lo), to_x),
            go(src.at[hi], self.part(y, x, c, hi), to_y),
        ]
        self.core = [go(src, self.whole.at[y, x, c], to_c)]

    def start_second(self, src):
        (y, x, c), (to_x, to_y, _), lo, hi = self.here, self.targets, self.lo, self.hi
        go = self.sends.start
        self.second = [
            go(src.at[lo], self.part(y, x, c, lo), to_y),
            go(src.at[hi], self.part(y, x, c, hi), to_x),
        ]

    def after_first(self):
        (y, x, c), (to_x, to_y, to_c), lo, hi = self.here, self.targets, self.lo, self.hi
        for copy in self.first:
            copy.wait_recv()
        by_x, by_y = self.part(y, 1 - x, c, lo), self.part(1 - y, x, c, hi)
        go = self.sends.start
        self.third = [go(by_x, by_x, to_y), go(by_y, by_y, to_x)]
        self.side = [go(by_x, by_x, to_c), go(by_y, by_y, to_c)]

    def after_second(self):
        (y, x, c), (to_x, to_y, to_c), lo, hi = self.here, self.targets, self.lo, self.hi
        for copy in self.second:
            copy.wait_recv()
        by_x, by_y = self.part(y, 1 - x, c, hi), self.part(1 - y, x, c, lo)
        go = self.sends.start
        self.side += [go(by_x, by_x, to_c), go(by_y, by_y, to_c)]

    def after_third(self):
        y, x, c = self.here
        for copy in self.third:
            copy.wait_recv()
        ref = self.whole.at[1 - y, 1 - x, c]
        self.last = self.sends.start(ref, ref, self.targets[2])


def fore_kernel(
    nz,
    tok_ref,
    og_ref,
    qkv_ref,
    out_ref,
    gains_ref,
    biases_ref,
    fc1_ref,
    fc2_ref,
    gain_ref,
    shift_ref,
    doc_ref,
    scale_ref,
    qkv_out,
    out_out,
    vec_out,
    proj_out,
    att_out,
    lse_out,
    branch_out,
    middle_out,
    nin_out,
    scaled_out,
    ffn_out,
    fc2_out,
    late_out,
    fc1_out,
    gnm_out,
    unit_out,
    qkv_all,
    out_all,
    vec_all,
    vec_mine,
    vec_turn,
    unit_ref,
    fc1_all,
    fc2_all,
    og_all,
    tok,
    branch,
    nin,
    proj,
    att,
    lse,
    scaled,
    middle,
    mask,
    vec,
    mid_all,
    act,
    slope,
    grad,
    hidden,
    grad_pre,
    mid_part,
    pre,
    stats,
    pair,
    got,
    totals,
    from_core,
    sums,
    from_one,
    from_two,
    f_part,
    f_core,
    f_sums,
    fc1_part,
    late_part,
    fc2_part,
    fc1_got,
    local_sems,
    send_sems,
    recv_sems,
):
    z, y, x, c = place()
    to_x, to_y, to_c = at(z, y, 1 - x, c), at(z, 1 - y, x, c), at(z, y, x, 1 - c)
    to_xy = at(z, 1 - y, 1 - x, c)
    others = [lax.rem(z + k, nz) for k in range(1, nz)]
    slots = [z] + [lax.rem(z + nz - k, nz) for k in range(1, nz)]
    peers = [at(other, y, x, c) for other in others]
    locals_ = []

    def fetch(src, dst):
        copy = pltpu.make_async_copy(src, dst, local_sems.at[len(locals_)])
        copy.start()
        locals_.append(copy)
        return copy

    rows, width = tok.shape
    fourth = width // 4
    qkv_in = [
        fetch(
            qkv_ref.at[:, pl.ds(i * width + g * fourth, fourth)],
            qkv_all.at[z, y, x, c, :, pl.ds((3 * g + i) * fourth, fourth)],
        )
        for g in range(4)
        for i in range(3)
    ]
    vec_turn[...] = jnp.zeros_like(vec_turn)
    share = vec_mine.shape[0]
    vec_turn[0:3, 0:share] = gains_ref[...]
    vec_turn[3:10, 0:share] = biases_ref[...]
    vec_mine[...] = vec_turn[...].T[:share]
    greet([to_x, to_y, to_c, to_xy] + peers)
    sends = Sends(send_sems, recv_sems)
    low, f32 = jnp.bfloat16, jnp.float32
    units = fc1_all.shape[1]
    width1, width2 = fc1_ref.shape[0], fc2_ref.shape[1]
    own1 = fc1_all.at[pl.ds(pl.multiple_of(z * width1, width1), width1)]
    own2 = fc2_all.at[:, pl.ds(pl.multiple_of(z * width2, width2), width2)]
    def wait_all(copies):
        for copy in copies:
            copy.wait_recv()

    vec_z = [sends.start(vec_mine, vec_all.at[z, y, x, c], peer) for peer in peers]
    phase = 6 * fourth
    spans = (pl.ds(0, phase), pl.ds(phase, phase))
    for copy in qkv_in:
        copy.wait()
    own_qkv = qkv_all.at[z, y, x, c]
    qkv_z = [
        [sends.start(own_qkv.at[:, span], own_qkv.at[:, span], peer) for peer in peers]
        for span in spans
    ]

    def sides(whole, p):
        size = phase // 2 if whole is qkv_all else whole.shape[-1] // 2
        return pl.ds(2 * p * size, size), pl.ds((2 * p + 1) * size, size)

    def first(whole, slot, p=0):
        lo, hi = sides(whole, p)
        by_x, by_y = whole.at[slot, y, x, c, :, lo], whole.at[slot, y, x, c, :, hi]
        return (sends.start(by_x, by_x, to_x), sends.start(by_y, by_y, to_y))

    def second(whole, slot, p=0):
        lo, hi = sides(whole, p)
        by_x, by_y = whole.at[slot, y, :, c, :, lo], whole.at[slot, :, x, c, :, hi]
        return (sends.start(by_x, by_x, to_y), sends.start(by_y, by_y, to_x))

    def third(whole, slot, p=None):
        ref = whole.at[slot, :, :, c] if p is None else whole.at[slot, :, :, c, :, spans[p]]
        return sends.start(ref, ref, to_c)

    a0, a1 = [first(qkv_all, z, 0)], [first(qkv_all, z, 1)]
    og = Plane(sends, og_all, (y, x, c), (to_x, to_y, to_c))
    og.start_first(og_ref)
    tok_in = fetch(tok_ref, tok)
    out_in = fetch(out_ref, out_all.at[z, y, x, c])
    fc1_in = fetch(fc1_ref, own1)
    fc2_in = fetch(fc2_ref, own2)
    og_in = fetch(og_ref, og_all.at[y, x, c])
    vec_all[z, y, x, c] = vec_mine[...]
    unit_ref[...] = jnp.zeros_like(unit_ref)
    unit_ref[0:1] = shift_ref[0:1]
    unit_ref[1:2] = gain_ref[...]
    unit_ref[2:3] = shift_ref[1:2]
    step = 32
    wait_all(vec_z)
    by_x = vec_all.at[:, y, x, c]
    vec_x = sends.start(by_x, by_x, to_x)
    wait_all(a0[0])
    b0 = [second(qkv_all, z, 0)]
    wait_all(a1[0])
    b1 = [second(qkv_all, z, 1)]
    vec_x.wait_recv()
    by_y = vec_all.at[:, y, :, c]
    vec_y = sends.start(by_y, by_y, to_y)
    for k in range(1, nz):
        qkv_z[0][k - 1].wait_recv()
        a0.append(first(qkv_all, slots[k], 0))
    vec_y.wait_recv()
    by_c = vec_all.at[:, :, :, c]
    vec_c = sends.start(by_c, by_c, to_c)
    for k in range(1, nz):
        wait_all(a0[k])
        b0.append(second(qkv_all, slots[k], 0))
    mask[...] = doc_mask(doc_ref, rows)
    tok_in.wait()

    def normed(k, carry):
        part = pl.ds(pl.multiple_of(k * step, step), step)
        branch[part] = centered(tok[part].astype(f32))[0]
        return carry

    lax.fori_loop(0, rows // step, normed, 0)
    vec_c.wait_recv()
    vec[...] = vec_all[...].reshape(width, 128).T[:16]
    spot = lax.broadcasted_iota(jnp.int32, (1, width), 1)
    head = 64
    wide = jnp.zeros((1, width), f32)
    for h in range(HEADS):
        inside = jnp.logical_and(spot >= h * head, spot < (h + 1) * head)
        wide = jnp.where(inside, scale_ref[h], wide)
    vec[10:11] = wide

    def scaled_in(k, carry):
        part = pl.ds(pl.multiple_of(k * step, step), step)
        nin[part] = (branch[part] * vec[0:1] + vec[3:4]).astype(low)
        return carry

    lax.fori_loop(0, rows // step, scaled_in, 0)
    c0 = []
    for k in range(1, nz):
        qkv_z[1][k - 1].wait_recv()
        a1.append(first(qkv_all, slots[k], 1))
        wait_all(b0[k - 1])
        c0.append(third(qkv_all, slots[k - 1], 0))
    out_in.wait()
    own_out = out_all.at[z, y, x, c]
    out_z = [sends.start(own_out, own_out, peer) for peer in peers]
    pair_peer = at(z + 1 - 2 * lax.rem(z, 2), y, x, c)
    far_peer = peers[1]
    fc2_far = sends.start(fc2_ref, own2, far_peer)
    fc2_near = sends.start(fc2_ref, own2, pair_peer)
    fc1_z = [sends.start(fc1_ref, own1, peer) for peer in peers]
    wait_all(b0[nz - 1])
    c0.append(third(qkv_all, slots[nz - 1], 0))
    wait_all(a1[1])
    b1.append(second(qkv_all, slots[1], 1))
    wait_all(c0)

    def project(p):
        for g in (2 * p, 2 * p + 1):
            cols = pl.ds(3 * g * fourth, 3 * fourth)
            here = pl.ds(g * fourth, fourth)
            bias = jnp.concatenate(
                [vec[4:5, here], jnp.zeros((1, fourth), f32), vec[5:6, here]], axis=1
            )
            block = dot(nin[...], qkv_all[:, :, :, :, :, cols].reshape(width, 3 * fourth))
            proj[:, cols] = (block + bias).astype(low)

    project(0)
    lane = lax.broadcasted_iota(jnp.int32, (1, 128), 1)
    is_low = lane < head
    keep = (is_low.astype(low), (lane >= head).astype(low))
    factor = 1.0 / math.sqrt(head)
    lane_wide = lax.broadcasted_iota(jnp.int32, (rows, 128), 1)
    lse[...] = jnp.zeros_like(lse)

    def attend(p, carry):
        base = lax.div(p, 2) * (3 * fourth) + lax.rem(p, 2) * 128
        q_at = pl.ds(pl.multiple_of(base, 128), 128)
        k_at = pl.ds(pl.multiple_of(base + fourth, 128), 128)
        v_at = pl.ds(pl.multiple_of(base + 2 * fourth, 128), 128)
        here = pl.ds(pl.multiple_of(p * 128, 128), 128)
        q2, k2, v2 = proj[:, q_at], proj[:, k_at], proj[:, v_at]
        found = []
        for i in range(2):
            scores = dot(q2 * keep[i], k2, NT) * factor
            scores = jnp.where(mask[...] > 0, scores, NEGATIVE)
            peak = jnp.max(scores, axis=1, keepdims=True)
            exponent = jnp.exp(scores - peak)
            total = jnp.sum(exponent, axis=1, keepdims=True)
            prob = (exponent * (1.0 / total)).astype(low)
            found.append(dot(prob, v2))
            lse[...] = jnp.where(lane_wide == 2 * p + i, peak + jnp.log(total), lse[...])
        both = jnp.where(is_low, *found)
        att[:, here] = both
        scaled[:, here] = (both * vec[10:11, here]).astype(low)
        return carry

    lax.fori_loop(0, 1, attend, 0)
    for k in range(2, nz):
        wait_all(a1[k])
        b1.append(second(qkv_all, slots[k], 1))
    out_a = [first(out_all, z)]
    for k in range(1, nz):
        out_z[k - 1].wait_recv()
        out_a.append(first(out_all, slots[k]))
    og.start_second(og_ref)
    lax.fori_loop(1, 2, attend, 0)
    c1 = []
    for k in range(2):
        wait_all(b1[k])
        c1.append(third(qkv_all, slots[k], 1))
    lax.fori_loop(2, 4, attend, 0)
    for k in range(2, nz):
        wait_all(b1[k])
        c1.append(third(qkv_all, slots[k], 1))
    wait_all(c1)
    saves = [fetch(qkv_all, qkv_out), fetch(vec, vec_out), fetch(nin, nin_out)]
    project(1)
    saves.append(fetch(proj, proj_out))
    out_b = []
    for k in range(nz):
        wait_all(out_a[k])
        out_b.append(second(out_all, slots[k]))
    lax.fori_loop(4, 6, attend, 0)
    og.after_first()
    lax.fori_loop(6, 8, attend, 0)
    out_c = []
    for k in range(nz):
        wait_all(out_b[k])
        out_c.append(third(out_all, slots[k]))
    saves += [fetch(att, att_out), fetch(lse, lse_out), fetch(scaled, scaled_out)]
    wait_all(out_c)
    saves.append(fetch(out_all, out_out))
    quarter = width // 4
    for k in range(4):
        cols = pl.ds(k * quarter, quarter)
        block = dot(scaled[...], out_all[:, :, :, :, :, cols].reshape(width, quarter))
        branch[:, cols] = block + vec[6:7, cols]

    def middles(k, carry):
        part = pl.ds(pl.multiple_of(k * step, step), step)
        post = centered(branch[part])[0]
        value = tok[part].astype(f32) + post * vec[1:2] + vec[7:8]
        middle[part] = value
        mid_all[y, x, c, part] = (centered(value)[0] * vec[2:3] + vec[8:9]).astype(low)
        return carry

    lax.fori_loop(0, rows // step, middles, 0)
    mid = Plane(sends, mid_all, (y, x, c), (to_x, to_y, to_c))
    mid.start_first(mid_all.at[y, x, c])
    mid.start_second(mid_all.at[y, x, c])
    saves += [fetch(branch, branch_out), fetch(middle, middle_out)]

    def grads(yy, xx, cc):
        grad[yy, xx, cc] = dot(og_all[yy, xx, cc], fc2_all[...], NT)

    def fold(v):
        quarters = [v[:, k * (units // 4) : (k + 1) * (units // 4)] for k in range(4)]
        return (quarters[0] + quarters[1]) + (quarters[2] + quarters[3])

    def forward(yy, xx, cc):
        pre[...] = dot(mid_all[yy, xx, cc], fc1_all[...])

        def block(k, carry):
            part = pl.ds(pl.multiple_of(k * step, step), step)
            u = pre[part] + unit_ref[0:1]
            square = u * u
            th = jnp.tanh(u * (SQRT_2_PI + (SQRT_2_PI * 0.044715) * square))
            lift = 0.5 + 0.5 * th
            a = u * lift
            act[yy, xx, cc, part] = a
            bend = u * (2.0 * SQRT_2_PI + (6.0 * 0.044715 * SQRT_2_PI) * square)
            slope[yy, xx, cc, part] = lift + bend * (lift - lift * lift)
            gm = grad[yy, xx, cc, part] * unit_ref[1:2]
            for j, value in enumerate((a, a * a, gm, gm * a)):
                pre[part, j * (units // 4) : (j + 1) * (units // 4)] = fold(value)
            return carry

        lax.fori_loop(0, rows // step, block, 0)
        for j in range(4):
            folded = pre[:, j * (units // 4) : (j + 1) * (units // 4)]
            stats[yy, xx, cc, j : j + 1] = jnp.sum(folded.T, axis=0, keepdims=True)

    og.after_second()
    fc2_in.wait()
    fc2_far.wait_recv()
    near = fc2_all.at[:, pl.ds(pl.multiple_of(others[1] * width2, width2), width2)]
    fc2_last = sends.start(near, near, pair_peer)
    fc2_near.wait_recv()
    og.after_third()
    fc1_in.wait()
    mid.after_first()
    fc2_last.wait_recv()
    og_in.wait()
    grads(y, x, c)
    wait_all(og.core)
    grads(y, x, 1 - c)
    grads(y, 1 - x, c)
    grads(1 - y, x, c)
    mid.after_second()
    wait_all(og.side)
    grads(y, 1 - x, 1 - c)
    grads(1 - y, x, 1 - c)
    grads(1 - y, 1 - x, c)
    og.last.wait_recv()
    grads(1 - y, 1 - x, 1 - c)
    wait_all(fc1_z)
    forward(y, x, c)
    wait_all(mid.core)
    forward(y, x, 1 - c)
    mid.after_third()
    forward(y, 1 - x, c)
    forward(1 - y, x, c)
    wait_all(mid.side)
    forward(y, 1 - x, 1 - c)
    forward(1 - y, x, 1 - c)
    forward(1 - y, 1 - x, c)
    mid.last.wait_recv()
    forward(1 - y, 1 - x, 1 - c)

    sends.start(stats, got.at[3], to_c).wait_recv()
    pair[...] = stats[...] + got[3]
    wait_all([sends.start(pair, got.at[k], to) for k, to in enumerate((to_x, to_y, to_xy))])
    total = (pair[...] + got[0]) + (got[1] + got[2])
    total = total * (1.0 / (units * 8))
    center, square = total[:, :, :, 0:1], total[:, :, :, 1:2]
    mean, cross = total[:, :, :, 2:3], total[:, :, :, 3:4]
    inverse = lax.rsqrt(square - center * center + EPS)
    totals[:, :, :, 0:1] = inverse
    totals[:, :, :, 1:2] = -center * inverse
    totals[:, :, :, 2:3] = inverse * mean
    totals[:, :, :, 3:4] = inverse * (inverse * (cross - center * mean))
    unit_out[...] = jnp.zeros_like(unit_out)

    def backward(yy, xx, cc):
        for j in range(4):
            spread = jnp.broadcast_to(totals[yy, xx, cc, j : j + 1], (128, rows))
            pre[:, j * 128 : (j + 1) * 128] = spread.T

        def block(k, carry):
            part = pl.ds(pl.multiple_of(k * step, step), step)

            def across(j):
                return jnp.concatenate([pre[part, j * 128 : (j + 1) * 128]] * (units // 128), axis=1)

            g = grad[yy, xx, cc, part]
            inverse = across(0)
            normed = act[yy, xx, cc, part] * inverse + across(1)
            gain = unit_ref[1:2]
            hidden[yy, xx, cc, part] = (normed * gain + unit_ref[2:3]).astype(low)
            back = g * gain * inverse - across(2) - normed * across(3)
            value = (back * slope[yy, xx, cc, part]).astype(low)
            grad_pre[yy, xx, cc, part] = value
            return (
                carry[0] + eights(g * normed),
                carry[1] + eights(value.astype(f32)),
                carry[2] + eights(g),
            )

        zero = jnp.zeros((8, units), f32)
        parts = lax.fori_loop(0, rows // step, block, (zero, zero, zero))
        for j, part in enumerate(parts):
            unit_out[j : j + 1] += jnp.sum(part, axis=0, keepdims=True)
        return dot(grad_pre[yy, xx, cc], fc1_all[...], NT)

    left, right = pl.ds(0, width // 2), pl.ds(width // 2, width // 2)
    order = [(1 - y, 1 - x), (y, 1 - x), (1 - y, x), (y, x)]
    stage_x, stage_y, cores = [], [], []

    def to_core(k):
        yy, xx = order[k]
        mid_part[yy, xx] = backward(yy, xx, 1 - c).astype(low)
        cores.append(sends.start(mid_part.at[yy, xx], from_core.at[yy, xx], to_c))

    def from_pair(k):
        yy, xx = order[k]
        block = backward(yy, xx, c)
        cores[k].wait_recv()
        sums[yy, xx] = (block + from_core[yy, xx].astype(f32)).astype(low)
        if k in (0, 1):
            stage_x.append(sends.start(sums.at[yy, xx, :, left], from_one.at[yy, :, left], to_x))
        if k in (0, 2):
            stage_y.append(sends.start(sums.at[yy, xx, :, right], from_one.at[xx, :, right], to_y))

    to_core(0)
    to_core(1)
    from_pair(0)
    to_core(2)
    from_pair(1)
    to_core(3)
    from_pair(2)
    from_pair(3)

    def ffn_of(yy, xx, cc):
        return dot(hidden[yy, xx, cc], fc2_all[...])

    blocks = nz
    size = width // blocks

    early = fc1_part.shape[-1]
    soon, late = slice(0, early), slice(early, units)

    def fc1_block(which, cols):
        part = pl.ds(pl.multiple_of(which * size, 128), size)
        block = jnp.zeros((size, cols.stop - cols.start), f32)
        for j in range(8):
            yxc = (j // 4, (j // 2) % 2, j % 2)
            block = block + dot(mid_all[(*yxc, slice(None), part)], grad_pre[(*yxc, slice(None), cols)], TN)
        return block

    fc1_far = {}
    for k in (1, 0, 2):
        fc1_part[k] = fc1_block(others[k], soon).astype(low)
        fc1_far[k] = sends.start(fc1_part.at[k], fc1_got.at[k], peers[k])
    wait_all((stage_x[0], stage_y[0]))
    sums[1 - y, x, :, left] = add_low(sums[1 - y, x, :, left], from_one[1 - y, :, left])
    sums[y, 1 - x, :, right] = add_low(sums[y, 1 - x, :, right], from_one[1 - x, :, right])
    last_y = sends.start(sums.at[1 - y, x, :, left], from_two.at[:, left], to_y)
    last_x = sends.start(sums.at[y, 1 - x, :, right], from_two.at[:, right], to_x)
    fc1_out[:, soon] = fc1_block(z, soon)
    fc1_out[:, late] = fc1_block(z, late)

    def late_block(k, carry):
        part = pl.ds(pl.multiple_of(k * size, 128), size)
        late_part[part] = fc1_block(k, late).astype(low)
        return carry

    lax.fori_loop(0, blocks, late_block, 0)
    saves.append(fetch(late_part, late_out))
    cores = []
    for yy, xx in order:
        f_part[yy, xx] = ffn_of(yy, xx, 1 - c).astype(low)
        cores.append(sends.start(f_part.at[yy, xx], f_core.at[yy, xx], to_c))
    for k, (yy, xx) in enumerate(order):
        block = ffn_of(yy, xx, c)
        cores[k].wait_recv()
        f_sums[yy, xx] = (block + f_core[yy, xx].astype(f32)).astype(low)
    saves.append(fetch(f_sums, ffn_out))

    def fc2_block(k, carry):
        part = pl.ds(pl.multiple_of(k * size, 128), size)
        block = jnp.zeros((units, size), f32)
        for j in range(8):
            yxc = (j // 4, (j // 2) % 2, j % 2)
            block = block + dot(hidden[yxc], og_all[(*yxc, slice(None), part)], TN)
        fc2_part[:, part] = block.astype(low)
        return carry

    lax.fori_loop(0, blocks, fc2_block, 0)
    saves.append(fetch(fc2_part, fc2_out))
    wait_all((stage_x[1], stage_y[1], last_x, last_y))
    for cols, k in ((left, y), (right, x)):
        gnm_out[:, cols] = (
            sums[y, x, :, cols].astype(f32)
            + from_one[k, :, cols].astype(f32)
            + from_two[:, cols].astype(f32)
        )
    for k in range(nz - 1):
        fc1_far[k].wait_recv()
        fc1_out[:, soon] += fc1_got[k].astype(f32)
    for copy in saves:
        copy.wait()
    sends.finish()


def fore(nz, tokens, og, doc_lengths, w_qkv, w_out, gains, biases, scale, fc1, fc2, gain, shift):
    rows, width = tokens.shape
    share, units = w_qkv.shape[0], fc1.shape[1]
    low, f32, plane, every = jnp.bfloat16, jnp.float32, (2, 2, 2), (nz, 2, 2, 2)
    sds, vm = jax.ShapeDtypeStruct, pltpu.VMEM
    count = 160
    smem = pl.BlockSpec(memory_space=pltpu.SMEM)
    shapes = (
        (every + w_qkv.shape, low),
        (every + w_out.shape, low),
        ((16, width), f32),
        ((rows, w_qkv.shape[1]), low),
        ((rows, width), f32),
        ((rows, 128), f32),
        ((rows, width), f32),
        ((rows, width), f32),
        ((rows, width), low),
        ((rows, width), low),
        ((2, 2, rows, width), low),
        ((units, width), low),
        ((width, units // 2), low),
        (fc1.shape, f32),
        ((rows, width), f32),
        ((8, units), f32),
    )
    return pl.pallas_call(
        functools.partial(fore_kernel, nz),
        name="fore",
        out_shape=tuple(sds(shape, kind) for shape, kind in shapes),
        in_specs=[ANY] * 4 + [IN_VMEM] * 2 + [ANY] * 2 + [IN_VMEM] * 2 + [smem] * 2,
        out_specs=[ANY] * 13 + [IN_VMEM] * 3,
        scratch_shapes=[
            vm(every + w_qkv.shape, low),
            vm(every + w_out.shape, low),
            vm(every + (share, 128), f32),
            vm((share, 128), f32),
            vm((128, 128), f32),
            vm((8, units), f32),
            vm((width, units), low),
            vm((units, width), low),
            vm(plane + (rows, width), low),
            vm((rows, width), low),
            vm((rows, width), f32),
            vm((rows, width), low),
            vm((rows, w_qkv.shape[1]), low),
            vm((rows, width), f32),
            vm((rows, 128), f32),
            vm((rows, width), low),
            vm((rows, width), f32),
            vm((rows, rows), f32),
            vm((16, width), f32),
            vm(plane + (rows, width), low),
            vm(plane + (rows, units), f32),
            vm(plane + (rows, units), f32),
            vm(plane + (rows, units), f32),
            vm(plane + (rows, units), low),
            vm(plane + (rows, units), low),
            vm((2, 2, rows, width), low),
            vm((rows, units), f32),
            vm(plane + (4, rows), f32),
            vm(plane + (4, rows), f32),
            vm((4,) + plane + (4, rows), f32),
            vm(plane + (4, rows), f32),
            vm((2, 2, rows, width), low),
            vm((2, 2, rows, width), low),
            vm((2, rows, width), low),
            vm((rows, width), low),
            vm((2, 2, rows, width), low),
            vm((2, 2, rows, width), low),
            vm((2, 2, rows, width), low),
            vm((nz - 1, fc1.shape[0], units // 2), low),
            vm((width, units // 2), low),
            vm((units, width), low),
            vm((nz - 1, fc1.shape[0], units // 2), low),
            pltpu.SemaphoreType.DMA((36,)),
            pltpu.SemaphoreType.DMA((count,)),
            pltpu.SemaphoreType.DMA((count,)),
        ],
        compiler_params=pltpu.CompilerParams(
            collective_id=1, has_side_effects=True, vmem_limit_bytes=63 * 2**20
        ),
    )(tokens, og, w_qkv, w_out, gains.T, biases.T, fc1, fc2, gain, shift, doc_lengths, scale)


def back_kernel(
    nz,
    gnm_in,
    ffn_ref,
    late_ref,
    own1_in,
    fc2_ref,
    unit_ref,
    proj_in,
    att_in,
    lse_in,
    branch_in,
    middle_in,
    scaled_in,
    nin_in,
    qkv_in,
    out_in,
    vec_ref,
    og_in,
    tok_in,
    doc_ref,
    mixed_out,
    token_out,
    weight_out,
    gains_out,
    biases_out,
    scale_out,
    fc1_out,
    fc2_out,
    unit_out,
    f_sums,
    f_one,
    f_two,
    got1,
    got2,
    got_unit,
    w_part,
    w_core,
    w_sums,
    w_one,
    w_two,
    w_far,
    gpost,
    gmid,
    gatt,
    gni,
    dproj,
    nin_t,
    mask,
    accs,
    small,
    small_far,
    small_y,
    small_half,
    small_got,
    turned,
    mixed_at,
    weight_at,
    fc1_at,
    fc2_at,
    gnm_ref,
    proj_ref,
    att_ref,
    lse_ref,
    branch_ref,
    middle_ref,
    scaled_ref,
    nin_ref,
    qkv_ref,
    out_ref,
    og_ref,
    tok_ref,
    local_sems,
    send_sems,
    recv_sems,
):
    z, y, x, c = place()
    to_x, to_y, to_c = at(z, y, 1 - x, c), at(z, 1 - y, x, c), at(z, y, x, 1 - c)
    to_xy = at(z, 1 - y, 1 - x, c)
    others = [lax.rem(z + k, nz) for k in range(1, nz)]
    peers = [at(other, y, x, c) for other in others]
    locals_ = []

    def fetch(src, dst):
        copy = pltpu.make_async_copy(src, dst, local_sems.at[len(locals_)])
        copy.start()
        locals_.append(copy)
        return copy

    middle_got = fetch(middle_in, middle_ref)
    gnm_got = fetch(gnm_in, gnm_ref)
    og_got = fetch(og_in, og_ref)
    branch_got = fetch(branch_in, branch_ref)
    ffn_got = fetch(ffn_ref, f_sums)
    out_got = fetch(out_in, out_ref)
    att_got = fetch(att_in, att_ref)
    scaled_got = fetch(scaled_in, scaled_ref)
    nin_got = fetch(nin_in, nin_ref)
    proj_got = fetch(proj_in, proj_ref)
    lse_got = fetch(lse_in, lse_ref)
    qkv_got = fetch(qkv_in, qkv_ref)
    tok_got = fetch(tok_in, tok_ref)

    greet([to_x, to_y, to_c, to_xy] + peers)
    sends = Sends(send_sems, recv_sems)
    rows, width = middle_ref.shape
    low = jnp.bfloat16
    f32 = jnp.float32
    share = weight_out.shape[0]
    width1, width2 = fc1_out.shape[0], fc2_out.shape[1]

    pieces = 2
    parts = [pl.ds(k * (rows // pieces), rows // pieces) for k in range(pieces)]
    left, right = pl.ds(0, width // 2), pl.ds(width // 2, width // 2)
    def block1(which):
        return late_ref.at[pl.ds(pl.multiple_of(which * width1, width1), width1)]

    def block2(which):
        return fc2_ref.at[:, pl.ds(pl.multiple_of(which * width2, width2), width2)]

    own1_got = fetch(own1_in, fc1_at)
    own2_got = fetch(block2(z), got2.at[nz - 1])
    far = []
    for k, peer in enumerate(peers):
        far.append(sends.start(unit_ref, got_unit.at[k], peer))
        far.append(sends.start(block1(others[k]), got1.at[k], peer))
        far.append(sends.start(block2(others[k]), got2.at[k], peer))

    f_first, f_second = [], []

    def ffn_one(k):
        part = parts[k]
        f_first.append(
            (
                sends.start(ffn_ref.at[:, 1 - x, part, left], f_one.at[0, :, part, left], to_x),
                sends.start(ffn_ref.at[1 - y, :, part, right], f_one.at[1, :, part, right], to_y),
            )
        )

    def ffn_two(k):
        part = parts[k]
        if k == 0:
            ffn_got.wait()
        for copy in f_first[k]:
            copy.wait_recv()
        f_sums[1 - y, x, part, left] = add_low(
            f_sums[1 - y, x, part, left], f_one[0, 1 - y, part, left]
        )
        f_sums[y, 1 - x, part, right] = add_low(
            f_sums[y, 1 - x, part, right], f_one[1, 1 - x, part, right]
        )
        f_second.append(
            (
                sends.start(f_sums.at[1 - y, x, part, left], f_two.at[part, left], to_y),
                sends.start(f_sums.at[y, 1 - x, part, right], f_two.at[part, right], to_x),
            )
        )

    def ffn_three(k):
        part = parts[k]
        for copy in f_second[k]:
            copy.wait_recv()
        for i, (cols, at_) in enumerate(((left, y), (right, x))):
            total = (
                f_sums[y, x, part, cols].astype(f32)
                + f_one[i, at_, part, cols].astype(f32)
                + f_two[part, cols].astype(f32)
            )
            mixed_at[part, cols] = (
                middle_ref[part, cols] + total + vec_ref[9:10, cols]
            ).astype(low)
        puts.append(fetch(mixed_at.at[part], mixed_out.at[part]))

    spans = [(0, width)] + [(width + g * 3 * width // 4, 3 * width // 4) for g in range(4)]
    w_first, w_second, w_third, w_c = {}, {}, {}, {}

    def sides(j):
        start, size = spans[j]
        return pl.ds(start, size), pl.ds(start, size // 2), pl.ds(start + size // 2, size // 2)

    def w_zero(j):
        every = sides(j)[0]
        w_c[j] = sends.start(w_part.at[:, :, :, 1 - c, :, every], w_core.at[..., every], to_c)

    def w_step1(j):
        every, lo, hi = sides(j)
        w_c[j].wait_recv()

        def one(which, carry):
            for yy in range(2):
                for xx in range(2):
                    w_sums[which, yy, xx, :, every] = add_low(
                        w_part[which, yy, xx, c, :, every], w_core[which, yy, xx, :, every]
                    )
            return carry

        lax.fori_loop(0, nz, one, 0)
        w_first[j] = (
            sends.start(w_sums.at[:, :, 1 - x, :, lo], w_one.at[:, :, :, lo], to_x),
            sends.start(w_sums.at[:, 1 - y, :, :, hi], w_one.at[:, :, :, hi], to_y),
        )

    def w_step2(j):
        every, lo, hi = sides(j)
        for copy in w_first[j]:
            copy.wait_recv()

        def one(which, carry):
            for k in range(2):
                w_sums[which, k, x, :, lo] = add_low(
                    w_sums[which, k, x, :, lo], w_one[which, k, :, lo]
                )
                w_sums[which, y, k, :, hi] = add_low(
                    w_sums[which, y, k, :, hi], w_one[which, k, :, hi]
                )
            return carry

        lax.fori_loop(0, nz, one, 0)
        w_second[j] = (
            sends.start(w_sums.at[:, 1 - y, x, :, lo], w_two.at[:, :, lo], to_y),
            sends.start(w_sums.at[:, y, 1 - x, :, hi], w_two.at[:, :, hi], to_x),
        )

    def w_step3(j):
        every = sides(j)[0]
        for copy in w_second[j]:
            copy.wait_recv()
        for which in range(nz):
            w_sums[which, y, x, :, every] = add_low(
                w_sums[which, y, x, :, every], w_two[which, :, every]
            )
        w_third[j] = [
            sends.start(w_sums.at[others[k], y, x, :, every], w_far.at[k, :, every], peer)
            for k, peer in enumerate(peers)
        ]

    def w_step4(j):
        start, size = spans[j]
        every = sides(j)[0]
        total = w_sums[z, y, x, :, every].astype(f32)
        for k in range(nz - 1):
            w_third[j][k].wait_recv()
            total = total + w_far[k, :, every].astype(f32)
        if j == 0:
            weight_at[:, 3 * width :] = total
            spots = [pl.ds(3 * width, width)]
        else:
            third = size // 3
            spots = [pl.ds(i * width + (j - 1) * third, third) for i in range(3)]
            for i, spot in enumerate(spots):
                weight_at[:, spot] = total[:, i * third : (i + 1) * third]
        for spot in spots:
            puts.append(fetch(weight_at.at[:, spot], weight_out.at[:, spot]))

    ffn_one(0)
    accs[...] = jnp.zeros_like(accs)
    step = 32

    def norms(k, carry):
        part = pl.ds(pl.multiple_of(k * step, step), step)
        normed_two, inverse_two = centered(middle_ref[part])
        grad = gnm_ref[part]
        og = og_ref[part].astype(f32)
        grad_middle = og + centered_back(grad * vec_ref[2:3], normed_two, inverse_two)
        accs[2] += eights(grad * normed_two)
        accs[8] += eights(grad)
        accs[9] += eights(og)
        normed_post, inverse_post = centered(branch_ref[part])
        post = centered_back(grad_middle * vec_ref[1:2], normed_post, inverse_post).astype(low)
        accs[1] += eights(grad_middle * normed_post)
        accs[7] += eights(grad_middle)
        accs[6] += eights(post.astype(f32))
        gpost[part] = post
        gmid[part] = grad_middle
        return carry

    for copy in (middle_got, gnm_got, og_got, branch_got):
        copy.wait()
    lax.fori_loop(0, rows // step, norms, 0)
    mask[...] = doc_mask(doc_ref, rows)
    quarter = width // 4

    def scaled_block(k, carry):
        part = pl.ds(pl.multiple_of(k * quarter, quarter), quarter)
        block = dot(gpost[...], out_ref[part], NT)
        accs[10, :, part] = eights(block * att_ref[:, part])
        gatt[:, part] = (block * vec_ref[10:11, part]).astype(low)
        return carry

    out_got.wait()
    att_got.wait()
    lax.fori_loop(0, 4, scaled_block, 0)

    def out_block(k, carry):
        part = pl.ds(pl.multiple_of(k * (width // nz), width // nz), width // nz)
        block = dot(scaled_ref[:, part], gpost[...], TN).astype(low)
        w_part[k, :, :, :, :, pl.ds(0, width)] = block.reshape(2, 2, 2, share, width)
        return carry

    scaled_got.wait()
    lax.fori_loop(0, nz, out_block, 0)
    w_zero(0)
    nin_got.wait()
    nin_t[...] = nin_ref[...].T
    proj_got.wait()
    lse_got.wait()
    head = 64
    lane = lax.broadcasted_iota(jnp.int32, (1, 128), 1)
    is_low = lane < head
    factor = 1.0 / math.sqrt(head)
    lane_wide = lax.broadcasted_iota(jnp.int32, (rows, 128), 1)
    keep = (is_low.astype(low), (lane >= head).astype(low))

    def pair(p, carry):
        base = lax.div(p, 2) * (3 * quarter) + lax.rem(p, 2) * 128
        q_at = pl.ds(pl.multiple_of(base, 128), 128)
        k_at = pl.ds(pl.multiple_of(base + quarter, 128), 128)
        v_at = pl.ds(pl.multiple_of(base + 2 * quarter, 128), 128)
        here = pl.ds(pl.multiple_of(p * 128, 128), 128)
        q2, k2, v2, do2 = proj_ref[:, q_at], proj_ref[:, k_at], proj_ref[:, v_at], gatt[:, here]
        lses = lse_ref[...]
        found = []
        for i in range(2):
            scores = dot(q2 * keep[i], k2, NT) * factor
            scores = jnp.where(mask[...] > 0, scores, NEGATIVE)
            lse = jnp.sum(jnp.where(lane_wide == 2 * p + i, lses, 0.0), axis=1, keepdims=True)
            prob = jnp.exp(scores - lse)
            grad_prob = dot(do2 * keep[i], v2, NT)
            inner = jnp.sum(prob * grad_prob, axis=1, keepdims=True)
            ds = (prob * (grad_prob - inner) * factor).astype(low)
            found.append(
                (dot(ds, k2), dot(ds, q2, TN), dot(prob.astype(low), do2, TN))
            )
        for where, a, b in zip((q_at, k_at, v_at), *found):
            dproj[:, where] = jnp.where(is_low, a, b).astype(low)
        accs[4, :, here] = eights(dproj[:, q_at].astype(f32))
        accs[5, :, here] = eights(dproj[:, v_at].astype(f32))
        return carry

    def wgrad(j):
        start, size = spans[j]
        cols = pl.ds((j - 1) * size, size)

        def one(k, carry):
            part = pl.ds(pl.multiple_of(k * (width // nz), width // nz), width // nz)
            block = dot(nin_t[part], dproj[:, cols]).astype(low)
            w_part[k, :, :, :, :, pl.ds(start, size)] = block.reshape(2, 2, 2, share, size)
            return carry

        lax.fori_loop(0, nz, one, 0)
        w_zero(j)

    def gni_block(k, carry):
        part = pl.ds(pl.multiple_of(k * quarter, quarter), quarter)
        gni[:, part] = dot(dproj[...], qkv_ref[part], NT)
        return carry

    def tokens_back(k, carry):
        part = pl.ds(pl.multiple_of(k * step, step), step)
        normed, inverse = centered(tok_ref[part].astype(f32))
        grad = gni[part]
        gmid[part] = gmid[part] + centered_back(grad * vec_ref[0:1], normed, inverse)
        accs[0] += eights(grad * normed)
        accs[3] += eights(grad)
        return carry

    part_z = width // nz
    chain = {}

    def lanes(which):
        return pl.ds(pl.multiple_of(which * part_z, 128), part_z)

    def small_start():
        for j in range(16):
            small[j : j + 1] = jnp.sum(accs[j], axis=0, keepdims=True)
        spot = lax.broadcasted_iota(jnp.int32, (1, width), 1)
        tile = jnp.zeros((1, 128), f32)
        for h in range(HEADS):
            inside = jnp.logical_and(spot >= h * head, spot < (h + 1) * head)
            found = jnp.sum(jnp.where(inside, small[10:11], 0.0), axis=1, keepdims=True)
            tile = jnp.where(lane == h, found, tile)
        small[11:12] = jnp.concatenate([tile] * (width // 128), axis=1)
        chain["z"] = [
            sends.start(small.at[:, lanes(others[k])], small_far.at[k], peer)
            for k, peer in enumerate(peers)
        ]

    def small_second():
        total = small[:, lanes(z)]
        for k in range(nz - 1):
            chain["z"][k].wait_recv()
            total = total + small_far[k]
        small_y[...] = total
        other = small_y.at[:, pl.ds(pl.multiple_of((1 - y) * 128, 128), 128)]
        chain["y"] = sends.start(other, small_got.at[0], to_y)

    def small_third():
        chain["y"].wait_recv()
        small_half[0] = small_y[:, pl.ds(pl.multiple_of(y * 128, 128), 128)] + small_got[0]
        chain["x"] = sends.start(small_half.at[0], small_got.at[1], to_x)

    def small_fourth():
        chain["x"].wait_recv()
        small_half[1] = small_half[0] + small_got[1]
        chain["c"] = sends.start(small_half.at[1], small_got.at[2], to_c)

    def small_last():
        chain["c"].wait_recv()
        total = small_half[1] + small_got[2]
        scale_out[...] = jnp.broadcast_to(total[11:12], (8, 128))
        ours = pl.ds(pl.multiple_of((2 * x + c) * share, share), share)
        turned[...] = jnp.concatenate([total, jnp.zeros((112, 128), f32)], axis=0).T
        mine = jnp.concatenate([turned[ours], jnp.zeros((128 - share, 128), f32)], axis=0).T
        gains_out[...] = mine[0:3, :share]
        biases_out[...] = mine[3:10, :share]

    puts = []

    def far_last():
        for copy in far:
            copy.wait_recv()
        own1_got.wait()
        own2_got.wait()
        late = pl.ds(fc1_at.shape[1] - got1.shape[2], got1.shape[2])
        own2, unit = got2[nz - 1].astype(f32), unit_ref[...]
        for k in range(nz - 1):
            fc1_at[:, late] += got1[k].astype(f32)
            own2 = own2 + got2[k].astype(f32)
            unit = unit + got_unit[k]
        fc2_at[...] = own2
        unit_out[...] = unit
        puts.append(fetch(fc1_at, fc1_out))
        puts.append(fetch(fc2_at, fc2_out))

    def pairs(first, last):
        lax.fori_loop(first, last, pair, 0)

    def gni_all():
        qkv_got.wait()
        lax.fori_loop(0, 4, gni_block, 0)

    def tokens_all():
        tok_got.wait()
        lax.fori_loop(0, rows // step, tokens_back, 0)
        puts.append(fetch(gmid, token_out))

    pairs(0, 1)
    w_step1(0)
    pairs(1, 2)
    wgrad(1)
    ffn_two(0)
    pairs(2, 3)
    w_step1(1)
    pairs(3, 4)
    wgrad(2)
    w_step2(0)
    pairs(4, 5)
    w_step1(2)
    pairs(5, 6)
    wgrad(3)
    w_step2(1)
    w_step3(0)
    pairs(6, 7)
    w_step1(3)
    pairs(7, 8)
    wgrad(4)
    w_step2(2)
    gni_all()
    w_step3(1)
    w_step1(4)
    tokens_all()
    small_start()
    w_step2(3)
    w_step3(2)
    ffn_one(1)
    small_second()
    w_step2(4)
    w_step3(3)
    ffn_three(0)
    small_third()
    w_step4(0)
    w_step4(1)
    small_fourth()
    ffn_two(1)
    w_step3(4)
    w_step4(2)
    small_last()
    far_last()
    w_step4(3)
    ffn_three(1)
    w_step4(4)
    for put in puts:
        put.wait()
    sends.finish()


def back(nz, *operands):
    gnm, ffn_part, late, fc1, fc2, unit, proj, att, lse, branch, middle = operands[:11]
    scaled, nin, qkv, out, vec = operands[11:16]
    rows, width = middle.shape
    share = width // (nz * 8)
    columns = proj.shape[1] + width
    low, f32 = jnp.bfloat16, jnp.float32
    sds = jax.ShapeDtypeStruct
    fc2_own = (fc2.shape[0], fc2.shape[1] // nz)
    count = 64 + 8 * nz
    specs = [ANY] * 5 + [IN_VMEM] + [ANY] * 9 + [IN_VMEM] + [ANY] * 2
    specs.append(pl.BlockSpec(memory_space=pltpu.SMEM))
    return pl.pallas_call(
        functools.partial(back_kernel, nz),
        name="back",
        out_shape=(
            sds((rows, width), low),
            sds((rows, width), f32),
            sds((share, columns), f32),
            sds((3, share), f32),
            sds((7, share), f32),
            sds((8, 128), f32),
            sds(fc1.shape, f32),
            sds(fc2_own, f32),
            sds(unit.shape, f32),
        ),
        in_specs=specs,
        out_specs=[ANY] * 3 + [IN_VMEM] * 3 + [ANY] * 2 + [IN_VMEM],
        scratch_shapes=[
            pltpu.VMEM((2, 2, rows, width), low),
            pltpu.VMEM((2, 2, rows, width), low),
            pltpu.VMEM((rows, width), low),
            pltpu.VMEM((nz - 1, fc1.shape[0], late.shape[1]), low),
            pltpu.VMEM((nz,) + fc2_own, low),
            pltpu.VMEM((nz - 1,) + unit.shape, f32),
            pltpu.VMEM((nz, 2, 2, 2, share, columns), low),
            pltpu.VMEM((nz, 2, 2, share, columns), low),
            pltpu.VMEM((nz, 2, 2, share, columns), low),
            pltpu.VMEM((nz, 2, share, columns), low),
            pltpu.VMEM((nz, share, columns), low),
            pltpu.VMEM((nz - 1, share, columns), low),
            pltpu.VMEM((rows, width), low),
            pltpu.VMEM((rows, width), f32),
            pltpu.VMEM((rows, width), low),
            pltpu.VMEM((rows, width), f32),
            pltpu.VMEM((rows, 3 * width), low),
            pltpu.VMEM((width, rows), low),
            pltpu.VMEM((rows, rows), f32),
            pltpu.VMEM((16, 8, width), f32),
            pltpu.VMEM((16, width), f32),
            pltpu.VMEM((nz - 1, 16, width // nz), f32),
            pltpu.VMEM((16, width // nz), f32),
            pltpu.VMEM((3, 16, 128), f32),
            pltpu.VMEM((3, 16, 128), f32),
            pltpu.VMEM((128, 128), f32),
            pltpu.VMEM((rows, width), low),
            pltpu.VMEM((share, columns), f32),
            pltpu.VMEM(fc1.shape, f32),
            pltpu.VMEM(fc2_own, f32),
            pltpu.VMEM((rows, width), f32),
            pltpu.VMEM(proj.shape, low),
            pltpu.VMEM((rows, width), f32),
            pltpu.VMEM(lse.shape, f32),
            pltpu.VMEM((rows, width), f32),
            pltpu.VMEM((rows, width), f32),
            pltpu.VMEM((rows, width), low),
            pltpu.VMEM((rows, width), low),
            pltpu.VMEM(qkv.shape, low),
            pltpu.VMEM(out.shape, low),
            pltpu.VMEM((rows, width), low),
            pltpu.VMEM((rows, width), low),
            pltpu.SemaphoreType.DMA((48,)),
            pltpu.SemaphoreType.DMA((count,)),
            pltpu.SemaphoreType.DMA((count,)),
        ],
        compiler_params=pltpu.CompilerParams(
            collective_id=3, has_side_effects=True, vmem_limit_bytes=63 * 2**20
        ),
    )(*operands)


def finish_kernel(
    mixed,
    token,
    weight,
    fc1,
    fc2,
    gains,
    biases,
    scale,
    unit,
    mixed_out,
    token_out,
    qkv_out,
    out_out,
    fc1_out,
    fc2_out,
    gains_out,
    biases_out,
    scale_out,
    gain_out,
    shift_out,
    mixed_at,
    token_at,
    weight_at,
    fc1_at,
    fc2_at,
    in_sems,
    out_sems,
):
    columns = qkv_out.shape[1]
    moves = (
        (token, token_at, ((token_at, token_out),)),
        (
            weight,
            weight_at,
            (
                (weight_at.at[:, pl.ds(0, columns)], qkv_out),
                (weight_at.at[:, pl.ds(columns, out_out.shape[1])], out_out),
            ),
        ),
        (mixed, mixed_at, ((mixed_at, mixed_out),)),
        (fc1, fc1_at, ((fc1_at, fc1_out),)),
        (fc2, fc2_at, ((fc2_at, fc2_out),)),
    )
    reads, writes = [], []
    for k, (src, here, _) in enumerate(moves):
        reads.append(pltpu.make_async_copy(src, here, in_sems.at[k]))
        reads[-1].start()
    gains_out[...] = gains[...]
    biases_out[...] = biases[...]
    scale_out[...] = scale[0:1, : scale_out.shape[1]]
    gain_out[...] = unit[0:1]
    shift_out[0:1] = unit[1:2]
    shift_out[1:2] = unit[2:3]
    for read, (_, _, outs) in zip(reads, moves):
        read.wait()
        for src, dst in outs:
            writes.append(pltpu.make_async_copy(src, dst, out_sems.at[len(writes)]))
            writes[-1].start()
    for write in writes:
        write.wait()


def finish(mixed, token, weight, gains, biases, scale, fc1, fc2, unit):
    share, columns = weight.shape
    width, units = token.shape[1], unit.shape[1]
    f32 = jnp.float32
    shapes = (
        (mixed.shape, mixed.dtype),
        (token.shape, f32),
        ((share, columns - width), f32),
        ((share, width), f32),
        (fc1.shape, f32),
        (fc2.shape, f32),
        (gains.shape, f32),
        (biases.shape, f32),
        ((1, HEADS), f32),
        ((1, units), f32),
        ((2, units), f32),
    )
    return pl.pallas_call(
        finish_kernel,
        name="finish",
        out_shape=tuple(jax.ShapeDtypeStruct(shape, kind) for shape, kind in shapes),
        in_specs=[ANY] * 5 + [IN_VMEM] * 4,
        out_specs=[ANY] * 6 + [IN_VMEM] * 5,
        scratch_shapes=[
            pltpu.VMEM(mixed.shape, mixed.dtype),
            pltpu.VMEM(token.shape, f32),
            pltpu.VMEM(weight.shape, f32),
            pltpu.VMEM(fc1.shape, f32),
            pltpu.VMEM(fc2.shape, f32),
            pltpu.SemaphoreType.DMA((5,)),
            pltpu.SemaphoreType.DMA((6,)),
        ],
        compiler_params=pltpu.CompilerParams(vmem_limit_bytes=63 * 2**20),
    )(mixed, token, weight, fc1, fc2, gains, biases, scale, unit)


def fused(
    nz,
    tokens,
    out_grad,
    doc_lengths,
    w_qkv,
    w_out,
    gains,
    biases,
    head_scale,
    w_fc1,
    w_fc2,
    mid_gain,
    ffn_biases,
):
    (
        qkv_full,
        out_full,
        vec,
        proj,
        att,
        lse,
        branch,
        middle,
        nin,
        scaled,
        ffn_part,
        fc2_part,
        fc1_late,
        fc1_own,
        gnm,
        unit_sums,
    ) = fore(
        nz,
        tokens,
        out_grad,
        doc_lengths,
        w_qkv,
        w_out,
        gains,
        biases,
        head_scale,
        w_fc1,
        w_fc2,
        mid_gain[None],
        ffn_biases,
    )
    model_width = tokens.shape[1]
    (
        mixed,
        token_grad,
        weight_grad,
        gains_grad,
        biases_grad,
        scale,
        fc1_grad,
        fc2_grad,
        unit_sums,
    ) = back(
        nz,
        gnm,
        ffn_part,
        fc1_late,
        fc1_own,
        fc2_part,
        unit_sums,
        proj,
        att,
        lse,
        branch,
        middle,
        scaled,
        nin,
        qkv_full.reshape(model_width, -1),
        out_full.reshape(model_width, -1),
        vec,
        out_grad,
        tokens,
        doc_lengths,
    )
    mixed, token_grad, qkv, out, fc1, fc2, gains_grad, biases_grad, scale, gain, shift = finish(
        mixed,
        token_grad,
        weight_grad,
        gains_grad,
        biases_grad,
        scale,
        fc1_grad,
        fc2_grad,
        unit_sums,
    )
    return (
        mixed,
        token_grad,
        qkv,
        out,
        gains_grad.T,
        biases_grad.T,
        scale[0],
        fc1,
        fc2,
        gain[0],
        shift,
    )


def layer(nz, nt, tokens, out_grad, doc_lengths, w_qkv, *rest):
    if nz == 4 and nt == 8 and w_qkv.shape[0] % 16 == 0:
        return fused(nz, tokens, out_grad, doc_lengths, w_qkv, *rest)
    return plain(tokens, out_grad, doc_lengths, w_qkv, *rest)


def solution(mesh):
    return jax.shard_map(
        functools.partial(layer, mesh.shape["dp"], mesh.shape["tensor"]),
        mesh=mesh,
        in_specs=(
            P(("dp", "tensor"), None),
            P(("dp", "tensor"), None),
            P(("dp", "tensor"), None),
            P(("dp", "tensor"), None),
            P(("dp", "tensor"), None),
            P(("dp", "tensor"), None),
            P(("dp", "tensor"), None),
            P(),
            P("dp", "tensor"),
            P("tensor", "dp"),
            P("tensor"),
            P(None, "tensor"),
        ),
        out_specs=(
            P(("dp", "tensor"), None),
            P(("dp", "tensor"), None),
            P(("dp", "tensor"), None),
            P(("dp", "tensor"), None),
            P(("dp", "tensor"), None),
            P(("dp", "tensor"), None),
            P(),
            P("dp", "tensor"),
            P("tensor", "dp"),
            P("tensor"),
            P(None, "tensor"),
        ),
        check_vma=False,
    )
```

```python
import functools
import math

import jax
import jax.numpy as jnp
from jax import lax
from jax.experimental import pallas as pl
from jax.experimental.pallas import tpu as pltpu
from jax.sharding import PartitionSpec as P

HEADS = 16
FF = 4096


EPS = 1e-05
NEGATIVE = -1000000000.0


def normalize(values):
    center = jnp.mean(values, axis=-1, keepdims=True)
    spread = jnp.mean(values * values, axis=-1, keepdims=True) - center * center
    inverse = lax.rsqrt(spread + EPS)
    return ((values - center) * inverse, inverse)


def normalize_back(grad_normed, normed, inverse):
    first_mean = jnp.mean(grad_normed, axis=-1, keepdims=True)
    second = jnp.mean(grad_normed * normed, axis=-1, keepdims=True)
    return inverse * (grad_normed - first_mean - normed * second)


def block_scores(query_rows, key_rows, doc_ids, row_first, row_last, factor):
    scores = (
        jnp.einsum("qhd,khd->hqk", query_rows, key_rows, preferred_element_type=jnp.float32)
        * factor
    )
    query_pos = jnp.arange(row_first, row_last)
    key_pos = jnp.arange(row_last)
    same_doc = doc_ids[row_first:row_last, None] == doc_ids[None, :row_last]
    allowed = jnp.logical_and(same_doc, key_pos[None, :] <= query_pos[:, None])
    return (jnp.where(allowed[None], scores, NEGATIVE), allowed)


def attend_forward(query_rows, key_rows, value_rows, doc_ids, factor):
    total_rows = query_rows.shape[0]
    block_rows = min(512, total_rows)
    scores, allowed = block_scores(query_rows, key_rows, doc_ids, 0, block_rows, factor)
    row_peak = jnp.max(scores, axis=-1, keepdims=True)
    exponent = jnp.exp(scores - row_peak)
    row_total = jnp.sum(exponent, axis=-1, keepdims=True)
    prob_low = (exponent / row_total).astype(jnp.bfloat16)
    pieces = jnp.einsum("hqk,khd->qhd", prob_low, value_rows, preferred_element_type=jnp.float32)
    sums_log = [row_peak + jnp.log(row_total)]
    return (pieces, sums_log)


def attend_backward(query_rows, key_rows, value_rows, grad_out, doc_ids, sums_log, factor):
    total_rows = query_rows.shape[0]
    block_rows = min(512, total_rows)
    query_parts = []
    grad_keys = jnp.zeros(key_rows.shape, jnp.float32)
    grad_values = jnp.zeros(value_rows.shape, jnp.float32)
    for block_index, row_first in enumerate(range(0, total_rows, block_rows)):
        row_last = row_first + block_rows
        scores, allowed = block_scores(query_rows, key_rows, doc_ids, row_first, row_last, factor)
        prob_rows = jnp.where(allowed[None], jnp.exp(scores - sums_log[block_index]), 0.0)
        prob_low = prob_rows.astype(jnp.bfloat16)
        grad_probs = jnp.einsum(
            "qhd,khd->hqk", grad_out, value_rows, preferred_element_type=jnp.float32
        )
        inner_sum = jnp.sum(prob_rows * grad_probs, axis=-1, keepdims=True)
        grad_scores = (prob_rows * (grad_probs - inner_sum) * factor).astype(jnp.bfloat16)
        query_parts.append(
            jnp.einsum("hqk,khd->qhd", grad_scores, key_rows, preferred_element_type=jnp.float32)
        )
        grad_keys = grad_keys.at[:row_last].add(
            jnp.einsum("hqk,qhd->khd", grad_scores, query_rows, preferred_element_type=jnp.float32)
        )
        grad_values = grad_values.at[:row_last].add(
            jnp.einsum("hqk,qhd->khd", prob_low, grad_out, preferred_element_type=jnp.float32)
        )
    return (query_parts[0], grad_keys, grad_values)


def plain(
    tokens,
    out_grad,
    doc_lengths,
    w_qkv,
    w_out,
    gains,
    biases,
    head_scale,
    w_fc1,
    w_fc2,
    mid_gain,
    ffn_biases,
):
    qkv_full, out_full, gain_full, bias_full = (
        lax.all_gather(w_qkv, ("dp", "tensor"), axis=0, tiled=True),
        lax.all_gather(w_out, ("dp", "tensor"), axis=0, tiled=True),
        lax.all_gather(gains.astype(jnp.bfloat16), ("dp", "tensor"), axis=0, tiled=True).astype(
            gains.dtype
        ),
        lax.all_gather(biases.astype(jnp.bfloat16), ("dp", "tensor"), axis=0, tiled=True).astype(
            biases.dtype
        ),
    )
    fc1_rows, fc2_cols = (
        lax.all_gather(w_fc1, "dp", axis=0, tiled=True),
        lax.all_gather(w_fc2, "dp", axis=1, tiled=True),
    )
    model_width = tokens.shape[1]
    local_rows = tokens.shape[0]
    head_dim = model_width // HEADS
    factor = 1.0 / math.sqrt(head_dim)
    doc_ends = jnp.cumsum(doc_lengths[0])[:-1]
    places = jnp.arange(local_rows)
    doc_ids = jnp.sum((places[:, None] >= doc_ends[None, :]).astype(jnp.int32), axis=1)
    inputs = tokens.astype(jnp.float32)
    normed_one, inverse_one = normalize(inputs)
    normed_in = (normed_one * gain_full[:, 0] + bias_full[:, 0]).astype(jnp.bfloat16)
    zero_bias = jnp.zeros((model_width,), jnp.float32)
    qkv_bias = jnp.concatenate([bias_full[:, 1], zero_bias, bias_full[:, 2]])
    projected = (
        jnp.dot(normed_in, qkv_full, preferred_element_type=jnp.float32) + qkv_bias
    ).astype(jnp.bfloat16)
    query_rows = projected[:, :model_width].reshape(local_rows, HEADS, head_dim)
    key_rows = projected[:, model_width : 2 * model_width].reshape(local_rows, HEADS, head_dim)
    value_rows = projected[:, 2 * model_width :].reshape(local_rows, HEADS, head_dim)
    attended, sums_log = attend_forward(query_rows, key_rows, value_rows, doc_ids, factor)
    attended = attended.reshape(local_rows, model_width)
    scale_wide = jnp.repeat(head_scale, head_dim)
    scaled = (attended * scale_wide).astype(jnp.bfloat16)
    branch = jnp.dot(scaled, out_full, preferred_element_type=jnp.float32) + bias_full[:, 3]
    normed_post, inverse_post = normalize(branch)
    middle = inputs + normed_post * gain_full[:, 1] + bias_full[:, 4]
    normed_two, inverse_two = normalize(middle)
    normed_mid = (normed_two * gain_full[:, 2] + bias_full[:, 5]).astype(jnp.bfloat16)
    gathered = lax.all_gather(normed_mid, "tensor", axis=0, tiled=True)
    hidden_pre = jnp.dot(gathered, fc1_rows, preferred_element_type=jnp.float32) + ffn_biases[0]
    activated, gelu_pull = jax.vjp(jax.nn.gelu, hidden_pre)
    act_sum, act_square = (
        lax.psum(jnp.sum(activated, axis=1).astype(jnp.bfloat16), "tensor").astype(jnp.float32),
        lax.psum(jnp.sum(activated * activated, axis=1).astype(jnp.bfloat16), "tensor").astype(
            jnp.float32
        ),
    )
    center = act_sum / FF
    inverse_mid = lax.rsqrt(act_square / FF - center * center + EPS)[:, None]
    normed_act = (activated - center[:, None]) * inverse_mid
    hidden = (normed_act * mid_gain + ffn_biases[1]).astype(jnp.bfloat16)
    hidden_rows = hidden
    ffn_out = lax.psum_scatter(
        jnp.dot(hidden_rows, fc2_cols, preferred_element_type=jnp.float32).astype(jnp.bfloat16),
        "tensor",
        scatter_dimension=0,
        tiled=True,
    ).astype(jnp.float32)
    shard_rows = lax.all_gather(out_grad, "tensor", axis=0, tiled=True)
    grad_piece = jnp.einsum("rd,fd->rf", shard_rows, fc2_cols, preferred_element_type=jnp.float32)
    hidden_rows = hidden
    fc2_run = jnp.einsum("rf,rd->fd", hidden_rows, shard_rows, preferred_element_type=jnp.float32)
    mid_gain_part = jnp.sum(grad_piece * normed_act, axis=0)
    mid_bias_part = jnp.sum(grad_piece, axis=0)
    grad_normed_act = grad_piece * mid_gain
    first_sum, second_sum = (
        lax.psum(jnp.sum(grad_normed_act, axis=1).astype(jnp.bfloat16), "tensor").astype(
            jnp.float32
        ),
        lax.psum(
            jnp.sum(grad_normed_act * normed_act, axis=1).astype(jnp.bfloat16), "tensor"
        ).astype(jnp.float32),
    )
    grad_act = inverse_mid * (
        grad_normed_act - first_sum[:, None] / FF - normed_act * (second_sum[:, None] / FF)
    )
    grad_pre = gelu_pull(grad_act)[0].astype(jnp.bfloat16)
    fc1_part = jnp.einsum("rd,rf->df", gathered, grad_pre, preferred_element_type=jnp.float32)
    fc1_bias_part = jnp.sum(grad_pre.astype(jnp.float32), axis=0)
    grad_normed_mid = lax.psum_scatter(
        jnp.einsum("rf,df->rd", grad_pre, fc1_rows, preferred_element_type=jnp.float32).astype(
            jnp.bfloat16
        ),
        "tensor",
        scatter_dimension=0,
        tiled=True,
    ).astype(jnp.float32)
    ffn_bias_part = jnp.stack([fc1_bias_part, mid_bias_part])
    fc1_grad, fc2_grad = (
        lax.psum_scatter(
            fc1_part.astype(jnp.bfloat16), "dp", scatter_dimension=0, tiled=True
        ).astype(jnp.float32),
        lax.psum_scatter(
            fc2_run.astype(jnp.bfloat16), "dp", scatter_dimension=1, tiled=True
        ).astype(jnp.float32),
    )
    mid_gain_grad, ffn_bias_grad = lax.psum((mid_gain_part, ffn_bias_part), "dp")
    mixed_out = (middle + ffn_out + bias_full[:, 6]).astype(jnp.bfloat16)
    final_grad = out_grad.astype(jnp.float32)
    grad_middle = final_grad + normalize_back(
        grad_normed_mid * gain_full[:, 2], normed_two, inverse_two
    )
    grad_post = normalize_back(grad_middle * gain_full[:, 1], normed_post, inverse_post).astype(
        jnp.bfloat16
    )
    out_local = jnp.einsum("td,te->de", scaled, grad_post, preferred_element_type=jnp.float32)
    grad_scaled = jnp.einsum("te,de->td", grad_post, out_full, preferred_element_type=jnp.float32)
    scale_local = jnp.sum(
        (grad_scaled * attended).reshape(local_rows, HEADS, head_dim), axis=(0, 2)
    )
    grad_attended = (
        (grad_scaled * scale_wide).astype(jnp.bfloat16).reshape(local_rows, HEADS, head_dim)
    )
    grad_query, grad_keys, grad_values = attend_backward(
        query_rows, key_rows, value_rows, grad_attended, doc_ids, sums_log, factor
    )
    grad_projected = jnp.concatenate(
        [
            grad_query.reshape(local_rows, model_width),
            grad_keys.reshape(local_rows, model_width),
            grad_values.reshape(local_rows, model_width),
        ],
        axis=1,
    ).astype(jnp.bfloat16)
    qkv_local = jnp.einsum(
        "td,te->de", normed_in, grad_projected, preferred_element_type=jnp.float32
    )
    grad_normed_in = jnp.einsum(
        "te,de->td", grad_projected, qkv_full, preferred_element_type=jnp.float32
    )
    token_grad = grad_middle + normalize_back(
        grad_normed_in * gain_full[:, 0], normed_one, inverse_one
    )
    projected_sums = jnp.sum(grad_projected.astype(jnp.float32), axis=0)
    gains_local = jnp.stack(
        [
            jnp.sum(grad_normed_in * normed_one, axis=0),
            jnp.sum(grad_middle * normed_post, axis=0),
            jnp.sum(grad_normed_mid * normed_two, axis=0),
        ],
        axis=1,
    )
    biases_local = jnp.stack(
        [
            jnp.sum(grad_normed_in, axis=0),
            projected_sums[:model_width],
            projected_sums[2 * model_width :],
            jnp.sum(grad_post.astype(jnp.float32), axis=0),
            jnp.sum(grad_middle, axis=0),
            jnp.sum(grad_normed_mid, axis=0),
            jnp.sum(final_grad, axis=0),
        ],
        axis=1,
    )
    qkv_grad, out_weight_grad, gains_grad, biases_grad = (
        lax.psum_scatter(qkv_local, ("dp", "tensor"), scatter_dimension=0, tiled=True),
        lax.psum_scatter(out_local, ("dp", "tensor"), scatter_dimension=0, tiled=True),
        lax.psum_scatter(gains_local, ("dp", "tensor"), scatter_dimension=0, tiled=True),
        lax.psum_scatter(biases_local, ("dp", "tensor"), scatter_dimension=0, tiled=True),
    )
    scale_grad = lax.psum(scale_local, ("dp", "tensor"))
    return (
        mixed_out,
        token_grad,
        qkv_grad,
        out_weight_grad,
        gains_grad,
        biases_grad,
        scale_grad,
        fc1_grad,
        fc2_grad,
        mid_gain_grad,
        ffn_bias_grad,
    )


MESH = pl.DeviceIdType.MESH
ANY = pl.BlockSpec(memory_space=pl.ANY)
IN_VMEM = pl.BlockSpec(memory_space=pltpu.VMEM)


def place():
    z = lax.axis_index("dp")
    t = lax.axis_index("tensor")
    return z, lax.div(t, 4), lax.rem(lax.div(t, 2), 2), lax.rem(t, 2)


def at(z, y, x, c):
    return (z, y * 4 + x * 2 + c)


def greet(partners):
    barrier = pltpu.get_barrier_semaphore()
    for partner in partners:
        pl.semaphore_signal(barrier, inc=1, device_id=partner, device_id_type=MESH)
    pl.semaphore_wait(barrier, len(partners))


class Sends:
    def __init__(self, send_sems, recv_sems):
        self.send_sems, self.recv_sems, self.copies = send_sems, recv_sems, []

    def start(self, src, dst, target):
        index = len(self.copies)
        copy = pltpu.make_async_remote_copy(
            src_ref=src,
            dst_ref=dst,
            send_sem=self.send_sems.at[index],
            recv_sem=self.recv_sems.at[index],
            device_id=target,
            device_id_type=MESH,
        )
        copy.start()
        self.copies.append(copy)
        return copy

    def finish(self):
        for copy in self.copies:
            copy.wait_send()


def add_low(left, right):
    return (left.astype(jnp.float32) + right.astype(jnp.float32)).astype(jnp.bfloat16)


SQRT_2_PI = math.sqrt(2.0 / math.pi)
NT = (((1,), (1,)), ((), ()))
TN = (((0,), (0,)), ((), ()))


def dot(left, right, dims=None):
    if dims is None:
        return jnp.dot(left, right, preferred_element_type=jnp.float32)
    return lax.dot_general(left, right, dims, preferred_element_type=jnp.float32)


def centered(values):
    center = jnp.mean(values, axis=-1, keepdims=True)
    spread = jnp.mean(values * values, axis=-1, keepdims=True) - center * center
    inverse = lax.rsqrt(spread + EPS)
    return (values - center) * inverse, inverse


def centered_back(grad, normed, inverse):
    first = jnp.mean(grad, axis=-1, keepdims=True)
    second = jnp.mean(grad * normed, axis=-1, keepdims=True)
    return inverse * (grad - first - normed * second)


def eights(values):
    return jnp.sum(values.reshape(values.shape[0] // 8, 8, values.shape[1]), axis=0)


def doc_mask(doc_ref, rows):
    query = lax.broadcasted_iota(jnp.int32, (rows, rows), 0)
    key = lax.broadcasted_iota(jnp.int32, (rows, rows), 1)
    query_doc, key_doc = jnp.zeros_like(query), jnp.zeros_like(key)
    end = 0
    for j in range(doc_ref.shape[1] - 1):
        end = end + doc_ref[0, j]
        query_doc = query_doc + (query >= end).astype(jnp.int32)
        key_doc = key_doc + (key >= end).astype(jnp.int32)
    allowed = jnp.logical_and(query_doc == key_doc, key <= query)
    return allowed.astype(jnp.float32)


class Plane:
    def __init__(self, sends, whole, here, targets):
        self.sends, self.whole, self.here, self.targets = sends, whole, here, targets
        half = whole.shape[3] // 2
        self.lo, self.hi = pl.ds(0, half), pl.ds(half, half)

    def part(self, y, x, c, rows):
        return self.whole.at[y, x, c, rows]

    def start_first(self, src):
        (y, x, c), (to_x, to_y, to_c), lo, hi = self.here, self.targets, self.lo, self.hi
        go = self.sends.start
        self.first = [
            go(src.at[lo], self.part(y, x, c, lo), to_x),
            go(src.at[hi], self.part(y, x, c, hi), to_y),
        ]
        self.core = [go(src, self.whole.at[y, x, c], to_c)]

    def start_second(self, src):
        (y, x, c), (to_x, to_y, _), lo, hi = self.here, self.targets, self.lo, self.hi
        go = self.sends.start
        self.second = [
            go(src.at[lo], self.part(y, x, c, lo), to_y),
            go(src.at[hi], self.part(y, x, c, hi), to_x),
        ]

    def after_first(self):
        (y, x, c), (to_x, to_y, to_c), lo, hi = self.here, self.targets, self.lo, self.hi
        for copy in self.first:
            copy.wait_recv()
        by_x, by_y = self.part(y, 1 - x, c, lo), self.part(1 - y, x, c, hi)
        go = self.sends.start
        self.third = [go(by_x, by_x, to_y), go(by_y, by_y, to_x)]
        self.side = [go(by_x, by_x, to_c), go(by_y, by_y, to_c)]

    def after_second(self):
        (y, x, c), (to_x, to_y, to_c), lo, hi = self.here, self.targets, self.lo, self.hi
        for copy in self.second:
            copy.wait_recv()
        by_x, by_y = self.part(y, 1 - x, c, hi), self.part(1 - y, x, c, lo)
        go = self.sends.start
        self.side += [go(by_x, by_x, to_c), go(by_y, by_y, to_c)]

    def after_third(self):
        y, x, c = self.here
        self.last = []
        for copy, part in zip(self.third, (self.lo, self.hi)):
            copy.wait_recv()
            ref = self.part(1 - y, 1 - x, c, part)
            self.last.append(self.sends.start(ref, ref, self.targets[2]))


def fore_kernel(
    nz,
    tok_ref,
    og_ref,
    qkv_ref,
    out_ref,
    gains_ref,
    biases_ref,
    fc1_ref,
    fc2_ref,
    gain_ref,
    shift_ref,
    doc_ref,
    scale_ref,
    qkv_out,
    out_out,
    vec_out,
    proj_out,
    att_out,
    lse_out,
    branch_out,
    middle_out,
    nin_out,
    scaled_out,
    ffn_out,
    first_out,
    fc2_out,
    late_out,
    gnm_out,
    fc1_out,
    unit_out,
    qkv_all,
    out_all,
    vec_all,
    vec_mine,
    vec_turn,
    unit_ref,
    fc1_all,
    fc2_all,
    og_all,
    tok,
    branch,
    nin,
    proj,
    att,
    lse,
    scaled,
    middle,
    mask,
    vec,
    mid_all,
    act,
    slope,
    grad,
    hidden,
    grad_pre,
    mid_part,
    pre,
    stats,
    pair,
    got,
    totals,
    from_core,
    sums,
    from_one,
    from_two,
    f_part,
    f_core,
    f_sums,
    fc1_part,
    late_part,
    fc2_part,
    fc1_got,
    local_sems,
    send_sems,
    recv_sems,
):
    z, y, x, c = place()
    to_x, to_y, to_c = at(z, y, 1 - x, c), at(z, 1 - y, x, c), at(z, y, x, 1 - c)
    to_xy = at(z, 1 - y, 1 - x, c)
    others = [lax.rem(z + k, nz) for k in range(1, nz)]
    slots = [z] + [lax.rem(z + nz - k, nz) for k in range(1, nz)]
    peers = [at(other, y, x, c) for other in others]
    locals_ = []

    def fetch(src, dst):
        copy = pltpu.make_async_copy(src, dst, local_sems.at[len(locals_)])
        copy.start()
        locals_.append(copy)
        return copy

    rows, width = tok.shape
    fourth = width // 4
    qkv_in = [
        fetch(
            qkv_ref.at[:, pl.ds(i * width + g * fourth, fourth)],
            qkv_all.at[z, y, x, c, :, pl.ds((3 * g + i) * fourth, fourth)],
        )
        for g in range(4)
        for i in range(3)
    ]
    vec_turn[...] = jnp.zeros_like(vec_turn)
    share = vec_mine.shape[0]
    vec_turn[0:3, 0:share] = gains_ref[...]
    vec_turn[3:10, 0:share] = biases_ref[...]
    vec_mine[...] = vec_turn[...].T[:share]
    greet([to_x, to_y, to_c, to_xy] + peers)
    sends = Sends(send_sems, recv_sems)
    low, f32 = jnp.bfloat16, jnp.float32
    units = fc1_all.shape[1]
    width1, width2 = fc1_ref.shape[0], fc2_ref.shape[1]
    own1 = fc1_all.at[pl.ds(pl.multiple_of(z * width1, width1), width1)]
    own2 = fc2_all.at[:, pl.ds(pl.multiple_of(z * width2, width2), width2)]
    def wait_all(copies):
        for copy in copies:
            copy.wait_recv()

    vec_z = [sends.start(vec_mine, vec_all.at[z, y, x, c], peer) for peer in peers]
    phase = 6 * fourth
    spans = (pl.ds(0, phase), pl.ds(phase, phase))
    for copy in qkv_in:
        copy.wait()
    own_qkv = qkv_all.at[z, y, x, c]
    qkv_z = [
        [sends.start(own_qkv.at[:, span], own_qkv.at[:, span], peer) for peer in peers]
        for span in spans
    ]

    z_pair = z + 1 - 2 * lax.rem(z, 2)
    pair_peer, far_peer = at(z_pair, y, x, c), peers[1]
    qkv_slots = slots

    def go_on(p):
        qkv_z[p][0].wait_recv()

    def sides(whole, p):
        size = phase // 2 if whole is qkv_all else whole.shape[-1] // 2
        return pl.ds(2 * p * size, size), pl.ds((2 * p + 1) * size, size)

    def first(whole, slot, p=0):
        lo, hi = sides(whole, p)
        by_x, by_y = whole.at[slot, y, x, c, :, lo], whole.at[slot, y, x, c, :, hi]
        return (sends.start(by_x, by_x, to_x), sends.start(by_y, by_y, to_y))

    def second(whole, slot, p=0):
        lo, hi = sides(whole, p)
        by_x, by_y = whole.at[slot, y, :, c, :, lo], whole.at[slot, :, x, c, :, hi]
        return (sends.start(by_x, by_x, to_y), sends.start(by_y, by_y, to_x))

    def third(whole, slot, p=None):
        ref = whole.at[slot, :, :, c] if p is None else whole.at[slot, :, :, c, :, spans[p]]
        return sends.start(ref, ref, to_c)

    a0, a1 = [first(qkv_all, z, 0)], [first(qkv_all, z, 1)]
    og = Plane(sends, og_all, (y, x, c), (to_x, to_y, to_c))
    og.start_first(og_ref)
    tok_in = fetch(tok_ref, tok)
    out_in = fetch(out_ref, out_all.at[z, y, x, c])
    fc1_in = fetch(fc1_ref, own1)
    fc2_in = fetch(fc2_ref, own2)
    og_in = fetch(og_ref, og_all.at[y, x, c])
    vec_all[z, y, x, c] = vec_mine[...]
    unit_ref[...] = jnp.zeros_like(unit_ref)
    unit_ref[0:1] = shift_ref[0:1]
    unit_ref[1:2] = gain_ref[...]
    unit_ref[2:3] = shift_ref[1:2]
    step = 32
    mask[...] = doc_mask(doc_ref, rows)
    tok_in.wait()

    def normed(k, carry):
        part = pl.ds(pl.multiple_of(k * step, step), step)
        branch[part] = centered(tok[part].astype(f32))[0]
        return carry

    lax.fori_loop(0, rows // step, normed, 0)
    wait_all(vec_z)
    by_x = vec_all.at[:, y, x, c]
    vec_x = sends.start(by_x, by_x, to_x)
    wait_all(a0[0])
    b0 = [second(qkv_all, z, 0)]
    wait_all(a1[0])
    b1 = [second(qkv_all, z, 1)]
    go_on(0)
    a0.append(first(qkv_all, qkv_slots[1], 0))
    vec_x.wait_recv()
    by_y = vec_all.at[:, y, :, c]
    vec_y = sends.start(by_y, by_y, to_y)
    for k in range(2, nz):
        qkv_z[0][k - 1].wait_recv()
        a0.append(first(qkv_all, qkv_slots[k], 0))
    vec_y.wait_recv()
    by_c = vec_all.at[:, :, :, c]
    vec_c = sends.start(by_c, by_c, to_c)
    for k in range(1, nz):
        wait_all(a0[k])
        b0.append(second(qkv_all, qkv_slots[k], 0))
    go_on(1)
    a1.append(first(qkv_all, qkv_slots[1], 1))
    vec_c.wait_recv()
    vec[...] = vec_all[...].reshape(width, 128).T[:16]
    spot = lax.broadcasted_iota(jnp.int32, (1, width), 1)
    head = 64
    wide = jnp.zeros((1, width), f32)
    for h in range(HEADS):
        inside = jnp.logical_and(spot >= h * head, spot < (h + 1) * head)
        wide = jnp.where(inside, scale_ref[h], wide)
    vec[10:11] = wide

    def scaled_in(k, carry):
        part = pl.ds(pl.multiple_of(k * step, step), step)
        nin[part] = (branch[part] * vec[0:1] + vec[3:4]).astype(low)
        return carry

    lax.fori_loop(0, rows // step, scaled_in, 0)
    wait_all(b0[0])
    c0 = [third(qkv_all, z, 0)]
    for k in range(2, nz):
        qkv_z[1][k - 1].wait_recv()
        a1.append(first(qkv_all, qkv_slots[k], 1))
        wait_all(b0[k - 1])
        c0.append(third(qkv_all, qkv_slots[k - 1], 0))
    out_in.wait()
    own_out = out_all.at[z, y, x, c]
    out_z = [sends.start(own_out, own_out, peer) for peer in peers]
    fc2_far = sends.start(fc2_ref, own2, far_peer)
    fc2_near = sends.start(fc2_ref, own2, pair_peer)
    fc1_z = [sends.start(fc1_ref, own1, peer) for peer in peers]
    wait_all(b0[nz - 1])
    c0.append(third(qkv_all, qkv_slots[nz - 1], 0))
    wait_all(a1[1])
    b1.append(second(qkv_all, qkv_slots[1], 1))
    wait_all(c0)

    def project(p):
        for g in (2 * p, 2 * p + 1):
            cols = pl.ds(3 * g * fourth, 3 * fourth)
            here = pl.ds(g * fourth, fourth)
            bias = jnp.concatenate(
                [vec[4:5, here], jnp.zeros((1, fourth), f32), vec[5:6, here]], axis=1
            )
            block = dot(nin[...], qkv_all[:, :, :, :, :, cols].reshape(width, 3 * fourth))
            proj[:, cols] = (block + bias).astype(low)

    project(0)
    lane = lax.broadcasted_iota(jnp.int32, (1, 128), 1)
    is_low = lane < head
    keep = (is_low.astype(low), (lane >= head).astype(low))
    factor = 1.0 / math.sqrt(head)
    lane_wide = lax.broadcasted_iota(jnp.int32, (rows, 128), 1)
    lse[...] = jnp.zeros_like(lse)

    def attend(p, carry):
        base = lax.div(p, 2) * (3 * fourth) + lax.rem(p, 2) * 128
        q_at = pl.ds(pl.multiple_of(base, 128), 128)
        k_at = pl.ds(pl.multiple_of(base + fourth, 128), 128)
        v_at = pl.ds(pl.multiple_of(base + 2 * fourth, 128), 128)
        here = pl.ds(pl.multiple_of(p * 128, 128), 128)
        q2, k2, v2 = proj[:, q_at], proj[:, k_at], proj[:, v_at]
        found, logs = [], []
        for i in range(2):
            scores = dot(q2 * keep[i], k2, NT) * factor
            scores = jnp.where(mask[...] > 0, scores, NEGATIVE)
            peak = jnp.max(scores, axis=1, keepdims=True)
            exponent = jnp.exp(scores - peak)
            total = jnp.sum(exponent, axis=1, keepdims=True)
            prob = (exponent * (1.0 / total)).astype(low)
            found.append(dot(prob, v2))
            logs.append(peak + jnp.log(total))
        spread_logs = jnp.where(lane_wide == 2 * p, logs[0], logs[1])
        at_pair = lax.div(lane_wide, 2) == p
        lse[...] = jnp.where(at_pair, spread_logs, lse[...])
        both = jnp.where(is_low, *found)
        att[:, here] = both
        scaled[:, here] = (both * vec[10:11, here]).astype(low)
        return carry

    lax.fori_loop(0, 1, attend, 0)
    for k in range(2, nz):
        wait_all(a1[k])
        b1.append(second(qkv_all, qkv_slots[k], 1))
    out_a = [first(out_all, z)]
    for k in range(1, nz):
        out_z[k - 1].wait_recv()
        out_a.append(first(out_all, slots[k]))
    og.start_second(og_ref)
    lax.fori_loop(1, 2, attend, 0)
    c1 = []
    for k in range(2):
        wait_all(b1[k])
        c1.append(third(qkv_all, qkv_slots[k], 1))
    lax.fori_loop(2, 4, attend, 0)
    for k in range(2, nz):
        wait_all(b1[k])
        c1.append(third(qkv_all, qkv_slots[k], 1))
    wait_all(c1)
    saves = [fetch(qkv_all, qkv_out), fetch(vec, vec_out), fetch(nin, nin_out)]
    project(1)
    saves.append(fetch(proj, proj_out))
    out_b = []
    for k in range(nz):
        wait_all(out_a[k])
        out_b.append(second(out_all, slots[k]))
    lax.fori_loop(4, 6, attend, 0, unroll=True)
    og.after_first()
    lax.fori_loop(6, 8, attend, 0, unroll=True)
    out_c = []
    for k in range(nz):
        wait_all(out_b[k])
        out_c.append(third(out_all, slots[k]))
    saves += [fetch(att, att_out), fetch(lse, lse_out), fetch(scaled, scaled_out)]
    wait_all(out_c)
    saves.append(fetch(out_all, out_out))
    quarter = width // 4
    for k in range(4):
        cols = pl.ds(k * quarter, quarter)
        block = dot(scaled[...], out_all[:, :, :, :, :, cols].reshape(width, quarter))
        branch[:, cols] = block + vec[6:7, cols]

    def middles(k, carry):
        part = pl.ds(pl.multiple_of(k * step, step), step)
        post = centered(branch[part])[0]
        value = tok[part].astype(f32) + post * vec[1:2] + vec[7:8]
        middle[part] = value
        mid_all[y, x, c, part] = (centered(value)[0] * vec[2:3] + vec[8:9]).astype(low)
        return carry

    lax.fori_loop(0, rows // step, middles, 0, unroll=2)
    mid = Plane(sends, mid_all, (y, x, c), (to_x, to_y, to_c))
    mid.start_first(mid_all.at[y, x, c])
    mid.start_second(mid_all.at[y, x, c])
    branch_put = fetch(branch, branch_out)
    saves.append(fetch(middle, middle_out))

    def grads(yy, xx, cc):
        grad[yy, xx, cc] = dot(og_all[yy, xx, cc], fc2_all[...], NT)

    def fold(v):
        quarters = [v[:, k * (units // 4) : (k + 1) * (units // 4)] for k in range(4)]
        return (quarters[0] + quarters[1]) + (quarters[2] + quarters[3])

    def forward(yy, xx, cc):
        pre[...] = dot(mid_all[yy, xx, cc], fc1_all[...])

        def block(k, carry):
            part = pl.ds(pl.multiple_of(k * step, step), step)
            u = pre[part] + unit_ref[0:1]
            square = u * u
            th = jnp.tanh(u * (SQRT_2_PI + (SQRT_2_PI * 0.044715) * square))
            lift = 0.5 + 0.5 * th
            a = u * lift
            act[yy, xx, cc, part] = a
            bend = u * (2.0 * SQRT_2_PI + (6.0 * 0.044715 * SQRT_2_PI) * square)
            slope[yy, xx, cc, part] = lift + bend * (lift - lift * lift)
            gm = grad[yy, xx, cc, part] * unit_ref[1:2]
            for j, value in enumerate((a, a * a, gm, gm * a)):
                pre[part, j * (units // 4) : (j + 1) * (units // 4)] = fold(value)
            return carry

        lax.fori_loop(0, rows // step, block, 0)
        for j in range(4):
            folded = pre[:, j * (units // 4) : (j + 1) * (units // 4)]
            stats[yy, xx, cc, j : j + 1] = jnp.sum(folded.T, axis=0, keepdims=True)

    og.after_second()
    fc2_in.wait()
    fc2_far.wait_recv()
    near = fc2_all.at[:, pl.ds(pl.multiple_of(others[1] * width2, width2), width2)]
    fc2_last = sends.start(near, near, pair_peer)
    fc2_near.wait_recv()
    og.after_third()
    fc1_in.wait()
    mid.after_first()
    fc2_last.wait_recv()
    og_in.wait()
    grads(y, x, c)
    wait_all(og.core)
    grads(y, x, 1 - c)
    grads(y, 1 - x, c)
    grads(1 - y, x, c)
    mid.after_second()
    wait_all(og.side)
    grads(y, 1 - x, 1 - c)
    grads(1 - y, x, 1 - c)
    grads(1 - y, 1 - x, c)
    wait_all(og.last)
    grads(1 - y, 1 - x, 1 - c)
    wait_all(fc1_z)
    forward(y, x, c)
    wait_all(mid.core)
    forward(y, x, 1 - c)
    forward(y, 1 - x, c)
    forward(1 - y, x, c)
    wait_all(mid.side)
    forward(y, 1 - x, 1 - c)
    forward(1 - y, x, 1 - c)
    mid.after_third()
    forward(1 - y, 1 - x, c)
    wait_all(mid.last)
    forward(1 - y, 1 - x, 1 - c)

    sends.start(stats, got.at[3], to_c).wait_recv()
    pair[...] = stats[...] + got[3]
    wait_all([sends.start(pair, got.at[k], to) for k, to in enumerate((to_x, to_y, to_xy))])
    total = (pair[...] + got[0]) + (got[1] + got[2])
    total = total * (1.0 / (units * 8))
    center, square = total[:, :, :, 0:1], total[:, :, :, 1:2]
    mean, cross = total[:, :, :, 2:3], total[:, :, :, 3:4]
    inverse = lax.rsqrt(square - center * center + EPS)
    totals[:, :, :, 0:1] = inverse
    totals[:, :, :, 1:2] = -center * inverse
    totals[:, :, :, 2:3] = inverse * mean
    totals[:, :, :, 3:4] = inverse * (inverse * (cross - center * mean))
    unit_out[...] = jnp.zeros_like(unit_out)

    def backward(yy, xx, cc):
        for j in range(4):
            spread = jnp.broadcast_to(totals[yy, xx, cc, j : j + 1], (128, rows))
            pre[:, j * 128 : (j + 1) * 128] = spread.T

        def block(k, carry):
            part = pl.ds(pl.multiple_of(k * step, step), step)

            def across(j):
                return jnp.concatenate([pre[part, j * 128 : (j + 1) * 128]] * (units // 128), axis=1)

            g = grad[yy, xx, cc, part]
            inverse = across(0)
            normed = act[yy, xx, cc, part] * inverse + across(1)
            gain = unit_ref[1:2]
            hidden[yy, xx, cc, part] = (normed * gain + unit_ref[2:3]).astype(low)
            back = g * gain * inverse - across(2) - normed * across(3)
            value = (back * slope[yy, xx, cc, part]).astype(low)
            grad_pre[yy, xx, cc, part] = value
            return (
                carry[0] + eights(g * normed),
                carry[1] + eights(value.astype(f32)),
                carry[2] + eights(g),
            )

        zero = jnp.zeros((8, units), f32)
        parts = lax.fori_loop(0, rows // step, block, (zero, zero, zero))
        for j, part in enumerate(parts):
            unit_out[j : j + 1] += jnp.sum(part, axis=0, keepdims=True)
        return dot(grad_pre[yy, xx, cc], fc1_all[...], NT)

    left, right = pl.ds(0, width // 2), pl.ds(width // 2, width // 2)
    order = [(1 - y, 1 - x), (y, 1 - x), (1 - y, x), (y, x)]
    stage_x, stage_y, cores = [], [], []

    def to_core(k):
        yy, xx = order[k]
        mid_part[yy, xx] = backward(yy, xx, 1 - c).astype(low)
        cores.append(sends.start(mid_part.at[yy, xx], from_core.at[yy, xx], to_c))

    def from_pair(k):
        yy, xx = order[k]
        block = backward(yy, xx, c)
        cores[k].wait_recv()
        sums[yy, xx] = (block + from_core[yy, xx].astype(f32)).astype(low)
        if k in (0, 1):
            stage_x.append(sends.start(sums.at[yy, xx, :, left], from_one.at[yy, :, left], to_x))
        if k in (0, 2):
            stage_y.append(sends.start(sums.at[yy, xx, :, right], from_one.at[xx, :, right], to_y))

    to_core(0)
    to_core(1)
    from_pair(0)
    to_core(2)
    from_pair(1)
    to_core(3)
    from_pair(2)
    from_pair(3)

    def ffn_of(yy, xx, cc):
        return dot(hidden[yy, xx, cc], fc2_all[...])

    blocks = nz
    size = width // blocks

    early = fc1_part.shape[-1]
    soon, late = slice(0, early), slice(early, units)

    def fc1_block(which, cols):
        part = pl.ds(pl.multiple_of(which * size, 128), size)
        block = jnp.zeros((size, cols.stop - cols.start), f32)
        for j in range(8):
            yxc = (j // 4, (j // 2) % 2, j % 2)
            block = block + dot(mid_all[(*yxc, slice(None), part)], grad_pre[(*yxc, slice(None), cols)], TN)
        return block

    fc1_far = {}
    for k in (1, 0, 2):
        fc1_part[k] = fc1_block(others[k], soon).astype(low)
        fc1_far[k] = sends.start(fc1_part.at[k], fc1_got.at[k], peers[k])
    wait_all((stage_x[0], stage_y[0]))
    sums[1 - y, x, :, left] = add_low(sums[1 - y, x, :, left], from_one[1 - y, :, left])
    sums[y, 1 - x, :, right] = add_low(sums[y, 1 - x, :, right], from_one[1 - x, :, right])
    last_y = sends.start(sums.at[1 - y, x, :, left], from_two.at[:, left], to_y)
    last_x = sends.start(sums.at[y, 1 - x, :, right], from_two.at[:, right], to_x)
    fc1_out[:, soon] = fc1_block(z, soon)
    fc1_out[:, late] = fc1_block(z, late)

    def late_block(k, carry):
        part = pl.ds(pl.multiple_of(k * size, 128), size)
        late_part[part] = fc1_block(k, late).astype(low)
        return carry

    lax.fori_loop(0, blocks, late_block, 0)
    saves.append(fetch(late_part, late_out))
    cores = []
    for yy, xx in order:
        f_part[yy, xx] = ffn_of(yy, xx, 1 - c).astype(low)
        cores.append(sends.start(f_part.at[yy, xx], f_core.at[yy, xx], to_c))
    for k, (yy, xx) in enumerate(order):
        block = ffn_of(yy, xx, c)
        cores[k].wait_recv()
        f_sums[yy, xx] = (block + f_core[yy, xx].astype(f32)).astype(low)
    saves.append(fetch(f_sums, ffn_out))
    top = pl.ds(0, first_out.shape[1])
    out_x = sends.start(f_sums.at[:, 1 - x, top, left], first_out.at[:, :, left], to_x)
    out_y = sends.start(f_sums.at[1 - y, :, top, right], first_out.at[:, :, right], to_y)

    def fc2_block(k, carry):
        part = pl.ds(pl.multiple_of(k * size, 128), size)
        block = jnp.zeros((units, size), f32)
        for j in range(8):
            yxc = (j // 4, (j // 2) % 2, j % 2)
            block = block + dot(hidden[yxc], og_all[(*yxc, slice(None), part)], TN)
        fc2_part[:, part] = block.astype(low)
        return carry

    lax.fori_loop(0, blocks, fc2_block, 0)
    saves.append(fetch(fc2_part, fc2_out))
    branch_put.wait()
    wait_all((stage_x[1], stage_y[1], last_x, last_y))
    for cols, k in ((left, y), (right, x)):
        branch[:, cols] = (
            sums[y, x, :, cols].astype(f32)
            + from_one[k, :, cols].astype(f32)
            + from_two[:, cols].astype(f32)
        )
        saves.append(fetch(branch.at[:, cols], gnm_out.at[:, cols]))
    for k in range(nz - 1):
        fc1_far[k].wait_recv()
        fc1_out[:, soon] += fc1_got[k].astype(f32)
    wait_all((out_x, out_y))
    for copy in saves:
        copy.wait()
    sends.finish()


def fore(nz, tokens, og, doc_lengths, w_qkv, w_out, gains, biases, scale, fc1, fc2, gain, shift):
    rows, width = tokens.shape
    share, units = w_qkv.shape[0], fc1.shape[1]
    low, f32, plane, every = jnp.bfloat16, jnp.float32, (2, 2, 2), (nz, 2, 2, 2)
    sds, vm = jax.ShapeDtypeStruct, pltpu.VMEM
    count = 160
    smem = pl.BlockSpec(memory_space=pltpu.SMEM)
    shapes = (
        (every + w_qkv.shape, low),
        (every + w_out.shape, low),
        ((16, width), f32),
        ((rows, w_qkv.shape[1]), low),
        ((rows, width), f32),
        ((rows, 128), f32),
        ((rows, width), f32),
        ((rows, width), f32),
        ((rows, width), low),
        ((rows, width), low),
        ((2, 2, rows, width), low),
        ((2, rows // 4, width), low),
        ((units, width), low),
        ((width, units - 3 * units // 4), low),
        ((rows, width), f32),
        (fc1.shape, f32),
        ((8, units), f32),
    )
    return pl.pallas_call(
        functools.partial(fore_kernel, nz),
        name="fore",
        out_shape=tuple(sds(shape, kind) for shape, kind in shapes),
        in_specs=[ANY] * 4 + [IN_VMEM] * 2 + [ANY] * 2 + [IN_VMEM] * 2 + [smem] * 2,
        out_specs=[ANY] * 15 + [IN_VMEM] * 2,
        scratch_shapes=[
            vm(every + w_qkv.shape, low),
            vm(every + w_out.shape, low),
            vm(every + (share, 128), f32),
            vm((share, 128), f32),
            vm((128, 128), f32),
            vm((8, units), f32),
            vm((width, units), low),
            vm((units, width), low),
            vm(plane + (rows, width), low),
            vm((rows, width), low),
            vm((rows, width), f32),
            vm((rows, width), low),
            vm((rows, w_qkv.shape[1]), low),
            vm((rows, width), f32),
            vm((rows, 128), f32),
            vm((rows, width), low),
            vm((rows, width), f32),
            vm((rows, rows), f32),
            vm((16, width), f32),
            vm(plane + (rows, width), low),
            vm(plane + (rows, units), f32),
            vm(plane + (rows, units), f32),
            vm(plane + (rows, units), f32),
            vm(plane + (rows, units), low),
            vm(plane + (rows, units), low),
            vm((2, 2, rows, width), low),
            vm((rows, units), f32),
            vm(plane + (4, rows), f32),
            vm(plane + (4, rows), f32),
            vm((4,) + plane + (4, rows), f32),
            vm(plane + (4, rows), f32),
            vm((2, 2, rows, width), low),
            vm((2, 2, rows, width), low),
            vm((2, rows, width), low),
            vm((rows, width), low),
            vm((2, 2, rows, width), low),
            vm((2, 2, rows, width), low),
            vm((2, 2, rows, width), low),
            vm((nz - 1, fc1.shape[0], 3 * units // 4), low),
            vm((width, units - 3 * units // 4), low),
            vm((units, width), low),
            vm((nz - 1, fc1.shape[0], 3 * units // 4), low),
            pltpu.SemaphoreType.DMA((40,)),
            pltpu.SemaphoreType.DMA((count,)),
            pltpu.SemaphoreType.DMA((count,)),
        ],
        compiler_params=pltpu.CompilerParams(
            collective_id=1, has_side_effects=True, vmem_limit_bytes=63 * 2**20
        ),
    )(tokens, og, w_qkv, w_out, gains.T, biases.T, fc1, fc2, gain, shift, doc_lengths, scale)


def back_kernel(
    nz,
    gnm_in,
    ffn_ref,
    first_in,
    late_ref,
    own1_in,
    fc2_ref,
    unit_ref,
    proj_in,
    att_in,
    lse_in,
    branch_in,
    middle_in,
    scaled_in,
    nin_in,
    qkv_in,
    out_in,
    vec_ref,
    og_in,
    tok_in,
    doc_ref,
    mixed_out,
    token_out,
    weight_out,
    gains_out,
    biases_out,
    scale_out,
    fc1_out,
    fc2_out,
    unit_out,
    f_sums,
    f_one,
    f_two,
    got1,
    got2,
    got_unit,
    w_part,
    w_core,
    w_sums,
    w_one,
    w_two,
    w_far,
    gpost,
    gmid,
    gatt,
    gni,
    dproj,
    nin_t,
    mask,
    accs,
    small,
    small_far,
    small_y,
    small_half,
    small_got,
    turned,
    mixed_at,
    weight_at,
    fc1_at,
    fc2_at,
    gnm_ref,
    proj_ref,
    att_ref,
    lse_ref,
    branch_ref,
    middle_ref,
    scaled_ref,
    nin_ref,
    qkv_ref,
    out_ref,
    og_ref,
    tok_ref,
    local_sems,
    send_sems,
    recv_sems,
):
    z, y, x, c = place()
    to_x, to_y, to_c = at(z, y, 1 - x, c), at(z, 1 - y, x, c), at(z, y, x, 1 - c)
    to_xy = at(z, 1 - y, 1 - x, c)
    others = [lax.rem(z + k, nz) for k in range(1, nz)]
    peers = [at(other, y, x, c) for other in others]
    locals_ = []

    def fetch(src, dst):
        copy = pltpu.make_async_copy(src, dst, local_sems.at[len(locals_)])
        copy.start()
        locals_.append(copy)
        return copy

    middle_got = fetch(middle_in, middle_ref)
    gnm_got = fetch(gnm_in, gnm_ref)
    og_got = fetch(og_in, og_ref)
    branch_got = fetch(branch_in, branch_ref)
    top, half = pl.ds(0, first_in.shape[1]), first_in.shape[2] // 2
    first_got = [
        fetch(first_in.at[:, :, pl.ds(i * half, half)], f_one.at[i, :, top, pl.ds(i * half, half)])
        for i in range(2)
    ]
    ffn_got = fetch(ffn_ref, f_sums)
    out_got = fetch(out_in, out_ref)
    att_got = fetch(att_in, att_ref)
    scaled_got = fetch(scaled_in, scaled_ref)
    nin_got = fetch(nin_in, nin_ref)
    proj_got = fetch(proj_in, proj_ref)
    lse_got = fetch(lse_in, lse_ref)
    qkv_got = fetch(qkv_in, qkv_ref)
    tok_got = fetch(tok_in, tok_ref)

    greet([to_x, to_y, to_c, to_xy] + peers)
    sends = Sends(send_sems, recv_sems)
    rows, width = middle_ref.shape
    low = jnp.bfloat16
    f32 = jnp.float32
    share = weight_out.shape[0]
    width1, width2 = fc1_out.shape[0], fc2_out.shape[1]

    pieces = 4
    parts = [pl.ds(k * (rows // pieces), rows // pieces) for k in range(pieces)]
    left, right = pl.ds(0, width // 2), pl.ds(width // 2, width // 2)
    def block1(which):
        return late_ref.at[pl.ds(pl.multiple_of(which * width1, width1), width1)]

    def block2(which):
        return fc2_ref.at[:, pl.ds(pl.multiple_of(which * width2, width2), width2)]

    own1_got = fetch(own1_in, fc1_at)
    own2_got = fetch(block2(z), got2.at[nz - 1])
    far = []
    for k, peer in enumerate(peers):
        far.append(sends.start(unit_ref, got_unit.at[k], peer))
        far.append(sends.start(block1(others[k]), got1.at[k], peer))
        far.append(sends.start(block2(others[k]), got2.at[k], peer))

    f_first, f_second = [], []

    def ffn_one(k):
        part = parts[k]
        f_first.append(
            (
                sends.start(ffn_ref.at[:, 1 - x, part, left], f_one.at[0, :, part, left], to_x),
                sends.start(ffn_ref.at[1 - y, :, part, right], f_one.at[1, :, part, right], to_y),
            )
        )

    def ffn_two(k):
        part = parts[k]
        if k == 0:
            ffn_got.wait()
            for copy in first_got:
                copy.wait()
        else:
            for copy in f_first[k - 1]:
                copy.wait_recv()
        f_sums[1 - y, x, part, left] = add_low(
            f_sums[1 - y, x, part, left], f_one[0, 1 - y, part, left]
        )
        f_sums[y, 1 - x, part, right] = add_low(
            f_sums[y, 1 - x, part, right], f_one[1, 1 - x, part, right]
        )
        f_second.append(
            (
                sends.start(f_sums.at[1 - y, x, part, left], f_two.at[part, left], to_y),
                sends.start(f_sums.at[y, 1 - x, part, right], f_two.at[part, right], to_x),
            )
        )

    def ffn_three(k):
        part = parts[k]
        for copy in f_second[k]:
            copy.wait_recv()
        for i, (cols, at_) in enumerate(((left, y), (right, x))):
            total = (
                f_sums[y, x, part, cols].astype(f32)
                + f_one[i, at_, part, cols].astype(f32)
                + f_two[part, cols].astype(f32)
            )
            mixed_at[part, cols] = (
                middle_ref[part, cols] + total + vec_ref[9:10, cols]
            ).astype(low)
        puts.append(fetch(mixed_at.at[part], mixed_out.at[part]))

    spans = [(0, width)] + [(width + g * 3 * width // 4, 3 * width // 4) for g in range(4)]
    w_first, w_second, w_third, w_c = {}, {}, {}, {}

    def sides(j):
        start, size = spans[j]
        return pl.ds(start, size), pl.ds(start, size // 2), pl.ds(start + size // 2, size // 2)

    def w_zero(j):
        every = sides(j)[0]
        w_c[j] = sends.start(w_part.at[:, :, :, 1 - c, :, every], w_core.at[..., every], to_c)

    def w_step1(j):
        every, lo, hi = sides(j)
        w_c[j].wait_recv()

        def one(which, carry):
            for yy in range(2):
                for xx in range(2):
                    w_sums[which, yy, xx, :, every] = add_low(
                        w_part[which, yy, xx, c, :, every], w_core[which, yy, xx, :, every]
                    )
            return carry

        lax.fori_loop(0, nz, one, 0)
        w_first[j] = (
            sends.start(w_sums.at[:, :, 1 - x, :, lo], w_one.at[:, :, :, lo], to_x),
            sends.start(w_sums.at[:, 1 - y, :, :, hi], w_one.at[:, :, :, hi], to_y),
        )

    def w_step2(j):
        every, lo, hi = sides(j)
        for copy in w_first[j]:
            copy.wait_recv()

        def one(which, carry):
            for k in range(2):
                w_sums[which, k, x, :, lo] = add_low(
                    w_sums[which, k, x, :, lo], w_one[which, k, :, lo]
                )
                w_sums[which, y, k, :, hi] = add_low(
                    w_sums[which, y, k, :, hi], w_one[which, k, :, hi]
                )
            return carry

        lax.fori_loop(0, nz, one, 0)
        w_second[j] = (
            sends.start(w_sums.at[:, 1 - y, x, :, lo], w_two.at[:, :, lo], to_y),
            sends.start(w_sums.at[:, y, 1 - x, :, hi], w_two.at[:, :, hi], to_x),
        )

    def w_step3(j):
        every = sides(j)[0]
        for copy in w_second[j]:
            copy.wait_recv()
        for which in range(nz):
            w_sums[which, y, x, :, every] = add_low(
                w_sums[which, y, x, :, every], w_two[which, :, every]
            )
        w_third[j] = [
            sends.start(w_sums.at[others[k], y, x, :, every], w_far.at[k, :, every], peer)
            for k, peer in enumerate(peers)
        ]

    def w_step4(j):
        start, size = spans[j]
        every = sides(j)[0]
        total = w_sums[z, y, x, :, every].astype(f32)
        for k in range(nz - 1):
            w_third[j][k].wait_recv()
            total = total + w_far[k, :, every].astype(f32)
        if j == 0:
            weight_at[:, 3 * width :] = total
            spots = [pl.ds(3 * width, width)]
        else:
            third = size // 3
            spots = [pl.ds(i * width + (j - 1) * third, third) for i in range(3)]
            for i, spot in enumerate(spots):
                weight_at[:, spot] = total[:, i * third : (i + 1) * third]
        for spot in spots:
            puts.append(fetch(weight_at.at[:, spot], weight_out.at[:, spot]))

    ffn_one(1)
    ffn_two(0)
    accs[...] = jnp.zeros_like(accs)
    step = 32

    def norms(k, carry):
        part = pl.ds(pl.multiple_of(k * step, step), step)
        normed_two, inverse_two = centered(middle_ref[part])
        grad = gnm_ref[part]
        og = og_ref[part].astype(f32)
        grad_middle = og + centered_back(grad * vec_ref[2:3], normed_two, inverse_two)
        accs[2] += eights(grad * normed_two)
        accs[8] += eights(grad)
        accs[9] += eights(og)
        normed_post, inverse_post = centered(branch_ref[part])
        post = centered_back(grad_middle * vec_ref[1:2], normed_post, inverse_post).astype(low)
        accs[1] += eights(grad_middle * normed_post)
        accs[7] += eights(grad_middle)
        accs[6] += eights(post.astype(f32))
        gpost[part] = post
        gmid[part] = grad_middle
        return carry

    for copy in (middle_got, gnm_got, og_got, branch_got):
        copy.wait()
    lax.fori_loop(0, rows // step, norms, 0)
    mask[...] = doc_mask(doc_ref, rows)
    quarter = width // 4

    def scaled_block(k, carry):
        part = pl.ds(pl.multiple_of(k * quarter, quarter), quarter)
        block = dot(gpost[...], out_ref[part], NT)
        accs[10, :, part] = eights(block * att_ref[:, part])
        gatt[:, part] = (block * vec_ref[10:11, part]).astype(low)
        return carry

    out_got.wait()
    att_got.wait()
    lax.fori_loop(0, 4, scaled_block, 0)

    def out_block(k, carry):
        part = pl.ds(pl.multiple_of(k * (width // nz), width // nz), width // nz)
        block = dot(scaled_ref[:, part], gpost[...], TN).astype(low)
        w_part[k, :, :, :, :, pl.ds(0, width)] = block.reshape(2, 2, 2, share, width)
        return carry

    scaled_got.wait()
    lax.fori_loop(0, nz, out_block, 0)
    w_zero(0)
    nin_got.wait()
    nin_t[...] = nin_ref[...].T
    proj_got.wait()
    lse_got.wait()
    head = 64
    lane = lax.broadcasted_iota(jnp.int32, (1, 128), 1)
    is_low = lane < head
    factor = 1.0 / math.sqrt(head)
    lane_wide = lax.broadcasted_iota(jnp.int32, (rows, 128), 1)
    keep = (is_low.astype(low), (lane >= head).astype(low))

    def pair(p, carry):
        base = lax.div(p, 2) * (3 * quarter) + lax.rem(p, 2) * 128
        q_at = pl.ds(pl.multiple_of(base, 128), 128)
        k_at = pl.ds(pl.multiple_of(base + quarter, 128), 128)
        v_at = pl.ds(pl.multiple_of(base + 2 * quarter, 128), 128)
        here = pl.ds(pl.multiple_of(p * 128, 128), 128)
        q2, k2, v2, do2 = proj_ref[:, q_at], proj_ref[:, k_at], proj_ref[:, v_at], gatt[:, here]
        lses = lse_ref[...]
        found = []
        for i in range(2):
            scores = dot(q2 * keep[i], k2, NT) * factor
            scores = jnp.where(mask[...] > 0, scores, NEGATIVE)
            lse = jnp.sum(jnp.where(lane_wide == 2 * p + i, lses, 0.0), axis=1, keepdims=True)
            prob = jnp.exp(scores - lse)
            grad_prob = dot(do2 * keep[i], v2, NT)
            inner = jnp.sum(prob * grad_prob, axis=1, keepdims=True)
            ds = (prob * (grad_prob - inner) * factor).astype(low)
            found.append(
                (dot(ds, k2), dot(ds, q2, TN), dot(prob.astype(low), do2, TN))
            )
        for where, a, b in zip((q_at, k_at, v_at), *found):
            dproj[:, where] = jnp.where(is_low, a, b).astype(low)
        accs[4, :, here] = eights(dproj[:, q_at].astype(f32))
        accs[5, :, here] = eights(dproj[:, v_at].astype(f32))
        return carry

    def wgrad(j):
        start, size = spans[j]
        cols = pl.ds((j - 1) * size, size)

        def one(k, carry):
            part = pl.ds(pl.multiple_of(k * (width // nz), width // nz), width // nz)
            block = dot(nin_t[part], dproj[:, cols]).astype(low)
            w_part[k, :, :, :, :, pl.ds(start, size)] = block.reshape(2, 2, 2, share, size)
            return carry

        lax.fori_loop(0, nz, one, 0)
        w_zero(j)

    def gni_block(k, carry):
        part = pl.ds(pl.multiple_of(k * quarter, quarter), quarter)
        gni[:, part] = dot(dproj[...], qkv_ref[part], NT)
        return carry

    def tokens_back(k, carry):
        part = pl.ds(pl.multiple_of(k * step, step), step)
        normed, inverse = centered(tok_ref[part].astype(f32))
        grad = gni[part]
        gmid[part] = gmid[part] + centered_back(grad * vec_ref[0:1], normed, inverse)
        accs[0] += eights(grad * normed)
        accs[3] += eights(grad)
        return carry

    part_z = width // nz
    chain = {}

    def lanes(which):
        return pl.ds(pl.multiple_of(which * part_z, 128), part_z)

    def small_start():
        for j in range(16):
            small[j : j + 1] = jnp.sum(accs[j], axis=0, keepdims=True)
        spot = lax.broadcasted_iota(jnp.int32, (1, width), 1)
        tile = jnp.zeros((1, 128), f32)
        for h in range(HEADS):
            inside = jnp.logical_and(spot >= h * head, spot < (h + 1) * head)
            found = jnp.sum(jnp.where(inside, small[10:11], 0.0), axis=1, keepdims=True)
            tile = jnp.where(lane == h, found, tile)
        small[11:12] = jnp.concatenate([tile] * (width // 128), axis=1)
        chain["z"] = [
            sends.start(small.at[:, lanes(others[k])], small_far.at[k], peer)
            for k, peer in enumerate(peers)
        ]

    def small_second():
        total = small[:, lanes(z)]
        for k in range(nz - 1):
            chain["z"][k].wait_recv()
            total = total + small_far[k]
        small_y[...] = total
        other = small_y.at[:, pl.ds(pl.multiple_of((1 - y) * 128, 128), 128)]
        chain["y"] = sends.start(other, small_got.at[0], to_y)

    def small_third():
        chain["y"].wait_recv()
        small_half[0] = small_y[:, pl.ds(pl.multiple_of(y * 128, 128), 128)] + small_got[0]
        chain["x"] = sends.start(small_half.at[0], small_got.at[1], to_x)

    def small_fourth():
        chain["x"].wait_recv()
        small_half[1] = small_half[0] + small_got[1]
        chain["c"] = sends.start(small_half.at[1], small_got.at[2], to_c)

    def small_last():
        chain["c"].wait_recv()
        total = small_half[1] + small_got[2]
        scale_out[...] = jnp.broadcast_to(total[11:12], (8, 128))
        ours = pl.ds(pl.multiple_of((2 * x + c) * share, share), share)
        turned[...] = jnp.concatenate([total, jnp.zeros((112, 128), f32)], axis=0).T
        mine = jnp.concatenate([turned[ours], jnp.zeros((128 - share, 128), f32)], axis=0).T
        gains_out[...] = mine[0:3, :share]
        biases_out[...] = mine[3:10, :share]

    puts = []

    def far_last():
        for copy in far:
            copy.wait_recv()
        own1_got.wait()
        own2_got.wait()
        late = pl.ds(fc1_at.shape[1] - got1.shape[2], got1.shape[2])
        own2, unit = got2[nz - 1].astype(f32), unit_ref[...]
        for k in range(nz - 1):
            fc1_at[:, late] += got1[k].astype(f32)
            own2 = own2 + got2[k].astype(f32)
            unit = unit + got_unit[k]
        fc2_at[...] = own2
        unit_out[...] = unit
        puts.append(fetch(fc1_at, fc1_out))
        puts.append(fetch(fc2_at, fc2_out))

    def pairs(first, last):
        lax.fori_loop(first, last, pair, 0)

    def gni_all():
        qkv_got.wait()
        lax.fori_loop(0, 4, gni_block, 0)

    def tokens_all():
        tok_got.wait()
        lax.fori_loop(0, rows // step, tokens_back, 0)
        puts.append(fetch(gmid, token_out))

    ffn_one(2)
    pairs(0, 1)
    w_step1(0)
    pairs(1, 2)
    wgrad(1)
    ffn_two(1)
    pairs(2, 3)
    w_step1(1)
    ffn_two(2)
    pairs(3, 4)
    wgrad(2)
    w_step2(0)
    pairs(4, 5)
    w_step1(2)
    pairs(5, 6)
    wgrad(3)
    w_step2(1)
    w_step3(0)
    pairs(6, 7)
    w_step1(3)
    pairs(7, 8)
    wgrad(4)
    w_step2(2)
    gni_all()
    w_step3(1)
    w_step1(4)
    tokens_all()
    small_start()
    w_step2(3)
    w_step3(2)
    small_second()
    w_step2(4)
    ffn_one(3)
    w_step3(3)
    small_third()
    ffn_three(0)
    ffn_three(1)
    ffn_three(2)
    w_step4(0)
    w_step3(4)
    ffn_two(3)
    small_fourth()
    small_last()
    w_step4(1)
    w_step4(2)
    w_step4(3)
    far_last()
    ffn_three(3)
    w_step4(4)
    for put in puts:
        put.wait()
    sends.finish()


def back(nz, *operands):
    gnm, ffn_part, ffn_first, late, fc1, fc2, unit, proj, att, lse, branch = operands[:11]
    middle, scaled, nin, qkv, out, vec = operands[11:17]
    rows, width = middle.shape
    share = width // (nz * 8)
    columns = proj.shape[1] + width
    low, f32 = jnp.bfloat16, jnp.float32
    sds = jax.ShapeDtypeStruct
    fc2_own = (fc2.shape[0], fc2.shape[1] // nz)
    count = 96 + 8 * nz
    specs = [ANY] * 6 + [IN_VMEM] + [ANY] * 9 + [IN_VMEM] + [ANY] * 2
    specs.append(pl.BlockSpec(memory_space=pltpu.SMEM))
    return pl.pallas_call(
        functools.partial(back_kernel, nz),
        name="back",
        out_shape=(
            sds((rows, width), low),
            sds((rows, width), f32),
            sds((share, columns), f32),
            sds((3, share), f32),
            sds((7, share), f32),
            sds((8, 128), f32),
            sds(fc1.shape, f32),
            sds(fc2_own, f32),
            sds(unit.shape, f32),
        ),
        in_specs=specs,
        out_specs=[ANY] * 3 + [IN_VMEM] * 3 + [ANY] * 2 + [IN_VMEM],
        scratch_shapes=[
            pltpu.VMEM((2, 2, rows, width), low),
            pltpu.VMEM((2, 2, rows, width), low),
            pltpu.VMEM((rows, width), low),
            pltpu.VMEM((nz - 1, fc1.shape[0], late.shape[1]), low),
            pltpu.VMEM((nz,) + fc2_own, low),
            pltpu.VMEM((nz - 1,) + unit.shape, f32),
            pltpu.VMEM((nz, 2, 2, 2, share, columns), low),
            pltpu.VMEM((nz, 2, 2, share, columns), low),
            pltpu.VMEM((nz, 2, 2, share, columns), low),
            pltpu.VMEM((nz, 2, share, columns), low),
            pltpu.VMEM((nz, share, columns), low),
            pltpu.VMEM((nz - 1, share, columns), low),
            pltpu.VMEM((rows, width), low),
            pltpu.VMEM((rows, width), f32),
            pltpu.VMEM((rows, width), low),
            pltpu.VMEM((rows, width), f32),
            pltpu.VMEM((rows, 3 * width), low),
            pltpu.VMEM((width, rows), low),
            pltpu.VMEM((rows, rows), f32),
            pltpu.VMEM((16, 8, width), f32),
            pltpu.VMEM((16, width), f32),
            pltpu.VMEM((nz - 1, 16, width // nz), f32),
            pltpu.VMEM((16, width // nz), f32),
            pltpu.VMEM((3, 16, 128), f32),
            pltpu.VMEM((3, 16, 128), f32),
            pltpu.VMEM((128, 128), f32),
            pltpu.VMEM((rows, width), low),
            pltpu.VMEM((share, columns), f32),
            pltpu.VMEM(fc1.shape, f32),
            pltpu.VMEM(fc2_own, f32),
            pltpu.VMEM((rows, width), f32),
            pltpu.VMEM(proj.shape, low),
            pltpu.VMEM((rows, width), f32),
            pltpu.VMEM(lse.shape, f32),
            pltpu.VMEM((rows, width), f32),
            pltpu.VMEM((rows, width), f32),
            pltpu.VMEM((rows, width), low),
            pltpu.VMEM((rows, width), low),
            pltpu.VMEM(qkv.shape, low),
            pltpu.VMEM(out.shape, low),
            pltpu.VMEM((rows, width), low),
            pltpu.VMEM((rows, width), low),
            pltpu.SemaphoreType.DMA((64,)),
            pltpu.SemaphoreType.DMA((count,)),
            pltpu.SemaphoreType.DMA((count,)),
        ],
        compiler_params=pltpu.CompilerParams(
            collective_id=3, has_side_effects=True, vmem_limit_bytes=63 * 2**20
        ),
    )(*operands)


def finish_kernel(
    mixed,
    token,
    weight,
    fc1,
    fc2,
    gains,
    biases,
    scale,
    unit,
    mixed_out,
    token_out,
    qkv_out,
    out_out,
    fc1_out,
    fc2_out,
    gains_out,
    biases_out,
    scale_out,
    gain_out,
    shift_out,
    mixed_at,
    token_at,
    weight_at,
    fc1_at,
    fc2_at,
    in_sems,
    out_sems,
):
    columns = qkv_out.shape[1]
    moves = (
        (token, token_at, ((token_at, token_out),)),
        (
            weight,
            weight_at,
            (
                (weight_at.at[:, pl.ds(0, columns)], qkv_out),
                (weight_at.at[:, pl.ds(columns, out_out.shape[1])], out_out),
            ),
        ),
        (mixed, mixed_at, ((mixed_at, mixed_out),)),
        (fc1, fc1_at, ((fc1_at, fc1_out),)),
        (fc2, fc2_at, ((fc2_at, fc2_out),)),
    )
    reads, writes = [], []
    for k, (src, here, _) in enumerate(moves):
        reads.append(pltpu.make_async_copy(src, here, in_sems.at[k]))
        reads[-1].start()
    gains_out[...] = gains[...]
    biases_out[...] = biases[...]
    scale_out[...] = scale[0:1, : scale_out.shape[1]]
    gain_out[...] = unit[0:1]
    shift_out[0:1] = unit[1:2]
    shift_out[1:2] = unit[2:3]
    for read, (_, _, outs) in zip(reads, moves):
        read.wait()
        for src, dst in outs:
            writes.append(pltpu.make_async_copy(src, dst, out_sems.at[len(writes)]))
            writes[-1].start()
    for write in writes:
        write.wait()


def finish(mixed, token, weight, gains, biases, scale, fc1, fc2, unit):
    share, columns = weight.shape
    width, units = token.shape[1], unit.shape[1]
    f32 = jnp.float32
    shapes = (
        (mixed.shape, mixed.dtype),
        (token.shape, f32),
        ((share, columns - width), f32),
        ((share, width), f32),
        (fc1.shape, f32),
        (fc2.shape, f32),
        (gains.shape, f32),
        (biases.shape, f32),
        ((1, HEADS), f32),
        ((1, units), f32),
        ((2, units), f32),
    )
    return pl.pallas_call(
        finish_kernel,
        name="finish",
        out_shape=tuple(jax.ShapeDtypeStruct(shape, kind) for shape, kind in shapes),
        in_specs=[ANY] * 5 + [IN_VMEM] * 4,
        out_specs=[ANY] * 6 + [IN_VMEM] * 5,
        scratch_shapes=[
            pltpu.VMEM(mixed.shape, mixed.dtype),
            pltpu.VMEM(token.shape, f32),
            pltpu.VMEM(weight.shape, f32),
            pltpu.VMEM(fc1.shape, f32),
            pltpu.VMEM(fc2.shape, f32),
            pltpu.SemaphoreType.DMA((5,)),
            pltpu.SemaphoreType.DMA((6,)),
        ],
        compiler_params=pltpu.CompilerParams(vmem_limit_bytes=63 * 2**20),
    )(mixed, token, weight, fc1, fc2, gains, biases, scale, unit)


def fused(
    nz,
    tokens,
    out_grad,
    doc_lengths,
    w_qkv,
    w_out,
    gains,
    biases,
    head_scale,
    w_fc1,
    w_fc2,
    mid_gain,
    ffn_biases,
):
    (
        qkv_full,
        out_full,
        vec,
        proj,
        att,
        lse,
        branch,
        middle,
        nin,
        scaled,
        ffn_part,
        ffn_first,
        fc2_part,
        fc1_late,
        gnm,
        fc1_own,
        unit_sums,
    ) = fore(
        nz,
        tokens,
        out_grad,
        doc_lengths,
        w_qkv,
        w_out,
        gains,
        biases,
        head_scale,
        w_fc1,
        w_fc2,
        mid_gain[None],
        ffn_biases,
    )
    model_width = tokens.shape[1]
    (
        mixed,
        token_grad,
        weight_grad,
        gains_grad,
        biases_grad,
        scale,
        fc1_grad,
        fc2_grad,
        unit_sums,
    ) = back(
        nz,
        gnm,
        ffn_part,
        ffn_first,
        fc1_late,
        fc1_own,
        fc2_part,
        unit_sums,
        proj,
        att,
        lse,
        branch,
        middle,
        scaled,
        nin,
        qkv_full.reshape(model_width, -1),
        out_full.reshape(model_width, -1),
        vec,
        out_grad,
        tokens,
        doc_lengths,
    )
    mixed, token_grad, qkv, out, fc1, fc2, gains_grad, biases_grad, scale, gain, shift = finish(
        mixed,
        token_grad,
        weight_grad,
        gains_grad,
        biases_grad,
        scale,
        fc1_grad,
        fc2_grad,
        unit_sums,
    )
    return (
        mixed,
        token_grad,
        qkv,
        out,
        gains_grad.T,
        biases_grad.T,
        scale[0],
        fc1,
        fc2,
        gain[0],
        shift,
    )


def layer(nz, nt, tokens, out_grad, doc_lengths, w_qkv, *rest):
    if nz == 4 and nt == 8 and w_qkv.shape[0] % 16 == 0:
        return fused(nz, tokens, out_grad, doc_lengths, w_qkv, *rest)
    return plain(tokens, out_grad, doc_lengths, w_qkv, *rest)


def solution(mesh):
    return jax.shard_map(
        functools.partial(layer, mesh.shape["dp"], mesh.shape["tensor"]),
        mesh=mesh,
        in_specs=(
            P(("dp", "tensor"), None),
            P(("dp", "tensor"), None),
            P(("dp", "tensor"), None),
            P(("dp", "tensor"), None),
            P(("dp", "tensor"), None),
            P(("dp", "tensor"), None),
            P(("dp", "tensor"), None),
            P(),
            P("dp", "tensor"),
            P("tensor", "dp"),
            P("tensor"),
            P(None, "tensor"),
        ),
        out_specs=(
            P(("dp", "tensor"), None),
            P(("dp", "tensor"), None),
            P(("dp", "tensor"), None),
            P(("dp", "tensor"), None),
            P(("dp", "tensor"), None),
            P(("dp", "tensor"), None),
            P(),
            P("dp", "tensor"),
            P("tensor", "dp"),
            P("tensor"),
            P(None, "tensor"),
        ),
        check_vma=False,
    )
```

```python
import functools
import math

import jax
import jax.numpy as jnp
from jax import lax
from jax.experimental import pallas as pl
from jax.experimental.pallas import tpu as pltpu
from jax.sharding import PartitionSpec as P

HEADS = 16
FF = 4096


EPS = 1e-05
NEGATIVE = -1000000000.0


def normalize(values):
    center = jnp.mean(values, axis=-1, keepdims=True)
    spread = jnp.mean(values * values, axis=-1, keepdims=True) - center * center
    inverse = lax.rsqrt(spread + EPS)
    return ((values - center) * inverse, inverse)


def normalize_back(grad_normed, normed, inverse):
    first_mean = jnp.mean(grad_normed, axis=-1, keepdims=True)
    second = jnp.mean(grad_normed * normed, axis=-1, keepdims=True)
    return inverse * (grad_normed - first_mean - normed * second)


def block_scores(query_rows, key_rows, doc_ids, row_first, row_last, factor):
    scores = (
        jnp.einsum("qhd,khd->hqk", query_rows, key_rows, preferred_element_type=jnp.float32)
        * factor
    )
    query_pos = jnp.arange(row_first, row_last)
    key_pos = jnp.arange(row_last)
    same_doc = doc_ids[row_first:row_last, None] == doc_ids[None, :row_last]
    allowed = jnp.logical_and(same_doc, key_pos[None, :] <= query_pos[:, None])
    return (jnp.where(allowed[None], scores, NEGATIVE), allowed)


def attend_forward(query_rows, key_rows, value_rows, doc_ids, factor):
    total_rows = query_rows.shape[0]
    block_rows = min(512, total_rows)
    scores, allowed = block_scores(query_rows, key_rows, doc_ids, 0, block_rows, factor)
    row_peak = jnp.max(scores, axis=-1, keepdims=True)
    exponent = jnp.exp(scores - row_peak)
    row_total = jnp.sum(exponent, axis=-1, keepdims=True)
    prob_low = (exponent / row_total).astype(jnp.bfloat16)
    pieces = jnp.einsum("hqk,khd->qhd", prob_low, value_rows, preferred_element_type=jnp.float32)
    sums_log = [row_peak + jnp.log(row_total)]
    return (pieces, sums_log)


def attend_backward(query_rows, key_rows, value_rows, grad_out, doc_ids, sums_log, factor):
    total_rows = query_rows.shape[0]
    block_rows = min(512, total_rows)
    query_parts = []
    grad_keys = jnp.zeros(key_rows.shape, jnp.float32)
    grad_values = jnp.zeros(value_rows.shape, jnp.float32)
    for block_index, row_first in enumerate(range(0, total_rows, block_rows)):
        row_last = row_first + block_rows
        scores, allowed = block_scores(query_rows, key_rows, doc_ids, row_first, row_last, factor)
        prob_rows = jnp.where(allowed[None], jnp.exp(scores - sums_log[block_index]), 0.0)
        prob_low = prob_rows.astype(jnp.bfloat16)
        grad_probs = jnp.einsum(
            "qhd,khd->hqk", grad_out, value_rows, preferred_element_type=jnp.float32
        )
        inner_sum = jnp.sum(prob_rows * grad_probs, axis=-1, keepdims=True)
        grad_scores = (prob_rows * (grad_probs - inner_sum) * factor).astype(jnp.bfloat16)
        query_parts.append(
            jnp.einsum("hqk,khd->qhd", grad_scores, key_rows, preferred_element_type=jnp.float32)
        )
        grad_keys = grad_keys.at[:row_last].add(
            jnp.einsum("hqk,qhd->khd", grad_scores, query_rows, preferred_element_type=jnp.float32)
        )
        grad_values = grad_values.at[:row_last].add(
            jnp.einsum("hqk,qhd->khd", prob_low, grad_out, preferred_element_type=jnp.float32)
        )
    return (query_parts[0], grad_keys, grad_values)


def plain(
    tokens,
    out_grad,
    doc_lengths,
    w_qkv,
    w_out,
    gains,
    biases,
    head_scale,
    w_fc1,
    w_fc2,
    mid_gain,
    ffn_biases,
):
    qkv_full, out_full, gain_full, bias_full = (
        lax.all_gather(w_qkv, ("dp", "tensor"), axis=0, tiled=True),
        lax.all_gather(w_out, ("dp", "tensor"), axis=0, tiled=True),
        lax.all_gather(gains.astype(jnp.bfloat16), ("dp", "tensor"), axis=0, tiled=True).astype(
            gains.dtype
        ),
        lax.all_gather(biases.astype(jnp.bfloat16), ("dp", "tensor"), axis=0, tiled=True).astype(
            biases.dtype
        ),
    )
    fc1_rows, fc2_cols = (
        lax.all_gather(w_fc1, "dp", axis=0, tiled=True),
        lax.all_gather(w_fc2, "dp", axis=1, tiled=True),
    )
    model_width = tokens.shape[1]
    local_rows = tokens.shape[0]
    head_dim = model_width // HEADS
    factor = 1.0 / math.sqrt(head_dim)
    doc_ends = jnp.cumsum(doc_lengths[0])[:-1]
    places = jnp.arange(local_rows)
    doc_ids = jnp.sum((places[:, None] >= doc_ends[None, :]).astype(jnp.int32), axis=1)
    inputs = tokens.astype(jnp.float32)
    normed_one, inverse_one = normalize(inputs)
    normed_in = (normed_one * gain_full[:, 0] + bias_full[:, 0]).astype(jnp.bfloat16)
    zero_bias = jnp.zeros((model_width,), jnp.float32)
    qkv_bias = jnp.concatenate([bias_full[:, 1], zero_bias, bias_full[:, 2]])
    projected = (
        jnp.dot(normed_in, qkv_full, preferred_element_type=jnp.float32) + qkv_bias
    ).astype(jnp.bfloat16)
    query_rows = projected[:, :model_width].reshape(local_rows, HEADS, head_dim)
    key_rows = projected[:, model_width : 2 * model_width].reshape(local_rows, HEADS, head_dim)
    value_rows = projected[:, 2 * model_width :].reshape(local_rows, HEADS, head_dim)
    attended, sums_log = attend_forward(query_rows, key_rows, value_rows, doc_ids, factor)
    attended = attended.reshape(local_rows, model_width)
    scale_wide = jnp.repeat(head_scale, head_dim)
    scaled = (attended * scale_wide).astype(jnp.bfloat16)
    branch = jnp.dot(scaled, out_full, preferred_element_type=jnp.float32) + bias_full[:, 3]
    normed_post, inverse_post = normalize(branch)
    middle = inputs + normed_post * gain_full[:, 1] + bias_full[:, 4]
    normed_two, inverse_two = normalize(middle)
    normed_mid = (normed_two * gain_full[:, 2] + bias_full[:, 5]).astype(jnp.bfloat16)
    gathered = lax.all_gather(normed_mid, "tensor", axis=0, tiled=True)
    hidden_pre = jnp.dot(gathered, fc1_rows, preferred_element_type=jnp.float32) + ffn_biases[0]
    activated, gelu_pull = jax.vjp(jax.nn.gelu, hidden_pre)
    act_sum, act_square = (
        lax.psum(jnp.sum(activated, axis=1).astype(jnp.bfloat16), "tensor").astype(jnp.float32),
        lax.psum(jnp.sum(activated * activated, axis=1).astype(jnp.bfloat16), "tensor").astype(
            jnp.float32
        ),
    )
    center = act_sum / FF
    inverse_mid = lax.rsqrt(act_square / FF - center * center + EPS)[:, None]
    normed_act = (activated - center[:, None]) * inverse_mid
    hidden = (normed_act * mid_gain + ffn_biases[1]).astype(jnp.bfloat16)
    hidden_rows = hidden
    ffn_out = lax.psum_scatter(
        jnp.dot(hidden_rows, fc2_cols, preferred_element_type=jnp.float32).astype(jnp.bfloat16),
        "tensor",
        scatter_dimension=0,
        tiled=True,
    ).astype(jnp.float32)
    shard_rows = lax.all_gather(out_grad, "tensor", axis=0, tiled=True)
    grad_piece = jnp.einsum("rd,fd->rf", shard_rows, fc2_cols, preferred_element_type=jnp.float32)
    hidden_rows = hidden
    fc2_run = jnp.einsum("rf,rd->fd", hidden_rows, shard_rows, preferred_element_type=jnp.float32)
    mid_gain_part = jnp.sum(grad_piece * normed_act, axis=0)
    mid_bias_part = jnp.sum(grad_piece, axis=0)
    grad_normed_act = grad_piece * mid_gain
    first_sum, second_sum = (
        lax.psum(jnp.sum(grad_normed_act, axis=1).astype(jnp.bfloat16), "tensor").astype(
            jnp.float32
        ),
        lax.psum(
            jnp.sum(grad_normed_act * normed_act, axis=1).astype(jnp.bfloat16), "tensor"
        ).astype(jnp.float32),
    )
    grad_act = inverse_mid * (
        grad_normed_act - first_sum[:, None] / FF - normed_act * (second_sum[:, None] / FF)
    )
    grad_pre = gelu_pull(grad_act)[0].astype(jnp.bfloat16)
    fc1_part = jnp.einsum("rd,rf->df", gathered, grad_pre, preferred_element_type=jnp.float32)
    fc1_bias_part = jnp.sum(grad_pre.astype(jnp.float32), axis=0)
    grad_normed_mid = lax.psum_scatter(
        jnp.einsum("rf,df->rd", grad_pre, fc1_rows, preferred_element_type=jnp.float32).astype(
            jnp.bfloat16
        ),
        "tensor",
        scatter_dimension=0,
        tiled=True,
    ).astype(jnp.float32)
    ffn_bias_part = jnp.stack([fc1_bias_part, mid_bias_part])
    fc1_grad, fc2_grad = (
        lax.psum_scatter(
            fc1_part.astype(jnp.bfloat16), "dp", scatter_dimension=0, tiled=True
        ).astype(jnp.float32),
        lax.psum_scatter(
            fc2_run.astype(jnp.bfloat16), "dp", scatter_dimension=1, tiled=True
        ).astype(jnp.float32),
    )
    mid_gain_grad, ffn_bias_grad = lax.psum((mid_gain_part, ffn_bias_part), "dp")
    mixed_out = (middle + ffn_out + bias_full[:, 6]).astype(jnp.bfloat16)
    final_grad = out_grad.astype(jnp.float32)
    grad_middle = final_grad + normalize_back(
        grad_normed_mid * gain_full[:, 2], normed_two, inverse_two
    )
    grad_post = normalize_back(grad_middle * gain_full[:, 1], normed_post, inverse_post).astype(
        jnp.bfloat16
    )
    out_local = jnp.einsum("td,te->de", scaled, grad_post, preferred_element_type=jnp.float32)
    grad_scaled = jnp.einsum("te,de->td", grad_post, out_full, preferred_element_type=jnp.float32)
    scale_local = jnp.sum(
        (grad_scaled * attended).reshape(local_rows, HEADS, head_dim), axis=(0, 2)
    )
    grad_attended = (
        (grad_scaled * scale_wide).astype(jnp.bfloat16).reshape(local_rows, HEADS, head_dim)
    )
    grad_query, grad_keys, grad_values = attend_backward(
        query_rows, key_rows, value_rows, grad_attended, doc_ids, sums_log, factor
    )
    grad_projected = jnp.concatenate(
        [
            grad_query.reshape(local_rows, model_width),
            grad_keys.reshape(local_rows, model_width),
            grad_values.reshape(local_rows, model_width),
        ],
        axis=1,
    ).astype(jnp.bfloat16)
    qkv_local = jnp.einsum(
        "td,te->de", normed_in, grad_projected, preferred_element_type=jnp.float32
    )
    grad_normed_in = jnp.einsum(
        "te,de->td", grad_projected, qkv_full, preferred_element_type=jnp.float32
    )
    token_grad = grad_middle + normalize_back(
        grad_normed_in * gain_full[:, 0], normed_one, inverse_one
    )
    projected_sums = jnp.sum(grad_projected.astype(jnp.float32), axis=0)
    gains_local = jnp.stack(
        [
            jnp.sum(grad_normed_in * normed_one, axis=0),
            jnp.sum(grad_middle * normed_post, axis=0),
            jnp.sum(grad_normed_mid * normed_two, axis=0),
        ],
        axis=1,
    )
    biases_local = jnp.stack(
        [
            jnp.sum(grad_normed_in, axis=0),
            projected_sums[:model_width],
            projected_sums[2 * model_width :],
            jnp.sum(grad_post.astype(jnp.float32), axis=0),
            jnp.sum(grad_middle, axis=0),
            jnp.sum(grad_normed_mid, axis=0),
            jnp.sum(final_grad, axis=0),
        ],
        axis=1,
    )
    qkv_grad, out_weight_grad, gains_grad, biases_grad = (
        lax.psum_scatter(qkv_local, ("dp", "tensor"), scatter_dimension=0, tiled=True),
        lax.psum_scatter(out_local, ("dp", "tensor"), scatter_dimension=0, tiled=True),
        lax.psum_scatter(gains_local, ("dp", "tensor"), scatter_dimension=0, tiled=True),
        lax.psum_scatter(biases_local, ("dp", "tensor"), scatter_dimension=0, tiled=True),
    )
    scale_grad = lax.psum(scale_local, ("dp", "tensor"))
    return (
        mixed_out,
        token_grad,
        qkv_grad,
        out_weight_grad,
        gains_grad,
        biases_grad,
        scale_grad,
        fc1_grad,
        fc2_grad,
        mid_gain_grad,
        ffn_bias_grad,
    )


MESH = pl.DeviceIdType.MESH
ANY = pl.BlockSpec(memory_space=pl.ANY)
IN_VMEM = pl.BlockSpec(memory_space=pltpu.VMEM)


def place():
    z = lax.axis_index("dp")
    t = lax.axis_index("tensor")
    return z, lax.div(t, 4), lax.rem(lax.div(t, 2), 2), lax.rem(t, 2)


def at(z, y, x, c):
    return (z, y * 4 + x * 2 + c)


def greet(partners):
    barrier = pltpu.get_barrier_semaphore()
    for partner in partners:
        pl.semaphore_signal(barrier, inc=1, device_id=partner, device_id_type=MESH)
    pl.semaphore_wait(barrier, len(partners))


class Sends:
    def __init__(self, send_sems, recv_sems):
        self.send_sems, self.recv_sems, self.copies = send_sems, recv_sems, []

    def start(self, src, dst, target):
        index = len(self.copies)
        copy = pltpu.make_async_remote_copy(
            src_ref=src,
            dst_ref=dst,
            send_sem=self.send_sems.at[index],
            recv_sem=self.recv_sems.at[index],
            device_id=target,
            device_id_type=MESH,
        )
        copy.start()
        self.copies.append(copy)
        return copy

    def finish(self):
        for copy in self.copies:
            copy.wait_send()


def add_low(left, right):
    return (left.astype(jnp.float32) + right.astype(jnp.float32)).astype(jnp.bfloat16)


SQRT_2_PI = math.sqrt(2.0 / math.pi)
NT = (((1,), (1,)), ((), ()))
TN = (((0,), (0,)), ((), ()))


def dot(left, right, dims=None):
    if dims is None:
        return jnp.dot(left, right, preferred_element_type=jnp.float32)
    return lax.dot_general(left, right, dims, preferred_element_type=jnp.float32)


def centered(values):
    center = jnp.mean(values, axis=-1, keepdims=True)
    spread = jnp.mean(values * values, axis=-1, keepdims=True) - center * center
    inverse = lax.rsqrt(spread + EPS)
    return (values - center) * inverse, inverse


def centered_back(grad, normed, inverse):
    first = jnp.mean(grad, axis=-1, keepdims=True)
    second = jnp.mean(grad * normed, axis=-1, keepdims=True)
    return inverse * (grad - first - normed * second)


def eights(values):
    return jnp.sum(values.reshape(values.shape[0] // 8, 8, values.shape[1]), axis=0)


def doc_mask(doc_ref, rows):
    query = lax.broadcasted_iota(jnp.int32, (rows, rows), 0)
    key = lax.broadcasted_iota(jnp.int32, (rows, rows), 1)
    query_doc, key_doc = jnp.zeros_like(query), jnp.zeros_like(key)
    end = 0
    for j in range(doc_ref.shape[1] - 1):
        end = end + doc_ref[0, j]
        query_doc = query_doc + (query >= end).astype(jnp.int32)
        key_doc = key_doc + (key >= end).astype(jnp.int32)
    allowed = jnp.logical_and(query_doc == key_doc, key <= query)
    return allowed.astype(jnp.float32)


class Plane:
    def __init__(self, sends, whole, here, targets):
        self.sends, self.whole, self.here, self.targets = sends, whole, here, targets
        half = whole.shape[3] // 2
        self.lo, self.hi = pl.ds(0, half), pl.ds(half, half)

    def part(self, y, x, c, rows):
        return self.whole.at[y, x, c, rows]

    def start_first(self, src):
        (y, x, c), (to_x, to_y, to_c), lo, hi = self.here, self.targets, self.lo, self.hi
        go = self.sends.start
        self.first = [
            go(src.at[lo], self.part(y, x, c, lo), to_x),
            go(src.at[hi], self.part(y, x, c, hi), to_y),
        ]
        self.core = [go(src, self.whole.at[y, x, c], to_c)]

    def start_second(self, src):
        (y, x, c), (to_x, to_y, _), lo, hi = self.here, self.targets, self.lo, self.hi
        go = self.sends.start
        self.second = [
            go(src.at[lo], self.part(y, x, c, lo), to_y),
            go(src.at[hi], self.part(y, x, c, hi), to_x),
        ]

    def after_first(self):
        (y, x, c), (to_x, to_y, to_c), lo, hi = self.here, self.targets, self.lo, self.hi
        for copy in self.first:
            copy.wait_recv()
        by_x, by_y = self.part(y, 1 - x, c, lo), self.part(1 - y, x, c, hi)
        go = self.sends.start
        self.third = [go(by_x, by_x, to_y), go(by_y, by_y, to_x)]
        self.side = [go(by_x, by_x, to_c), go(by_y, by_y, to_c)]

    def after_second(self):
        (y, x, c), (to_x, to_y, to_c), lo, hi = self.here, self.targets, self.lo, self.hi
        for copy in self.second:
            copy.wait_recv()
        by_x, by_y = self.part(y, 1 - x, c, hi), self.part(1 - y, x, c, lo)
        go = self.sends.start
        self.side += [go(by_x, by_x, to_c), go(by_y, by_y, to_c)]

    def after_third(self):
        y, x, c = self.here
        self.last = []
        for copy, part in zip(self.third, (self.lo, self.hi)):
            copy.wait_recv()
            ref = self.part(1 - y, 1 - x, c, part)
            self.last.append(self.sends.start(ref, ref, self.targets[2]))


def fore_kernel(
    nz,
    tok_ref,
    og_ref,
    qkv_ref,
    out_ref,
    gains_ref,
    biases_ref,
    fc1_ref,
    fc2_ref,
    gain_ref,
    shift_ref,
    doc_ref,
    scale_ref,
    qkv_out,
    out_out,
    vec_out,
    proj_out,
    att_out,
    lse_out,
    branch_out,
    middle_out,
    nin_out,
    scaled_out,
    ffn_out,
    first_out,
    fc2_out,
    late_out,
    gnm_out,
    fc1_out,
    unit_out,
    qkv_all,
    out_all,
    vec_all,
    vec_mine,
    vec_turn,
    unit_ref,
    fc1_all,
    fc2_all,
    og_all,
    tok,
    branch,
    nin,
    proj,
    att,
    lse,
    scaled,
    middle,
    mask,
    vec,
    mid_all,
    act,
    slope,
    grad,
    hidden,
    grad_pre,
    mid_part,
    pre,
    stats,
    pair,
    got,
    totals,
    from_core,
    sums,
    from_one,
    from_two,
    f_part,
    f_core,
    f_sums,
    fc1_part,
    late_part,
    fc2_part,
    fc1_got,
    local_sems,
    send_sems,
    recv_sems,
):
    z, y, x, c = place()
    to_x, to_y, to_c = at(z, y, 1 - x, c), at(z, 1 - y, x, c), at(z, y, x, 1 - c)
    to_xy = at(z, 1 - y, 1 - x, c)
    others = [lax.rem(z + k, nz) for k in range(1, nz)]
    slots = [z] + [lax.rem(z + nz - k, nz) for k in range(1, nz)]
    peers = [at(other, y, x, c) for other in others]
    locals_ = []

    def fetch(src, dst):
        copy = pltpu.make_async_copy(src, dst, local_sems.at[len(locals_)])
        copy.start()
        locals_.append(copy)
        return copy

    rows, width = tok.shape
    fourth = width // 4
    qkv_in = [
        fetch(
            qkv_ref.at[:, pl.ds(i * width + g * fourth, fourth)],
            qkv_all.at[z, y, x, c, :, pl.ds((3 * g + i) * fourth, fourth)],
        )
        for g in range(4)
        for i in range(3)
    ]
    vec_turn[...] = jnp.zeros_like(vec_turn)
    share = vec_mine.shape[0]
    vec_turn[0:3, 0:share] = gains_ref[...]
    vec_turn[3:10, 0:share] = biases_ref[...]
    vec_mine[...] = vec_turn[...].T[:share]
    greet([to_x, to_y, to_c, to_xy] + peers)
    sends = Sends(send_sems, recv_sems)
    low, f32 = jnp.bfloat16, jnp.float32
    units = fc1_all.shape[1]
    width1, width2 = fc1_ref.shape[0], fc2_ref.shape[1]
    own1 = fc1_all.at[pl.ds(pl.multiple_of(z * width1, width1), width1)]
    own2 = fc2_all.at[:, pl.ds(pl.multiple_of(z * width2, width2), width2)]
    def wait_all(copies):
        for copy in copies:
            copy.wait_recv()

    vec_z = [sends.start(vec_mine, vec_all.at[z, y, x, c], peer) for peer in peers]
    phase = 6 * fourth
    spans = (pl.ds(0, phase), pl.ds(phase, phase))
    for copy in qkv_in:
        copy.wait()
    own_qkv = qkv_all.at[z, y, x, c]
    qkv_z = [
        [sends.start(own_qkv.at[:, span], own_qkv.at[:, span], peer) for peer in peers]
        for span in spans
    ]

    z_pair = z + 1 - 2 * lax.rem(z, 2)
    pair_peer, far_peer = at(z_pair, y, x, c), peers[1]
    qkv_slots = slots

    def go_on(p):
        qkv_z[p][0].wait_recv()

    def sides(whole, p):
        size = phase // 2 if whole is qkv_all else whole.shape[-1] // 2
        return pl.ds(2 * p * size, size), pl.ds((2 * p + 1) * size, size)

    def first(whole, slot, p=0):
        lo, hi = sides(whole, p)
        by_x, by_y = whole.at[slot, y, x, c, :, lo], whole.at[slot, y, x, c, :, hi]
        return (sends.start(by_x, by_x, to_x), sends.start(by_y, by_y, to_y))

    def second(whole, slot, p=0):
        lo, hi = sides(whole, p)
        by_x, by_y = whole.at[slot, y, :, c, :, lo], whole.at[slot, :, x, c, :, hi]
        return (sends.start(by_x, by_x, to_y), sends.start(by_y, by_y, to_x))

    def third(whole, slot, p=None):
        ref = whole.at[slot, :, :, c] if p is None else whole.at[slot, :, :, c, :, spans[p]]
        return sends.start(ref, ref, to_c)

    a0, a1 = [first(qkv_all, z, 0)], [first(qkv_all, z, 1)]
    og = Plane(sends, og_all, (y, x, c), (to_x, to_y, to_c))
    og.start_first(og_ref)
    tok_in = fetch(tok_ref, tok)
    out_in = fetch(out_ref, out_all.at[z, y, x, c])
    fc1_in = fetch(fc1_ref, own1)
    fc2_in = fetch(fc2_ref, own2)
    og_in = fetch(og_ref, og_all.at[y, x, c])
    vec_all[z, y, x, c] = vec_mine[...]
    unit_ref[...] = jnp.zeros_like(unit_ref)
    unit_ref[0:1] = shift_ref[0:1]
    unit_ref[1:2] = gain_ref[...]
    unit_ref[2:3] = shift_ref[1:2]
    step = 32
    mask[...] = doc_mask(doc_ref, rows)
    tok_in.wait()

    def normed(k, carry):
        part = pl.ds(pl.multiple_of(k * step, step), step)
        branch[part] = centered(tok[part].astype(f32))[0]
        return carry

    lax.fori_loop(0, rows // step, normed, 0)
    wait_all(vec_z)
    by_x = vec_all.at[:, y, x, c]
    vec_x = sends.start(by_x, by_x, to_x)
    wait_all(a0[0])
    b0 = [second(qkv_all, z, 0)]
    wait_all(a1[0])
    b1 = [second(qkv_all, z, 1)]
    go_on(0)
    a0.append(first(qkv_all, qkv_slots[1], 0))
    vec_x.wait_recv()
    by_y = vec_all.at[:, y, :, c]
    vec_y = sends.start(by_y, by_y, to_y)
    for k in range(2, nz):
        qkv_z[0][k - 1].wait_recv()
        a0.append(first(qkv_all, qkv_slots[k], 0))
    vec_y.wait_recv()
    by_c = vec_all.at[:, :, :, c]
    vec_c = sends.start(by_c, by_c, to_c)
    for k in range(1, nz):
        wait_all(a0[k])
        b0.append(second(qkv_all, qkv_slots[k], 0))
    go_on(1)
    a1.append(first(qkv_all, qkv_slots[1], 1))
    vec_c.wait_recv()
    vec[...] = vec_all[...].reshape(width, 128).T[:16]
    spot = lax.broadcasted_iota(jnp.int32, (1, width), 1)
    head = 64
    wide = jnp.zeros((1, width), f32)
    for h in range(HEADS):
        inside = jnp.logical_and(spot >= h * head, spot < (h + 1) * head)
        wide = jnp.where(inside, scale_ref[h], wide)
    vec[10:11] = wide

    def scaled_in(k, carry):
        part = pl.ds(pl.multiple_of(k * step, step), step)
        nin[part] = (branch[part] * vec[0:1] + vec[3:4]).astype(low)
        return carry

    lax.fori_loop(0, rows // step, scaled_in, 0)
    wait_all(b0[0])
    c0 = [third(qkv_all, z, 0)]
    for k in range(2, nz):
        qkv_z[1][k - 1].wait_recv()
        a1.append(first(qkv_all, qkv_slots[k], 1))
        wait_all(b0[k - 1])
        c0.append(third(qkv_all, qkv_slots[k - 1], 0))
    out_in.wait()
    own_out = out_all.at[z, y, x, c]
    out_z = [sends.start(own_out, own_out, peer) for peer in peers]
    fc2_far = sends.start(fc2_ref, own2, far_peer)
    fc2_near = sends.start(fc2_ref, own2, pair_peer)
    fc1_z = [sends.start(fc1_ref, own1, peer) for peer in peers]
    wait_all(b0[nz - 1])
    c0.append(third(qkv_all, qkv_slots[nz - 1], 0))
    wait_all(a1[1])
    b1.append(second(qkv_all, qkv_slots[1], 1))
    wait_all(c0)

    def project(p):
        for g in (2 * p, 2 * p + 1):
            cols = pl.ds(3 * g * fourth, 3 * fourth)
            here = pl.ds(g * fourth, fourth)
            bias = jnp.concatenate(
                [vec[4:5, here], jnp.zeros((1, fourth), f32), vec[5:6, here]], axis=1
            )
            block = dot(nin[...], qkv_all[:, :, :, :, :, cols].reshape(width, 3 * fourth))
            proj[:, cols] = (block + bias).astype(low)

    project(0)
    lane = lax.broadcasted_iota(jnp.int32, (1, 128), 1)
    is_low = lane < head
    keep = (is_low.astype(low), (lane >= head).astype(low))
    factor = 1.0 / math.sqrt(head)
    lane_wide = lax.broadcasted_iota(jnp.int32, (rows, 128), 1)
    lse[...] = jnp.zeros_like(lse)

    def attend(p, carry):
        base = lax.div(p, 2) * (3 * fourth) + lax.rem(p, 2) * 128
        q_at = pl.ds(pl.multiple_of(base, 128), 128)
        k_at = pl.ds(pl.multiple_of(base + fourth, 128), 128)
        v_at = pl.ds(pl.multiple_of(base + 2 * fourth, 128), 128)
        here = pl.ds(pl.multiple_of(p * 128, 128), 128)
        q2, k2, v2 = proj[:, q_at], proj[:, k_at], proj[:, v_at]
        found, logs = [], []
        for i in range(2):
            scores = dot(q2 * keep[i], k2, NT) * factor
            scores = jnp.where(mask[...] > 0, scores, NEGATIVE)
            peak = jnp.max(scores, axis=1, keepdims=True)
            exponent = jnp.exp(scores - peak)
            total = jnp.sum(exponent, axis=1, keepdims=True)
            prob = (exponent * (1.0 / total)).astype(low)
            found.append(dot(prob, v2))
            logs.append(peak + jnp.log(total))
        spread_logs = jnp.where(lane_wide == 2 * p, logs[0], logs[1])
        at_pair = lax.div(lane_wide, 2) == p
        lse[...] = jnp.where(at_pair, spread_logs, lse[...])
        both = jnp.where(is_low, *found)
        att[:, here] = both
        scaled[:, here] = (both * vec[10:11, here]).astype(low)
        return carry

    lax.fori_loop(0, 1, attend, 0)
    for k in range(2, nz):
        wait_all(a1[k])
        b1.append(second(qkv_all, qkv_slots[k], 1))
    out_a = [first(out_all, z)]
    for k in range(1, nz):
        out_z[k - 1].wait_recv()
        out_a.append(first(out_all, slots[k]))
    og.start_second(og_ref)
    lax.fori_loop(1, 2, attend, 0)
    c1 = []
    for k in range(2):
        wait_all(b1[k])
        c1.append(third(qkv_all, qkv_slots[k], 1))
    lax.fori_loop(2, 4, attend, 0)
    for k in range(2, nz):
        wait_all(b1[k])
        c1.append(third(qkv_all, qkv_slots[k], 1))
    wait_all(c1)
    saves = [fetch(qkv_all, qkv_out), fetch(vec, vec_out), fetch(nin, nin_out)]
    project(1)
    saves.append(fetch(proj, proj_out))
    out_b = []
    for k in range(nz):
        wait_all(out_a[k])
        out_b.append(second(out_all, slots[k]))
    lax.fori_loop(4, 6, attend, 0, unroll=True)
    og.after_first()
    lax.fori_loop(6, 8, attend, 0, unroll=True)
    out_c = []
    for k in range(nz):
        wait_all(out_b[k])
        out_c.append(third(out_all, slots[k]))
    saves += [fetch(att, att_out), fetch(lse, lse_out), fetch(scaled, scaled_out)]
    wait_all(out_c)
    saves.append(fetch(out_all, out_out))
    quarter = width // 4
    for k in range(4):
        cols = pl.ds(k * quarter, quarter)
        block = dot(scaled[...], out_all[:, :, :, :, :, cols].reshape(width, quarter))
        branch[:, cols] = block + vec[6:7, cols]

    def middles(k, carry):
        part = pl.ds(pl.multiple_of(k * step, step), step)
        post = centered(branch[part])[0]
        value = tok[part].astype(f32) + post * vec[1:2] + vec[7:8]
        middle[part] = value
        mid_all[y, x, c, part] = (centered(value)[0] * vec[2:3] + vec[8:9]).astype(low)
        return carry

    lax.fori_loop(0, rows // step, middles, 0, unroll=2)
    mid = Plane(sends, mid_all, (y, x, c), (to_x, to_y, to_c))
    mid.start_first(mid_all.at[y, x, c])
    mid.start_second(mid_all.at[y, x, c])
    branch_put = fetch(branch, branch_out)
    saves.append(fetch(middle, middle_out))

    def grads(yy, xx, cc):
        grad[yy, xx, cc] = dot(og_all[yy, xx, cc], fc2_all[...], NT)

    def fold(v):
        quarters = [v[:, k * (units // 4) : (k + 1) * (units // 4)] for k in range(4)]
        return (quarters[0] + quarters[1]) + (quarters[2] + quarters[3])

    def forward(yy, xx, cc):
        pre[...] = dot(mid_all[yy, xx, cc], fc1_all[...])

        def block(k, carry):
            part = pl.ds(pl.multiple_of(k * step, step), step)
            u = pre[part] + unit_ref[0:1]
            square = u * u
            th = jnp.tanh(u * (SQRT_2_PI + (SQRT_2_PI * 0.044715) * square))
            lift = 0.5 + 0.5 * th
            a = u * lift
            act[yy, xx, cc, part] = a
            bend = u * (2.0 * SQRT_2_PI + (6.0 * 0.044715 * SQRT_2_PI) * square)
            slope[yy, xx, cc, part] = lift + bend * (lift - lift * lift)
            gm = grad[yy, xx, cc, part] * unit_ref[1:2]
            for j, value in enumerate((a, a * a, gm, gm * a)):
                pre[part, j * (units // 4) : (j + 1) * (units // 4)] = fold(value)
            return carry

        lax.fori_loop(0, rows // step, block, 0)
        for j in range(4):
            folded = pre[:, j * (units // 4) : (j + 1) * (units // 4)]
            stats[yy, xx, cc, j : j + 1] = jnp.sum(folded.T, axis=0, keepdims=True)

    og.after_second()
    fc2_in.wait()
    fc2_far.wait_recv()
    near = fc2_all.at[:, pl.ds(pl.multiple_of(others[1] * width2, width2), width2)]
    fc2_last = sends.start(near, near, pair_peer)
    fc2_near.wait_recv()
    og.after_third()
    fc1_in.wait()
    mid.after_first()
    fc2_last.wait_recv()
    og_in.wait()
    grads(y, x, c)
    wait_all(og.core)
    grads(y, x, 1 - c)
    grads(y, 1 - x, c)
    grads(1 - y, x, c)
    mid.after_second()
    wait_all(og.side)
    grads(y, 1 - x, 1 - c)
    grads(1 - y, x, 1 - c)
    grads(1 - y, 1 - x, c)
    wait_all(og.last)
    grads(1 - y, 1 - x, 1 - c)
    wait_all(fc1_z)
    forward(y, x, c)
    wait_all(mid.core)
    forward(y, x, 1 - c)
    forward(y, 1 - x, c)
    forward(1 - y, x, c)
    wait_all(mid.side)
    forward(y, 1 - x, 1 - c)
    forward(1 - y, x, 1 - c)
    mid.after_third()
    forward(1 - y, 1 - x, c)
    wait_all(mid.last)
    forward(1 - y, 1 - x, 1 - c)

    sends.start(stats, got.at[3], to_c).wait_recv()
    pair[...] = stats[...] + got[3]
    wait_all([sends.start(pair, got.at[k], to) for k, to in enumerate((to_x, to_y, to_xy))])
    total = (pair[...] + got[0]) + (got[1] + got[2])
    total = total * (1.0 / (units * 8))
    center, square = total[:, :, :, 0:1], total[:, :, :, 1:2]
    mean, cross = total[:, :, :, 2:3], total[:, :, :, 3:4]
    inverse = lax.rsqrt(square - center * center + EPS)
    totals[:, :, :, 0:1] = inverse
    totals[:, :, :, 1:2] = -center * inverse
    totals[:, :, :, 2:3] = inverse * mean
    totals[:, :, :, 3:4] = inverse * (inverse * (cross - center * mean))
    unit_out[...] = jnp.zeros_like(unit_out)

    def backward(yy, xx, cc):
        for j in range(4):
            spread = jnp.broadcast_to(totals[yy, xx, cc, j : j + 1], (128, rows))
            pre[:, j * 128 : (j + 1) * 128] = spread.T

        def block(k, carry):
            part = pl.ds(pl.multiple_of(k * step, step), step)

            def across(j):
                return jnp.concatenate([pre[part, j * 128 : (j + 1) * 128]] * (units // 128), axis=1)

            g = grad[yy, xx, cc, part]
            inverse = across(0)
            normed = act[yy, xx, cc, part] * inverse + across(1)
            gain = unit_ref[1:2]
            hidden[yy, xx, cc, part] = (normed * gain + unit_ref[2:3]).astype(low)
            back = g * gain * inverse - across(2) - normed * across(3)
            value = (back * slope[yy, xx, cc, part]).astype(low)
            grad_pre[yy, xx, cc, part] = value
            return (
                carry[0] + eights(g * normed),
                carry[1] + eights(value.astype(f32)),
                carry[2] + eights(g),
            )

        zero = jnp.zeros((8, units), f32)
        parts = lax.fori_loop(0, rows // step, block, (zero, zero, zero))
        for j, part in enumerate(parts):
            unit_out[j : j + 1] += jnp.sum(part, axis=0, keepdims=True)
        return dot(grad_pre[yy, xx, cc], fc1_all[...], NT)

    left, right = pl.ds(0, width // 2), pl.ds(width // 2, width // 2)
    order = [(1 - y, 1 - x), (y, 1 - x), (1 - y, x), (y, x)]
    stage_x, stage_y, cores = [], [], []

    def to_core(k):
        yy, xx = order[k]
        mid_part[yy, xx] = backward(yy, xx, 1 - c).astype(low)
        cores.append(sends.start(mid_part.at[yy, xx], from_core.at[yy, xx], to_c))

    def from_pair(k):
        yy, xx = order[k]
        block = backward(yy, xx, c)
        cores[k].wait_recv()
        sums[yy, xx] = (block + from_core[yy, xx].astype(f32)).astype(low)
        if k in (0, 1):
            stage_x.append(sends.start(sums.at[yy, xx, :, left], from_one.at[yy, :, left], to_x))
        if k in (0, 2):
            stage_y.append(sends.start(sums.at[yy, xx, :, right], from_one.at[xx, :, right], to_y))

    to_core(0)
    to_core(1)
    from_pair(0)
    to_core(2)
    from_pair(1)
    to_core(3)
    from_pair(2)
    from_pair(3)

    def ffn_of(yy, xx, cc):
        return dot(hidden[yy, xx, cc], fc2_all[...])

    blocks = nz
    size = width // blocks

    early = fc1_part.shape[-1]
    soon, late = slice(0, early), slice(early, units)

    def fc1_block(which, cols):
        part = pl.ds(pl.multiple_of(which * size, 128), size)
        block = jnp.zeros((size, cols.stop - cols.start), f32)
        for j in range(8):
            yxc = (j // 4, (j // 2) % 2, j % 2)
            block = block + dot(mid_all[(*yxc, slice(None), part)], grad_pre[(*yxc, slice(None), cols)], TN)
        return block

    fc1_far = {}
    for k in (1, 0, 2):
        fc1_part[k] = fc1_block(others[k], soon).astype(low)
        fc1_far[k] = sends.start(fc1_part.at[k], fc1_got.at[k], peers[k])
    wait_all((stage_x[0], stage_y[0]))
    sums[1 - y, x, :, left] = add_low(sums[1 - y, x, :, left], from_one[1 - y, :, left])
    sums[y, 1 - x, :, right] = add_low(sums[y, 1 - x, :, right], from_one[1 - x, :, right])
    last_y = sends.start(sums.at[1 - y, x, :, left], from_two.at[:, left], to_y)
    last_x = sends.start(sums.at[y, 1 - x, :, right], from_two.at[:, right], to_x)
    fc1_out[:, soon] = fc1_block(z, soon)
    fc1_out[:, late] = fc1_block(z, late)

    def late_block(k, carry):
        part = pl.ds(pl.multiple_of(k * size, 128), size)
        late_part[part] = fc1_block(k, late).astype(low)
        return carry

    lax.fori_loop(0, blocks, late_block, 0)
    saves.append(fetch(late_part, late_out))
    cores = []
    for yy, xx in order:
        f_part[yy, xx] = ffn_of(yy, xx, 1 - c).astype(low)
        cores.append(sends.start(f_part.at[yy, xx], f_core.at[yy, xx], to_c))
    for k, (yy, xx) in enumerate(order):
        block = ffn_of(yy, xx, c)
        cores[k].wait_recv()
        f_sums[yy, xx] = (block + f_core[yy, xx].astype(f32)).astype(low)
    saves.append(fetch(f_sums, ffn_out))
    top = pl.ds(0, first_out.shape[1])
    out_x = sends.start(f_sums.at[:, 1 - x, top, left], first_out.at[:, :, left], to_x)
    out_y = sends.start(f_sums.at[1 - y, :, top, right], first_out.at[:, :, right], to_y)

    def fc2_block(k, carry):
        part = pl.ds(pl.multiple_of(k * size, 128), size)
        block = jnp.zeros((units, size), f32)
        for j in range(8):
            yxc = (j // 4, (j // 2) % 2, j % 2)
            block = block + dot(hidden[yxc], og_all[(*yxc, slice(None), part)], TN)
        fc2_part[:, part] = block.astype(low)
        return carry

    lax.fori_loop(0, blocks, fc2_block, 0)
    saves.append(fetch(fc2_part, fc2_out))
    branch_put.wait()
    wait_all((stage_x[1], stage_y[1], last_x, last_y))
    for cols, k in ((left, y), (right, x)):
        branch[:, cols] = (
            sums[y, x, :, cols].astype(f32)
            + from_one[k, :, cols].astype(f32)
            + from_two[:, cols].astype(f32)
        )
        saves.append(fetch(branch.at[:, cols], gnm_out.at[:, cols]))
    for k in range(nz - 1):
        fc1_far[k].wait_recv()
        fc1_out[:, soon] += fc1_got[k].astype(f32)
    wait_all((out_x, out_y))
    for copy in saves:
        copy.wait()
    sends.finish()


def fore(nz, tokens, og, doc_lengths, w_qkv, w_out, gains, biases, scale, fc1, fc2, gain, shift):
    rows, width = tokens.shape
    share, units = w_qkv.shape[0], fc1.shape[1]
    low, f32, plane, every = jnp.bfloat16, jnp.float32, (2, 2, 2), (nz, 2, 2, 2)
    sds, vm = jax.ShapeDtypeStruct, pltpu.VMEM
    count = 160
    smem = pl.BlockSpec(memory_space=pltpu.SMEM)
    shapes = (
        (every + w_qkv.shape, low),
        (every + w_out.shape, low),
        ((16, width), f32),
        ((rows, w_qkv.shape[1]), low),
        ((rows, width), f32),
        ((rows, 128), f32),
        ((rows, width), f32),
        ((rows, width), f32),
        ((rows, width), low),
        ((rows, width), low),
        ((2, 2, rows, width), low),
        ((2, rows // 4, width), low),
        ((units, width), low),
        ((width, units - 3 * units // 4), low),
        ((rows, width), f32),
        (fc1.shape, f32),
        ((8, units), f32),
    )
    return pl.pallas_call(
        functools.partial(fore_kernel, nz),
        name="fore",
        out_shape=tuple(sds(shape, kind) for shape, kind in shapes),
        in_specs=[ANY] * 4 + [IN_VMEM] * 2 + [ANY] * 2 + [IN_VMEM] * 2 + [smem] * 2,
        out_specs=[ANY] * 15 + [IN_VMEM] * 2,
        scratch_shapes=[
            vm(every + w_qkv.shape, low),
            vm(every + w_out.shape, low),
            vm(every + (share, 128), f32),
            vm((share, 128), f32),
            vm((128, 128), f32),
            vm((8, units), f32),
            vm((width, units), low),
            vm((units, width), low),
            vm(plane + (rows, width), low),
            vm((rows, width), low),
            vm((rows, width), f32),
            vm((rows, width), low),
            vm((rows, w_qkv.shape[1]), low),
            vm((rows, width), f32),
            vm((rows, 128), f32),
            vm((rows, width), low),
            vm((rows, width), f32),
            vm((rows, rows), f32),
            vm((16, width), f32),
            vm(plane + (rows, width), low),
            vm(plane + (rows, units), f32),
            vm(plane + (rows, units), f32),
            vm(plane + (rows, units), f32),
            vm(plane + (rows, units), low),
            vm(plane + (rows, units), low),
            vm((2, 2, rows, width), low),
            vm((rows, units), f32),
            vm(plane + (4, rows), f32),
            vm(plane + (4, rows), f32),
            vm((4,) + plane + (4, rows), f32),
            vm(plane + (4, rows), f32),
            vm((2, 2, rows, width), low),
            vm((2, 2, rows, width), low),
            vm((2, rows, width), low),
            vm((rows, width), low),
            vm((2, 2, rows, width), low),
            vm((2, 2, rows, width), low),
            vm((2, 2, rows, width), low),
            vm((nz - 1, fc1.shape[0], 3 * units // 4), low),
            vm((width, units - 3 * units // 4), low),
            vm((units, width), low),
            vm((nz - 1, fc1.shape[0], 3 * units // 4), low),
            pltpu.SemaphoreType.DMA((40,)),
            pltpu.SemaphoreType.DMA((count,)),
            pltpu.SemaphoreType.DMA((count,)),
        ],
        compiler_params=pltpu.CompilerParams(
            collective_id=1, has_side_effects=True, vmem_limit_bytes=63 * 2**20
        ),
    )(tokens, og, w_qkv, w_out, gains.T, biases.T, fc1, fc2, gain, shift, doc_lengths, scale)


def back_kernel(
    nz,
    gnm_in,
    ffn_ref,
    first_in,
    late_ref,
    own1_in,
    fc2_ref,
    unit_ref,
    proj_in,
    att_in,
    lse_in,
    branch_in,
    middle_in,
    scaled_in,
    nin_in,
    qkv_in,
    out_in,
    vec_ref,
    og_in,
    tok_in,
    doc_ref,
    mixed_out,
    token_out,
    weight_out,
    gains_out,
    biases_out,
    scale_out,
    fc1_out,
    fc2_out,
    unit_out,
    f_sums,
    f_one,
    f_two,
    got1,
    got2,
    got_unit,
    w_part,
    w_core,
    w_sums,
    w_one,
    w_two,
    w_far,
    gpost,
    gmid,
    gatt,
    gni,
    dproj,
    nin_t,
    mask,
    accs,
    small,
    small_far,
    small_y,
    small_half,
    small_got,
    turned,
    mixed_at,
    weight_at,
    fc1_at,
    fc2_at,
    gnm_ref,
    proj_ref,
    att_ref,
    lse_ref,
    branch_ref,
    middle_ref,
    scaled_ref,
    nin_ref,
    qkv_ref,
    out_ref,
    og_ref,
    tok_ref,
    local_sems,
    send_sems,
    recv_sems,
):
    z, y, x, c = place()
    to_x, to_y, to_c = at(z, y, 1 - x, c), at(z, 1 - y, x, c), at(z, y, x, 1 - c)
    to_xy = at(z, 1 - y, 1 - x, c)
    others = [lax.rem(z + k, nz) for k in range(1, nz)]
    peers = [at(other, y, x, c) for other in others]
    locals_ = []

    def fetch(src, dst):
        copy = pltpu.make_async_copy(src, dst, local_sems.at[len(locals_)])
        copy.start()
        locals_.append(copy)
        return copy

    middle_got = fetch(middle_in, middle_ref)
    gnm_got = fetch(gnm_in, gnm_ref)
    og_got = fetch(og_in, og_ref)
    branch_got = fetch(branch_in, branch_ref)
    top, half = pl.ds(0, first_in.shape[1]), first_in.shape[2] // 2
    first_got = [
        fetch(first_in.at[:, :, pl.ds(i * half, half)], f_one.at[i, :, top, pl.ds(i * half, half)])
        for i in range(2)
    ]
    ffn_got = fetch(ffn_ref, f_sums)
    out_got = fetch(out_in, out_ref)
    att_got = fetch(att_in, att_ref)
    scaled_got = fetch(scaled_in, scaled_ref)
    nin_got = fetch(nin_in, nin_ref)
    proj_got = fetch(proj_in, proj_ref)
    lse_got = fetch(lse_in, lse_ref)
    qkv_got = fetch(qkv_in, qkv_ref)
    tok_got = fetch(tok_in, tok_ref)

    greet([to_x, to_y, to_c, to_xy] + peers)
    sends = Sends(send_sems, recv_sems)
    rows, width = middle_ref.shape
    low = jnp.bfloat16
    f32 = jnp.float32
    share = weight_out.shape[0]
    width1, width2 = fc1_out.shape[0], fc2_out.shape[1]

    pieces = 4
    parts = [pl.ds(k * (rows // pieces), rows // pieces) for k in range(pieces)]
    left, right = pl.ds(0, width // 2), pl.ds(width // 2, width // 2)
    def block1(which):
        return late_ref.at[pl.ds(pl.multiple_of(which * width1, width1), width1)]

    def block2(which):
        return fc2_ref.at[:, pl.ds(pl.multiple_of(which * width2, width2), width2)]

    own1_got = fetch(own1_in, fc1_at)
    own2_got = fetch(block2(z), got2.at[nz - 1])
    far = []
    for k, peer in enumerate(peers):
        far.append(sends.start(unit_ref, got_unit.at[k], peer))
        far.append(sends.start(block1(others[k]), got1.at[k], peer))
        far.append(sends.start(block2(others[k]), got2.at[k], peer))

    f_first, f_second = [], []

    def ffn_one(k):
        part = parts[k]
        f_first.append(
            (
                sends.start(ffn_ref.at[:, 1 - x, part, left], f_one.at[0, :, part, left], to_x),
                sends.start(ffn_ref.at[1 - y, :, part, right], f_one.at[1, :, part, right], to_y),
            )
        )

    def ffn_two(k):
        part = parts[k]
        if k == 0:
            ffn_got.wait()
            for copy in first_got:
                copy.wait()
        else:
            for copy in f_first[k - 1]:
                copy.wait_recv()
        f_sums[1 - y, x, part, left] = add_low(
            f_sums[1 - y, x, part, left], f_one[0, 1 - y, part, left]
        )
        f_sums[y, 1 - x, part, right] = add_low(
            f_sums[y, 1 - x, part, right], f_one[1, 1 - x, part, right]
        )
        f_second.append(
            (
                sends.start(f_sums.at[1 - y, x, part, left], f_two.at[part, left], to_y),
                sends.start(f_sums.at[y, 1 - x, part, right], f_two.at[part, right], to_x),
            )
        )

    def ffn_three(k):
        part = parts[k]
        for copy in f_second[k]:
            copy.wait_recv()
        for i, (cols, at_) in enumerate(((left, y), (right, x))):
            total = (
                f_sums[y, x, part, cols].astype(f32)
                + f_one[i, at_, part, cols].astype(f32)
                + f_two[part, cols].astype(f32)
            )
            mixed_at[part, cols] = (
                middle_ref[part, cols] + total + vec_ref[9:10, cols]
            ).astype(low)
        puts.append(fetch(mixed_at.at[part], mixed_out.at[part]))

    spans = [(0, width)] + [(width + g * 3 * width // 4, 3 * width // 4) for g in range(4)]
    w_first, w_second, w_third, w_c = {}, {}, {}, {}

    def sides(j):
        start, size = spans[j]
        return pl.ds(start, size), pl.ds(start, size // 2), pl.ds(start + size // 2, size // 2)

    def w_zero(j):
        every = sides(j)[0]
        w_c[j] = sends.start(w_part.at[:, :, :, 1 - c, :, every], w_core.at[..., every], to_c)

    def w_step1(j):
        every, lo, hi = sides(j)
        w_c[j].wait_recv()

        def one(which, carry):
            for yy in range(2):
                for xx in range(2):
                    w_sums[which, yy, xx, :, every] = add_low(
                        w_part[which, yy, xx, c, :, every], w_core[which, yy, xx, :, every]
                    )
            return carry

        lax.fori_loop(0, nz, one, 0)
        w_first[j] = (
            sends.start(w_sums.at[:, :, 1 - x, :, lo], w_one.at[:, :, :, lo], to_x),
            sends.start(w_sums.at[:, 1 - y, :, :, hi], w_one.at[:, :, :, hi], to_y),
        )

    def w_step2(j):
        every, lo, hi = sides(j)
        for copy in w_first[j]:
            copy.wait_recv()

        def one(which, carry):
            for k in range(2):
                w_sums[which, k, x, :, lo] = add_low(
                    w_sums[which, k, x, :, lo], w_one[which, k, :, lo]
                )
                w_sums[which, y, k, :, hi] = add_low(
                    w_sums[which, y, k, :, hi], w_one[which, k, :, hi]
                )
            return carry

        lax.fori_loop(0, nz, one, 0)
        w_second[j] = (
            sends.start(w_sums.at[:, 1 - y, x, :, lo], w_two.at[:, :, lo], to_y),
            sends.start(w_sums.at[:, y, 1 - x, :, hi], w_two.at[:, :, hi], to_x),
        )

    def w_step3(j):
        every = sides(j)[0]
        for copy in w_second[j]:
            copy.wait_recv()
        for which in range(nz):
            w_sums[which, y, x, :, every] = add_low(
                w_sums[which, y, x, :, every], w_two[which, :, every]
            )
        w_third[j] = [
            sends.start(w_sums.at[others[k], y, x, :, every], w_far.at[k, :, every], peer)
            for k, peer in enumerate(peers)
        ]

    def w_step4(j):
        start, size = spans[j]
        every = sides(j)[0]
        total = w_sums[z, y, x, :, every].astype(f32)
        for k in range(nz - 1):
            w_third[j][k].wait_recv()
            total = total + w_far[k, :, every].astype(f32)
        if j == 0:
            weight_at[:, 3 * width :] = total
            spots = [pl.ds(3 * width, width)]
        else:
            third = size // 3
            spots = [pl.ds(i * width + (j - 1) * third, third) for i in range(3)]
            for i, spot in enumerate(spots):
                weight_at[:, spot] = total[:, i * third : (i + 1) * third]
        for spot in spots:
            puts.append(fetch(weight_at.at[:, spot], weight_out.at[:, spot]))

    ffn_one(1)
    ffn_two(0)
    accs[...] = jnp.zeros_like(accs)
    step = 32

    def norms(k, carry):
        part = pl.ds(pl.multiple_of(k * step, step), step)
        normed_two, inverse_two = centered(middle_ref[part])
        grad = gnm_ref[part]
        og = og_ref[part].astype(f32)
        grad_middle = og + centered_back(grad * vec_ref[2:3], normed_two, inverse_two)
        accs[2] += eights(grad * normed_two)
        accs[8] += eights(grad)
        accs[9] += eights(og)
        normed_post, inverse_post = centered(branch_ref[part])
        post = centered_back(grad_middle * vec_ref[1:2], normed_post, inverse_post).astype(low)
        accs[1] += eights(grad_middle * normed_post)
        accs[7] += eights(grad_middle)
        accs[6] += eights(post.astype(f32))
        gpost[part] = post
        gmid[part] = grad_middle
        return carry

    for copy in (middle_got, gnm_got, og_got, branch_got):
        copy.wait()
    lax.fori_loop(0, rows // step, norms, 0)
    quarter = width // 4

    def out_block(k, carry):
        part = pl.ds(pl.multiple_of(k * (width // nz), width // nz), width // nz)
        block = dot(scaled_ref[:, part], gpost[...], TN).astype(low)
        w_part[k, :, :, :, :, pl.ds(0, width)] = block.reshape(2, 2, 2, share, width)
        return carry

    scaled_got.wait()
    lax.fori_loop(0, nz, out_block, 0)
    w_zero(0)
    mask[...] = doc_mask(doc_ref, rows)

    def scaled_block(k, carry):
        part = pl.ds(pl.multiple_of(k * quarter, quarter), quarter)
        block = dot(gpost[...], out_ref[part], NT)
        accs[10, :, part] = eights(block * att_ref[:, part])
        gatt[:, part] = (block * vec_ref[10:11, part]).astype(low)
        return carry

    out_got.wait()
    att_got.wait()
    lax.fori_loop(0, 4, scaled_block, 0)

    nin_got.wait()
    nin_t[...] = nin_ref[...].T
    proj_got.wait()
    lse_got.wait()
    head = 64
    lane = lax.broadcasted_iota(jnp.int32, (1, 128), 1)
    is_low = lane < head
    factor = 1.0 / math.sqrt(head)
    lane_wide = lax.broadcasted_iota(jnp.int32, (rows, 128), 1)
    keep = (is_low.astype(low), (lane >= head).astype(low))

    def pair(p, carry):
        base = lax.div(p, 2) * (3 * quarter) + lax.rem(p, 2) * 128
        q_at = pl.ds(pl.multiple_of(base, 128), 128)
        k_at = pl.ds(pl.multiple_of(base + quarter, 128), 128)
        v_at = pl.ds(pl.multiple_of(base + 2 * quarter, 128), 128)
        here = pl.ds(pl.multiple_of(p * 128, 128), 128)
        q2, k2, v2, do2 = proj_ref[:, q_at], proj_ref[:, k_at], proj_ref[:, v_at], gatt[:, here]
        lses = lse_ref[...]
        found = []
        for i in range(2):
            scores = dot(q2 * keep[i], k2, NT) * factor
            scores = jnp.where(mask[...] > 0, scores, NEGATIVE)
            lse = jnp.sum(jnp.where(lane_wide == 2 * p + i, lses, 0.0), axis=1, keepdims=True)
            prob = jnp.exp(scores - lse)
            grad_prob = dot(do2 * keep[i], v2, NT)
            inner = jnp.sum(prob * grad_prob, axis=1, keepdims=True)
            ds = (prob * (grad_prob - inner) * factor).astype(low)
            found.append(
                (dot(ds, k2), dot(ds, q2, TN), dot(prob.astype(low), do2, TN))
            )
        for where, a, b in zip((q_at, k_at, v_at), *found):
            dproj[:, where] = jnp.where(is_low, a, b).astype(low)
        accs[4, :, here] = eights(dproj[:, q_at].astype(f32))
        accs[5, :, here] = eights(dproj[:, v_at].astype(f32))
        return carry

    def wgrad(j):
        start, size = spans[j]
        cols = pl.ds((j - 1) * size, size)

        def one(k, carry):
            part = pl.ds(pl.multiple_of(k * (width // nz), width // nz), width // nz)
            block = dot(nin_t[part], dproj[:, cols]).astype(low)
            w_part[k, :, :, :, :, pl.ds(start, size)] = block.reshape(2, 2, 2, share, size)
            return carry

        lax.fori_loop(0, nz, one, 0)
        w_zero(j)

    def gni_block(k, carry):
        part = pl.ds(pl.multiple_of(k * quarter, quarter), quarter)
        gni[:, part] = dot(dproj[...], qkv_ref[part], NT)
        return carry

    def tokens_back(k, carry):
        part = pl.ds(pl.multiple_of(k * step, step), step)
        normed, inverse = centered(tok_ref[part].astype(f32))
        grad = gni[part]
        gmid[part] = gmid[part] + centered_back(grad * vec_ref[0:1], normed, inverse)
        accs[0] += eights(grad * normed)
        accs[3] += eights(grad)
        return carry

    part_z = width // nz
    chain = {}

    def lanes(which):
        return pl.ds(pl.multiple_of(which * part_z, 128), part_z)

    def small_start():
        for j in range(16):
            small[j : j + 1] = jnp.sum(accs[j], axis=0, keepdims=True)
        spot = lax.broadcasted_iota(jnp.int32, (1, width), 1)
        tile = jnp.zeros((1, 128), f32)
        for h in range(HEADS):
            inside = jnp.logical_and(spot >= h * head, spot < (h + 1) * head)
            found = jnp.sum(jnp.where(inside, small[10:11], 0.0), axis=1, keepdims=True)
            tile = jnp.where(lane == h, found, tile)
        small[11:12] = jnp.concatenate([tile] * (width // 128), axis=1)
        chain["z"] = [
            sends.start(small.at[:, lanes(others[k])], small_far.at[k], peer)
            for k, peer in enumerate(peers)
        ]

    def small_second():
        total = small[:, lanes(z)]
        for k in range(nz - 1):
            chain["z"][k].wait_recv()
            total = total + small_far[k]
        small_y[...] = total
        other = small_y.at[:, pl.ds(pl.multiple_of((1 - y) * 128, 128), 128)]
        chain["y"] = sends.start(other, small_got.at[0], to_y)

    def small_third():
        chain["y"].wait_recv()
        small_half[0] = small_y[:, pl.ds(pl.multiple_of(y * 128, 128), 128)] + small_got[0]
        chain["x"] = sends.start(small_half.at[0], small_got.at[1], to_x)

    def small_fourth():
        chain["x"].wait_recv()
        small_half[1] = small_half[0] + small_got[1]
        chain["c"] = sends.start(small_half.at[1], small_got.at[2], to_c)

    def small_last():
        chain["c"].wait_recv()
        total = small_half[1] + small_got[2]
        scale_out[...] = jnp.broadcast_to(total[11:12], (8, 128))
        ours = pl.ds(pl.multiple_of((2 * x + c) * share, share), share)
        turned[...] = jnp.concatenate([total, jnp.zeros((112, 128), f32)], axis=0).T
        mine = jnp.concatenate([turned[ours], jnp.zeros((128 - share, 128), f32)], axis=0).T
        gains_out[...] = mine[0:3, :share]
        biases_out[...] = mine[3:10, :share]

    puts = []

    def far_last():
        for copy in far:
            copy.wait_recv()
        own1_got.wait()
        own2_got.wait()
        late = pl.ds(fc1_at.shape[1] - got1.shape[2], got1.shape[2])
        own2, unit = got2[nz - 1].astype(f32), unit_ref[...]
        for k in range(nz - 1):
            fc1_at[:, late] += got1[k].astype(f32)
            own2 = own2 + got2[k].astype(f32)
            unit = unit + got_unit[k]
        fc2_at[...] = own2
        unit_out[...] = unit
        puts.append(fetch(fc1_at, fc1_out))
        puts.append(fetch(fc2_at, fc2_out))

    def pairs(first, last):
        lax.fori_loop(first, last, pair, 0)

    def gni_all():
        qkv_got.wait()
        lax.fori_loop(0, 4, gni_block, 0)

    def tokens_all():
        tok_got.wait()
        lax.fori_loop(0, rows // step, tokens_back, 0)
        puts.append(fetch(gmid, token_out))

    ffn_one(2)
    w_step1(0)
    pairs(0, 1)
    pairs(1, 2)
    wgrad(1)
    ffn_two(1)
    pairs(2, 3)
    w_step1(1)
    ffn_two(2)
    pairs(3, 4)
    wgrad(2)
    w_step2(0)
    pairs(4, 5)
    w_step1(2)
    pairs(5, 6)
    wgrad(3)
    w_step2(1)
    w_step3(0)
    pairs(6, 7)
    w_step1(3)
    pairs(7, 8)
    wgrad(4)
    w_step2(2)
    gni_all()
    w_step3(1)
    w_step1(4)
    tokens_all()
    small_start()
    w_step2(3)
    w_step3(2)
    small_second()
    w_step2(4)
    ffn_one(3)
    w_step3(3)
    small_third()
    ffn_three(0)
    ffn_three(1)
    ffn_three(2)
    w_step4(0)
    w_step3(4)
    ffn_two(3)
    small_fourth()
    small_last()
    w_step4(1)
    w_step4(2)
    w_step4(3)
    far_last()
    ffn_three(3)
    w_step4(4)
    for put in puts:
        put.wait()
    sends.finish()


def back(nz, *operands):
    gnm, ffn_part, ffn_first, late, fc1, fc2, unit, proj, att, lse, branch = operands[:11]
    middle, scaled, nin, qkv, out, vec = operands[11:17]
    rows, width = middle.shape
    share = width // (nz * 8)
    columns = proj.shape[1] + width
    low, f32 = jnp.bfloat16, jnp.float32
    sds = jax.ShapeDtypeStruct
    fc2_own = (fc2.shape[0], fc2.shape[1] // nz)
    count = 96 + 8 * nz
    specs = [ANY] * 6 + [IN_VMEM] + [ANY] * 9 + [IN_VMEM] + [ANY] * 2
    specs.append(pl.BlockSpec(memory_space=pltpu.SMEM))
    return pl.pallas_call(
        functools.partial(back_kernel, nz),
        name="back",
        out_shape=(
            sds((rows, width), low),
            sds((rows, width), f32),
            sds((share, columns), f32),
            sds((3, share), f32),
            sds((7, share), f32),
            sds((8, 128), f32),
            sds(fc1.shape, f32),
            sds(fc2_own, f32),
            sds(unit.shape, f32),
        ),
        in_specs=specs,
        out_specs=[ANY] * 3 + [IN_VMEM] * 3 + [ANY] * 2 + [IN_VMEM],
        scratch_shapes=[
            pltpu.VMEM((2, 2, rows, width), low),
            pltpu.VMEM((2, 2, rows, width), low),
            pltpu.VMEM((rows, width), low),
            pltpu.VMEM((nz - 1, fc1.shape[0], late.shape[1]), low),
            pltpu.VMEM((nz,) + fc2_own, low),
            pltpu.VMEM((nz - 1,) + unit.shape, f32),
            pltpu.VMEM((nz, 2, 2, 2, share, columns), low),
            pltpu.VMEM((nz, 2, 2, share, columns), low),
            pltpu.VMEM((nz, 2, 2, share, columns), low),
            pltpu.VMEM((nz, 2, share, columns), low),
            pltpu.VMEM((nz, share, columns), low),
            pltpu.VMEM((nz - 1, share, columns), low),
            pltpu.VMEM((rows, width), low),
            pltpu.VMEM((rows, width), f32),
            pltpu.VMEM((rows, width), low),
            pltpu.VMEM((rows, width), f32),
            pltpu.VMEM((rows, 3 * width), low),
            pltpu.VMEM((width, rows), low),
            pltpu.VMEM((rows, rows), f32),
            pltpu.VMEM((16, 8, width), f32),
            pltpu.VMEM((16, width), f32),
            pltpu.VMEM((nz - 1, 16, width // nz), f32),
            pltpu.VMEM((16, width // nz), f32),
            pltpu.VMEM((3, 16, 128), f32),
            pltpu.VMEM((3, 16, 128), f32),
            pltpu.VMEM((128, 128), f32),
            pltpu.VMEM((rows, width), low),
            pltpu.VMEM((share, columns), f32),
            pltpu.VMEM(fc1.shape, f32),
            pltpu.VMEM(fc2_own, f32),
            pltpu.VMEM((rows, width), f32),
            pltpu.VMEM(proj.shape, low),
            pltpu.VMEM((rows, width), f32),
            pltpu.VMEM(lse.shape, f32),
            pltpu.VMEM((rows, width), f32),
            pltpu.VMEM((rows, width), f32),
            pltpu.VMEM((rows, width), low),
            pltpu.VMEM((rows, width), low),
            pltpu.VMEM(qkv.shape, low),
            pltpu.VMEM(out.shape, low),
            pltpu.VMEM((rows, width), low),
            pltpu.VMEM((rows, width), low),
            pltpu.SemaphoreType.DMA((64,)),
            pltpu.SemaphoreType.DMA((count,)),
            pltpu.SemaphoreType.DMA((count,)),
        ],
        compiler_params=pltpu.CompilerParams(
            collective_id=3, has_side_effects=True, vmem_limit_bytes=63 * 2**20
        ),
    )(*operands)


def finish_kernel(
    mixed,
    token,
    weight,
    fc1,
    fc2,
    gains,
    biases,
    scale,
    unit,
    mixed_out,
    token_out,
    qkv_out,
    out_out,
    fc1_out,
    fc2_out,
    gains_out,
    biases_out,
    scale_out,
    gain_out,
    shift_out,
    mixed_at,
    token_at,
    weight_at,
    fc1_at,
    fc2_at,
    in_sems,
    out_sems,
):
    columns = qkv_out.shape[1]
    moves = (
        (token, token_at, ((token_at, token_out),)),
        (
            weight,
            weight_at,
            (
                (weight_at.at[:, pl.ds(0, columns)], qkv_out),
                (weight_at.at[:, pl.ds(columns, out_out.shape[1])], out_out),
            ),
        ),
        (mixed, mixed_at, ((mixed_at, mixed_out),)),
        (fc1, fc1_at, ((fc1_at, fc1_out),)),
        (fc2, fc2_at, ((fc2_at, fc2_out),)),
    )
    reads, writes = [], []
    for k, (src, here, _) in enumerate(moves):
        reads.append(pltpu.make_async_copy(src, here, in_sems.at[k]))
        reads[-1].start()
    gains_out[...] = gains[...]
    biases_out[...] = biases[...]
    scale_out[...] = scale[0:1, : scale_out.shape[1]]
    gain_out[...] = unit[0:1]
    shift_out[0:1] = unit[1:2]
    shift_out[1:2] = unit[2:3]
    for read, (_, _, outs) in zip(reads, moves):
        read.wait()
        for src, dst in outs:
            writes.append(pltpu.make_async_copy(src, dst, out_sems.at[len(writes)]))
            writes[-1].start()
    for write in writes:
        write.wait()


def finish(mixed, token, weight, gains, biases, scale, fc1, fc2, unit):
    share, columns = weight.shape
    width, units = token.shape[1], unit.shape[1]
    f32 = jnp.float32
    shapes = (
        (mixed.shape, mixed.dtype),
        (token.shape, f32),
        ((share, columns - width), f32),
        ((share, width), f32),
        (fc1.shape, f32),
        (fc2.shape, f32),
        (gains.shape, f32),
        (biases.shape, f32),
        ((1, HEADS), f32),
        ((1, units), f32),
        ((2, units), f32),
    )
    return pl.pallas_call(
        finish_kernel,
        name="finish",
        out_shape=tuple(jax.ShapeDtypeStruct(shape, kind) for shape, kind in shapes),
        in_specs=[ANY] * 5 + [IN_VMEM] * 4,
        out_specs=[ANY] * 6 + [IN_VMEM] * 5,
        scratch_shapes=[
            pltpu.VMEM(mixed.shape, mixed.dtype),
            pltpu.VMEM(token.shape, f32),
            pltpu.VMEM(weight.shape, f32),
            pltpu.VMEM(fc1.shape, f32),
            pltpu.VMEM(fc2.shape, f32),
            pltpu.SemaphoreType.DMA((5,)),
            pltpu.SemaphoreType.DMA((6,)),
        ],
        compiler_params=pltpu.CompilerParams(vmem_limit_bytes=63 * 2**20),
    )(mixed, token, weight, fc1, fc2, gains, biases, scale, unit)


def fused(
    nz,
    tokens,
    out_grad,
    doc_lengths,
    w_qkv,
    w_out,
    gains,
    biases,
    head_scale,
    w_fc1,
    w_fc2,
    mid_gain,
    ffn_biases,
):
    (
        qkv_full,
        out_full,
        vec,
        proj,
        att,
        lse,
        branch,
        middle,
        nin,
        scaled,
        ffn_part,
        ffn_first,
        fc2_part,
        fc1_late,
        gnm,
        fc1_own,
        unit_sums,
    ) = fore(
        nz,
        tokens,
        out_grad,
        doc_lengths,
        w_qkv,
        w_out,
        gains,
        biases,
        head_scale,
        w_fc1,
        w_fc2,
        mid_gain[None],
        ffn_biases,
    )
    model_width = tokens.shape[1]
    (
        mixed,
        token_grad,
        weight_grad,
        gains_grad,
        biases_grad,
        scale,
        fc1_grad,
        fc2_grad,
        unit_sums,
    ) = back(
        nz,
        gnm,
        ffn_part,
        ffn_first,
        fc1_late,
        fc1_own,
        fc2_part,
        unit_sums,
        proj,
        att,
        lse,
        branch,
        middle,
        scaled,
        nin,
        qkv_full.reshape(model_width, -1),
        out_full.reshape(model_width, -1),
        vec,
        out_grad,
        tokens,
        doc_lengths,
    )
    mixed, token_grad, qkv, out, fc1, fc2, gains_grad, biases_grad, scale, gain, shift = finish(
        mixed,
        token_grad,
        weight_grad,
        gains_grad,
        biases_grad,
        scale,
        fc1_grad,
        fc2_grad,
        unit_sums,
    )
    return (
        mixed,
        token_grad,
        qkv,
        out,
        gains_grad.T,
        biases_grad.T,
        scale[0],
        fc1,
        fc2,
        gain[0],
        shift,
    )


def layer(nz, nt, tokens, out_grad, doc_lengths, w_qkv, *rest):
    if nz == 4 and nt == 8 and w_qkv.shape[0] % 16 == 0:
        return fused(nz, tokens, out_grad, doc_lengths, w_qkv, *rest)
    return plain(tokens, out_grad, doc_lengths, w_qkv, *rest)


def solution(mesh):
    return jax.shard_map(
        functools.partial(layer, mesh.shape["dp"], mesh.shape["tensor"]),
        mesh=mesh,
        in_specs=(
            P(("dp", "tensor"), None),
            P(("dp", "tensor"), None),
            P(("dp", "tensor"), None),
            P(("dp", "tensor"), None),
            P(("dp", "tensor"), None),
            P(("dp", "tensor"), None),
            P(("dp", "tensor"), None),
            P(),
            P("dp", "tensor"),
            P("tensor", "dp"),
            P("tensor"),
            P(None, "tensor"),
        ),
        out_specs=(
            P(("dp", "tensor"), None),
            P(("dp", "tensor"), None),
            P(("dp", "tensor"), None),
            P(("dp", "tensor"), None),
            P(("dp", "tensor"), None),
            P(("dp", "tensor"), None),
            P(),
            P("dp", "tensor"),
            P("tensor", "dp"),
            P("tensor"),
            P(None, "tensor"),
        ),
        check_vma=False,
    )
```

```python
import functools
import math

import jax
import jax.numpy as jnp
from jax import lax
from jax.experimental import pallas as pl
from jax.experimental.pallas import tpu as pltpu
from jax.sharding import PartitionSpec as P

HEADS = 16
FF = 4096


EPS = 1e-05
NEGATIVE = -1000000000.0


def normalize(values):
    center = jnp.mean(values, axis=-1, keepdims=True)
    spread = jnp.mean(values * values, axis=-1, keepdims=True) - center * center
    inverse = lax.rsqrt(spread + EPS)
    return ((values - center) * inverse, inverse)


def normalize_back(grad_normed, normed, inverse):
    first_mean = jnp.mean(grad_normed, axis=-1, keepdims=True)
    second = jnp.mean(grad_normed * normed, axis=-1, keepdims=True)
    return inverse * (grad_normed - first_mean - normed * second)


def block_scores(query_rows, key_rows, doc_ids, row_first, row_last, factor):
    scores = (
        jnp.einsum("qhd,khd->hqk", query_rows, key_rows, preferred_element_type=jnp.float32)
        * factor
    )
    query_pos = jnp.arange(row_first, row_last)
    key_pos = jnp.arange(row_last)
    same_doc = doc_ids[row_first:row_last, None] == doc_ids[None, :row_last]
    allowed = jnp.logical_and(same_doc, key_pos[None, :] <= query_pos[:, None])
    return (jnp.where(allowed[None], scores, NEGATIVE), allowed)


def attend_forward(query_rows, key_rows, value_rows, doc_ids, factor):
    total_rows = query_rows.shape[0]
    block_rows = min(512, total_rows)
    scores, allowed = block_scores(query_rows, key_rows, doc_ids, 0, block_rows, factor)
    row_peak = jnp.max(scores, axis=-1, keepdims=True)
    exponent = jnp.exp(scores - row_peak)
    row_total = jnp.sum(exponent, axis=-1, keepdims=True)
    prob_low = (exponent / row_total).astype(jnp.bfloat16)
    pieces = jnp.einsum("hqk,khd->qhd", prob_low, value_rows, preferred_element_type=jnp.float32)
    sums_log = [row_peak + jnp.log(row_total)]
    return (pieces, sums_log)


def attend_backward(query_rows, key_rows, value_rows, grad_out, doc_ids, sums_log, factor):
    total_rows = query_rows.shape[0]
    block_rows = min(512, total_rows)
    query_parts = []
    grad_keys = jnp.zeros(key_rows.shape, jnp.float32)
    grad_values = jnp.zeros(value_rows.shape, jnp.float32)
    for block_index, row_first in enumerate(range(0, total_rows, block_rows)):
        row_last = row_first + block_rows
        scores, allowed = block_scores(query_rows, key_rows, doc_ids, row_first, row_last, factor)
        prob_rows = jnp.where(allowed[None], jnp.exp(scores - sums_log[block_index]), 0.0)
        prob_low = prob_rows.astype(jnp.bfloat16)
        grad_probs = jnp.einsum(
            "qhd,khd->hqk", grad_out, value_rows, preferred_element_type=jnp.float32
        )
        inner_sum = jnp.sum(prob_rows * grad_probs, axis=-1, keepdims=True)
        grad_scores = (prob_rows * (grad_probs - inner_sum) * factor).astype(jnp.bfloat16)
        query_parts.append(
            jnp.einsum("hqk,khd->qhd", grad_scores, key_rows, preferred_element_type=jnp.float32)
        )
        grad_keys = grad_keys.at[:row_last].add(
            jnp.einsum("hqk,qhd->khd", grad_scores, query_rows, preferred_element_type=jnp.float32)
        )
        grad_values = grad_values.at[:row_last].add(
            jnp.einsum("hqk,qhd->khd", prob_low, grad_out, preferred_element_type=jnp.float32)
        )
    return (query_parts[0], grad_keys, grad_values)


def plain(
    tokens,
    out_grad,
    doc_lengths,
    w_qkv,
    w_out,
    gains,
    biases,
    head_scale,
    w_fc1,
    w_fc2,
    mid_gain,
    ffn_biases,
):
    qkv_full, out_full, gain_full, bias_full = (
        lax.all_gather(w_qkv, ("dp", "tensor"), axis=0, tiled=True),
        lax.all_gather(w_out, ("dp", "tensor"), axis=0, tiled=True),
        lax.all_gather(gains.astype(jnp.bfloat16), ("dp", "tensor"), axis=0, tiled=True).astype(
            gains.dtype
        ),
        lax.all_gather(biases.astype(jnp.bfloat16), ("dp", "tensor"), axis=0, tiled=True).astype(
            biases.dtype
        ),
    )
    fc1_rows, fc2_cols = (
        lax.all_gather(w_fc1, "dp", axis=0, tiled=True),
        lax.all_gather(w_fc2, "dp", axis=1, tiled=True),
    )
    model_width = tokens.shape[1]
    local_rows = tokens.shape[0]
    head_dim = model_width // HEADS
    factor = 1.0 / math.sqrt(head_dim)
    doc_ends = jnp.cumsum(doc_lengths[0])[:-1]
    places = jnp.arange(local_rows)
    doc_ids = jnp.sum((places[:, None] >= doc_ends[None, :]).astype(jnp.int32), axis=1)
    inputs = tokens.astype(jnp.float32)
    normed_one, inverse_one = normalize(inputs)
    normed_in = (normed_one * gain_full[:, 0] + bias_full[:, 0]).astype(jnp.bfloat16)
    zero_bias = jnp.zeros((model_width,), jnp.float32)
    qkv_bias = jnp.concatenate([bias_full[:, 1], zero_bias, bias_full[:, 2]])
    projected = (
        jnp.dot(normed_in, qkv_full, preferred_element_type=jnp.float32) + qkv_bias
    ).astype(jnp.bfloat16)
    query_rows = projected[:, :model_width].reshape(local_rows, HEADS, head_dim)
    key_rows = projected[:, model_width : 2 * model_width].reshape(local_rows, HEADS, head_dim)
    value_rows = projected[:, 2 * model_width :].reshape(local_rows, HEADS, head_dim)
    attended, sums_log = attend_forward(query_rows, key_rows, value_rows, doc_ids, factor)
    attended = attended.reshape(local_rows, model_width)
    scale_wide = jnp.repeat(head_scale, head_dim)
    scaled = (attended * scale_wide).astype(jnp.bfloat16)
    branch = jnp.dot(scaled, out_full, preferred_element_type=jnp.float32) + bias_full[:, 3]
    normed_post, inverse_post = normalize(branch)
    middle = inputs + normed_post * gain_full[:, 1] + bias_full[:, 4]
    normed_two, inverse_two = normalize(middle)
    normed_mid = (normed_two * gain_full[:, 2] + bias_full[:, 5]).astype(jnp.bfloat16)
    gathered = lax.all_gather(normed_mid, "tensor", axis=0, tiled=True)
    hidden_pre = jnp.dot(gathered, fc1_rows, preferred_element_type=jnp.float32) + ffn_biases[0]
    activated, gelu_pull = jax.vjp(jax.nn.gelu, hidden_pre)
    act_sum, act_square = (
        lax.psum(jnp.sum(activated, axis=1).astype(jnp.bfloat16), "tensor").astype(jnp.float32),
        lax.psum(jnp.sum(activated * activated, axis=1).astype(jnp.bfloat16), "tensor").astype(
            jnp.float32
        ),
    )
    center = act_sum / FF
    inverse_mid = lax.rsqrt(act_square / FF - center * center + EPS)[:, None]
    normed_act = (activated - center[:, None]) * inverse_mid
    hidden = (normed_act * mid_gain + ffn_biases[1]).astype(jnp.bfloat16)
    hidden_rows = hidden
    ffn_out = lax.psum_scatter(
        jnp.dot(hidden_rows, fc2_cols, preferred_element_type=jnp.float32).astype(jnp.bfloat16),
        "tensor",
        scatter_dimension=0,
        tiled=True,
    ).astype(jnp.float32)
    shard_rows = lax.all_gather(out_grad, "tensor", axis=0, tiled=True)
    grad_piece = jnp.einsum("rd,fd->rf", shard_rows, fc2_cols, preferred_element_type=jnp.float32)
    hidden_rows = hidden
    fc2_run = jnp.einsum("rf,rd->fd", hidden_rows, shard_rows, preferred_element_type=jnp.float32)
    mid_gain_part = jnp.sum(grad_piece * normed_act, axis=0)
    mid_bias_part = jnp.sum(grad_piece, axis=0)
    grad_normed_act = grad_piece * mid_gain
    first_sum, second_sum = (
        lax.psum(jnp.sum(grad_normed_act, axis=1).astype(jnp.bfloat16), "tensor").astype(
            jnp.float32
        ),
        lax.psum(
            jnp.sum(grad_normed_act * normed_act, axis=1).astype(jnp.bfloat16), "tensor"
        ).astype(jnp.float32),
    )
    grad_act = inverse_mid * (
        grad_normed_act - first_sum[:, None] / FF - normed_act * (second_sum[:, None] / FF)
    )
    grad_pre = gelu_pull(grad_act)[0].astype(jnp.bfloat16)
    fc1_part = jnp.einsum("rd,rf->df", gathered, grad_pre, preferred_element_type=jnp.float32)
    fc1_bias_part = jnp.sum(grad_pre.astype(jnp.float32), axis=0)
    grad_normed_mid = lax.psum_scatter(
        jnp.einsum("rf,df->rd", grad_pre, fc1_rows, preferred_element_type=jnp.float32).astype(
            jnp.bfloat16
        ),
        "tensor",
        scatter_dimension=0,
        tiled=True,
    ).astype(jnp.float32)
    ffn_bias_part = jnp.stack([fc1_bias_part, mid_bias_part])
    fc1_grad, fc2_grad = (
        lax.psum_scatter(
            fc1_part.astype(jnp.bfloat16), "dp", scatter_dimension=0, tiled=True
        ).astype(jnp.float32),
        lax.psum_scatter(
            fc2_run.astype(jnp.bfloat16), "dp", scatter_dimension=1, tiled=True
        ).astype(jnp.float32),
    )
    mid_gain_grad, ffn_bias_grad = lax.psum((mid_gain_part, ffn_bias_part), "dp")
    mixed_out = (middle + ffn_out + bias_full[:, 6]).astype(jnp.bfloat16)
    final_grad = out_grad.astype(jnp.float32)
    grad_middle = final_grad + normalize_back(
        grad_normed_mid * gain_full[:, 2], normed_two, inverse_two
    )
    grad_post = normalize_back(grad_middle * gain_full[:, 1], normed_post, inverse_post).astype(
        jnp.bfloat16
    )
    out_local = jnp.einsum("td,te->de", scaled, grad_post, preferred_element_type=jnp.float32)
    grad_scaled = jnp.einsum("te,de->td", grad_post, out_full, preferred_element_type=jnp.float32)
    scale_local = jnp.sum(
        (grad_scaled * attended).reshape(local_rows, HEADS, head_dim), axis=(0, 2)
    )
    grad_attended = (
        (grad_scaled * scale_wide).astype(jnp.bfloat16).reshape(local_rows, HEADS, head_dim)
    )
    grad_query, grad_keys, grad_values = attend_backward(
        query_rows, key_rows, value_rows, grad_attended, doc_ids, sums_log, factor
    )
    grad_projected = jnp.concatenate(
        [
            grad_query.reshape(local_rows, model_width),
            grad_keys.reshape(local_rows, model_width),
            grad_values.reshape(local_rows, model_width),
        ],
        axis=1,
    ).astype(jnp.bfloat16)
    qkv_local = jnp.einsum(
        "td,te->de", normed_in, grad_projected, preferred_element_type=jnp.float32
    )
    grad_normed_in = jnp.einsum(
        "te,de->td", grad_projected, qkv_full, preferred_element_type=jnp.float32
    )
    token_grad = grad_middle + normalize_back(
        grad_normed_in * gain_full[:, 0], normed_one, inverse_one
    )
    projected_sums = jnp.sum(grad_projected.astype(jnp.float32), axis=0)
    gains_local = jnp.stack(
        [
            jnp.sum(grad_normed_in * normed_one, axis=0),
            jnp.sum(grad_middle * normed_post, axis=0),
            jnp.sum(grad_normed_mid * normed_two, axis=0),
        ],
        axis=1,
    )
    biases_local = jnp.stack(
        [
            jnp.sum(grad_normed_in, axis=0),
            projected_sums[:model_width],
            projected_sums[2 * model_width :],
            jnp.sum(grad_post.astype(jnp.float32), axis=0),
            jnp.sum(grad_middle, axis=0),
            jnp.sum(grad_normed_mid, axis=0),
            jnp.sum(final_grad, axis=0),
        ],
        axis=1,
    )
    qkv_grad, out_weight_grad, gains_grad, biases_grad = (
        lax.psum_scatter(qkv_local, ("dp", "tensor"), scatter_dimension=0, tiled=True),
        lax.psum_scatter(out_local, ("dp", "tensor"), scatter_dimension=0, tiled=True),
        lax.psum_scatter(gains_local, ("dp", "tensor"), scatter_dimension=0, tiled=True),
        lax.psum_scatter(biases_local, ("dp", "tensor"), scatter_dimension=0, tiled=True),
    )
    scale_grad = lax.psum(scale_local, ("dp", "tensor"))
    return (
        mixed_out,
        token_grad,
        qkv_grad,
        out_weight_grad,
        gains_grad,
        biases_grad,
        scale_grad,
        fc1_grad,
        fc2_grad,
        mid_gain_grad,
        ffn_bias_grad,
    )


MESH = pl.DeviceIdType.MESH
ANY = pl.BlockSpec(memory_space=pl.ANY)
IN_VMEM = pl.BlockSpec(memory_space=pltpu.VMEM)


def place():
    z = lax.axis_index("dp")
    t = lax.axis_index("tensor")
    return z, lax.div(t, 4), lax.rem(lax.div(t, 2), 2), lax.rem(t, 2)


def at(z, y, x, c):
    return (z, y * 4 + x * 2 + c)


def greet(partners):
    barrier = pltpu.get_barrier_semaphore()
    for partner in partners:
        pl.semaphore_signal(barrier, inc=1, device_id=partner, device_id_type=MESH)
    pl.semaphore_wait(barrier, len(partners))


class Sends:
    def __init__(self, send_sems, recv_sems):
        self.send_sems, self.recv_sems, self.copies = send_sems, recv_sems, []

    def start(self, src, dst, target):
        index = len(self.copies)
        copy = pltpu.make_async_remote_copy(
            src_ref=src,
            dst_ref=dst,
            send_sem=self.send_sems.at[index],
            recv_sem=self.recv_sems.at[index],
            device_id=target,
            device_id_type=MESH,
        )
        copy.start()
        self.copies.append(copy)
        return copy

    def finish(self):
        for copy in self.copies:
            copy.wait_send()


def add_low(left, right):
    return (left.astype(jnp.float32) + right.astype(jnp.float32)).astype(jnp.bfloat16)


SQRT_2_PI = math.sqrt(2.0 / math.pi)
NT = (((1,), (1,)), ((), ()))
TN = (((0,), (0,)), ((), ()))


def dot(left, right, dims=None):
    if dims is None:
        return jnp.dot(left, right, preferred_element_type=jnp.float32)
    return lax.dot_general(left, right, dims, preferred_element_type=jnp.float32)


def centered(values):
    center = jnp.mean(values, axis=-1, keepdims=True)
    spread = jnp.mean(values * values, axis=-1, keepdims=True) - center * center
    inverse = lax.rsqrt(spread + EPS)
    return (values - center) * inverse, inverse


def centered_back(grad, normed, inverse):
    first = jnp.mean(grad, axis=-1, keepdims=True)
    second = jnp.mean(grad * normed, axis=-1, keepdims=True)
    return inverse * (grad - first - normed * second)


def eights(values):
    return jnp.sum(values.reshape(values.shape[0] // 8, 8, values.shape[1]), axis=0)


def doc_mask(doc_ref, rows):
    query = lax.broadcasted_iota(jnp.int32, (rows, rows), 0)
    key = lax.broadcasted_iota(jnp.int32, (rows, rows), 1)
    query_doc, key_doc = jnp.zeros_like(query), jnp.zeros_like(key)
    end = 0
    for j in range(doc_ref.shape[1] - 1):
        end = end + doc_ref[0, j]
        query_doc = query_doc + (query >= end).astype(jnp.int32)
        key_doc = key_doc + (key >= end).astype(jnp.int32)
    allowed = jnp.logical_and(query_doc == key_doc, key <= query)
    return allowed.astype(jnp.float32)


class Plane:
    def __init__(self, sends, whole, here, targets):
        self.sends, self.whole, self.here, self.targets = sends, whole, here, targets
        half = whole.shape[3] // 2
        self.lo, self.hi = pl.ds(0, half), pl.ds(half, half)

    def part(self, y, x, c, rows):
        return self.whole.at[y, x, c, rows]

    def start_first(self, src):
        (y, x, c), (to_x, to_y, to_c), lo, hi = self.here, self.targets, self.lo, self.hi
        go = self.sends.start
        self.first = [
            go(src.at[lo], self.part(y, x, c, lo), to_x),
            go(src.at[hi], self.part(y, x, c, hi), to_y),
        ]
        self.core = [go(src, self.whole.at[y, x, c], to_c)]

    def start_second(self, src):
        (y, x, c), (to_x, to_y, _), lo, hi = self.here, self.targets, self.lo, self.hi
        go = self.sends.start
        self.second = [
            go(src.at[lo], self.part(y, x, c, lo), to_y),
            go(src.at[hi], self.part(y, x, c, hi), to_x),
        ]

    def after_first(self):
        (y, x, c), (to_x, to_y, to_c), lo, hi = self.here, self.targets, self.lo, self.hi
        for copy in self.first:
            copy.wait_recv()
        by_x, by_y = self.part(y, 1 - x, c, lo), self.part(1 - y, x, c, hi)
        go = self.sends.start
        self.third = [go(by_x, by_x, to_y), go(by_y, by_y, to_x)]
        self.side = [go(by_x, by_x, to_c), go(by_y, by_y, to_c)]

    def after_second(self):
        (y, x, c), (to_x, to_y, to_c), lo, hi = self.here, self.targets, self.lo, self.hi
        for copy in self.second:
            copy.wait_recv()
        by_x, by_y = self.part(y, 1 - x, c, hi), self.part(1 - y, x, c, lo)
        go = self.sends.start
        self.side += [go(by_x, by_x, to_c), go(by_y, by_y, to_c)]

    def after_third(self):
        y, x, c = self.here
        self.last = []
        for copy, part in zip(self.third, (self.lo, self.hi)):
            copy.wait_recv()
            ref = self.part(1 - y, 1 - x, c, part)
            self.last.append(self.sends.start(ref, ref, self.targets[2]))


def fore_kernel(
    nz,
    tok_ref,
    og_ref,
    qkv_ref,
    out_ref,
    gains_ref,
    biases_ref,
    fc1_ref,
    fc2_ref,
    gain_ref,
    shift_ref,
    doc_ref,
    scale_ref,
    qkv_out,
    out_out,
    vec_out,
    proj_out,
    att_out,
    lse_out,
    branch_out,
    middle_out,
    nin_out,
    scaled_out,
    ffn_out,
    first_out,
    fc2_out,
    late_out,
    gnm_out,
    fc1_out,
    unit_out,
    qkv_all,
    out_all,
    vec_all,
    vec_plane,
    vec_pair,
    vec_mine,
    vec_turn,
    unit_ref,
    fc1_all,
    fc2_all,
    og_all,
    tok,
    branch,
    nin,
    proj,
    att,
    lse,
    scaled,
    middle,
    mask,
    vec,
    mid_all,
    act,
    slope,
    grad,
    hidden,
    grad_pre,
    mid_part,
    pre,
    stats,
    pair,
    got,
    totals,
    from_core,
    sums,
    from_one,
    from_two,
    f_part,
    f_core,
    f_sums,
    fc1_part,
    late_part,
    fc2_part,
    fc1_got,
    local_sems,
    send_sems,
    recv_sems,
):
    z, y, x, c = place()
    to_x, to_y, to_c = at(z, y, 1 - x, c), at(z, 1 - y, x, c), at(z, y, x, 1 - c)
    to_xy = at(z, 1 - y, 1 - x, c)
    others = [lax.rem(z + k, nz) for k in range(1, nz)]
    slots = [z] + [lax.rem(z + nz - k, nz) for k in range(1, nz)]
    peers = [at(other, y, x, c) for other in others]
    locals_ = []

    def fetch(src, dst):
        copy = pltpu.make_async_copy(src, dst, local_sems.at[len(locals_)])
        copy.start()
        locals_.append(copy)
        return copy

    rows, width = tok.shape
    fourth = width // 4
    qkv_in = [
        fetch(
            qkv_ref.at[:, pl.ds(i * width + g * fourth, fourth)],
            qkv_all.at[z, y, x, c, :, pl.ds((3 * g + i) * fourth, fourth)],
        )
        for g in range(4)
        for i in range(3)
    ]
    vec_turn[...] = jnp.zeros_like(vec_turn)
    share = qkv_ref.shape[0]
    vec_turn[0:3, 0:share] = gains_ref[...]
    vec_turn[3:10, 0:share] = biases_ref[...]
    across = vec_turn[...].T[:share]
    vec_turn[...] = jnp.zeros_like(vec_turn)
    vec_turn[pl.ds(pl.multiple_of((2 * x + c) * share, share), share)] = across
    vec_mine[...] = vec_turn[...].T[:16]
    greet([to_x, to_y, to_c, to_xy] + peers)
    sends = Sends(send_sems, recv_sems)
    low, f32 = jnp.bfloat16, jnp.float32
    units = fc1_all.shape[1]
    width1, width2 = fc1_ref.shape[0], fc2_ref.shape[1]
    own1 = fc1_all.at[pl.ds(pl.multiple_of(z * width1, width1), width1)]
    own2 = fc2_all.at[:, pl.ds(pl.multiple_of(z * width2, width2), width2)]
    def wait_all(copies):
        for copy in copies:
            copy.wait_recv()

    vec_z = [sends.start(vec_mine, vec_all.at[0, z], peer) for peer in peers]
    phase = 6 * fourth
    spans = (pl.ds(0, phase), pl.ds(phase, phase))
    for copy in qkv_in:
        copy.wait()
    own_qkv = qkv_all.at[z, y, x, c]
    qkv_z = [
        [sends.start(own_qkv.at[:, span], own_qkv.at[:, span], peer) for peer in peers]
        for span in spans
    ]

    z_pair = z + 1 - 2 * lax.rem(z, 2)
    pair_peer, far_peer = at(z_pair, y, x, c), peers[1]
    qkv_slots = slots

    def go_on(p):
        qkv_z[p][0].wait_recv()

    def sides(whole, p):
        size = phase // 2 if whole is qkv_all else whole.shape[-1] // 2
        return pl.ds(2 * p * size, size), pl.ds((2 * p + 1) * size, size)

    def first(whole, slot, p=0):
        lo, hi = sides(whole, p)
        by_x, by_y = whole.at[slot, y, x, c, :, lo], whole.at[slot, y, x, c, :, hi]
        return (sends.start(by_x, by_x, to_x), sends.start(by_y, by_y, to_y))

    def second(whole, slot, p=0):
        lo, hi = sides(whole, p)
        by_x, by_y = whole.at[slot, y, :, c, :, lo], whole.at[slot, :, x, c, :, hi]
        return (sends.start(by_x, by_x, to_y), sends.start(by_y, by_y, to_x))

    def third(whole, slot, p=None):
        ref = whole.at[slot, :, :, c] if p is None else whole.at[slot, :, :, c, :, spans[p]]
        return sends.start(ref, ref, to_c)

    a0, a1 = [first(qkv_all, z, 0)], [first(qkv_all, z, 1)]
    og = Plane(sends, og_all, (y, x, c), (to_x, to_y, to_c))
    og.start_first(og_ref)
    tok_in = fetch(tok_ref, tok)
    out_in = fetch(out_ref, out_all.at[z, y, x, c])
    fc1_in = fetch(fc1_ref, own1)
    fc2_in = fetch(fc2_ref, own2)
    og_in = fetch(og_ref, og_all.at[y, x, c])
    vec_all[0, z] = vec_mine[...]
    unit_ref[...] = jnp.zeros_like(unit_ref)
    unit_ref[0:1] = shift_ref[0:1]
    unit_ref[1:2] = gain_ref[...]
    unit_ref[2:3] = shift_ref[1:2]
    step = 32
    mask[...] = doc_mask(doc_ref, rows)
    tok_in.wait()

    def normed(k, carry):
        part = pl.ds(pl.multiple_of(k * step, step), step)
        branch[part] = centered(tok[part].astype(f32))[0]
        return carry

    lax.fori_loop(0, rows // step, normed, 0)
    wait_all(vec_z)
    vec_x = sends.start(vec_all.at[0], vec_all.at[1], to_x)
    wait_all(a0[0])
    b0 = [second(qkv_all, z, 0)]
    wait_all(a1[0])
    b1 = [second(qkv_all, z, 1)]
    go_on(0)
    a0.append(first(qkv_all, qkv_slots[1], 0))
    vec_x.wait_recv()
    vec_plane[y] = vec_all[0] + vec_all[1]
    vec_y = sends.start(vec_plane.at[y], vec_plane.at[y], to_y)
    for k in range(2, nz):
        qkv_z[0][k - 1].wait_recv()
        a0.append(first(qkv_all, qkv_slots[k], 0))
    vec_y.wait_recv()
    vec_c = sends.start(vec_plane, vec_pair, to_c)
    for k in range(1, nz):
        wait_all(a0[k])
        b0.append(second(qkv_all, qkv_slots[k], 0))
    go_on(1)
    a1.append(first(qkv_all, qkv_slots[1], 1))
    vec_c.wait_recv()
    for n in range(2 * nz):
        vec[:, n * 128 : (n + 1) * 128] = vec_plane[n % 2, n // 2] + vec_pair[n % 2, n // 2]
    spot = lax.broadcasted_iota(jnp.int32, (1, width), 1)
    head = 64
    wide = jnp.zeros((1, width), f32)
    for h in range(HEADS):
        inside = jnp.logical_and(spot >= h * head, spot < (h + 1) * head)
        wide = jnp.where(inside, scale_ref[h], wide)
    vec[10:11] = wide

    def scaled_in(k, carry):
        part = pl.ds(pl.multiple_of(k * step, step), step)
        nin[part] = (branch[part] * vec[0:1] + vec[3:4]).astype(low)
        return carry

    lax.fori_loop(0, rows // step, scaled_in, 0)
    wait_all(b0[0])
    c0 = [third(qkv_all, z, 0)]
    for k in range(2, nz):
        qkv_z[1][k - 1].wait_recv()
        a1.append(first(qkv_all, qkv_slots[k], 1))
        wait_all(b0[k - 1])
        c0.append(third(qkv_all, qkv_slots[k - 1], 0))
    out_in.wait()
    own_out = out_all.at[z, y, x, c]
    out_z = [sends.start(own_out, own_out, peer) for peer in peers]
    fc2_far = sends.start(fc2_ref, own2, far_peer)
    fc2_near = sends.start(fc2_ref, own2, pair_peer)
    fc1_z = [sends.start(fc1_ref, own1, peer) for peer in peers]
    wait_all(b0[nz - 1])
    c0.append(third(qkv_all, qkv_slots[nz - 1], 0))
    wait_all(a1[1])
    b1.append(second(qkv_all, qkv_slots[1], 1))
    wait_all(c0)

    def project(p):
        for g in (2 * p, 2 * p + 1):
            cols = pl.ds(3 * g * fourth, 3 * fourth)
            here = pl.ds(g * fourth, fourth)
            bias = jnp.concatenate(
                [vec[4:5, here], jnp.zeros((1, fourth), f32), vec[5:6, here]], axis=1
            )
            block = dot(nin[...], qkv_all[:, :, :, :, :, cols].reshape(width, 3 * fourth))
            proj[:, cols] = (block + bias).astype(low)

    project(0)
    lane = lax.broadcasted_iota(jnp.int32, (1, 128), 1)
    is_low = lane < head
    keep = (is_low.astype(low), (lane >= head).astype(low))
    factor = 1.0 / math.sqrt(head)
    lane_wide = lax.broadcasted_iota(jnp.int32, (rows, 128), 1)
    lse[...] = jnp.zeros_like(lse)

    def attend(p, carry):
        base = lax.div(p, 2) * (3 * fourth) + lax.rem(p, 2) * 128
        q_at = pl.ds(pl.multiple_of(base, 128), 128)
        k_at = pl.ds(pl.multiple_of(base + fourth, 128), 128)
        v_at = pl.ds(pl.multiple_of(base + 2 * fourth, 128), 128)
        here = pl.ds(pl.multiple_of(p * 128, 128), 128)
        q2, k2, v2 = proj[:, q_at], proj[:, k_at], proj[:, v_at]
        found, logs = [], []
        for i in range(2):
            scores = dot(q2 * keep[i], k2, NT) * factor
            scores = jnp.where(mask[...] > 0, scores, NEGATIVE)
            peak = jnp.max(scores, axis=1, keepdims=True)
            exponent = jnp.exp(scores - peak)
            total = jnp.sum(exponent, axis=1, keepdims=True)
            prob = (exponent * (1.0 / total)).astype(low)
            found.append(dot(prob, v2))
            logs.append(peak + jnp.log(total))
        spread_logs = jnp.where(lane_wide == 2 * p, logs[0], logs[1])
        at_pair = lax.div(lane_wide, 2) == p
        lse[...] = jnp.where(at_pair, spread_logs, lse[...])
        both = jnp.where(is_low, *found)
        att[:, here] = both
        scaled[:, here] = (both * vec[10:11, here]).astype(low)
        return carry

    lax.fori_loop(0, 1, attend, 0)
    for k in range(2, nz):
        wait_all(a1[k])
        b1.append(second(qkv_all, qkv_slots[k], 1))
    out_a = [first(out_all, z)]
    for k in range(1, nz):
        out_z[k - 1].wait_recv()
        out_a.append(first(out_all, slots[k]))
    og.start_second(og_ref)
    lax.fori_loop(1, 2, attend, 0)
    c1 = []
    for k in range(2):
        wait_all(b1[k])
        c1.append(third(qkv_all, qkv_slots[k], 1))
    lax.fori_loop(2, 4, attend, 0)
    for k in range(2, nz):
        wait_all(b1[k])
        c1.append(third(qkv_all, qkv_slots[k], 1))
    wait_all(c1)
    saves = [fetch(qkv_all, qkv_out), fetch(vec, vec_out), fetch(nin, nin_out)]
    project(1)
    saves.append(fetch(proj, proj_out))
    out_b = []
    for k in range(nz):
        wait_all(out_a[k])
        out_b.append(second(out_all, slots[k]))
    lax.fori_loop(4, 6, attend, 0, unroll=True)
    og.after_first()
    lax.fori_loop(6, 8, attend, 0, unroll=True)
    out_c = []
    for k in range(nz):
        wait_all(out_b[k])
        out_c.append(third(out_all, slots[k]))
    saves += [fetch(att, att_out), fetch(lse, lse_out), fetch(scaled, scaled_out)]
    wait_all(out_c)
    saves.append(fetch(out_all, out_out))
    quarter = width // 4
    for k in range(4):
        cols = pl.ds(k * quarter, quarter)
        block = dot(scaled[...], out_all[:, :, :, :, :, cols].reshape(width, quarter))
        branch[:, cols] = block + vec[6:7, cols]

    def middles(k, carry):
        part = pl.ds(pl.multiple_of(k * step, step), step)
        post = centered(branch[part])[0]
        value = tok[part].astype(f32) + post * vec[1:2] + vec[7:8]
        middle[part] = value
        mid_all[y, x, c, part] = (centered(value)[0] * vec[2:3] + vec[8:9]).astype(low)
        return carry

    lax.fori_loop(0, rows // step, middles, 0, unroll=2)
    mid = Plane(sends, mid_all, (y, x, c), (to_x, to_y, to_c))
    mid.start_first(mid_all.at[y, x, c])
    mid.start_second(mid_all.at[y, x, c])
    branch_put = fetch(branch, branch_out)
    saves.append(fetch(middle, middle_out))

    def grads(yy, xx, cc):
        grad[yy, xx, cc] = dot(og_all[yy, xx, cc], fc2_all[...], NT)

    def fold(v):
        quarters = [v[:, k * (units // 4) : (k + 1) * (units // 4)] for k in range(4)]
        return (quarters[0] + quarters[1]) + (quarters[2] + quarters[3])

    def forward(yy, xx, cc):
        pre[...] = dot(mid_all[yy, xx, cc], fc1_all[...])

        def block(k, carry):
            part = pl.ds(pl.multiple_of(k * step, step), step)
            u = pre[part] + unit_ref[0:1]
            square = u * u
            th = jnp.tanh(u * (SQRT_2_PI + (SQRT_2_PI * 0.044715) * square))
            lift = 0.5 + 0.5 * th
            a = u * lift
            act[yy, xx, cc, part] = a
            bend = u * (2.0 * SQRT_2_PI + (6.0 * 0.044715 * SQRT_2_PI) * square)
            slope[yy, xx, cc, part] = lift + bend * (lift - lift * lift)
            gm = grad[yy, xx, cc, part] * unit_ref[1:2]
            for j, value in enumerate((a, a * a, gm, gm * a)):
                pre[part, j * (units // 4) : (j + 1) * (units // 4)] = fold(value)
            return carry

        lax.fori_loop(0, rows // step, block, 0)
        for j in range(4):
            folded = pre[:, j * (units // 4) : (j + 1) * (units // 4)]
            stats[yy, xx, cc, j : j + 1] = jnp.sum(folded.T, axis=0, keepdims=True)

    og.after_second()
    fc2_in.wait()
    fc2_far.wait_recv()
    near = fc2_all.at[:, pl.ds(pl.multiple_of(others[1] * width2, width2), width2)]
    fc2_last = sends.start(near, near, pair_peer)
    fc2_near.wait_recv()
    og.after_third()
    fc1_in.wait()
    mid.after_first()
    fc2_last.wait_recv()
    og_in.wait()
    grads(y, x, c)
    wait_all(og.core)
    grads(y, x, 1 - c)
    grads(y, 1 - x, c)
    grads(1 - y, x, c)
    mid.after_second()
    wait_all(og.side)
    grads(y, 1 - x, 1 - c)
    grads(1 - y, x, 1 - c)
    grads(1 - y, 1 - x, c)
    wait_all(og.last)
    grads(1 - y, 1 - x, 1 - c)
    wait_all(fc1_z)
    forward(y, x, c)
    wait_all(mid.core)
    forward(y, x, 1 - c)
    forward(y, 1 - x, c)
    forward(1 - y, x, c)
    wait_all(mid.side)
    forward(y, 1 - x, 1 - c)
    forward(1 - y, x, 1 - c)
    mid.after_third()
    forward(1 - y, 1 - x, c)
    wait_all(mid.last)
    forward(1 - y, 1 - x, 1 - c)

    sends.start(stats, got.at[3], to_c).wait_recv()
    pair[...] = stats[...] + got[3]
    wait_all([sends.start(pair, got.at[k], to) for k, to in enumerate((to_x, to_y, to_xy))])
    total = (pair[...] + got[0]) + (got[1] + got[2])
    total = total * (1.0 / (units * 8))
    center, square = total[:, :, :, 0:1], total[:, :, :, 1:2]
    mean, cross = total[:, :, :, 2:3], total[:, :, :, 3:4]
    inverse = lax.rsqrt(square - center * center + EPS)
    totals[:, :, :, 0:1] = inverse
    totals[:, :, :, 1:2] = -center * inverse
    totals[:, :, :, 2:3] = inverse * mean
    totals[:, :, :, 3:4] = inverse * (inverse * (cross - center * mean))
    unit_out[...] = jnp.zeros_like(unit_out)

    def backward(yy, xx, cc):
        for j in range(4):
            spread = jnp.broadcast_to(totals[yy, xx, cc, j : j + 1], (128, rows))
            pre[:, j * 128 : (j + 1) * 128] = spread.T

        def block(k, carry):
            part = pl.ds(pl.multiple_of(k * step, step), step)

            def across(j):
                return jnp.concatenate([pre[part, j * 128 : (j + 1) * 128]] * (units // 128), axis=1)

            g = grad[yy, xx, cc, part]
            inverse = across(0)
            normed = act[yy, xx, cc, part] * inverse + across(1)
            gain = unit_ref[1:2]
            hidden[yy, xx, cc, part] = (normed * gain + unit_ref[2:3]).astype(low)
            back = g * gain * inverse - across(2) - normed * across(3)
            value = (back * slope[yy, xx, cc, part]).astype(low)
            grad_pre[yy, xx, cc, part] = value
            return (
                carry[0] + eights(g * normed),
                carry[1] + eights(value.astype(f32)),
                carry[2] + eights(g),
            )

        zero = jnp.zeros((8, units), f32)
        parts = lax.fori_loop(0, rows // step, block, (zero, zero, zero))
        for j, part in enumerate(parts):
            unit_out[j : j + 1] += jnp.sum(part, axis=0, keepdims=True)
        return dot(grad_pre[yy, xx, cc], fc1_all[...], NT)

    left, right = pl.ds(0, width // 2), pl.ds(width // 2, width // 2)
    order = [(1 - y, 1 - x), (y, 1 - x), (1 - y, x), (y, x)]
    stage_x, stage_y, cores = [], [], []

    def to_core(k):
        yy, xx = order[k]
        mid_part[yy, xx] = backward(yy, xx, 1 - c).astype(low)
        cores.append(sends.start(mid_part.at[yy, xx], from_core.at[yy, xx], to_c))

    def from_pair(k):
        yy, xx = order[k]
        block = backward(yy, xx, c)
        cores[k].wait_recv()
        sums[yy, xx] = (block + from_core[yy, xx].astype(f32)).astype(low)
        if k in (0, 1):
            stage_x.append(sends.start(sums.at[yy, xx, :, left], from_one.at[yy, :, left], to_x))
        if k in (0, 2):
            stage_y.append(sends.start(sums.at[yy, xx, :, right], from_one.at[xx, :, right], to_y))

    to_core(0)
    to_core(1)
    from_pair(0)
    to_core(2)
    from_pair(1)
    to_core(3)
    from_pair(2)
    from_pair(3)

    def ffn_of(yy, xx, cc):
        return dot(hidden[yy, xx, cc], fc2_all[...])

    blocks = nz
    size = width // blocks

    early = fc1_part.shape[-1]
    soon, late = slice(0, early), slice(early, units)

    def fc1_block(which, cols):
        part = pl.ds(pl.multiple_of(which * size, 128), size)
        block = jnp.zeros((size, cols.stop - cols.start), f32)
        for j in range(8):
            yxc = (j // 4, (j // 2) % 2, j % 2)
            block = block + dot(mid_all[(*yxc, slice(None), part)], grad_pre[(*yxc, slice(None), cols)], TN)
        return block

    fc1_far = {}
    for k in (1, 0, 2):
        fc1_part[k] = fc1_block(others[k], soon).astype(low)
        fc1_far[k] = sends.start(fc1_part.at[k], fc1_got.at[k], peers[k])
    wait_all((stage_x[0], stage_y[0]))
    sums[1 - y, x, :, left] = add_low(sums[1 - y, x, :, left], from_one[1 - y, :, left])
    sums[y, 1 - x, :, right] = add_low(sums[y, 1 - x, :, right], from_one[1 - x, :, right])
    last_y = sends.start(sums.at[1 - y, x, :, left], from_two.at[:, left], to_y)
    last_x = sends.start(sums.at[y, 1 - x, :, right], from_two.at[:, right], to_x)
    fc1_out[:, soon] = fc1_block(z, soon)
    fc1_out[:, late] = fc1_block(z, late)

    def late_block(k, carry):
        part = pl.ds(pl.multiple_of(k * size, 128), size)
        late_part[part] = fc1_block(k, late).astype(low)
        return carry

    lax.fori_loop(0, blocks, late_block, 0)
    saves.append(fetch(late_part, late_out))
    cores = []
    for yy, xx in order:
        f_part[yy, xx] = ffn_of(yy, xx, 1 - c).astype(low)
        cores.append(sends.start(f_part.at[yy, xx], f_core.at[yy, xx], to_c))
    for k, (yy, xx) in enumerate(order):
        block = ffn_of(yy, xx, c)
        cores[k].wait_recv()
        f_sums[yy, xx] = (block + f_core[yy, xx].astype(f32)).astype(low)
    saves.append(fetch(f_sums, ffn_out))
    top = pl.ds(0, first_out.shape[1])
    out_x = sends.start(f_sums.at[:, 1 - x, top, left], first_out.at[:, :, left], to_x)
    out_y = sends.start(f_sums.at[1 - y, :, top, right], first_out.at[:, :, right], to_y)

    def fc2_block(k, carry):
        part = pl.ds(pl.multiple_of(k * size, 128), size)
        block = jnp.zeros((units, size), f32)
        for j in range(8):
            yxc = (j // 4, (j // 2) % 2, j % 2)
            block = block + dot(hidden[yxc], og_all[(*yxc, slice(None), part)], TN)
        fc2_part[:, part] = block.astype(low)
        return carry

    lax.fori_loop(0, blocks, fc2_block, 0)
    saves.append(fetch(fc2_part, fc2_out))
    branch_put.wait()
    wait_all((stage_x[1], stage_y[1], last_x, last_y))
    for cols, k in ((left, y), (right, x)):
        branch[:, cols] = (
            sums[y, x, :, cols].astype(f32)
            + from_one[k, :, cols].astype(f32)
            + from_two[:, cols].astype(f32)
        )
        saves.append(fetch(branch.at[:, cols], gnm_out.at[:, cols]))
    for k in range(nz - 1):
        fc1_far[k].wait_recv()
        fc1_out[:, soon] += fc1_got[k].astype(f32)
    wait_all((out_x, out_y))
    for copy in saves:
        copy.wait()
    sends.finish()


def fore(nz, tokens, og, doc_lengths, w_qkv, w_out, gains, biases, scale, fc1, fc2, gain, shift):
    rows, width = tokens.shape
    share, units = w_qkv.shape[0], fc1.shape[1]
    low, f32, plane, every = jnp.bfloat16, jnp.float32, (2, 2, 2), (nz, 2, 2, 2)
    sds, vm = jax.ShapeDtypeStruct, pltpu.VMEM
    count = 160
    smem = pl.BlockSpec(memory_space=pltpu.SMEM)
    shapes = (
        (every + w_qkv.shape, low),
        (every + w_out.shape, low),
        ((16, width), f32),
        ((rows, w_qkv.shape[1]), low),
        ((rows, width), f32),
        ((rows, 128), f32),
        ((rows, width), f32),
        ((rows, width), f32),
        ((rows, width), low),
        ((rows, width), low),
        ((2, 2, rows, width), low),
        ((2, rows // 4, width), low),
        ((units, width), low),
        ((width, units - 3 * units // 4), low),
        ((rows, width), f32),
        (fc1.shape, f32),
        ((8, units), f32),
    )
    return pl.pallas_call(
        functools.partial(fore_kernel, nz),
        name="fore",
        out_shape=tuple(sds(shape, kind) for shape, kind in shapes),
        in_specs=[ANY] * 4 + [IN_VMEM] * 2 + [ANY] * 2 + [IN_VMEM] * 2 + [smem] * 2,
        out_specs=[ANY] * 15 + [IN_VMEM] * 2,
        scratch_shapes=[
            vm(every + w_qkv.shape, low),
            vm(every + w_out.shape, low),
            vm((2, nz, 16, 128), f32),
            vm((2, nz, 16, 128), f32),
            vm((2, nz, 16, 128), f32),
            vm((16, 128), f32),
            vm((128, 128), f32),
            vm((8, units), f32),
            vm((width, units), low),
            vm((units, width), low),
            vm(plane + (rows, width), low),
            vm((rows, width), low),
            vm((rows, width), f32),
            vm((rows, width), low),
            vm((rows, w_qkv.shape[1]), low),
            vm((rows, width), f32),
            vm((rows, 128), f32),
            vm((rows, width), low),
            vm((rows, width), f32),
            vm((rows, rows), f32),
            vm((16, width), f32),
            vm(plane + (rows, width), low),
            vm(plane + (rows, units), f32),
            vm(plane + (rows, units), f32),
            vm(plane + (rows, units), f32),
            vm(plane + (rows, units), low),
            vm(plane + (rows, units), low),
            vm((2, 2, rows, width), low),
            vm((rows, units), f32),
            vm(plane + (4, rows), f32),
            vm(plane + (4, rows), f32),
            vm((4,) + plane + (4, rows), f32),
            vm(plane + (4, rows), f32),
            vm((2, 2, rows, width), low),
            vm((2, 2, rows, width), low),
            vm((2, rows, width), low),
            vm((rows, width), low),
            vm((2, 2, rows, width), low),
            vm((2, 2, rows, width), low),
            vm((2, 2, rows, width), low),
            vm((nz - 1, fc1.shape[0], 3 * units // 4), low),
            vm((width, units - 3 * units // 4), low),
            vm((units, width), low),
            vm((nz - 1, fc1.shape[0], 3 * units // 4), low),
            pltpu.SemaphoreType.DMA((40,)),
            pltpu.SemaphoreType.DMA((count,)),
            pltpu.SemaphoreType.DMA((count,)),
        ],
        compiler_params=pltpu.CompilerParams(
            collective_id=1, has_side_effects=True, vmem_limit_bytes=63 * 2**20
        ),
    )(tokens, og, w_qkv, w_out, gains.T, biases.T, fc1, fc2, gain, shift, doc_lengths, scale)


def back_kernel(
    nz,
    gnm_in,
    ffn_ref,
    first_in,
    late_ref,
    own1_in,
    fc2_ref,
    unit_ref,
    proj_in,
    att_in,
    lse_in,
    branch_in,
    middle_in,
    scaled_in,
    nin_in,
    qkv_in,
    out_in,
    vec_ref,
    og_in,
    tok_in,
    doc_ref,
    mixed_out,
    token_out,
    weight_out,
    gains_out,
    biases_out,
    scale_out,
    fc1_out,
    fc2_out,
    unit_out,
    f_sums,
    f_one,
    f_two,
    got1,
    got2,
    got_unit,
    w_part,
    w_core,
    w_sums,
    w_one,
    w_two,
    w_far,
    gpost,
    gmid,
    gatt,
    gni,
    dproj,
    nin_t,
    mask,
    accs,
    small,
    small_far,
    small_y,
    small_half,
    small_got,
    turned,
    mixed_at,
    weight_at,
    fc1_at,
    fc2_at,
    gnm_ref,
    proj_ref,
    att_ref,
    lse_ref,
    branch_ref,
    middle_ref,
    scaled_ref,
    nin_ref,
    qkv_ref,
    out_ref,
    og_ref,
    tok_ref,
    local_sems,
    send_sems,
    recv_sems,
):
    z, y, x, c = place()
    to_x, to_y, to_c = at(z, y, 1 - x, c), at(z, 1 - y, x, c), at(z, y, x, 1 - c)
    to_xy = at(z, 1 - y, 1 - x, c)
    others = [lax.rem(z + k, nz) for k in range(1, nz)]
    peers = [at(other, y, x, c) for other in others]
    locals_ = []

    def fetch(src, dst):
        copy = pltpu.make_async_copy(src, dst, local_sems.at[len(locals_)])
        copy.start()
        locals_.append(copy)
        return copy

    middle_got = fetch(middle_in, middle_ref)
    gnm_got = fetch(gnm_in, gnm_ref)
    og_got = fetch(og_in, og_ref)
    branch_got = fetch(branch_in, branch_ref)
    top, half = pl.ds(0, first_in.shape[1]), first_in.shape[2] // 2
    first_got = [
        fetch(first_in.at[:, :, pl.ds(i * half, half)], f_one.at[i, :, top, pl.ds(i * half, half)])
        for i in range(2)
    ]
    ffn_got = fetch(ffn_ref, f_sums)
    out_got = fetch(out_in, out_ref)
    att_got = fetch(att_in, att_ref)
    scaled_got = fetch(scaled_in, scaled_ref)
    nin_got = fetch(nin_in, nin_ref)
    proj_got = fetch(proj_in, proj_ref)
    lse_got = fetch(lse_in, lse_ref)
    qkv_got = fetch(qkv_in, qkv_ref)
    tok_got = fetch(tok_in, tok_ref)

    greet([to_x, to_y, to_c, to_xy] + peers)
    sends = Sends(send_sems, recv_sems)
    rows, width = middle_ref.shape
    low = jnp.bfloat16
    f32 = jnp.float32
    share = weight_out.shape[0]
    width1, width2 = fc1_out.shape[0], fc2_out.shape[1]

    pieces = 4
    parts = [pl.ds(k * (rows // pieces), rows // pieces) for k in range(pieces)]
    left, right = pl.ds(0, width // 2), pl.ds(width // 2, width // 2)
    def block1(which):
        return late_ref.at[pl.ds(pl.multiple_of(which * width1, width1), width1)]

    def block2(which):
        return fc2_ref.at[:, pl.ds(pl.multiple_of(which * width2, width2), width2)]

    own1_got = fetch(own1_in, fc1_at)
    own2_got = fetch(block2(z), got2.at[nz - 1])
    far = []
    for k, peer in enumerate(peers):
        far.append(sends.start(unit_ref, got_unit.at[k], peer))
        far.append(sends.start(block1(others[k]), got1.at[k], peer))
        far.append(sends.start(block2(others[k]), got2.at[k], peer))

    f_first, f_second = [], []

    def ffn_one(k):
        part = parts[k]
        f_first.append(
            (
                sends.start(ffn_ref.at[:, 1 - x, part, left], f_one.at[0, :, part, left], to_x),
                sends.start(ffn_ref.at[1 - y, :, part, right], f_one.at[1, :, part, right], to_y),
            )
        )

    def ffn_two(k):
        part = parts[k]
        if k == 0:
            ffn_got.wait()
            for copy in first_got:
                copy.wait()
        else:
            for copy in f_first[k - 1]:
                copy.wait_recv()
        f_sums[1 - y, x, part, left] = add_low(
            f_sums[1 - y, x, part, left], f_one[0, 1 - y, part, left]
        )
        f_sums[y, 1 - x, part, right] = add_low(
            f_sums[y, 1 - x, part, right], f_one[1, 1 - x, part, right]
        )
        f_second.append(
            (
                sends.start(f_sums.at[1 - y, x, part, left], f_two.at[part, left], to_y),
                sends.start(f_sums.at[y, 1 - x, part, right], f_two.at[part, right], to_x),
            )
        )

    def ffn_three(k):
        part = parts[k]
        for copy in f_second[k]:
            copy.wait_recv()
        for i, (cols, at_) in enumerate(((left, y), (right, x))):
            total = (
                f_sums[y, x, part, cols].astype(f32)
                + f_one[i, at_, part, cols].astype(f32)
                + f_two[part, cols].astype(f32)
            )
            mixed_at[part, cols] = (
                middle_ref[part, cols] + total + vec_ref[9:10, cols]
            ).astype(low)
        puts.append(fetch(mixed_at.at[part], mixed_out.at[part]))

    spans = [(0, width)] + [(width + g * 3 * width // 4, 3 * width // 4) for g in range(4)]
    w_first, w_second, w_third, w_c = {}, {}, {}, {}

    def sides(j):
        start, size = spans[j]
        return pl.ds(start, size), pl.ds(start, size // 2), pl.ds(start + size // 2, size // 2)

    def w_zero(j):
        every = sides(j)[0]
        w_c[j] = sends.start(w_part.at[:, :, :, 1 - c, :, every], w_core.at[..., every], to_c)

    def w_step1(j):
        every, lo, hi = sides(j)
        w_c[j].wait_recv()

        def one(which, carry):
            for yy in range(2):
                for xx in range(2):
                    w_sums[which, yy, xx, :, every] = add_low(
                        w_part[which, yy, xx, c, :, every], w_core[which, yy, xx, :, every]
                    )
            return carry

        lax.fori_loop(0, nz, one, 0)
        w_first[j] = (
            sends.start(w_sums.at[:, :, 1 - x, :, lo], w_one.at[:, :, :, lo], to_x),
            sends.start(w_sums.at[:, 1 - y, :, :, hi], w_one.at[:, :, :, hi], to_y),
        )

    def w_step2(j):
        every, lo, hi = sides(j)
        for copy in w_first[j]:
            copy.wait_recv()

        def one(which, carry):
            for k in range(2):
                w_sums[which, k, x, :, lo] = add_low(
                    w_sums[which, k, x, :, lo], w_one[which, k, :, lo]
                )
                w_sums[which, y, k, :, hi] = add_low(
                    w_sums[which, y, k, :, hi], w_one[which, k, :, hi]
                )
            return carry

        lax.fori_loop(0, nz, one, 0)
        w_second[j] = (
            sends.start(w_sums.at[:, 1 - y, x, :, lo], w_two.at[:, :, lo], to_y),
            sends.start(w_sums.at[:, y, 1 - x, :, hi], w_two.at[:, :, hi], to_x),
        )

    def w_step3(j):
        every = sides(j)[0]
        for copy in w_second[j]:
            copy.wait_recv()
        for which in range(nz):
            w_sums[which, y, x, :, every] = add_low(
                w_sums[which, y, x, :, every], w_two[which, :, every]
            )
        w_third[j] = [
            sends.start(w_sums.at[others[k], y, x, :, every], w_far.at[k, :, every], peer)
            for k, peer in enumerate(peers)
        ]

    def w_step4(j):
        start, size = spans[j]
        every = sides(j)[0]
        total = w_sums[z, y, x, :, every].astype(f32)
        for k in range(nz - 1):
            w_third[j][k].wait_recv()
            total = total + w_far[k, :, every].astype(f32)
        if j == 0:
            weight_at[:, 3 * width :] = total
            spots = [pl.ds(3 * width, width)]
        else:
            third = size // 3
            spots = [pl.ds(i * width + (j - 1) * third, third) for i in range(3)]
            for i, spot in enumerate(spots):
                weight_at[:, spot] = total[:, i * third : (i + 1) * third]
        for spot in spots:
            puts.append(fetch(weight_at.at[:, spot], weight_out.at[:, spot]))

    ffn_one(1)
    ffn_two(0)
    accs[...] = jnp.zeros_like(accs)
    step = 32

    def norms(k, carry):
        part = pl.ds(pl.multiple_of(k * step, step), step)
        normed_two, inverse_two = centered(middle_ref[part])
        grad = gnm_ref[part]
        og = og_ref[part].astype(f32)
        grad_middle = og + centered_back(grad * vec_ref[2:3], normed_two, inverse_two)
        accs[2] += eights(grad * normed_two)
        accs[8] += eights(grad)
        accs[9] += eights(og)
        normed_post, inverse_post = centered(branch_ref[part])
        post = centered_back(grad_middle * vec_ref[1:2], normed_post, inverse_post).astype(low)
        accs[1] += eights(grad_middle * normed_post)
        accs[7] += eights(grad_middle)
        accs[6] += eights(post.astype(f32))
        gpost[part] = post
        gmid[part] = grad_middle
        return carry

    for copy in (middle_got, gnm_got, og_got, branch_got):
        copy.wait()
    lax.fori_loop(0, rows // step, norms, 0)
    quarter = width // 4

    def out_block(k, carry):
        part = pl.ds(pl.multiple_of(k * (width // nz), width // nz), width // nz)
        block = dot(scaled_ref[:, part], gpost[...], TN).astype(low)
        w_part[k, :, :, :, :, pl.ds(0, width)] = block.reshape(2, 2, 2, share, width)
        return carry

    scaled_got.wait()
    lax.fori_loop(0, nz, out_block, 0)
    w_zero(0)
    mask[...] = doc_mask(doc_ref, rows)

    def scaled_block(k, carry):
        part = pl.ds(pl.multiple_of(k * quarter, quarter), quarter)
        block = dot(gpost[...], out_ref[part], NT)
        accs[10, :, part] = eights(block * att_ref[:, part])
        gatt[:, part] = (block * vec_ref[10:11, part]).astype(low)
        return carry

    out_got.wait()
    att_got.wait()
    lax.fori_loop(0, 4, scaled_block, 0)

    nin_got.wait()
    nin_t[...] = nin_ref[...].T
    proj_got.wait()
    lse_got.wait()
    head = 64
    lane = lax.broadcasted_iota(jnp.int32, (1, 128), 1)
    is_low = lane < head
    factor = 1.0 / math.sqrt(head)
    lane_wide = lax.broadcasted_iota(jnp.int32, (rows, 128), 1)
    keep = (is_low.astype(low), (lane >= head).astype(low))

    def pair(p, carry):
        base = lax.div(p, 2) * (3 * quarter) + lax.rem(p, 2) * 128
        q_at = pl.ds(pl.multiple_of(base, 128), 128)
        k_at = pl.ds(pl.multiple_of(base + quarter, 128), 128)
        v_at = pl.ds(pl.multiple_of(base + 2 * quarter, 128), 128)
        here = pl.ds(pl.multiple_of(p * 128, 128), 128)
        q2, k2, v2, do2 = proj_ref[:, q_at], proj_ref[:, k_at], proj_ref[:, v_at], gatt[:, here]
        lses = lse_ref[...]
        found = []
        for i in range(2):
            scores = dot(q2 * keep[i], k2, NT) * factor
            scores = jnp.where(mask[...] > 0, scores, NEGATIVE)
            lse = jnp.sum(jnp.where(lane_wide == 2 * p + i, lses, 0.0), axis=1, keepdims=True)
            prob = jnp.exp(scores - lse)
            grad_prob = dot(do2 * keep[i], v2, NT)
            inner = jnp.sum(prob * grad_prob, axis=1, keepdims=True)
            ds = (prob * (grad_prob - inner) * factor).astype(low)
            found.append(
                (dot(ds, k2), dot(ds, q2, TN), dot(prob.astype(low), do2, TN))
            )
        for where, a, b in zip((q_at, k_at, v_at), *found):
            dproj[:, where] = jnp.where(is_low, a, b).astype(low)
        accs[4, :, here] = eights(dproj[:, q_at].astype(f32))
        accs[5, :, here] = eights(dproj[:, v_at].astype(f32))
        return carry

    def wgrad(j):
        start, size = spans[j]
        cols = pl.ds((j - 1) * size, size)

        def one(k, carry):
            part = pl.ds(pl.multiple_of(k * (width // nz), width // nz), width // nz)
            block = dot(nin_t[part], dproj[:, cols]).astype(low)
            w_part[k, :, :, :, :, pl.ds(start, size)] = block.reshape(2, 2, 2, share, size)
            return carry

        lax.fori_loop(0, nz, one, 0)
        w_zero(j)

    def gni_block(k, carry):
        part = pl.ds(pl.multiple_of(k * quarter, quarter), quarter)
        gni[:, part] = dot(dproj[...], qkv_ref[part], NT)
        return carry

    def tokens_back(k, carry):
        part = pl.ds(pl.multiple_of(k * step, step), step)
        normed, inverse = centered(tok_ref[part].astype(f32))
        grad = gni[part]
        gmid[part] = gmid[part] + centered_back(grad * vec_ref[0:1], normed, inverse)
        accs[0] += eights(grad * normed)
        accs[3] += eights(grad)
        return carry

    part_z = width // nz
    chain = {}

    def lanes(which):
        return pl.ds(pl.multiple_of(which * part_z, 128), part_z)

    def small_start():
        for j in range(16):
            small[j : j + 1] = jnp.sum(accs[j], axis=0, keepdims=True)
        spot = lax.broadcasted_iota(jnp.int32, (1, width), 1)
        tile = jnp.zeros((1, 128), f32)
        for h in range(HEADS):
            inside = jnp.logical_and(spot >= h * head, spot < (h + 1) * head)
            found = jnp.sum(jnp.where(inside, small[10:11], 0.0), axis=1, keepdims=True)
            tile = jnp.where(lane == h, found, tile)
        small[11:12] = jnp.concatenate([tile] * (width // 128), axis=1)
        chain["z"] = [
            sends.start(small.at[:, lanes(others[k])], small_far.at[k], peer)
            for k, peer in enumerate(peers)
        ]

    def small_second():
        total = small[:, lanes(z)]
        for k in range(nz - 1):
            chain["z"][k].wait_recv()
            total = total + small_far[k]
        small_y[...] = total
        other = small_y.at[:, pl.ds(pl.multiple_of((1 - y) * 128, 128), 128)]
        chain["y"] = sends.start(other, small_got.at[0], to_y)

    def small_third():
        chain["y"].wait_recv()
        small_half[0] = small_y[:, pl.ds(pl.multiple_of(y * 128, 128), 128)] + small_got[0]
        chain["x"] = sends.start(small_half.at[0], small_got.at[1], to_x)

    def small_fourth():
        chain["x"].wait_recv()
        small_half[1] = small_half[0] + small_got[1]
        chain["c"] = sends.start(small_half.at[1], small_got.at[2], to_c)

    def small_last():
        chain["c"].wait_recv()
        total = small_half[1] + small_got[2]
        scale_out[...] = jnp.broadcast_to(total[11:12], (8, 128))
        ours = pl.ds(pl.multiple_of((2 * x + c) * share, share), share)
        turned[...] = jnp.concatenate([total, jnp.zeros((112, 128), f32)], axis=0).T
        mine = jnp.concatenate([turned[ours], jnp.zeros((128 - share, 128), f32)], axis=0).T
        gains_out[...] = mine[0:3, :share]
        biases_out[...] = mine[3:10, :share]

    puts = []

    def far_last():
        for copy in far:
            copy.wait_recv()
        own1_got.wait()
        own2_got.wait()
        late = pl.ds(fc1_at.shape[1] - got1.shape[2], got1.shape[2])
        own2, unit = got2[nz - 1].astype(f32), unit_ref[...]
        for k in range(nz - 1):
            fc1_at[:, late] += got1[k].astype(f32)
            own2 = own2 + got2[k].astype(f32)
            unit = unit + got_unit[k]
        fc2_at[...] = own2
        unit_out[...] = unit
        puts.append(fetch(fc1_at, fc1_out))
        puts.append(fetch(fc2_at, fc2_out))

    def pairs(first, last):
        lax.fori_loop(first, last, pair, 0)

    def gni_all():
        qkv_got.wait()
        lax.fori_loop(0, 4, gni_block, 0)

    def tokens_all():
        tok_got.wait()
        lax.fori_loop(0, rows // step, tokens_back, 0)
        puts.append(fetch(gmid, token_out))

    ffn_one(2)
    w_step1(0)
    pairs(0, 1)
    pairs(1, 2)
    wgrad(1)
    ffn_two(1)
    pairs(2, 3)
    w_step1(1)
    ffn_two(2)
    pairs(3, 4)
    wgrad(2)
    w_step2(0)
    pairs(4, 5)
    w_step1(2)
    pairs(5, 6)
    wgrad(3)
    w_step2(1)
    w_step3(0)
    pairs(6, 7)
    w_step1(3)
    pairs(7, 8)
    wgrad(4)
    w_step2(2)
    gni_all()
    w_step3(1)
    w_step1(4)
    tokens_all()
    small_start()
    w_step2(3)
    w_step3(2)
    small_second()
    w_step2(4)
    ffn_one(3)
    w_step3(3)
    small_third()
    ffn_three(0)
    ffn_three(1)
    ffn_three(2)
    w_step4(0)
    w_step3(4)
    ffn_two(3)
    small_fourth()
    small_last()
    w_step4(1)
    w_step4(2)
    w_step4(3)
    far_last()
    ffn_three(3)
    w_step4(4)
    for put in puts:
        put.wait()
    sends.finish()


def back(nz, *operands):
    gnm, ffn_part, ffn_first, late, fc1, fc2, unit, proj, att, lse, branch = operands[:11]
    middle, scaled, nin, qkv, out, vec = operands[11:17]
    rows, width = middle.shape
    share = width // (nz * 8)
    columns = proj.shape[1] + width
    low, f32 = jnp.bfloat16, jnp.float32
    sds = jax.ShapeDtypeStruct
    fc2_own = (fc2.shape[0], fc2.shape[1] // nz)
    count = 96 + 8 * nz
    specs = [ANY] * 6 + [IN_VMEM] + [ANY] * 9 + [IN_VMEM] + [ANY] * 2
    specs.append(pl.BlockSpec(memory_space=pltpu.SMEM))
    return pl.pallas_call(
        functools.partial(back_kernel, nz),
        name="back",
        out_shape=(
            sds((rows, width), low),
            sds((rows, width), f32),
            sds((share, columns), f32),
            sds((3, share), f32),
            sds((7, share), f32),
            sds((8, 128), f32),
            sds(fc1.shape, f32),
            sds(fc2_own, f32),
            sds(unit.shape, f32),
        ),
        in_specs=specs,
        out_specs=[ANY] * 3 + [IN_VMEM] * 3 + [ANY] * 2 + [IN_VMEM],
        scratch_shapes=[
            pltpu.VMEM((2, 2, rows, width), low),
            pltpu.VMEM((2, 2, rows, width), low),
            pltpu.VMEM((rows, width), low),
            pltpu.VMEM((nz - 1, fc1.shape[0], late.shape[1]), low),
            pltpu.VMEM((nz,) + fc2_own, low),
            pltpu.VMEM((nz - 1,) + unit.shape, f32),
            pltpu.VMEM((nz, 2, 2, 2, share, columns), low),
            pltpu.VMEM((nz, 2, 2, share, columns), low),
            pltpu.VMEM((nz, 2, 2, share, columns), low),
            pltpu.VMEM((nz, 2, share, columns), low),
            pltpu.VMEM((nz, share, columns), low),
            pltpu.VMEM((nz - 1, share, columns), low),
            pltpu.VMEM((rows, width), low),
            pltpu.VMEM((rows, width), f32),
            pltpu.VMEM((rows, width), low),
            pltpu.VMEM((rows, width), f32),
            pltpu.VMEM((rows, 3 * width), low),
            pltpu.VMEM((width, rows), low),
            pltpu.VMEM((rows, rows), f32),
            pltpu.VMEM((16, 8, width), f32),
            pltpu.VMEM((16, width), f32),
            pltpu.VMEM((nz - 1, 16, width // nz), f32),
            pltpu.VMEM((16, width // nz), f32),
            pltpu.VMEM((3, 16, 128), f32),
            pltpu.VMEM((3, 16, 128), f32),
            pltpu.VMEM((128, 128), f32),
            pltpu.VMEM((rows, width), low),
            pltpu.VMEM((share, columns), f32),
            pltpu.VMEM(fc1.shape, f32),
            pltpu.VMEM(fc2_own, f32),
            pltpu.VMEM((rows, width), f32),
            pltpu.VMEM(proj.shape, low),
            pltpu.VMEM((rows, width), f32),
            pltpu.VMEM(lse.shape, f32),
            pltpu.VMEM((rows, width), f32),
            pltpu.VMEM((rows, width), f32),
            pltpu.VMEM((rows, width), low),
            pltpu.VMEM((rows, width), low),
            pltpu.VMEM(qkv.shape, low),
            pltpu.VMEM(out.shape, low),
            pltpu.VMEM((rows, width), low),
            pltpu.VMEM((rows, width), low),
            pltpu.SemaphoreType.DMA((64,)),
            pltpu.SemaphoreType.DMA((count,)),
            pltpu.SemaphoreType.DMA((count,)),
        ],
        compiler_params=pltpu.CompilerParams(
            collective_id=3, has_side_effects=True, vmem_limit_bytes=63 * 2**20
        ),
    )(*operands)


def finish_kernel(
    mixed,
    token,
    weight,
    fc1,
    fc2,
    gains,
    biases,
    scale,
    unit,
    mixed_out,
    token_out,
    qkv_out,
    out_out,
    fc1_out,
    fc2_out,
    gains_out,
    biases_out,
    scale_out,
    gain_out,
    shift_out,
    mixed_at,
    token_at,
    weight_at,
    fc1_at,
    fc2_at,
    in_sems,
    out_sems,
):
    columns = qkv_out.shape[1]
    moves = (
        (token, token_at, ((token_at, token_out),)),
        (
            weight,
            weight_at,
            (
                (weight_at.at[:, pl.ds(0, columns)], qkv_out),
                (weight_at.at[:, pl.ds(columns, out_out.shape[1])], out_out),
            ),
        ),
        (mixed, mixed_at, ((mixed_at, mixed_out),)),
        (fc1, fc1_at, ((fc1_at, fc1_out),)),
        (fc2, fc2_at, ((fc2_at, fc2_out),)),
    )
    reads, writes = [], []
    for k, (src, here, _) in enumerate(moves):
        reads.append(pltpu.make_async_copy(src, here, in_sems.at[k]))
        reads[-1].start()
    gains_out[...] = gains[...]
    biases_out[...] = biases[...]
    scale_out[...] = scale[0:1, : scale_out.shape[1]]
    gain_out[...] = unit[0:1]
    shift_out[0:1] = unit[1:2]
    shift_out[1:2] = unit[2:3]
    for read, (_, _, outs) in zip(reads, moves):
        read.wait()
        for src, dst in outs:
            writes.append(pltpu.make_async_copy(src, dst, out_sems.at[len(writes)]))
            writes[-1].start()
    for write in writes:
        write.wait()


def finish(mixed, token, weight, gains, biases, scale, fc1, fc2, unit):
    share, columns = weight.shape
    width, units = token.shape[1], unit.shape[1]
    f32 = jnp.float32
    shapes = (
        (mixed.shape, mixed.dtype),
        (token.shape, f32),
        ((share, columns - width), f32),
        ((share, width), f32),
        (fc1.shape, f32),
        (fc2.shape, f32),
        (gains.shape, f32),
        (biases.shape, f32),
        ((1, HEADS), f32),
        ((1, units), f32),
        ((2, units), f32),
    )
    return pl.pallas_call(
        finish_kernel,
        name="finish",
        out_shape=tuple(jax.ShapeDtypeStruct(shape, kind) for shape, kind in shapes),
        in_specs=[ANY] * 5 + [IN_VMEM] * 4,
        out_specs=[ANY] * 6 + [IN_VMEM] * 5,
        scratch_shapes=[
            pltpu.VMEM(mixed.shape, mixed.dtype),
            pltpu.VMEM(token.shape, f32),
            pltpu.VMEM(weight.shape, f32),
            pltpu.VMEM(fc1.shape, f32),
            pltpu.VMEM(fc2.shape, f32),
            pltpu.SemaphoreType.DMA((5,)),
            pltpu.SemaphoreType.DMA((6,)),
        ],
        compiler_params=pltpu.CompilerParams(vmem_limit_bytes=63 * 2**20),
    )(mixed, token, weight, fc1, fc2, gains, biases, scale, unit)


def fused(
    nz,
    tokens,
    out_grad,
    doc_lengths,
    w_qkv,
    w_out,
    gains,
    biases,
    head_scale,
    w_fc1,
    w_fc2,
    mid_gain,
    ffn_biases,
):
    (
        qkv_full,
        out_full,
        vec,
        proj,
        att,
        lse,
        branch,
        middle,
        nin,
        scaled,
        ffn_part,
        ffn_first,
        fc2_part,
        fc1_late,
        gnm,
        fc1_own,
        unit_sums,
    ) = fore(
        nz,
        tokens,
        out_grad,
        doc_lengths,
        w_qkv,
        w_out,
        gains,
        biases,
        head_scale,
        w_fc1,
        w_fc2,
        mid_gain[None],
        ffn_biases,
    )
    model_width = tokens.shape[1]
    (
        mixed,
        token_grad,
        weight_grad,
        gains_grad,
        biases_grad,
        scale,
        fc1_grad,
        fc2_grad,
        unit_sums,
    ) = back(
        nz,
        gnm,
        ffn_part,
        ffn_first,
        fc1_late,
        fc1_own,
        fc2_part,
        unit_sums,
        proj,
        att,
        lse,
        branch,
        middle,
        scaled,
        nin,
        qkv_full.reshape(model_width, -1),
        out_full.reshape(model_width, -1),
        vec,
        out_grad,
        tokens,
        doc_lengths,
    )
    mixed, token_grad, qkv, out, fc1, fc2, gains_grad, biases_grad, scale, gain, shift = finish(
        mixed,
        token_grad,
        weight_grad,
        gains_grad,
        biases_grad,
        scale,
        fc1_grad,
        fc2_grad,
        unit_sums,
    )
    return (
        mixed,
        token_grad,
        qkv,
        out,
        gains_grad.T,
        biases_grad.T,
        scale[0],
        fc1,
        fc2,
        gain[0],
        shift,
    )


def layer(nz, nt, tokens, out_grad, doc_lengths, w_qkv, *rest):
    if nz == 4 and nt == 8 and w_qkv.shape[0] % 16 == 0:
        return fused(nz, tokens, out_grad, doc_lengths, w_qkv, *rest)
    return plain(tokens, out_grad, doc_lengths, w_qkv, *rest)


def solution(mesh):
    return jax.shard_map(
        functools.partial(layer, mesh.shape["dp"], mesh.shape["tensor"]),
        mesh=mesh,
        in_specs=(
            P(("dp", "tensor"), None),
            P(("dp", "tensor"), None),
            P(("dp", "tensor"), None),
            P(("dp", "tensor"), None),
            P(("dp", "tensor"), None),
            P(("dp", "tensor"), None),
            P(("dp", "tensor"), None),
            P(),
            P("dp", "tensor"),
            P("tensor", "dp"),
            P("tensor"),
            P(None, "tensor"),
        ),
        out_specs=(
            P(("dp", "tensor"), None),
            P(("dp", "tensor"), None),
            P(("dp", "tensor"), None),
            P(("dp", "tensor"), None),
            P(("dp", "tensor"), None),
            P(("dp", "tensor"), None),
            P(),
            P("dp", "tensor"),
            P("tensor", "dp"),
            P("tensor"),
            P(None, "tensor"),
        ),
        check_vma=False,
    )
```

```python
import functools
import math

import jax
import jax.numpy as jnp
from jax import lax
from jax.experimental import pallas as pl
from jax.experimental.pallas import tpu as pltpu
from jax.sharding import PartitionSpec as P

HEADS = 16
FF = 4096


EPS = 1e-05
NEGATIVE = -1000000000.0


def normalize(values):
    center = jnp.mean(values, axis=-1, keepdims=True)
    spread = jnp.mean(values * values, axis=-1, keepdims=True) - center * center
    inverse = lax.rsqrt(spread + EPS)
    return ((values - center) * inverse, inverse)


def normalize_back(grad_normed, normed, inverse):
    first_mean = jnp.mean(grad_normed, axis=-1, keepdims=True)
    second = jnp.mean(grad_normed * normed, axis=-1, keepdims=True)
    return inverse * (grad_normed - first_mean - normed * second)


def block_scores(query_rows, key_rows, doc_ids, row_first, row_last, factor):
    scores = (
        jnp.einsum("qhd,khd->hqk", query_rows, key_rows, preferred_element_type=jnp.float32)
        * factor
    )
    query_pos = jnp.arange(row_first, row_last)
    key_pos = jnp.arange(row_last)
    same_doc = doc_ids[row_first:row_last, None] == doc_ids[None, :row_last]
    allowed = jnp.logical_and(same_doc, key_pos[None, :] <= query_pos[:, None])
    return (jnp.where(allowed[None], scores, NEGATIVE), allowed)


def attend_forward(query_rows, key_rows, value_rows, doc_ids, factor):
    total_rows = query_rows.shape[0]
    block_rows = min(512, total_rows)
    scores, allowed = block_scores(query_rows, key_rows, doc_ids, 0, block_rows, factor)
    row_peak = jnp.max(scores, axis=-1, keepdims=True)
    exponent = jnp.exp(scores - row_peak)
    row_total = jnp.sum(exponent, axis=-1, keepdims=True)
    prob_low = (exponent / row_total).astype(jnp.bfloat16)
    pieces = jnp.einsum("hqk,khd->qhd", prob_low, value_rows, preferred_element_type=jnp.float32)
    sums_log = [row_peak + jnp.log(row_total)]
    return (pieces, sums_log)


def attend_backward(query_rows, key_rows, value_rows, grad_out, doc_ids, sums_log, factor):
    total_rows = query_rows.shape[0]
    block_rows = min(512, total_rows)
    query_parts = []
    grad_keys = jnp.zeros(key_rows.shape, jnp.float32)
    grad_values = jnp.zeros(value_rows.shape, jnp.float32)
    for block_index, row_first in enumerate(range(0, total_rows, block_rows)):
        row_last = row_first + block_rows
        scores, allowed = block_scores(query_rows, key_rows, doc_ids, row_first, row_last, factor)
        prob_rows = jnp.where(allowed[None], jnp.exp(scores - sums_log[block_index]), 0.0)
        prob_low = prob_rows.astype(jnp.bfloat16)
        grad_probs = jnp.einsum(
            "qhd,khd->hqk", grad_out, value_rows, preferred_element_type=jnp.float32
        )
        inner_sum = jnp.sum(prob_rows * grad_probs, axis=-1, keepdims=True)
        grad_scores = (prob_rows * (grad_probs - inner_sum) * factor).astype(jnp.bfloat16)
        query_parts.append(
            jnp.einsum("hqk,khd->qhd", grad_scores, key_rows, preferred_element_type=jnp.float32)
        )
        grad_keys = grad_keys.at[:row_last].add(
            jnp.einsum("hqk,qhd->khd", grad_scores, query_rows, preferred_element_type=jnp.float32)
        )
        grad_values = grad_values.at[:row_last].add(
            jnp.einsum("hqk,qhd->khd", prob_low, grad_out, preferred_element_type=jnp.float32)
        )
    return (query_parts[0], grad_keys, grad_values)


def plain(
    tokens,
    out_grad,
    doc_lengths,
    w_qkv,
    w_out,
    gains,
    biases,
    head_scale,
    w_fc1,
    w_fc2,
    mid_gain,
    ffn_biases,
):
    qkv_full, out_full, gain_full, bias_full = (
        lax.all_gather(w_qkv, ("dp", "tensor"), axis=0, tiled=True),
        lax.all_gather(w_out, ("dp", "tensor"), axis=0, tiled=True),
        lax.all_gather(gains.astype(jnp.bfloat16), ("dp", "tensor"), axis=0, tiled=True).astype(
            gains.dtype
        ),
        lax.all_gather(biases.astype(jnp.bfloat16), ("dp", "tensor"), axis=0, tiled=True).astype(
            biases.dtype
        ),
    )
    fc1_rows, fc2_cols = (
        lax.all_gather(w_fc1, "dp", axis=0, tiled=True),
        lax.all_gather(w_fc2, "dp", axis=1, tiled=True),
    )
    model_width = tokens.shape[1]
    local_rows = tokens.shape[0]
    head_dim = model_width // HEADS
    factor = 1.0 / math.sqrt(head_dim)
    doc_ends = jnp.cumsum(doc_lengths[0])[:-1]
    places = jnp.arange(local_rows)
    doc_ids = jnp.sum((places[:, None] >= doc_ends[None, :]).astype(jnp.int32), axis=1)
    inputs = tokens.astype(jnp.float32)
    normed_one, inverse_one = normalize(inputs)
    normed_in = (normed_one * gain_full[:, 0] + bias_full[:, 0]).astype(jnp.bfloat16)
    zero_bias = jnp.zeros((model_width,), jnp.float32)
    qkv_bias = jnp.concatenate([bias_full[:, 1], zero_bias, bias_full[:, 2]])
    projected = (
        jnp.dot(normed_in, qkv_full, preferred_element_type=jnp.float32) + qkv_bias
    ).astype(jnp.bfloat16)
    query_rows = projected[:, :model_width].reshape(local_rows, HEADS, head_dim)
    key_rows = projected[:, model_width : 2 * model_width].reshape(local_rows, HEADS, head_dim)
    value_rows = projected[:, 2 * model_width :].reshape(local_rows, HEADS, head_dim)
    attended, sums_log = attend_forward(query_rows, key_rows, value_rows, doc_ids, factor)
    attended = attended.reshape(local_rows, model_width)
    scale_wide = jnp.repeat(head_scale, head_dim)
    scaled = (attended * scale_wide).astype(jnp.bfloat16)
    branch = jnp.dot(scaled, out_full, preferred_element_type=jnp.float32) + bias_full[:, 3]
    normed_post, inverse_post = normalize(branch)
    middle = inputs + normed_post * gain_full[:, 1] + bias_full[:, 4]
    normed_two, inverse_two = normalize(middle)
    normed_mid = (normed_two * gain_full[:, 2] + bias_full[:, 5]).astype(jnp.bfloat16)
    gathered = lax.all_gather(normed_mid, "tensor", axis=0, tiled=True)
    hidden_pre = jnp.dot(gathered, fc1_rows, preferred_element_type=jnp.float32) + ffn_biases[0]
    activated, gelu_pull = jax.vjp(jax.nn.gelu, hidden_pre)
    act_sum, act_square = (
        lax.psum(jnp.sum(activated, axis=1).astype(jnp.bfloat16), "tensor").astype(jnp.float32),
        lax.psum(jnp.sum(activated * activated, axis=1).astype(jnp.bfloat16), "tensor").astype(
            jnp.float32
        ),
    )
    center = act_sum / FF
    inverse_mid = lax.rsqrt(act_square / FF - center * center + EPS)[:, None]
    normed_act = (activated - center[:, None]) * inverse_mid
    hidden = (normed_act * mid_gain + ffn_biases[1]).astype(jnp.bfloat16)
    hidden_rows = hidden
    ffn_out = lax.psum_scatter(
        jnp.dot(hidden_rows, fc2_cols, preferred_element_type=jnp.float32).astype(jnp.bfloat16),
        "tensor",
        scatter_dimension=0,
        tiled=True,
    ).astype(jnp.float32)
    shard_rows = lax.all_gather(out_grad, "tensor", axis=0, tiled=True)
    grad_piece = jnp.einsum("rd,fd->rf", shard_rows, fc2_cols, preferred_element_type=jnp.float32)
    hidden_rows = hidden
    fc2_run = jnp.einsum("rf,rd->fd", hidden_rows, shard_rows, preferred_element_type=jnp.float32)
    mid_gain_part = jnp.sum(grad_piece * normed_act, axis=0)
    mid_bias_part = jnp.sum(grad_piece, axis=0)
    grad_normed_act = grad_piece * mid_gain
    first_sum, second_sum = (
        lax.psum(jnp.sum(grad_normed_act, axis=1).astype(jnp.bfloat16), "tensor").astype(
            jnp.float32
        ),
        lax.psum(
            jnp.sum(grad_normed_act * normed_act, axis=1).astype(jnp.bfloat16), "tensor"
        ).astype(jnp.float32),
    )
    grad_act = inverse_mid * (
        grad_normed_act - first_sum[:, None] / FF - normed_act * (second_sum[:, None] / FF)
    )
    grad_pre = gelu_pull(grad_act)[0].astype(jnp.bfloat16)
    fc1_part = jnp.einsum("rd,rf->df", gathered, grad_pre, preferred_element_type=jnp.float32)
    fc1_bias_part = jnp.sum(grad_pre.astype(jnp.float32), axis=0)
    grad_normed_mid = lax.psum_scatter(
        jnp.einsum("rf,df->rd", grad_pre, fc1_rows, preferred_element_type=jnp.float32).astype(
            jnp.bfloat16
        ),
        "tensor",
        scatter_dimension=0,
        tiled=True,
    ).astype(jnp.float32)
    ffn_bias_part = jnp.stack([fc1_bias_part, mid_bias_part])
    fc1_grad, fc2_grad = (
        lax.psum_scatter(
            fc1_part.astype(jnp.bfloat16), "dp", scatter_dimension=0, tiled=True
        ).astype(jnp.float32),
        lax.psum_scatter(
            fc2_run.astype(jnp.bfloat16), "dp", scatter_dimension=1, tiled=True
        ).astype(jnp.float32),
    )
    mid_gain_grad, ffn_bias_grad = lax.psum((mid_gain_part, ffn_bias_part), "dp")
    mixed_out = (middle + ffn_out + bias_full[:, 6]).astype(jnp.bfloat16)
    final_grad = out_grad.astype(jnp.float32)
    grad_middle = final_grad + normalize_back(
        grad_normed_mid * gain_full[:, 2], normed_two, inverse_two
    )
    grad_post = normalize_back(grad_middle * gain_full[:, 1], normed_post, inverse_post).astype(
        jnp.bfloat16
    )
    out_local = jnp.einsum("td,te->de", scaled, grad_post, preferred_element_type=jnp.float32)
    grad_scaled = jnp.einsum("te,de->td", grad_post, out_full, preferred_element_type=jnp.float32)
    scale_local = jnp.sum(
        (grad_scaled * attended).reshape(local_rows, HEADS, head_dim), axis=(0, 2)
    )
    grad_attended = (
        (grad_scaled * scale_wide).astype(jnp.bfloat16).reshape(local_rows, HEADS, head_dim)
    )
    grad_query, grad_keys, grad_values = attend_backward(
        query_rows, key_rows, value_rows, grad_attended, doc_ids, sums_log, factor
    )
    grad_projected = jnp.concatenate(
        [
            grad_query.reshape(local_rows, model_width),
            grad_keys.reshape(local_rows, model_width),
            grad_values.reshape(local_rows, model_width),
        ],
        axis=1,
    ).astype(jnp.bfloat16)
    qkv_local = jnp.einsum(
        "td,te->de", normed_in, grad_projected, preferred_element_type=jnp.float32
    )
    grad_normed_in = jnp.einsum(
        "te,de->td", grad_projected, qkv_full, preferred_element_type=jnp.float32
    )
    token_grad = grad_middle + normalize_back(
        grad_normed_in * gain_full[:, 0], normed_one, inverse_one
    )
    projected_sums = jnp.sum(grad_projected.astype(jnp.float32), axis=0)
    gains_local = jnp.stack(
        [
            jnp.sum(grad_normed_in * normed_one, axis=0),
            jnp.sum(grad_middle * normed_post, axis=0),
            jnp.sum(grad_normed_mid * normed_two, axis=0),
        ],
        axis=1,
    )
    biases_local = jnp.stack(
        [
            jnp.sum(grad_normed_in, axis=0),
            projected_sums[:model_width],
            projected_sums[2 * model_width :],
            jnp.sum(grad_post.astype(jnp.float32), axis=0),
            jnp.sum(grad_middle, axis=0),
            jnp.sum(grad_normed_mid, axis=0),
            jnp.sum(final_grad, axis=0),
        ],
        axis=1,
    )
    qkv_grad, out_weight_grad, gains_grad, biases_grad = (
        lax.psum_scatter(qkv_local, ("dp", "tensor"), scatter_dimension=0, tiled=True),
        lax.psum_scatter(out_local, ("dp", "tensor"), scatter_dimension=0, tiled=True),
        lax.psum_scatter(gains_local, ("dp", "tensor"), scatter_dimension=0, tiled=True),
        lax.psum_scatter(biases_local, ("dp", "tensor"), scatter_dimension=0, tiled=True),
    )
    scale_grad = lax.psum(scale_local, ("dp", "tensor"))
    return (
        mixed_out,
        token_grad,
        qkv_grad,
        out_weight_grad,
        gains_grad,
        biases_grad,
        scale_grad,
        fc1_grad,
        fc2_grad,
        mid_gain_grad,
        ffn_bias_grad,
    )


MESH = pl.DeviceIdType.MESH
ANY = pl.BlockSpec(memory_space=pl.ANY)
IN_VMEM = pl.BlockSpec(memory_space=pltpu.VMEM)


def place():
    z = lax.axis_index("dp")
    t = lax.axis_index("tensor")
    return z, lax.div(t, 4), lax.rem(lax.div(t, 2), 2), lax.rem(t, 2)


def at(z, y, x, c):
    return (z, y * 4 + x * 2 + c)


def greet(partners):
    barrier = pltpu.get_barrier_semaphore()
    for partner in partners:
        pl.semaphore_signal(barrier, inc=1, device_id=partner, device_id_type=MESH)
    pl.semaphore_wait(barrier, len(partners))


class Sends:
    def __init__(self, send_sems, recv_sems):
        self.send_sems, self.recv_sems, self.copies = send_sems, recv_sems, []

    def start(self, src, dst, target):
        index = len(self.copies)
        copy = pltpu.make_async_remote_copy(
            src_ref=src,
            dst_ref=dst,
            send_sem=self.send_sems.at[index],
            recv_sem=self.recv_sems.at[index],
            device_id=target,
            device_id_type=MESH,
        )
        copy.start()
        self.copies.append(copy)
        return copy

    def finish(self):
        for copy in self.copies:
            copy.wait_send()


def add_low(left, right):
    return (left.astype(jnp.float32) + right.astype(jnp.float32)).astype(jnp.bfloat16)


SQRT_2_PI = math.sqrt(2.0 / math.pi)
NT = (((1,), (1,)), ((), ()))
TN = (((0,), (0,)), ((), ()))


def dot(left, right, dims=None):
    if dims is None:
        return jnp.dot(left, right, preferred_element_type=jnp.float32)
    return lax.dot_general(left, right, dims, preferred_element_type=jnp.float32)


def centered(values):
    center = jnp.mean(values, axis=-1, keepdims=True)
    spread = jnp.mean(values * values, axis=-1, keepdims=True) - center * center
    inverse = lax.rsqrt(spread + EPS)
    return (values - center) * inverse, inverse


def centered_back(grad, normed, inverse):
    first = jnp.mean(grad, axis=-1, keepdims=True)
    second = jnp.mean(grad * normed, axis=-1, keepdims=True)
    return inverse * (grad - first - normed * second)


def eights(values):
    return jnp.sum(values.reshape(values.shape[0] // 8, 8, values.shape[1]), axis=0)


def doc_mask(doc_ref, rows):
    query = lax.broadcasted_iota(jnp.int32, (rows, rows), 0)
    key = lax.broadcasted_iota(jnp.int32, (rows, rows), 1)
    query_doc, key_doc = jnp.zeros_like(query), jnp.zeros_like(key)
    end = 0
    for j in range(doc_ref.shape[1] - 1):
        end = end + doc_ref[0, j]
        query_doc = query_doc + (query >= end).astype(jnp.int32)
        key_doc = key_doc + (key >= end).astype(jnp.int32)
    allowed = jnp.logical_and(query_doc == key_doc, key <= query)
    return allowed.astype(jnp.float32)


class Plane:
    def __init__(self, sends, whole, here, targets):
        self.sends, self.whole, self.here, self.targets = sends, whole, here, targets
        half = whole.shape[3] // 2
        self.lo, self.hi = pl.ds(0, half), pl.ds(half, half)

    def part(self, y, x, c, rows):
        return self.whole.at[y, x, c, rows]

    def start_first(self, src):
        (y, x, c), (to_x, to_y, to_c), lo, hi = self.here, self.targets, self.lo, self.hi
        go = self.sends.start
        self.first = [
            go(src.at[lo], self.part(y, x, c, lo), to_x),
            go(src.at[hi], self.part(y, x, c, hi), to_y),
        ]
        self.core = [go(src, self.whole.at[y, x, c], to_c)]

    def start_second(self, src):
        (y, x, c), (to_x, to_y, _), lo, hi = self.here, self.targets, self.lo, self.hi
        go = self.sends.start
        self.second = [
            go(src.at[lo], self.part(y, x, c, lo), to_y),
            go(src.at[hi], self.part(y, x, c, hi), to_x),
        ]

    def after_first(self):
        (y, x, c), (to_x, to_y, to_c), lo, hi = self.here, self.targets, self.lo, self.hi
        for copy in self.first:
            copy.wait_recv()
        by_x, by_y = self.part(y, 1 - x, c, lo), self.part(1 - y, x, c, hi)
        go = self.sends.start
        self.third = [go(by_x, by_x, to_y), go(by_y, by_y, to_x)]
        self.side = [go(by_x, by_x, to_c), go(by_y, by_y, to_c)]

    def after_second(self):
        (y, x, c), (to_x, to_y, to_c), lo, hi = self.here, self.targets, self.lo, self.hi
        for copy in self.second:
            copy.wait_recv()
        by_x, by_y = self.part(y, 1 - x, c, hi), self.part(1 - y, x, c, lo)
        go = self.sends.start
        self.side += [go(by_x, by_x, to_c), go(by_y, by_y, to_c)]

    def after_third(self):
        y, x, c = self.here
        self.last = []
        for copy, part in zip(self.third, (self.lo, self.hi)):
            copy.wait_recv()
            ref = self.part(1 - y, 1 - x, c, part)
            self.last.append(self.sends.start(ref, ref, self.targets[2]))


def fore_kernel(
    nz,
    tok_ref,
    og_ref,
    qkv_ref,
    out_ref,
    gains_ref,
    biases_ref,
    fc1_ref,
    fc2_ref,
    gain_ref,
    shift_ref,
    doc_ref,
    scale_ref,
    qkv_out,
    out_out,
    vec_out,
    proj_out,
    att_out,
    lse_out,
    branch_out,
    middle_out,
    nin_out,
    scaled_out,
    ffn_out,
    first_out,
    fc2_out,
    late_out,
    gnm_out,
    fc1_out,
    unit_out,
    qkv_all,
    out_all,
    vec_all,
    vec_plane,
    vec_pair,
    vec_mine,
    vec_turn,
    unit_ref,
    fc1_all,
    fc2_all,
    og_all,
    tok,
    branch,
    nin,
    proj,
    att,
    lse,
    scaled,
    middle,
    mask,
    vec,
    mid_all,
    act,
    slope,
    grad,
    hidden,
    grad_pre,
    mid_part,
    pre,
    stats,
    pair,
    got,
    totals,
    from_core,
    sums,
    from_one,
    from_two,
    f_part,
    f_core,
    f_sums,
    fc1_part,
    late_part,
    fc2_part,
    fc1_got,
    local_sems,
    send_sems,
    recv_sems,
):
    z, y, x, c = place()
    to_x, to_y, to_c = at(z, y, 1 - x, c), at(z, 1 - y, x, c), at(z, y, x, 1 - c)
    to_xy = at(z, 1 - y, 1 - x, c)
    others = [lax.rem(z + k, nz) for k in range(1, nz)]
    slots = [z] + [lax.rem(z + nz - k, nz) for k in range(1, nz)]
    peers = [at(other, y, x, c) for other in others]
    locals_ = []

    def fetch(src, dst):
        copy = pltpu.make_async_copy(src, dst, local_sems.at[len(locals_)])
        copy.start()
        locals_.append(copy)
        return copy

    rows, width = tok.shape
    fourth = width // 4
    qkv_in = [
        fetch(
            qkv_ref.at[:, pl.ds(i * width + g * fourth, fourth)],
            qkv_all.at[z, y, x, c, :, pl.ds((3 * g + i) * fourth, fourth)],
        )
        for g in range(4)
        for i in range(3)
    ]
    vec_turn[...] = jnp.zeros_like(vec_turn)
    share = qkv_ref.shape[0]
    vec_turn[0:3, 0:share] = gains_ref[...]
    vec_turn[3:10, 0:share] = biases_ref[...]
    across = vec_turn[...].T[:share]
    vec_turn[...] = jnp.zeros_like(vec_turn)
    vec_turn[pl.ds(pl.multiple_of((2 * x + c) * share, share), share)] = across
    vec_mine[...] = vec_turn[...].T[:16]
    greet([to_x, to_y, to_c, to_xy] + peers)
    sends = Sends(send_sems, recv_sems)
    low, f32 = jnp.bfloat16, jnp.float32
    units = fc1_all.shape[1]
    width1, width2 = fc1_ref.shape[0], fc2_ref.shape[1]
    own1 = fc1_all.at[pl.ds(pl.multiple_of(z * width1, width1), width1)]
    own2 = fc2_all.at[:, pl.ds(pl.multiple_of(z * width2, width2), width2)]
    def wait_all(copies):
        for copy in copies:
            copy.wait_recv()

    vec_z = [sends.start(vec_mine, vec_all.at[0, z], peer) for peer in peers]
    phase = 6 * fourth
    spans = (pl.ds(0, phase), pl.ds(phase, phase))
    for copy in qkv_in:
        copy.wait()
    own_qkv = qkv_all.at[z, y, x, c]
    qkv_z = [
        [sends.start(own_qkv.at[:, span], own_qkv.at[:, span], peer) for peer in peers]
        for span in spans
    ]

    z_pair = z + 1 - 2 * lax.rem(z, 2)
    pair_peer, far_peer = at(z_pair, y, x, c), peers[1]
    qkv_slots = slots

    def go_on(p):
        qkv_z[p][0].wait_recv()

    def sides(whole, p):
        size = phase // 2 if whole is qkv_all else whole.shape[-1] // 2
        return pl.ds(2 * p * size, size), pl.ds((2 * p + 1) * size, size)

    def first(whole, slot, p=0):
        lo, hi = sides(whole, p)
        by_x, by_y = whole.at[slot, y, x, c, :, lo], whole.at[slot, y, x, c, :, hi]
        return (sends.start(by_x, by_x, to_x), sends.start(by_y, by_y, to_y))

    def second(whole, slot, p=0):
        lo, hi = sides(whole, p)
        by_x, by_y = whole.at[slot, y, :, c, :, lo], whole.at[slot, :, x, c, :, hi]
        return (sends.start(by_x, by_x, to_y), sends.start(by_y, by_y, to_x))

    def third(whole, slot, p=None):
        ref = whole.at[slot, :, :, c] if p is None else whole.at[slot, :, :, c, :, spans[p]]
        return sends.start(ref, ref, to_c)

    a0, a1 = [first(qkv_all, z, 0)], [first(qkv_all, z, 1)]
    og = Plane(sends, og_all, (y, x, c), (to_x, to_y, to_c))
    og.start_first(og_ref)
    tok_in = fetch(tok_ref, tok)
    out_in = fetch(out_ref, out_all.at[z, y, x, c])
    fc1_in = fetch(fc1_ref, own1)
    fc2_in = fetch(fc2_ref, own2)
    og_in = fetch(og_ref, og_all.at[y, x, c])
    vec_all[0, z] = vec_mine[...]
    unit_ref[...] = jnp.zeros_like(unit_ref)
    unit_ref[0:1] = shift_ref[0:1]
    unit_ref[1:2] = gain_ref[...]
    unit_ref[2:3] = shift_ref[1:2]
    step = 32
    mask[...] = doc_mask(doc_ref, rows)
    tok_in.wait()

    def normed(k, carry):
        part = pl.ds(pl.multiple_of(k * step, step), step)
        branch[part] = centered(tok[part].astype(f32))[0]
        return carry

    lax.fori_loop(0, rows // step, normed, 0)
    wait_all(vec_z)
    vec_x = sends.start(vec_all.at[0], vec_all.at[1], to_x)
    wait_all(a0[0])
    b0 = [second(qkv_all, z, 0)]
    wait_all(a1[0])
    b1 = [second(qkv_all, z, 1)]
    go_on(0)
    a0.append(first(qkv_all, qkv_slots[1], 0))
    vec_x.wait_recv()
    vec_plane[y] = vec_all[0] + vec_all[1]
    vec_y = sends.start(vec_plane.at[y], vec_plane.at[y], to_y)
    for k in range(2, nz):
        qkv_z[0][k - 1].wait_recv()
        a0.append(first(qkv_all, qkv_slots[k], 0))
    vec_y.wait_recv()
    vec_c = sends.start(vec_plane, vec_pair, to_c)
    for k in range(1, nz):
        wait_all(a0[k])
        b0.append(second(qkv_all, qkv_slots[k], 0))
    go_on(1)
    a1.append(first(qkv_all, qkv_slots[1], 1))
    vec_c.wait_recv()
    for n in range(2 * nz):
        vec[:, n * 128 : (n + 1) * 128] = vec_plane[n % 2, n // 2] + vec_pair[n % 2, n // 2]
    spot = lax.broadcasted_iota(jnp.int32, (1, width), 1)
    head = 64
    wide = jnp.zeros((1, width), f32)
    for h in range(HEADS):
        inside = jnp.logical_and(spot >= h * head, spot < (h + 1) * head)
        wide = jnp.where(inside, scale_ref[h], wide)
    vec[10:11] = wide

    def scaled_in(k, carry):
        part = pl.ds(pl.multiple_of(k * step, step), step)
        nin[part] = (branch[part] * vec[0:1] + vec[3:4]).astype(low)
        return carry

    lax.fori_loop(0, rows // step, scaled_in, 0)
    wait_all(b0[0])
    c0 = [third(qkv_all, z, 0)]
    for k in range(2, nz):
        qkv_z[1][k - 1].wait_recv()
        a1.append(first(qkv_all, qkv_slots[k], 1))
        wait_all(b0[k - 1])
        c0.append(third(qkv_all, qkv_slots[k - 1], 0))
    out_in.wait()
    own_out = out_all.at[z, y, x, c]
    out_z = [sends.start(own_out, own_out, peer) for peer in peers]
    fc2_far = sends.start(fc2_ref, own2, far_peer)
    fc2_near = sends.start(fc2_ref, own2, pair_peer)
    fc1_z = [sends.start(fc1_ref, own1, peer) for peer in peers]
    wait_all(b0[nz - 1])
    c0.append(third(qkv_all, qkv_slots[nz - 1], 0))
    wait_all(a1[1])
    b1.append(second(qkv_all, qkv_slots[1], 1))
    wait_all(c0)

    def project(p):
        for g in (2 * p, 2 * p + 1):
            cols = pl.ds(3 * g * fourth, 3 * fourth)
            here = pl.ds(g * fourth, fourth)
            bias = jnp.concatenate(
                [vec[4:5, here], jnp.zeros((1, fourth), f32), vec[5:6, here]], axis=1
            )
            block = dot(nin[...], qkv_all[:, :, :, :, :, cols].reshape(width, 3 * fourth))
            proj[:, cols] = (block + bias).astype(low)

    project(0)
    lane = lax.broadcasted_iota(jnp.int32, (1, 128), 1)
    is_low = lane < head
    keep = (is_low.astype(low), (lane >= head).astype(low))
    factor = 1.0 / math.sqrt(head)
    lane_wide = lax.broadcasted_iota(jnp.int32, (rows, 128), 1)
    lse[...] = jnp.zeros_like(lse)

    def attend(p, carry):
        base = lax.div(p, 2) * (3 * fourth) + lax.rem(p, 2) * 128
        q_at = pl.ds(pl.multiple_of(base, 128), 128)
        k_at = pl.ds(pl.multiple_of(base + fourth, 128), 128)
        v_at = pl.ds(pl.multiple_of(base + 2 * fourth, 128), 128)
        here = pl.ds(pl.multiple_of(p * 128, 128), 128)
        q2, k2, v2 = proj[:, q_at], proj[:, k_at], proj[:, v_at]
        found, logs = [], []
        for i in range(2):
            scores = dot(q2 * keep[i], k2, NT) * factor
            scores = jnp.where(mask[...] > 0, scores, NEGATIVE)
            peak = jnp.max(scores, axis=1, keepdims=True)
            exponent = jnp.exp(scores - peak)
            total = jnp.sum(exponent, axis=1, keepdims=True)
            prob = (exponent * (1.0 / total)).astype(low)
            found.append(dot(prob, v2))
            logs.append(peak + jnp.log(total))
        spread_logs = jnp.where(lane_wide == 2 * p, logs[0], logs[1])
        at_pair = lax.div(lane_wide, 2) == p
        lse[...] = jnp.where(at_pair, spread_logs, lse[...])
        both = jnp.where(is_low, *found)
        att[:, here] = both
        scaled[:, here] = (both * vec[10:11, here]).astype(low)
        return carry

    lax.fori_loop(0, 1, attend, 0)
    for k in range(2, nz):
        wait_all(a1[k])
        b1.append(second(qkv_all, qkv_slots[k], 1))
    out_a = [first(out_all, z)]
    for k in range(1, nz):
        out_z[k - 1].wait_recv()
        out_a.append(first(out_all, slots[k]))
    og.start_second(og_ref)
    lax.fori_loop(1, 2, attend, 0)
    c1 = []
    for k in range(2):
        wait_all(b1[k])
        c1.append(third(qkv_all, qkv_slots[k], 1))
    lax.fori_loop(2, 4, attend, 0)
    for k in range(2, nz):
        wait_all(b1[k])
        c1.append(third(qkv_all, qkv_slots[k], 1))
    wait_all(c1)
    saves = [fetch(qkv_all, qkv_out), fetch(vec, vec_out), fetch(nin, nin_out)]
    project(1)
    saves.append(fetch(proj, proj_out))
    out_b = []
    for k in range(nz):
        wait_all(out_a[k])
        out_b.append(second(out_all, slots[k]))
    lax.fori_loop(4, 6, attend, 0, unroll=True)
    og.after_first()
    lax.fori_loop(6, 8, attend, 0, unroll=True)
    out_c = []
    for k in range(nz):
        wait_all(out_b[k])
        out_c.append(third(out_all, slots[k]))
    saves += [fetch(att, att_out), fetch(lse, lse_out), fetch(scaled, scaled_out)]
    wait_all(out_c)
    saves.append(fetch(out_all, out_out))
    quarter = width // 4
    for k in range(4):
        cols = pl.ds(k * quarter, quarter)
        block = dot(scaled[...], out_all[:, :, :, :, :, cols].reshape(width, quarter))
        branch[:, cols] = block + vec[6:7, cols]

    def middles(k, carry):
        part = pl.ds(pl.multiple_of(k * step, step), step)
        post = centered(branch[part])[0]
        value = tok[part].astype(f32) + post * vec[1:2] + vec[7:8]
        middle[part] = value
        mid_all[y, x, c, part] = (centered(value)[0] * vec[2:3] + vec[8:9]).astype(low)
        return carry

    lax.fori_loop(0, rows // step, middles, 0, unroll=2)
    mid = Plane(sends, mid_all, (y, x, c), (to_x, to_y, to_c))
    mid.start_first(mid_all.at[y, x, c])
    mid.start_second(mid_all.at[y, x, c])
    branch_put = fetch(branch, branch_out)
    saves.append(fetch(middle, middle_out))

    def grads(yy, xx, cc):
        grad[yy, xx, cc] = dot(og_all[yy, xx, cc], fc2_all[...], NT)

    def fold(v):
        quarters = [v[:, k * (units // 4) : (k + 1) * (units // 4)] for k in range(4)]
        return (quarters[0] + quarters[1]) + (quarters[2] + quarters[3])

    def forward(yy, xx, cc):
        pre[...] = dot(mid_all[yy, xx, cc], fc1_all[...])

        def block(k, carry):
            part = pl.ds(pl.multiple_of(k * step, step), step)
            u = pre[part] + unit_ref[0:1]
            square = u * u
            th = jnp.tanh(u * (SQRT_2_PI + (SQRT_2_PI * 0.044715) * square))
            lift = 0.5 + 0.5 * th
            a = u * lift
            act[yy, xx, cc, part] = a
            bend = u * (2.0 * SQRT_2_PI + (6.0 * 0.044715 * SQRT_2_PI) * square)
            slope[yy, xx, cc, part] = lift + bend * (lift - lift * lift)
            gm = grad[yy, xx, cc, part] * unit_ref[1:2]
            for j, value in enumerate((a, a * a, gm, gm * a)):
                pre[part, j * (units // 4) : (j + 1) * (units // 4)] = fold(value)
            return carry

        lax.fori_loop(0, rows // step, block, 0)
        for j in range(4):
            folded = pre[:, j * (units // 4) : (j + 1) * (units // 4)]
            stats[yy, xx, cc, j : j + 1] = jnp.sum(folded.T, axis=0, keepdims=True)

    og.after_second()
    fc2_in.wait()
    fc2_far.wait_recv()
    near = fc2_all.at[:, pl.ds(pl.multiple_of(others[1] * width2, width2), width2)]
    fc2_last = sends.start(near, near, pair_peer)
    fc2_near.wait_recv()
    og.after_third()
    fc1_in.wait()
    mid.after_first()
    fc2_last.wait_recv()
    og_in.wait()
    grads(y, x, c)
    wait_all(og.core)
    grads(y, x, 1 - c)
    grads(y, 1 - x, c)
    grads(1 - y, x, c)
    mid.after_second()
    wait_all(og.side)
    grads(y, 1 - x, 1 - c)
    grads(1 - y, x, 1 - c)
    grads(1 - y, 1 - x, c)
    wait_all(og.last)
    grads(1 - y, 1 - x, 1 - c)
    wait_all(fc1_z)
    forward(y, x, c)
    wait_all(mid.core)
    forward(y, x, 1 - c)
    forward(y, 1 - x, c)
    forward(1 - y, x, c)
    wait_all(mid.side)
    forward(y, 1 - x, 1 - c)
    forward(1 - y, x, 1 - c)
    mid.after_third()
    forward(1 - y, 1 - x, c)
    wait_all(mid.last)
    forward(1 - y, 1 - x, 1 - c)

    sends.start(stats, got.at[3], to_c).wait_recv()
    pair[...] = stats[...] + got[3]
    wait_all([sends.start(pair, got.at[k], to) for k, to in enumerate((to_x, to_y, to_xy))])
    total = (pair[...] + got[0]) + (got[1] + got[2])
    total = total * (1.0 / (units * 8))
    center, square = total[:, :, :, 0:1], total[:, :, :, 1:2]
    mean, cross = total[:, :, :, 2:3], total[:, :, :, 3:4]
    inverse = lax.rsqrt(square - center * center + EPS)
    totals[:, :, :, 0:1] = inverse
    totals[:, :, :, 1:2] = -center * inverse
    totals[:, :, :, 2:3] = inverse * mean
    totals[:, :, :, 3:4] = inverse * (inverse * (cross - center * mean))
    unit_out[...] = jnp.zeros_like(unit_out)

    def backward(yy, xx, cc):
        for j in range(4):
            spread = jnp.broadcast_to(totals[yy, xx, cc, j : j + 1], (128, rows))
            pre[:, j * 128 : (j + 1) * 128] = spread.T

        def block(k, carry):
            part = pl.ds(pl.multiple_of(k * step, step), step)

            def across(j):
                return jnp.concatenate([pre[part, j * 128 : (j + 1) * 128]] * (units // 128), axis=1)

            g = grad[yy, xx, cc, part]
            inverse = across(0)
            normed = act[yy, xx, cc, part] * inverse + across(1)
            gain = unit_ref[1:2]
            hidden[yy, xx, cc, part] = (normed * gain + unit_ref[2:3]).astype(low)
            back = g * gain * inverse - across(2) - normed * across(3)
            value = (back * slope[yy, xx, cc, part]).astype(low)
            grad_pre[yy, xx, cc, part] = value
            return (
                carry[0] + eights(g * normed),
                carry[1] + eights(value.astype(f32)),
                carry[2] + eights(g),
            )

        zero = jnp.zeros((8, units), f32)
        parts = lax.fori_loop(0, rows // step, block, (zero, zero, zero))
        for j, part in enumerate(parts):
            unit_out[j : j + 1] += jnp.sum(part, axis=0, keepdims=True)
        return dot(grad_pre[yy, xx, cc], fc1_all[...], NT)

    left, right = pl.ds(0, width // 2), pl.ds(width // 2, width // 2)
    order = [(1 - y, 1 - x), (y, 1 - x), (1 - y, x), (y, x)]
    stage_x, stage_y, cores = [], [], []

    def to_core(k):
        yy, xx = order[k]
        mid_part[yy, xx] = backward(yy, xx, 1 - c).astype(low)
        cores.append(sends.start(mid_part.at[yy, xx], from_core.at[yy, xx], to_c))

    def from_pair(k):
        yy, xx = order[k]
        block = backward(yy, xx, c)
        cores[k].wait_recv()
        sums[yy, xx] = (block + from_core[yy, xx].astype(f32)).astype(low)
        if k in (0, 1):
            stage_x.append(sends.start(sums.at[yy, xx, :, left], from_one.at[yy, :, left], to_x))
        if k in (0, 2):
            stage_y.append(sends.start(sums.at[yy, xx, :, right], from_one.at[xx, :, right], to_y))

    to_core(0)
    to_core(1)
    from_pair(0)
    to_core(2)
    from_pair(1)
    to_core(3)
    from_pair(2)
    from_pair(3)

    def ffn_of(yy, xx, cc):
        return dot(hidden[yy, xx, cc], fc2_all[...])

    blocks = nz
    size = width // blocks

    early = fc1_part.shape[-1]
    soon, late = slice(0, early), slice(early, units)

    def fc1_block(which, cols):
        part = pl.ds(pl.multiple_of(which * size, 128), size)
        block = jnp.zeros((size, cols.stop - cols.start), f32)
        for j in range(8):
            yxc = (j // 4, (j // 2) % 2, j % 2)
            block = block + dot(mid_all[(*yxc, slice(None), part)], grad_pre[(*yxc, slice(None), cols)], TN)
        return block

    fc1_far = {}
    for k in (1, 0, 2):
        fc1_part[k] = fc1_block(others[k], soon).astype(low)
        fc1_far[k] = sends.start(fc1_part.at[k], fc1_got.at[k], peers[k])
    wait_all((stage_x[0], stage_y[0]))
    sums[1 - y, x, :, left] = add_low(sums[1 - y, x, :, left], from_one[1 - y, :, left])
    sums[y, 1 - x, :, right] = add_low(sums[y, 1 - x, :, right], from_one[1 - x, :, right])
    last_y = sends.start(sums.at[1 - y, x, :, left], from_two.at[:, left], to_y)
    last_x = sends.start(sums.at[y, 1 - x, :, right], from_two.at[:, right], to_x)
    fc1_out[:, soon] = fc1_block(z, soon)
    fc1_out[:, late] = fc1_block(z, late)

    def late_block(k, carry):
        part = pl.ds(pl.multiple_of(k * size, 128), size)
        late_part[part] = fc1_block(k, late).astype(low)
        return carry

    lax.fori_loop(0, blocks, late_block, 0)
    saves.append(fetch(late_part, late_out))
    cores = []
    for yy, xx in order:
        f_part[yy, xx] = ffn_of(yy, xx, 1 - c).astype(low)
        cores.append(sends.start(f_part.at[yy, xx], f_core.at[yy, xx], to_c))
    for k, (yy, xx) in enumerate(order):
        block = ffn_of(yy, xx, c)
        cores[k].wait_recv()
        f_sums[yy, xx] = (block + f_core[yy, xx].astype(f32)).astype(low)
    saves.append(fetch(f_sums, ffn_out))
    top = pl.ds(0, first_out.shape[1])
    out_x = sends.start(f_sums.at[:, 1 - x, top, left], first_out.at[:, :, left], to_x)
    out_y = sends.start(f_sums.at[1 - y, :, top, right], first_out.at[:, :, right], to_y)

    def fc2_block(k, carry):
        part = pl.ds(pl.multiple_of(k * size, 128), size)
        block = jnp.zeros((units, size), f32)
        for j in range(8):
            yxc = (j // 4, (j // 2) % 2, j % 2)
            block = block + dot(hidden[yxc], og_all[(*yxc, slice(None), part)], TN)
        fc2_part[:, part] = block.astype(low)
        return carry

    lax.fori_loop(0, blocks, fc2_block, 0)
    saves.append(fetch(fc2_part, fc2_out))
    branch_put.wait()
    wait_all((stage_x[1], stage_y[1], last_x, last_y))
    for cols, k in ((left, y), (right, x)):
        branch[:, cols] = (
            sums[y, x, :, cols].astype(f32)
            + from_one[k, :, cols].astype(f32)
            + from_two[:, cols].astype(f32)
        )
        saves.append(fetch(branch.at[:, cols], gnm_out.at[:, cols]))
    for k in range(nz - 1):
        fc1_far[k].wait_recv()
        fc1_out[:, soon] += fc1_got[k].astype(f32)
    wait_all((out_x, out_y))
    for copy in saves:
        copy.wait()
    sends.finish()


def fore(nz, tokens, og, doc_lengths, w_qkv, w_out, gains, biases, scale, fc1, fc2, gain, shift):
    rows, width = tokens.shape
    share, units = w_qkv.shape[0], fc1.shape[1]
    low, f32, plane, every = jnp.bfloat16, jnp.float32, (2, 2, 2), (nz, 2, 2, 2)
    sds, vm = jax.ShapeDtypeStruct, pltpu.VMEM
    count = 160
    smem = pl.BlockSpec(memory_space=pltpu.SMEM)
    shapes = (
        (every + w_qkv.shape, low),
        (every + w_out.shape, low),
        ((16, width), f32),
        ((rows, w_qkv.shape[1]), low),
        ((rows, width), f32),
        ((rows, 128), f32),
        ((rows, width), f32),
        ((rows, width), f32),
        ((rows, width), low),
        ((rows, width), low),
        ((2, 2, rows, width), low),
        ((2, rows // 4, width), low),
        ((units, width), low),
        ((width, units - 3 * units // 4), low),
        ((rows, width), f32),
        (fc1.shape, f32),
        ((8, units), f32),
    )
    return pl.pallas_call(
        functools.partial(fore_kernel, nz),
        name="fore",
        out_shape=tuple(sds(shape, kind) for shape, kind in shapes),
        in_specs=[ANY] * 4 + [IN_VMEM] * 2 + [ANY] * 2 + [IN_VMEM] * 2 + [smem] * 2,
        out_specs=[ANY] * 15 + [IN_VMEM] * 2,
        scratch_shapes=[
            vm(every + w_qkv.shape, low),
            vm(every + w_out.shape, low),
            vm((2, nz, 16, 128), f32),
            vm((2, nz, 16, 128), f32),
            vm((2, nz, 16, 128), f32),
            vm((16, 128), f32),
            vm((128, 128), f32),
            vm((8, units), f32),
            vm((width, units), low),
            vm((units, width), low),
            vm(plane + (rows, width), low),
            vm((rows, width), low),
            vm((rows, width), f32),
            vm((rows, width), low),
            vm((rows, w_qkv.shape[1]), low),
            vm((rows, width), f32),
            vm((rows, 128), f32),
            vm((rows, width), low),
            vm((rows, width), f32),
            vm((rows, rows), f32),
            vm((16, width), f32),
            vm(plane + (rows, width), low),
            vm(plane + (rows, units), f32),
            vm(plane + (rows, units), f32),
            vm(plane + (rows, units), f32),
            vm(plane + (rows, units), low),
            vm(plane + (rows, units), low),
            vm((2, 2, rows, width), low),
            vm((rows, units), f32),
            vm(plane + (4, rows), f32),
            vm(plane + (4, rows), f32),
            vm((4,) + plane + (4, rows), f32),
            vm(plane + (4, rows), f32),
            vm((2, 2, rows, width), low),
            vm((2, 2, rows, width), low),
            vm((2, rows, width), low),
            vm((rows, width), low),
            vm((2, 2, rows, width), low),
            vm((2, 2, rows, width), low),
            vm((2, 2, rows, width), low),
            vm((nz - 1, fc1.shape[0], 3 * units // 4), low),
            vm((width, units - 3 * units // 4), low),
            vm((units, width), low),
            vm((nz - 1, fc1.shape[0], 3 * units // 4), low),
            pltpu.SemaphoreType.DMA((40,)),
            pltpu.SemaphoreType.DMA((count,)),
            pltpu.SemaphoreType.DMA((count,)),
        ],
        compiler_params=pltpu.CompilerParams(
            collective_id=1, has_side_effects=True, vmem_limit_bytes=63 * 2**20
        ),
    )(tokens, og, w_qkv, w_out, gains.T, biases.T, fc1, fc2, gain, shift, doc_lengths, scale)


def back_kernel(
    nz,
    gnm_in,
    ffn_ref,
    first_in,
    late_ref,
    own1_in,
    fc2_ref,
    unit_ref,
    proj_in,
    att_in,
    lse_in,
    branch_in,
    middle_in,
    scaled_in,
    nin_in,
    qkv_in,
    out_in,
    vec_ref,
    og_in,
    tok_in,
    doc_ref,
    mixed_out,
    token_out,
    weight_out,
    gains_out,
    biases_out,
    scale_out,
    fc1_out,
    fc2_out,
    unit_out,
    f_sums,
    f_one,
    f_two,
    got1,
    got2,
    got_unit,
    w_part,
    w_core,
    w_sums,
    w_one,
    w_two,
    w_far,
    gpost,
    gmid,
    gatt,
    gni,
    dproj,
    nin_t,
    mask,
    accs,
    small,
    small_far,
    small_y,
    small_half,
    small_got,
    turned,
    mixed_at,
    weight_at,
    fc1_at,
    fc2_at,
    gnm_ref,
    proj_ref,
    att_ref,
    lse_ref,
    branch_ref,
    middle_ref,
    scaled_ref,
    nin_ref,
    qkv_ref,
    out_ref,
    og_ref,
    tok_ref,
    local_sems,
    send_sems,
    recv_sems,
):
    z, y, x, c = place()
    to_x, to_y, to_c = at(z, y, 1 - x, c), at(z, 1 - y, x, c), at(z, y, x, 1 - c)
    to_xy = at(z, 1 - y, 1 - x, c)
    others = [lax.rem(z + k, nz) for k in range(1, nz)]
    peers = [at(other, y, x, c) for other in others]
    locals_ = []

    def fetch(src, dst):
        copy = pltpu.make_async_copy(src, dst, local_sems.at[len(locals_)])
        copy.start()
        locals_.append(copy)
        return copy

    middle_got = fetch(middle_in, middle_ref)
    gnm_got = fetch(gnm_in, gnm_ref)
    og_got = fetch(og_in, og_ref)
    branch_got = fetch(branch_in, branch_ref)
    top, half = pl.ds(0, first_in.shape[1]), first_in.shape[2] // 2
    first_got = [
        fetch(first_in.at[:, :, pl.ds(i * half, half)], f_one.at[i, :, top, pl.ds(i * half, half)])
        for i in range(2)
    ]
    ffn_got = fetch(ffn_ref, f_sums)
    out_got = fetch(out_in, out_ref)
    att_got = fetch(att_in, att_ref)
    scaled_got = fetch(scaled_in, scaled_ref)
    nin_got = fetch(nin_in, nin_ref)
    proj_got = fetch(proj_in, proj_ref)
    lse_got = fetch(lse_in, lse_ref)
    qkv_got = fetch(qkv_in, qkv_ref)
    tok_got = fetch(tok_in, tok_ref)

    greet([to_x, to_y, to_c, to_xy] + peers)
    sends = Sends(send_sems, recv_sems)
    rows, width = middle_ref.shape
    low = jnp.bfloat16
    f32 = jnp.float32
    share = weight_out.shape[0]
    width1, width2 = fc1_out.shape[0], fc2_out.shape[1]

    pieces = 4
    parts = [pl.ds(k * (rows // pieces), rows // pieces) for k in range(pieces)]
    left, right = pl.ds(0, width // 2), pl.ds(width // 2, width // 2)
    def block1(which):
        return late_ref.at[pl.ds(pl.multiple_of(which * width1, width1), width1)]

    def block2(which):
        return fc2_ref.at[:, pl.ds(pl.multiple_of(which * width2, width2), width2)]

    own1_got = fetch(own1_in, fc1_at)
    own2_got = fetch(block2(z), got2.at[nz - 1])
    far = []
    for k, peer in enumerate(peers):
        far.append(sends.start(unit_ref, got_unit.at[k], peer))
        far.append(sends.start(block1(others[k]), got1.at[k], peer))
        far.append(sends.start(block2(others[k]), got2.at[k], peer))

    f_first, f_second = [], []

    def ffn_one(k):
        part = parts[k]
        f_first.append(
            (
                sends.start(ffn_ref.at[:, 1 - x, part, left], f_one.at[0, :, part, left], to_x),
                sends.start(ffn_ref.at[1 - y, :, part, right], f_one.at[1, :, part, right], to_y),
            )
        )

    def ffn_two(k):
        part = parts[k]
        if k == 0:
            ffn_got.wait()
            for copy in first_got:
                copy.wait()
        else:
            for copy in f_first[k - 1]:
                copy.wait_recv()
        f_sums[1 - y, x, part, left] = add_low(
            f_sums[1 - y, x, part, left], f_one[0, 1 - y, part, left]
        )
        f_sums[y, 1 - x, part, right] = add_low(
            f_sums[y, 1 - x, part, right], f_one[1, 1 - x, part, right]
        )
        f_second.append(
            (
                sends.start(f_sums.at[1 - y, x, part, left], f_two.at[part, left], to_y),
                sends.start(f_sums.at[y, 1 - x, part, right], f_two.at[part, right], to_x),
            )
        )

    def ffn_three(k):
        part = parts[k]
        for copy in f_second[k]:
            copy.wait_recv()
        for i, (cols, at_) in enumerate(((left, y), (right, x))):
            total = (
                f_sums[y, x, part, cols].astype(f32)
                + f_one[i, at_, part, cols].astype(f32)
                + f_two[part, cols].astype(f32)
            )
            mixed_at[part, cols] = (
                middle_ref[part, cols] + total + vec_ref[9:10, cols]
            ).astype(low)
        puts.append(fetch(mixed_at.at[part], mixed_out.at[part]))

    spans = [(0, width)] + [(width + g * 3 * width // 4, 3 * width // 4) for g in range(4)]
    w_first, w_second, w_third, w_c = {}, {}, {}, {}

    def sides(j):
        start, size = spans[j]
        return pl.ds(start, size), pl.ds(start, size // 2), pl.ds(start + size // 2, size // 2)

    def w_zero(j):
        every = sides(j)[0]
        w_c[j] = sends.start(w_part.at[:, :, :, 1 - c, :, every], w_core.at[..., every], to_c)

    def w_step1(j):
        every, lo, hi = sides(j)
        w_c[j].wait_recv()

        def one(which, carry):
            for yy in range(2):
                for xx in range(2):
                    w_sums[which, yy, xx, :, every] = add_low(
                        w_part[which, yy, xx, c, :, every], w_core[which, yy, xx, :, every]
                    )
            return carry

        lax.fori_loop(0, nz, one, 0)
        w_first[j] = (
            sends.start(w_sums.at[:, :, 1 - x, :, lo], w_one.at[:, :, :, lo], to_x),
            sends.start(w_sums.at[:, 1 - y, :, :, hi], w_one.at[:, :, :, hi], to_y),
        )

    def w_step2(j):
        every, lo, hi = sides(j)
        for copy in w_first[j]:
            copy.wait_recv()

        def one(which, carry):
            for k in range(2):
                w_sums[which, k, x, :, lo] = add_low(
                    w_sums[which, k, x, :, lo], w_one[which, k, :, lo]
                )
                w_sums[which, y, k, :, hi] = add_low(
                    w_sums[which, y, k, :, hi], w_one[which, k, :, hi]
                )
            return carry

        lax.fori_loop(0, nz, one, 0)
        w_second[j] = (
            sends.start(w_sums.at[:, 1 - y, x, :, lo], w_two.at[:, :, lo], to_y),
            sends.start(w_sums.at[:, y, 1 - x, :, hi], w_two.at[:, :, hi], to_x),
        )

    def w_step3(j):
        every = sides(j)[0]
        for copy in w_second[j]:
            copy.wait_recv()
        for which in range(nz):
            w_sums[which, y, x, :, every] = add_low(
                w_sums[which, y, x, :, every], w_two[which, :, every]
            )
        w_third[j] = [
            sends.start(w_sums.at[others[k], y, x, :, every], w_far.at[k, :, every], peer)
            for k, peer in enumerate(peers)
        ]

    def w_step4(j):
        start, size = spans[j]
        every = sides(j)[0]
        total = w_sums[z, y, x, :, every].astype(f32)
        for k in range(nz - 1):
            w_third[j][k].wait_recv()
            total = total + w_far[k, :, every].astype(f32)
        if j == 0:
            weight_at[:, 3 * width :] = total
            spots = [pl.ds(3 * width, width)]
        else:
            third = size // 3
            spots = [pl.ds(i * width + (j - 1) * third, third) for i in range(3)]
            for i, spot in enumerate(spots):
                weight_at[:, spot] = total[:, i * third : (i + 1) * third]
        for spot in spots:
            puts.append(fetch(weight_at.at[:, spot], weight_out.at[:, spot]))

    ffn_one(1)
    ffn_two(0)
    accs[...] = jnp.zeros_like(accs)
    step = 32

    def norms(k, carry):
        part = pl.ds(pl.multiple_of(k * step, step), step)
        normed_two, inverse_two = centered(middle_ref[part])
        grad = gnm_ref[part]
        og = og_ref[part].astype(f32)
        grad_middle = og + centered_back(grad * vec_ref[2:3], normed_two, inverse_two)
        accs[2] += eights(grad * normed_two)
        accs[8] += eights(grad)
        accs[9] += eights(og)
        normed_post, inverse_post = centered(branch_ref[part])
        post = centered_back(grad_middle * vec_ref[1:2], normed_post, inverse_post).astype(low)
        accs[1] += eights(grad_middle * normed_post)
        accs[7] += eights(grad_middle)
        accs[6] += eights(post.astype(f32))
        gpost[part] = post
        gmid[part] = grad_middle
        return carry

    for copy in (middle_got, gnm_got, og_got, branch_got):
        copy.wait()
    lax.fori_loop(0, rows // step, norms, 0, unroll=2)
    quarter = width // 4

    def out_block(k, carry):
        part = pl.ds(pl.multiple_of(k * (width // nz), width // nz), width // nz)
        block = dot(scaled_ref[:, part], gpost[...], TN).astype(low)
        w_part[k, :, :, :, :, pl.ds(0, width)] = block.reshape(2, 2, 2, share, width)
        return carry

    scaled_got.wait()
    lax.fori_loop(0, nz, out_block, 0)
    w_zero(0)
    mask[...] = doc_mask(doc_ref, rows)

    def scaled_block(k, carry):
        part = pl.ds(pl.multiple_of(k * quarter, quarter), quarter)
        block = dot(gpost[...], out_ref[part], NT)
        accs[10, :, part] = eights(block * att_ref[:, part])
        gatt[:, part] = (block * vec_ref[10:11, part]).astype(low)
        return carry

    out_got.wait()
    att_got.wait()
    lax.fori_loop(0, 4, scaled_block, 0)

    nin_got.wait()
    nin_t[...] = nin_ref[...].T
    proj_got.wait()
    lse_got.wait()
    head = 64
    lane = lax.broadcasted_iota(jnp.int32, (1, 128), 1)
    is_low = lane < head
    factor = 1.0 / math.sqrt(head)
    lane_wide = lax.broadcasted_iota(jnp.int32, (rows, 128), 1)
    keep = (is_low.astype(low), (lane >= head).astype(low))

    def pair(p, carry):
        base = lax.div(p, 2) * (3 * quarter) + lax.rem(p, 2) * 128
        q_at = pl.ds(pl.multiple_of(base, 128), 128)
        k_at = pl.ds(pl.multiple_of(base + quarter, 128), 128)
        v_at = pl.ds(pl.multiple_of(base + 2 * quarter, 128), 128)
        here = pl.ds(pl.multiple_of(p * 128, 128), 128)
        q2, k2, v2, do2 = proj_ref[:, q_at], proj_ref[:, k_at], proj_ref[:, v_at], gatt[:, here]
        lses = lse_ref[...]
        found = []
        for i in range(2):
            scores = dot(q2 * keep[i], k2, NT) * factor
            scores = jnp.where(mask[...] > 0, scores, NEGATIVE)
            lse = jnp.sum(jnp.where(lane_wide == 2 * p + i, lses, 0.0), axis=1, keepdims=True)
            prob = jnp.exp(scores - lse)
            grad_prob = dot(do2 * keep[i], v2, NT)
            inner = jnp.sum(prob * grad_prob, axis=1, keepdims=True)
            ds = (prob * (grad_prob - inner) * factor).astype(low)
            found.append(
                (dot(ds, k2), dot(ds, q2, TN), dot(prob.astype(low), do2, TN))
            )
        for where, a, b in zip((q_at, k_at, v_at), *found):
            dproj[:, where] = jnp.where(is_low, a, b).astype(low)
        accs[4, :, here] = eights(dproj[:, q_at].astype(f32))
        accs[5, :, here] = eights(dproj[:, v_at].astype(f32))
        return carry

    def wgrad(j):
        start, size = spans[j]
        cols = pl.ds((j - 1) * size, size)

        def one(k, carry):
            part = pl.ds(pl.multiple_of(k * (width // nz), width // nz), width // nz)
            block = dot(nin_t[part], dproj[:, cols]).astype(low)
            w_part[k, :, :, :, :, pl.ds(start, size)] = block.reshape(2, 2, 2, share, size)
            return carry

        lax.fori_loop(0, nz, one, 0)
        w_zero(j)

    def gni_block(k, carry):
        part = pl.ds(pl.multiple_of(k * quarter, quarter), quarter)
        gni[:, part] = dot(dproj[...], qkv_ref[part], NT)
        return carry

    def tokens_back(k, carry):
        part = pl.ds(pl.multiple_of(k * step, step), step)
        normed, inverse = centered(tok_ref[part].astype(f32))
        grad = gni[part]
        gmid[part] = gmid[part] + centered_back(grad * vec_ref[0:1], normed, inverse)
        accs[0] += eights(grad * normed)
        accs[3] += eights(grad)
        return carry

    part_z = width // nz
    chain = {}

    def lanes(which):
        return pl.ds(pl.multiple_of(which * part_z, 128), part_z)

    def small_start():
        for j in range(16):
            small[j : j + 1] = jnp.sum(accs[j], axis=0, keepdims=True)
        spot = lax.broadcasted_iota(jnp.int32, (1, width), 1)
        tile = jnp.zeros((1, 128), f32)
        for h in range(HEADS):
            inside = jnp.logical_and(spot >= h * head, spot < (h + 1) * head)
            found = jnp.sum(jnp.where(inside, small[10:11], 0.0), axis=1, keepdims=True)
            tile = jnp.where(lane == h, found, tile)
        small[11:12] = jnp.concatenate([tile] * (width // 128), axis=1)
        chain["z"] = [
            sends.start(small.at[:, lanes(others[k])], small_far.at[k], peer)
            for k, peer in enumerate(peers)
        ]

    def small_second():
        total = small[:, lanes(z)]
        for k in range(nz - 1):
            chain["z"][k].wait_recv()
            total = total + small_far[k]
        small_y[...] = total
        other = small_y.at[:, pl.ds(pl.multiple_of((1 - y) * 128, 128), 128)]
        chain["y"] = sends.start(other, small_got.at[0], to_y)

    def small_third():
        chain["y"].wait_recv()
        small_half[0] = small_y[:, pl.ds(pl.multiple_of(y * 128, 128), 128)] + small_got[0]
        chain["x"] = sends.start(small_half.at[0], small_got.at[1], to_x)

    def small_fourth():
        chain["x"].wait_recv()
        small_half[1] = small_half[0] + small_got[1]
        chain["c"] = sends.start(small_half.at[1], small_got.at[2], to_c)

    def small_last():
        chain["c"].wait_recv()
        total = small_half[1] + small_got[2]
        scale_out[...] = jnp.broadcast_to(total[11:12], (8, 128))
        ours = pl.ds(pl.multiple_of((2 * x + c) * share, share), share)
        turned[...] = jnp.concatenate([total, jnp.zeros((112, 128), f32)], axis=0).T
        mine = jnp.concatenate([turned[ours], jnp.zeros((128 - share, 128), f32)], axis=0).T
        gains_out[...] = mine[0:3, :share]
        biases_out[...] = mine[3:10, :share]

    puts = []

    def far_last():
        for copy in far:
            copy.wait_recv()
        own1_got.wait()
        own2_got.wait()
        late = pl.ds(fc1_at.shape[1] - got1.shape[2], got1.shape[2])
        own2, unit = got2[nz - 1].astype(f32), unit_ref[...]
        for k in range(nz - 1):
            fc1_at[:, late] += got1[k].astype(f32)
            own2 = own2 + got2[k].astype(f32)
            unit = unit + got_unit[k]
        fc2_at[...] = own2
        unit_out[...] = unit
        puts.append(fetch(fc1_at, fc1_out))
        puts.append(fetch(fc2_at, fc2_out))

    def pairs(first, last):
        lax.fori_loop(first, last, pair, 0)

    def gni_all():
        qkv_got.wait()
        lax.fori_loop(0, 4, gni_block, 0)

    def tokens_all():
        tok_got.wait()
        lax.fori_loop(0, rows // step, tokens_back, 0)
        puts.append(fetch(gmid, token_out))

    ffn_one(2)
    w_step1(0)
    pairs(0, 1)
    pairs(1, 2)
    wgrad(1)
    ffn_two(1)
    pairs(2, 3)
    w_step1(1)
    ffn_two(2)
    pairs(3, 4)
    wgrad(2)
    w_step2(0)
    pairs(4, 5)
    w_step1(2)
    pairs(5, 6)
    wgrad(3)
    w_step2(1)
    w_step3(0)
    pairs(6, 7)
    w_step1(3)
    pairs(7, 8)
    wgrad(4)
    w_step2(2)
    gni_all()
    w_step3(1)
    w_step1(4)
    tokens_all()
    small_start()
    w_step2(3)
    w_step3(2)
    small_second()
    w_step2(4)
    ffn_one(3)
    w_step3(3)
    small_third()
    ffn_three(0)
    ffn_three(1)
    ffn_three(2)
    w_step4(0)
    w_step3(4)
    ffn_two(3)
    small_fourth()
    small_last()
    w_step4(1)
    w_step4(2)
    w_step4(3)
    far_last()
    ffn_three(3)
    w_step4(4)
    for put in puts:
        put.wait()
    sends.finish()


def back(nz, *operands):
    gnm, ffn_part, ffn_first, late, fc1, fc2, unit, proj, att, lse, branch = operands[:11]
    middle, scaled, nin, qkv, out, vec = operands[11:17]
    rows, width = middle.shape
    share = width // (nz * 8)
    columns = proj.shape[1] + width
    low, f32 = jnp.bfloat16, jnp.float32
    sds = jax.ShapeDtypeStruct
    fc2_own = (fc2.shape[0], fc2.shape[1] // nz)
    count = 96 + 8 * nz
    specs = [ANY] * 6 + [IN_VMEM] + [ANY] * 9 + [IN_VMEM] + [ANY] * 2
    specs.append(pl.BlockSpec(memory_space=pltpu.SMEM))
    return pl.pallas_call(
        functools.partial(back_kernel, nz),
        name="back",
        out_shape=(
            sds((rows, width), low),
            sds((rows, width), f32),
            sds((share, columns), f32),
            sds((3, share), f32),
            sds((7, share), f32),
            sds((8, 128), f32),
            sds(fc1.shape, f32),
            sds(fc2_own, f32),
            sds(unit.shape, f32),
        ),
        in_specs=specs,
        out_specs=[ANY] * 3 + [IN_VMEM] * 3 + [ANY] * 2 + [IN_VMEM],
        scratch_shapes=[
            pltpu.VMEM((2, 2, rows, width), low),
            pltpu.VMEM((2, 2, rows, width), low),
            pltpu.VMEM((rows, width), low),
            pltpu.VMEM((nz - 1, fc1.shape[0], late.shape[1]), low),
            pltpu.VMEM((nz,) + fc2_own, low),
            pltpu.VMEM((nz - 1,) + unit.shape, f32),
            pltpu.VMEM((nz, 2, 2, 2, share, columns), low),
            pltpu.VMEM((nz, 2, 2, share, columns), low),
            pltpu.VMEM((nz, 2, 2, share, columns), low),
            pltpu.VMEM((nz, 2, share, columns), low),
            pltpu.VMEM((nz, share, columns), low),
            pltpu.VMEM((nz - 1, share, columns), low),
            pltpu.VMEM((rows, width), low),
            pltpu.VMEM((rows, width), f32),
            pltpu.VMEM((rows, width), low),
            pltpu.VMEM((rows, width), f32),
            pltpu.VMEM((rows, 3 * width), low),
            pltpu.VMEM((width, rows), low),
            pltpu.VMEM((rows, rows), f32),
            pltpu.VMEM((16, 8, width), f32),
            pltpu.VMEM((16, width), f32),
            pltpu.VMEM((nz - 1, 16, width // nz), f32),
            pltpu.VMEM((16, width // nz), f32),
            pltpu.VMEM((3, 16, 128), f32),
            pltpu.VMEM((3, 16, 128), f32),
            pltpu.VMEM((128, 128), f32),
            pltpu.VMEM((rows, width), low),
            pltpu.VMEM((share, columns), f32),
            pltpu.VMEM(fc1.shape, f32),
            pltpu.VMEM(fc2_own, f32),
            pltpu.VMEM((rows, width), f32),
            pltpu.VMEM(proj.shape, low),
            pltpu.VMEM((rows, width), f32),
            pltpu.VMEM(lse.shape, f32),
            pltpu.VMEM((rows, width), f32),
            pltpu.VMEM((rows, width), f32),
            pltpu.VMEM((rows, width), low),
            pltpu.VMEM((rows, width), low),
            pltpu.VMEM(qkv.shape, low),
            pltpu.VMEM(out.shape, low),
            pltpu.VMEM((rows, width), low),
            pltpu.VMEM((rows, width), low),
            pltpu.SemaphoreType.DMA((64,)),
            pltpu.SemaphoreType.DMA((count,)),
            pltpu.SemaphoreType.DMA((count,)),
        ],
        compiler_params=pltpu.CompilerParams(
            collective_id=3, has_side_effects=True, vmem_limit_bytes=63 * 2**20
        ),
    )(*operands)


def finish_kernel(
    mixed,
    token,
    weight,
    fc1,
    fc2,
    gains,
    biases,
    scale,
    unit,
    mixed_out,
    token_out,
    qkv_out,
    out_out,
    fc1_out,
    fc2_out,
    gains_out,
    biases_out,
    scale_out,
    gain_out,
    shift_out,
    mixed_at,
    token_at,
    weight_at,
    fc1_at,
    fc2_at,
    in_sems,
    out_sems,
):
    columns = qkv_out.shape[1]
    moves = (
        (token, token_at, ((token_at, token_out),)),
        (
            weight,
            weight_at,
            (
                (weight_at.at[:, pl.ds(0, columns)], qkv_out),
                (weight_at.at[:, pl.ds(columns, out_out.shape[1])], out_out),
            ),
        ),
        (mixed, mixed_at, ((mixed_at, mixed_out),)),
        (fc1, fc1_at, ((fc1_at, fc1_out),)),
        (fc2, fc2_at, ((fc2_at, fc2_out),)),
    )
    reads, writes = [], []
    for k, (src, here, _) in enumerate(moves):
        reads.append(pltpu.make_async_copy(src, here, in_sems.at[k]))
        reads[-1].start()
    gains_out[...] = gains[...]
    biases_out[...] = biases[...]
    scale_out[...] = scale[0:1, : scale_out.shape[1]]
    gain_out[...] = unit[0:1]
    shift_out[0:1] = unit[1:2]
    shift_out[1:2] = unit[2:3]
    for read, (_, _, outs) in zip(reads, moves):
        read.wait()
        for src, dst in outs:
            writes.append(pltpu.make_async_copy(src, dst, out_sems.at[len(writes)]))
            writes[-1].start()
    for write in writes:
        write.wait()


def finish(mixed, token, weight, gains, biases, scale, fc1, fc2, unit):
    share, columns = weight.shape
    width, units = token.shape[1], unit.shape[1]
    f32 = jnp.float32
    shapes = (
        (mixed.shape, mixed.dtype),
        (token.shape, f32),
        ((share, columns - width), f32),
        ((share, width), f32),
        (fc1.shape, f32),
        (fc2.shape, f32),
        (gains.shape, f32),
        (biases.shape, f32),
        ((1, HEADS), f32),
        ((1, units), f32),
        ((2, units), f32),
    )
    return pl.pallas_call(
        finish_kernel,
        name="finish",
        out_shape=tuple(jax.ShapeDtypeStruct(shape, kind) for shape, kind in shapes),
        in_specs=[ANY] * 5 + [IN_VMEM] * 4,
        out_specs=[ANY] * 6 + [IN_VMEM] * 5,
        scratch_shapes=[
            pltpu.VMEM(mixed.shape, mixed.dtype),
            pltpu.VMEM(token.shape, f32),
            pltpu.VMEM(weight.shape, f32),
            pltpu.VMEM(fc1.shape, f32),
            pltpu.VMEM(fc2.shape, f32),
            pltpu.SemaphoreType.DMA((5,)),
            pltpu.SemaphoreType.DMA((6,)),
        ],
        compiler_params=pltpu.CompilerParams(vmem_limit_bytes=63 * 2**20),
    )(mixed, token, weight, fc1, fc2, gains, biases, scale, unit)


def fused(
    nz,
    tokens,
    out_grad,
    doc_lengths,
    w_qkv,
    w_out,
    gains,
    biases,
    head_scale,
    w_fc1,
    w_fc2,
    mid_gain,
    ffn_biases,
):
    (
        qkv_full,
        out_full,
        vec,
        proj,
        att,
        lse,
        branch,
        middle,
        nin,
        scaled,
        ffn_part,
        ffn_first,
        fc2_part,
        fc1_late,
        gnm,
        fc1_own,
        unit_sums,
    ) = fore(
        nz,
        tokens,
        out_grad,
        doc_lengths,
        w_qkv,
        w_out,
        gains,
        biases,
        head_scale,
        w_fc1,
        w_fc2,
        mid_gain[None],
        ffn_biases,
    )
    model_width = tokens.shape[1]
    (
        mixed,
        token_grad,
        weight_grad,
        gains_grad,
        biases_grad,
        scale,
        fc1_grad,
        fc2_grad,
        unit_sums,
    ) = back(
        nz,
        gnm,
        ffn_part,
        ffn_first,
        fc1_late,
        fc1_own,
        fc2_part,
        unit_sums,
        proj,
        att,
        lse,
        branch,
        middle,
        scaled,
        nin,
        qkv_full.reshape(model_width, -1),
        out_full.reshape(model_width, -1),
        vec,
        out_grad,
        tokens,
        doc_lengths,
    )
    mixed, token_grad, qkv, out, fc1, fc2, gains_grad, biases_grad, scale, gain, shift = finish(
        mixed,
        token_grad,
        weight_grad,
        gains_grad,
        biases_grad,
        scale,
        fc1_grad,
        fc2_grad,
        unit_sums,
    )
    return (
        mixed,
        token_grad,
        qkv,
        out,
        gains_grad.T,
        biases_grad.T,
        scale[0],
        fc1,
        fc2,
        gain[0],
        shift,
    )


def layer(nz, nt, tokens, out_grad, doc_lengths, w_qkv, *rest):
    if nz == 4 and nt == 8 and w_qkv.shape[0] % 16 == 0:
        return fused(nz, tokens, out_grad, doc_lengths, w_qkv, *rest)
    return plain(tokens, out_grad, doc_lengths, w_qkv, *rest)


def solution(mesh):
    return jax.shard_map(
        functools.partial(layer, mesh.shape["dp"], mesh.shape["tensor"]),
        mesh=mesh,
        in_specs=(
            P(("dp", "tensor"), None),
            P(("dp", "tensor"), None),
            P(("dp", "tensor"), None),
            P(("dp", "tensor"), None),
            P(("dp", "tensor"), None),
            P(("dp", "tensor"), None),
            P(("dp", "tensor"), None),
            P(),
            P("dp", "tensor"),
            P("tensor", "dp"),
            P("tensor"),
            P(None, "tensor"),
        ),
        out_specs=(
            P(("dp", "tensor"), None),
            P(("dp", "tensor"), None),
            P(("dp", "tensor"), None),
            P(("dp", "tensor"), None),
            P(("dp", "tensor"), None),
            P(("dp", "tensor"), None),
            P(),
            P("dp", "tensor"),
            P("tensor", "dp"),
            P("tensor"),
            P(None, "tensor"),
        ),
        check_vma=False,
    )
```
